32 devices in a mesh: dp: 4 (over y, x), seq: 8 (over z, core).
Axes of the slice: x: 2, y: 2, z: 4, core: 2. Of those that a mesh axis runs over, the one named last changes fastest.
Arguments:
- caption_states: bfloat16 [4, 64, 4096], P('dp', None, 'seq'), may hold values from -1600 to 1600
- caption_gain: float32 [4096], P('seq'), may hold values from 0.25 to 2.5
- text_proj: bfloat16 [4096, 4608], P('seq'), may hold values from -0.09375 to 0.09375
- caption_len: int32 [4], P('dp'), may hold values from 1 to 64, 160 in all
- slot_source: int32 [4, 64], P('dp'), may hold values from 0 to 63, each once within a row
- query_gain: float32 [128], replicated, may hold values from 0.5 to 2
- key_gain: float32 [128], replicated, may hold values from 0.5 to 2
- image_q: bfloat16 [4, 1024, 1536], P('dp', 'seq'), may hold values from -34 to 34
- image_k: bfloat16 [4, 1024, 1536], P('dp', 'seq'), may hold values from -6.5 to 6.5
- image_v: bfloat16 [4, 1024, 1536], P('dp', 'seq'), may hold values from -6 to 6
- out_weight: bfloat16 [3072, 1536], replicated, may hold values from -0.15625 to 0.15625
- gate: float32 [4, 3072], P('dp'), may hold values from -4 to 4
- d_out: bfloat16 [4, 1024, 3072], P('dp', 'seq'), may hold values from -5 to 5
Outputs:
- image_out: bfloat16 [4, 1024, 3072], P('dp', 'seq')
- text_attn: bfloat16 [4, 64, 1536], P('dp', 'seq')
- d_attn: bfloat16 [4, 1024, 1536], P('dp', 'seq')
- grad_wo: float32 [3072, 1536], P(('dp', 'seq'))
- grad_gate: float32 [4, 3072], P('dp', 'seq')
The draws below stay inside these ranges and needn't reach their ends.
Inputs may be any that keep to these rules, and one draw needn't show every extreme that they name: `caption_len`: caption lengths in tokens; the longest is 64. `slot_source`: each row is a permutation: every caption row of the sequence sits in exactly one slot; slots whose row is not below the caption's length are padding.
All inputs are finite; a program needn't handle non-finite values. No bound on the sum of `caption_len` on one device may be relied on, other than what follows from the above.
Results may differ from the reference program's by a relative error of at most 0.0095.
Values may be sent and summed in bfloat16 or wider, within the bound.
No kernel may reach another device: no remote copies, remote signals or barrier semaphores. Data moves between devices by JAX's collectives and lax.ppermute only.
A program may use at most 128 MiB of HBM per device.

```python
import math
import jax
import jax.numpy as jnp
import numpy as np
from jax import lax

D = 3072
HD = 128
DT5 = 4096
TXT_DEV = 8
INNER = 1536
IMG_LEN = 1024
TXT_TOTAL = 64
BATCH = 4
N_DP = 4
N_SEQ = 8


def draw_caption_states(key, part):
    key_base = jax.random.fold_in(key, 1)
    key_cols = jax.random.fold_in(key, 2)
    key_rows = jax.random.fold_in(key, 3)
    shape = (BATCH, TXT_TOTAL, DT5)
    position = jnp.arange(DT5, dtype=jnp.float32) / (DT5 - 1)
    base = jnp.clip(jax.random.normal(key_base, shape, jnp.float32), -4.0, 4.0)
    rising = 3.0 ** position
    column_scale = rising * jnp.exp(math.log(10.0) * jax.random.uniform(key_cols, (DT5,), jnp.float32))
    row_scale = jnp.exp(math.log(10.0) * jax.random.uniform(key_rows, (BATCH, TXT_TOTAL, 1), jnp.float32))
    return (base * column_scale * row_scale).astype(jnp.bfloat16)


def paired_queries_keys(key):
    base_key = jax.random.fold_in(key, 11)
    query_key = jax.random.fold_in(base_key, 1)
    key_key = jax.random.fold_in(base_key, 2)
    shape = (BATCH, IMG_LEN, INNER)
    queries = 1.6 * jnp.clip(jax.random.normal(query_key, shape, jnp.float32), -4.0, 4.0)
    key_rows = 1.6 * jnp.clip(jax.random.normal(key_key, shape, jnp.float32), -4.0, 4.0)
    return (queries, key_rows)


def draw_image_q(key, part):
    queries, key_rows = paired_queries_keys(key)
    return queries.astype(jnp.bfloat16)


def draw_image_k(key, part):
    queries, key_rows = paired_queries_keys(key)
    return key_rows.astype(jnp.bfloat16)


def raised(entries, own_key, source, target, parts, factor):
    owner, partner = [(jnp.arange(entries.shape[axis_at]) // (entries.shape[axis_at] // parts)).reshape([-1 if axis == axis_at else 1 for axis in range(entries.ndim)]) for axis_at in (source, target)]
    chosen = jax.random.permutation(own_key, parts)[partner]
    strong = (owner == chosen) | (owner == (partner + parts // 2) % parts)
    return jnp.where(strong, factor * entries, entries)


def levels(key, extent, shards, least, high):
    def one(dim, parts):
        heights = jax.random.uniform(jax.random.fold_in(jax.random.fold_in(key, 6), dim), (parts,), jnp.float32, least / len(shards), high / len(shards))
        return jnp.repeat(jnp.exp(heights), extent[dim] // parts).reshape((-1,) + (1,) * (len(extent) - dim - 1))

    loudness = one(*shards[0])
    for cut in shards[1:]:
        loudness = loudness * one(*cut)
    return loudness


def length_profile(number_of, total, reach, lean):
    portions = [(1 << 20) // math.isqrt(grade ** lean) + 1 for grade in range(2, number_of + 1)]
    surplus, holding = total - reach - (number_of - 1), [1] * (number_of - 1)
    while surplus > 0:
        candidates = [i for i in range(number_of - 1) if holding[i] < reach]
        whole, remaining = sum([portions[i] for i in candidates]), surplus
        for i in candidates:
            more = min(reach - holding[i], max(1, remaining * portions[i] // whole), surplus)
            holding[i] = holding[i] + more
            surplus = surplus - more
    return np.array([reach] + holding)


def ragged_sizes(stream_key, count, total, limit, slope):
    if count == 2:
        one = jax.random.randint(stream_key, (), max(1, total - limit), min(limit, total - 1) + 1)
        return jnp.stack([one, total - one])
    lengths = jnp.asarray(length_profile(count, total, limit, slope), jnp.int32)
    couples = (count - 1) // 2
    donor, receiver = lengths[1:1 + 2 * couples:2], lengths[2:2 + 2 * couples:2]
    room = jnp.minimum(donor - 1, limit - receiver)
    shifted = jax.random.randint(jax.random.fold_in(stream_key, 1), (couples,), 0, 1 << 20) % (room + 1)
    lengths = lengths.at[1:1 + 2 * couples:2].set(donor - shifted).at[2:2 + 2 * couples:2].set(receiver + shifted)
    return lengths[jax.random.permutation(jax.random.fold_in(stream_key, 2), count)]


def scatter_about(own_key, shape, deviation, most, shards=(), kind=jnp.bfloat16):
    values = deviation * jax.random.normal(own_key, shape, jnp.float32)
    if shards:
        values = values * levels(own_key, shape, shards, -0.22, 0.18)
    return jnp.clip(values, -most, most).astype(kind)


def noise_with(rng, extent, spread, limit, pieces, heavy, held_as=jnp.bfloat16):
    result = spread * jax.random.normal(rng, extent, jnp.float32)
    if pieces:
        result = result * levels(rng, extent, pieces, -0.22, 0.18)
    return jnp.clip(raised(result, jax.random.fold_in(rng, 3), *heavy), -limit, limit).astype(held_as)


def setup_inputs(seed: int = 0) -> dict:
    seeds = jax.random.split(jax.random.key(seed), 14)
    caption_states = draw_caption_states(jax.random.fold_in(seeds[13], 71), 0)
    caption_gain = jnp.clip(jnp.exp(math.log(2.5) - 2.3025851 * jax.random.uniform(seeds[1], (DT5,), jnp.float32) ** levels(seeds[1], (DT5,), ((0, 8),), -0.2, 0.2)), 0.25, 2.5)
    text_proj = scatter_about(seeds[2], (DT5, 3 * INNER), DT5 ** -0.5, 0.09375, ((0, 8),))
    caption_len = ragged_sizes(seeds[3], BATCH, N_DP * TXT_DEV * N_SEQ * 5 // 8, TXT_DEV * N_SEQ, 1).astype(jnp.int32)
    slot_source = jax.vmap(lambda own: jax.random.permutation(own, TXT_TOTAL))(jax.random.split(seeds[4], BATCH)).reshape((BATCH, TXT_TOTAL)).astype(jnp.int32)
    query_gain = jnp.clip(jnp.exp(jax.random.uniform(seeds[5], (HD,), jnp.float32, math.log(0.5), math.log(2.0))), 0.5, 2.0)
    key_gain = jnp.clip(jnp.exp(jax.random.uniform(seeds[6], (HD,), jnp.float32, math.log(0.5), math.log(2.0))), 0.5, 2.0)
    image_q = draw_image_q(jax.random.fold_in(seeds[13], 71), 0)
    image_k = draw_image_k(jax.random.fold_in(seeds[13], 71), 0)
    image_v = scatter_about(seeds[9], (BATCH, IMG_LEN, INNER), 1.0, 6.0, ((0, 4), (1, 8)))
    out_weight = scatter_about(seeds[10], (D, INNER), INNER ** -0.5, 0.15625)
    gate = scatter_about(seeds[11], (BATCH, D), 1.0, 4.0, ((0, 4),), jnp.float32)
    d_out = noise_with(seeds[12], (BATCH, IMG_LEN, D), (16 * (N_DP * IMG_LEN) ** -0.5), 5.0, ((0, 4), (1, 8)), (1, 2, 8, 2.0))
    return {"caption_states": caption_states, "caption_gain": caption_gain, "text_proj": text_proj, "caption_len": caption_len, "slot_source": slot_source, "query_gain": query_gain, "key_gain": key_gain, "image_q": image_q, "image_k": image_k, "image_v": image_v, "out_weight": out_weight, "gate": gate, "d_out": d_out}


def head_norm(values_in, gain_vec):
    shaped = values_in.reshape(values_in.shape[:-1] + (-1, gain_vec.shape[0]))
    normed = shaped * lax.rsqrt(lax.optimization_barrier(jnp.mean(shaped * shaped, axis=-1, keepdims=True)) + 1e-06) * gain_vec
    return normed.reshape(values_in.shape)

def reference(caption_states, caption_gain, text_proj, caption_len, slot_source, query_gain, key_gain, image_q, image_k, image_v, out_weight, gate, d_out):
    batch_count, slot_total, enc_width = caption_states.shape
    inner_width = image_q.shape[2]
    head_size = query_gain.shape[0]
    image_rows = image_q.shape[1]
    model_width = out_weight.shape[0]
    states = caption_states.astype(jnp.float32)
    scaled = (states * caption_gain).astype(jnp.bfloat16)
    raw = jnp.dot(scaled.reshape(-1, enc_width), text_proj, preferred_element_type=jnp.float32).reshape(batch_count, slot_total, -1)
    rate = lax.rsqrt(lax.optimization_barrier(jnp.sum(states * states, axis=-1)) / enc_width + 1e-06)
    proj = raw * rate[..., None]
    proj = jnp.take_along_axis(proj, slot_source.astype(jnp.int32)[..., None], axis=1)
    valid = slot_source < caption_len[:, None]
    text_q = head_norm(proj[..., :inner_width], query_gain).astype(jnp.bfloat16)
    text_k = head_norm(proj[..., inner_width:2 * inner_width], key_gain).astype(jnp.bfloat16)
    text_v = proj[..., 2 * inner_width:].astype(jnp.bfloat16)
    queries = jnp.concatenate([image_q, text_q], axis=1)
    key_rows = jnp.concatenate([image_k, text_k], axis=1)
    value_rows = jnp.concatenate([image_v, text_v], axis=1)
    allowed = jnp.concatenate([jnp.ones((batch_count, image_rows), dtype=jnp.bool_), valid], axis=1)

    def attend_sequence(packed):
        query_seq, key_seq, value_seq, allowed_seq = packed
        joint = query_seq.shape[0]
        query_heads = jnp.transpose(query_seq.astype(jnp.float32).reshape(joint, -1, head_size), (1, 0, 2))
        key_heads = jnp.transpose(key_seq.astype(jnp.float32).reshape(joint, -1, head_size), (1, 0, 2))
        value_heads = jnp.transpose(value_seq.astype(jnp.float32).reshape(joint, -1, head_size), (1, 0, 2))

        def one_head(head_pack):
            query_one, key_one, value_one = head_pack
            scores = jnp.dot(query_one, key_one.T, preferred_element_type=jnp.float32) * head_size ** (-0.5)
            scores = jnp.where(allowed_seq[None, :], scores, -1e+30)
            row_max = lax.optimization_barrier(jnp.max(scores, axis=-1, keepdims=True))
            probs = jnp.where(allowed_seq[None, :], jnp.exp(scores - row_max), 0.0)
            denom = lax.optimization_barrier(jnp.sum(probs, axis=-1))
            probs_low = lax.optimization_barrier(probs.astype(jnp.bfloat16)).astype(jnp.float32)
            summed = jnp.dot(probs_low, value_one, preferred_element_type=jnp.float32)
            return summed / denom[:, None]
        output = lax.map(one_head, (query_heads, key_heads, value_heads))
        return jnp.transpose(output, (1, 0, 2)).reshape(joint, inner_width).astype(jnp.bfloat16)
    attn = lax.map(attend_sequence, (queries, key_rows, value_rows, allowed))
    image_attn = attn[:, :image_rows]
    text_attn = jnp.where(valid[..., None], attn[:, image_rows:], jnp.zeros((), jnp.bfloat16))
    projected = jnp.dot(image_attn.reshape(-1, inner_width), out_weight.T, preferred_element_type=jnp.float32).reshape(batch_count, image_rows, model_width)
    image_out = (gate[:, None, :] * projected).astype(jnp.bfloat16)
    cotangent = d_out.astype(jnp.float32)
    gated_grad = (gate[:, None, :] * cotangent).astype(jnp.bfloat16)
    d_attn = jnp.dot(gated_grad.reshape(-1, model_width), out_weight, preferred_element_type=jnp.float32).reshape(batch_count, image_rows, inner_width).astype(jnp.bfloat16)
    grad_wo = jnp.dot(gated_grad.reshape(-1, model_width).T, image_attn.reshape(-1, inner_width), preferred_element_type=jnp.float32)
    grad_gate = lax.optimization_barrier(jnp.sum(projected * cotangent, axis=1))
    return (image_out, text_attn, d_attn, grad_wo, grad_gate)
```

```python
import math
import functools
import jax
import jax.numpy as jnp
from jax import lax
from jax.experimental import pallas as pl
from jax.experimental.pallas import tpu as pltpu
from jax.sharding import PartitionSpec as P

DT5 = 4096
CORES = 2
GROUPS = 4

eps_norm = 1e-06
f32 = jnp.float32
bf16 = jnp.bfloat16


def head_norm(values_in, gain_vec):
    shaped = values_in.reshape(values_in.shape[0], -1, gain_vec.shape[0])
    normed = (
        shaped * lax.rsqrt(jnp.mean(shaped * shaped, axis=-1, keepdims=True) + eps_norm) * gain_vec
    )
    return normed.reshape(values_in.shape).astype(bf16)


def attention_kernel(pieces, head_size, *refs):
    n_q, n_kv, n_tkv = pieces
    q_refs = refs[:n_q]
    tq_ref = refs[n_q]
    kv_refs = refs[n_q + 1 : n_q + 1 + n_kv]
    tkv_refs = refs[n_q + 1 + n_kv : n_q + 1 + n_kv + n_tkv]
    bias_ref = refs[n_q + 1 + n_kv + n_tkv]
    out_refs = refs[n_q + 2 + n_kv + n_tkv :]
    width = q_refs[0].shape[1]
    factor = head_size ** (-0.5) * math.log2(math.e)
    bias = bias_ref[...]
    for head in range(width // head_size):
        cols = slice(head * head_size, (head + 1) * head_size)
        vcols = slice(width + head * head_size, width + (head + 1) * head_size)
        keys = jnp.concatenate([r[:, cols] for r in kv_refs], axis=0)
        values = jnp.concatenate([r[:, vcols] for r in kv_refs], axis=0)
        tkeys = jnp.concatenate([r[:, cols] for r in tkv_refs], axis=0)
        tvalues = jnp.concatenate([r[:, vcols] for r in tkv_refs], axis=0)
        for q_ref, out_ref in zip(tuple(q_refs) + (tq_ref,), out_refs):
            q = q_ref[:, cols]
            nt = (((1,), (1,)), ((), ()))
            s_img = lax.dot_general(q, keys, nt, preferred_element_type=f32)
            s_txt = lax.dot_general(q, tkeys, nt, preferred_element_type=f32) + bias
            top = jnp.maximum(
                jnp.max(s_img, axis=1, keepdims=True), jnp.max(s_txt, axis=1, keepdims=True)
            )
            p_img = jnp.exp2((s_img - top) * factor)
            p_txt = jnp.exp2((s_txt - top) * factor)
            total = jnp.sum(p_img, axis=1, keepdims=True) + jnp.sum(p_txt, axis=1, keepdims=True)
            acc = jnp.dot(p_img.astype(bf16), values, preferred_element_type=f32)
            acc = acc + jnp.dot(p_txt.astype(bf16), tvalues, preferred_element_type=f32)
            out_ref[:, cols] = (acc / total).astype(bf16)


def attention(queries, text_q, keyvals, text_keyvals, bias, head_size):
    args = tuple(queries) + (text_q,) + tuple(keyvals) + tuple(text_keyvals) + (bias,)
    outs = [jax.ShapeDtypeStruct(q.shape, bf16) for q in tuple(queries) + (text_q,)]
    vmem = pl.BlockSpec(memory_space=pltpu.VMEM)
    rows = sum(q.shape[0] for q in queries) + text_q.shape[0]
    cols = sum(k.shape[0] for k in keyvals) + sum(k.shape[0] for k in text_keyvals)
    width = text_q.shape[1]
    return pl.pallas_call(
        functools.partial(
            attention_kernel, (len(queries), len(keyvals), len(text_keyvals)), head_size
        ),
        out_shape=outs,
        in_specs=[vmem] * len(args),
        out_specs=[vmem] * len(outs),
        compiler_params=pltpu.CompilerParams(vmem_limit_bytes=32 * 1024 * 1024),
        cost_estimate=pl.CostEstimate(
            flops=4 * rows * cols * width,
            bytes_accessed=4 * (rows + cols) * width,
            transcendentals=rows * cols * width // head_size,
        ),
    )(*args)


def grad_kernel(n_pieces, *refs):
    left = refs[0]
    pieces = refs[1 : 1 + n_pieces]
    out = refs[1 + n_pieces]
    depth = pieces[0].shape[0]
    block = 256
    for start in range(0, out.shape[1], block):
        cols = slice(start, start + block)
        right = jnp.concatenate([p[:, cols] for p in pieces], axis=0)
        out[:, cols] = jnp.dot(left[...], right, preferred_element_type=f32).astype(bf16)


def grad_product(left, pieces):
    vmem = pl.BlockSpec(memory_space=pltpu.VMEM)
    rows, depth, width = left.shape[0], left.shape[1], pieces[0].shape[1]
    return pl.pallas_call(
        functools.partial(grad_kernel, len(pieces)),
        out_shape=jax.ShapeDtypeStruct((rows, width), bf16),
        in_specs=[vmem] * (1 + len(pieces)),
        out_specs=vmem,
        compiler_params=pltpu.CompilerParams(vmem_limit_bytes=32 * 1024 * 1024),
        cost_estimate=pl.CostEstimate(
            flops=2 * rows * depth * width,
            bytes_accessed=2 * (rows * depth + depth * width + rows * width),
            transcendentals=0,
        ),
    )(left, *pieces)


def on_device(
    caption_states,
    caption_gain,
    text_proj,
    caption_len,
    slot_source,
    query_gain,
    key_gain,
    image_q,
    image_k,
    image_v,
    out_weight,
    gate,
    d_out,
):
    n_dp = lax.axis_size("dp")
    n_seq = lax.axis_size("seq")
    G, C = GROUPS, CORES
    O = n_seq // (G * C)
    OC = O * C
    dp = lax.axis_index("dp")
    seq = lax.axis_index("seq")
    z = (seq // C) % G
    oc = (seq // (G * C)) * C + seq % C

    def place(oc_at, z_at):
        return ((oc_at // C) * G + z_at) * C + oc_at % C

    def to_z(x, k):
        perm = [(place(a, b), place(a, b ^ k)) for a in range(OC) for b in range(G)]
        return lax.ppermute(x, "seq", perm)

    def to_oc(x, j):
        perm = [(place(a, b), place(a ^ j, b)) for a in range(OC) for b in range(G)]
        return lax.ppermute(x, "seq", perm)

    def to_dp(x, k):
        return lax.ppermute(x, "dp", [(a, a ^ k) for a in range(n_dp)])

    def part(x, index, size, axis):
        return lax.dynamic_slice_in_dim(x, index * size, size, axis)

    slot_total = slot_source.shape[1]
    slot_local = slot_total // n_seq
    image_local = image_q.shape[1]
    inner_width = image_q.shape[2]
    model_width = out_weight.shape[0]
    head_size = query_gain.shape[0]
    gw = inner_width // G
    q_all, k_all, v_all = image_q[0], image_k[0], image_v[0]

    kv_own = [
        jnp.concatenate([part(k_all, z ^ k, gw, 1), part(v_all, z ^ k, gw, 1)], axis=1)
        for k in range(G)
    ]
    kv_near = [kv_own[0]] + [to_z(kv_own[k], k) for k in range(1, G)]
    q_own = [part(q_all, z ^ k, gw, 1) for k in range(G)]
    q_pieces = [q_own[0]] + [to_z(q_own[k], k) for k in range(1, G)]
    kv_pieces = list(kv_near)
    for j in range(1, OC):
        kv_pieces += [to_oc(p, j) for p in kv_near]

    sources = slot_source[0].reshape(O, G, C, slot_local)
    sources = jnp.transpose(sources, (0, 2, 1, 3)).reshape(-1)
    picked = jnp.take(caption_states[0], sources, axis=0).astype(f32)
    scaled_rows = (picked * caption_gain).astype(bf16)
    partial_proj = jnp.dot(scaled_rows, text_proj, preferred_element_type=f32)
    partial_squares = jnp.sum(picked * picked, axis=1, keepdims=True)
    usable = (sources < caption_len[0]).astype(jnp.int32).reshape(OC, G * slot_local)
    text_rows = G * slot_local

    def message(values, squares):
        high = lax.reduce_precision(squares, 8, 7)
        low = squares - high
        tail = jnp.concatenate(
            [high, low, jnp.zeros((squares.shape[0], 126), f32)], axis=1
        ).astype(bf16)
        return jnp.concatenate([values.astype(bf16), tail], axis=1)

    def opened(got):
        got = got.astype(f32)
        width = got.shape[1] - 128
        return got[:, :width], got[:, width : width + 1] + got[:, width + 1 : width + 2]

    chip_proj = part(partial_proj, oc, text_rows, 0)
    chip_squares = part(partial_squares, oc, text_rows, 0)
    for j in range(1, OC):
        sent = message(
            part(partial_proj, oc ^ j, text_rows, 0), part(partial_squares, oc ^ j, text_rows, 0)
        )
        more_proj, more_squares = opened(to_oc(sent, j))
        chip_proj = chip_proj + more_proj
        chip_squares = chip_squares + more_squares
    chip_proj = chip_proj.reshape(text_rows, 3, inner_width)

    def group_cols(index):
        return part(chip_proj, index, gw, 2).reshape(text_rows, 3 * gw)

    summed, squares = group_cols(z), chip_squares
    for k in range(1, G):
        more, more_squares = opened(to_z(message(group_cols(z ^ k), chip_squares), k))
        summed = summed + more
        squares = squares + more_squares
    normed = summed * lax.rsqrt(squares / DT5 + eps_norm)
    text_q = head_norm(normed[:, :gw], query_gain)
    text_k = head_norm(normed[:, gw : 2 * gw], key_gain)
    text_kv = jnp.concatenate([text_k, normed[:, 2 * gw :].astype(bf16)], axis=1)
    text_kvs = [text_kv] + [to_oc(text_kv, j) for j in range(1, OC)]
    usable_keys = jnp.concatenate([part(usable, oc ^ j, 1, 0) for j in range(OC)], axis=1)
    bias = jnp.where(usable_keys > 0, 0.0, -1e30).astype(f32)

    gate_row = gate[0]
    cotangent = d_out[0].astype(f32)
    gated_grad = (gate_row * cotangent).astype(bf16)
    R = model_width // (n_dp * n_seq)
    gg_t = gated_grad.T.reshape(n_dp, O, G, C, R, image_local)
    gg_t = jnp.transpose(gg_t, (0, 1, 3, 2, 4, 5)).reshape(n_dp, OC, G * R, image_local)
    gg_dp = []
    for k in range(n_dp):
        sel = lax.dynamic_index_in_dim(gg_t, dp ^ k, 0, keepdims=False)
        gg_dp.append(sel if k == 0 else to_dp(sel, k))
    gg_left = []
    for j in range(OC):
        sel = [lax.dynamic_index_in_dim(g, oc ^ j, 0, keepdims=False) for g in gg_dp]
        if j:
            sent = to_oc(jnp.stack(sel), j)
            sel = [sent[k] for k in range(n_dp)]
        gg_left += sel
    left = jnp.concatenate(gg_left, axis=1)
    d_attn = jnp.dot(gated_grad, out_weight, preferred_element_type=f32).astype(bf16)

    outs = attention(q_pieces, text_q, kv_pieces, text_kvs, bias, head_size)
    text_out = outs[-1]

    back = []
    for k in range(G):
        rows = jnp.concatenate([outs[k], part(text_out, z ^ k, slot_local, 0)], axis=0)
        back.append(rows if k == 0 else to_z(rows, k))
    attn = jnp.zeros((image_local + slot_local, inner_width), bf16)
    for k in range(G):
        attn = lax.dynamic_update_slice_in_dim(attn, back[k], (z ^ k) * gw, 1)
    image_attn = attn[:image_local]
    own_usable = part((slot_source[0] < caption_len[0]), seq, slot_local, 0)
    text_attn = jnp.where(own_usable[:, None], attn[image_local:], jnp.zeros((), bf16))

    attn_dp = [image_attn] + [to_dp(image_attn, k) for k in range(1, n_dp)]
    attn_pieces = list(attn_dp)
    for j in range(1, OC):
        attn_pieces += [to_oc(p, j) for p in attn_dp]

    projected = lax.dot_general(
        image_attn, out_weight, (((1,), (1,)), ((), ())), preferred_element_type=f32
    )
    image_out = (gate_row * projected).astype(bf16)
    gate_term = jnp.sum(projected * cotangent, axis=0)

    grad = grad_product(left, attn_pieces).reshape(G, R, inner_width)
    grad_wo = lax.dynamic_index_in_dim(grad, z, 0, keepdims=False).astype(f32)
    for k in range(1, G):
        sent = to_z(lax.dynamic_index_in_dim(grad, z ^ k, 0, keepdims=False), k)
        grad_wo = grad_wo + sent.astype(f32)

    gate_term = jnp.transpose(gate_term.reshape(O, G, C, -1), (0, 2, 1, 3)).reshape(OC, G, 1, -1)
    gate_chip = lax.dynamic_index_in_dim(gate_term, oc, 0, keepdims=False)
    for j in range(1, OC):
        gate_chip = gate_chip + to_oc(
            lax.dynamic_index_in_dim(gate_term, oc ^ j, 0, keepdims=False), j
        )
    grad_gate = lax.dynamic_index_in_dim(gate_chip, z, 0, keepdims=False)
    for k in range(1, G):
        grad_gate = grad_gate + to_z(
            lax.dynamic_index_in_dim(gate_chip, z ^ k, 0, keepdims=False), k
        )
    return (image_out[None], text_attn[None], d_attn[None], grad_wo, grad_gate)


def solution(mesh):
    in_specs = (
        P("dp", None, "seq"),
        P("seq"),
        P("seq", None),
        P("dp"),
        P("dp", None),
        P(),
        P(),
        P("dp", "seq", None),
        P("dp", "seq", None),
        P("dp", "seq", None),
        P(),
        P("dp", None),
        P("dp", "seq", None),
    )
    out_specs = (
        P("dp", "seq", None),
        P("dp", "seq", None),
        P("dp", "seq", None),
        P(("dp", "seq"), None),
        P("dp", "seq"),
    )
    return jax.shard_map(
        on_device, mesh=mesh, in_specs=in_specs, out_specs=out_specs, check_vma=False
    )
```

```python
import math
import functools
import jax
import jax.numpy as jnp
from jax import lax
from jax.experimental import pallas as pl
from jax.experimental.pallas import tpu as pltpu
from jax.sharding import PartitionSpec as P

DT5 = 4096
CORES = 2
GROUPS = 4

eps_norm = 1e-06
f32 = jnp.float32
bf16 = jnp.bfloat16


def head_norm(values_in, gain_vec):
    shaped = values_in.reshape(values_in.shape[0], -1, gain_vec.shape[0])
    normed = (
        shaped * lax.rsqrt(jnp.mean(shaped * shaped, axis=-1, keepdims=True) + eps_norm) * gain_vec
    )
    return normed.reshape(values_in.shape).astype(bf16)


def attention_kernel(n_kv, n_tkv, row_block, head_size, *refs):
    qkv_ref, tq_ref = refs[:2]
    kv_refs = refs[2 : 2 + n_kv]
    tkv_refs = refs[2 + n_kv : 2 + n_kv + n_tkv]
    bias_ref, out_ref, tout_ref = refs[2 + n_kv + n_tkv :]
    width = tq_ref.shape[1]
    factor = head_size ** (-0.5) * math.log2(math.e)
    bias = bias_ref[...]
    blocks = [
        (qkv_ref, 2 * width, out_ref, slice(r, r + row_block))
        for r in range(0, out_ref.shape[0], row_block)
    ]
    blocks.append((tq_ref, 0, tout_ref, slice(0, tout_ref.shape[0])))
    for head in range(width // head_size):
        cols = slice(head * head_size, (head + 1) * head_size)
        vcols = slice(width + head * head_size, width + (head + 1) * head_size)
        keys = jnp.concatenate([r[:, cols] for r in kv_refs], axis=0)
        values = jnp.concatenate([r[:, vcols] for r in kv_refs], axis=0)
        tkeys = jnp.concatenate([r[:, cols] for r in tkv_refs], axis=0)
        tvalues = jnp.concatenate([r[:, vcols] for r in tkv_refs], axis=0)
        for q_ref, q_at, o_ref, rows in blocks:
            q = q_ref[rows, q_at + head * head_size : q_at + (head + 1) * head_size]
            nt = (((1,), (1,)), ((), ()))
            s_img = lax.dot_general(q, keys, nt, preferred_element_type=f32)
            s_txt = lax.dot_general(q, tkeys, nt, preferred_element_type=f32) + bias
            top = jnp.maximum(
                jnp.max(s_img, axis=1, keepdims=True), jnp.max(s_txt, axis=1, keepdims=True)
            )
            p_img = jnp.exp2((s_img - top) * factor)
            p_txt = jnp.exp2((s_txt - top) * factor)
            total = jnp.sum(p_img, axis=1, keepdims=True) + jnp.sum(p_txt, axis=1, keepdims=True)
            acc = jnp.dot(p_img.astype(bf16), values, preferred_element_type=f32)
            acc = acc + jnp.dot(p_txt.astype(bf16), tvalues, preferred_element_type=f32)
            o_ref[rows, cols] = (acc / total).astype(bf16)


def attention(qkv, text_q, keyvals, text_keyvals, bias, head_size):
    args = (qkv, text_q) + tuple(keyvals) + tuple(text_keyvals) + (bias,)
    width = text_q.shape[1]
    outs = [jax.ShapeDtypeStruct((x.shape[0], width), bf16) for x in (qkv, text_q)]
    vmem = pl.BlockSpec(memory_space=pltpu.VMEM)
    rows = qkv.shape[0] + text_q.shape[0]
    cols = sum(k.shape[0] for k in keyvals) + sum(k.shape[0] for k in text_keyvals)
    return pl.pallas_call(
        functools.partial(attention_kernel, len(keyvals), len(text_keyvals), 128, head_size),
        out_shape=outs,
        in_specs=[vmem] * len(args),
        out_specs=[vmem] * len(outs),
        compiler_params=pltpu.CompilerParams(vmem_limit_bytes=32 * 1024 * 1024),
        cost_estimate=pl.CostEstimate(
            flops=4 * rows * cols * width,
            bytes_accessed=4 * (rows + cols) * width,
            transcendentals=rows * cols * width // head_size,
        ),
    )(*args)


def grad_kernel(n_pieces, *refs):
    left = refs[0]
    pieces = refs[1 : 1 + n_pieces]
    out = refs[1 + n_pieces]
    block = 256
    for start in range(0, out.shape[1], block):
        cols = slice(start, start + block)
        right = jnp.concatenate([p[:, cols] for p in pieces], axis=0)
        out[:, cols] = jnp.dot(left[...], right, preferred_element_type=f32).astype(bf16)


def grad_product(left, pieces):
    vmem = pl.BlockSpec(memory_space=pltpu.VMEM)
    rows, depth = left.shape
    width = pieces[0].shape[1]
    return pl.pallas_call(
        functools.partial(grad_kernel, len(pieces)),
        out_shape=jax.ShapeDtypeStruct((rows, width), bf16),
        in_specs=[vmem] * (1 + len(pieces)),
        out_specs=vmem,
        compiler_params=pltpu.CompilerParams(vmem_limit_bytes=32 * 1024 * 1024),
        cost_estimate=pl.CostEstimate(
            flops=2 * rows * depth * width,
            bytes_accessed=2 * (rows * depth + depth * width + rows * width),
            transcendentals=0,
        ),
    )(left, *pieces)


def on_device(
    caption_states,
    caption_gain,
    text_proj,
    caption_len,
    slot_source,
    query_gain,
    key_gain,
    image_q,
    image_k,
    image_v,
    out_weight,
    gate,
    d_out,
):
    n_dp = lax.axis_size("dp")
    n_seq = lax.axis_size("seq")
    G, C = GROUPS, CORES
    O = n_seq // (G * C)
    OC = O * C
    seq = lax.axis_index("seq")
    oc = (seq // (G * C)) * C + seq % C

    def place(oc_at, z_at):
        return ((oc_at // C) * G + z_at) * C + oc_at % C

    def to_oc(x, j):
        perm = [(place(a, b), place(a ^ j, b)) for a in range(OC) for b in range(G)]
        return lax.ppermute(x, "seq", perm)

    def part(x, index, size, axis):
        return lax.dynamic_slice_in_dim(x, index * size, size, axis)

    z_groups = [[place(a, b) for b in range(G)] for a in range(OC)]

    def swap_z(x):
        return lax.all_to_all(x, "seq", 0, 0, axis_index_groups=z_groups, tiled=True)

    slot_total = slot_source.shape[1]
    slot_local = slot_total // n_seq
    image_local = image_q.shape[1]
    inner_width = image_q.shape[2]
    model_width = out_weight.shape[0]
    head_size = query_gain.shape[0]
    gw = inner_width // G
    q_all, k_all, v_all = image_q[0], image_k[0], image_v[0]

    qkv = jnp.concatenate(
        [
            jnp.concatenate([x[:, b * gw : (b + 1) * gw] for x in (k_all, v_all, q_all)], axis=1)
            for b in range(G)
        ],
        axis=0,
    )
    qkv = swap_z(qkv)
    kv_near = qkv[:, : 2 * gw]
    kv_pieces = [qkv] + [to_oc(kv_near, j) for j in range(1, OC)]

    sources = slot_source[0].reshape(O, G, C, slot_local)
    sources = jnp.transpose(sources, (0, 2, 1, 3)).reshape(-1)
    picked = jnp.take(caption_states[0], sources, axis=0).astype(f32)
    scaled_rows = (picked * caption_gain).astype(bf16)
    partial_proj = jnp.dot(scaled_rows, text_proj, preferred_element_type=f32)
    partial_squares = jnp.sum(picked * picked, axis=1, keepdims=True)
    usable = (sources < caption_len[0]).astype(jnp.int32).reshape(OC, G * slot_local)
    text_rows = G * slot_local

    def message(values, squares):
        high = lax.reduce_precision(squares, 8, 7)
        low = squares - high
        tail = jnp.concatenate(
            [high, low, jnp.zeros((squares.shape[0], 126), f32)], axis=1
        ).astype(bf16)
        return jnp.concatenate([values.astype(bf16), tail], axis=1)

    def opened(got):
        got = got.astype(f32)
        width = got.shape[-1] - 128
        return got[..., :width], got[..., width : width + 1] + got[..., width + 1 : width + 2]

    chip_proj = part(partial_proj, oc, text_rows, 0)
    chip_squares = part(partial_squares, oc, text_rows, 0)
    for j in range(1, OC):
        sent = message(
            part(partial_proj, oc ^ j, text_rows, 0), part(partial_squares, oc ^ j, text_rows, 0)
        )
        more_proj, more_squares = opened(to_oc(sent, j))
        chip_proj = chip_proj + more_proj
        chip_squares = chip_squares + more_squares
    sent = jnp.concatenate(
        [
            message(
                jnp.concatenate(
                    [
                        chip_proj[:, i * inner_width + b * gw : i * inner_width + (b + 1) * gw]
                        for i in range(3)
                    ],
                    axis=1,
                ),
                chip_squares,
            )
            for b in range(G)
        ],
        axis=0,
    )
    got, got_squares = opened(swap_z(sent).reshape(G, text_rows, -1))
    summed = jnp.sum(got, axis=0)
    squares = jnp.sum(got_squares, axis=0)
    normed = summed * lax.rsqrt(squares / DT5 + eps_norm)
    text_q = head_norm(normed[:, :gw], query_gain)
    text_k = head_norm(normed[:, gw : 2 * gw], key_gain)
    text_kv = jnp.concatenate([text_k, normed[:, 2 * gw :].astype(bf16)], axis=1)
    text_kvs = [text_kv] + [to_oc(text_kv, j) for j in range(1, OC)]
    usable_keys = jnp.concatenate([part(usable, oc ^ j, 1, 0) for j in range(OC)], axis=1)
    bias = jnp.where(usable_keys > 0, 0.0, -1e30).astype(f32)

    gate_row = gate[0]
    cotangent = d_out[0].astype(f32)
    gated_grad = (gate_row * cotangent).astype(bf16)
    R = model_width // (n_dp * n_seq)
    gg_t = gated_grad.T.reshape(n_dp, O, G, C, R, image_local)
    gg_t = jnp.transpose(gg_t, (0, 1, 3, 2, 4, 5)).reshape(n_dp, OC, G * R, image_local)
    gg_dp = lax.all_to_all(gg_t, "dp", 0, 0, tiled=True)
    gg_left = []
    for j in range(OC):
        sel = lax.dynamic_index_in_dim(gg_dp, oc ^ j, 1, keepdims=False)
        if j:
            sel = to_oc(sel, j)
        gg_left += [sel[k] for k in range(n_dp)]
    left = jnp.concatenate(gg_left, axis=1)
    d_attn = jnp.dot(gated_grad, out_weight, preferred_element_type=f32).astype(bf16)

    out, text_out = attention(qkv, text_q, kv_pieces, text_kvs, bias, head_size)

    rows = jnp.concatenate(
        [out.reshape(G, image_local, gw), text_out.reshape(G, slot_local, gw)], axis=1
    )
    back = swap_z(rows.reshape(-1, gw)).reshape(G, image_local + slot_local, gw)
    attn = jnp.concatenate([back[b] for b in range(G)], axis=1)
    image_attn = attn[:image_local]
    own_usable = part((slot_source[0] < caption_len[0]), seq, slot_local, 0)
    text_attn = jnp.where(own_usable[:, None], attn[image_local:], jnp.zeros((), bf16))

    attn_dp = lax.all_gather(image_attn, "dp", axis=0, tiled=True)
    attn_pieces = [attn_dp] + [to_oc(attn_dp, j) for j in range(1, OC)]

    projected = lax.dot_general(
        image_attn, out_weight, (((1,), (1,)), ((), ())), preferred_element_type=f32
    )
    image_out = (gate_row * projected).astype(bf16)
    gate_term = jnp.sum(projected * cotangent, axis=0)

    grad = swap_z(grad_product(left, attn_pieces)).reshape(G, R, inner_width)
    grad_wo = jnp.sum(grad.astype(f32), axis=0)

    gate_term = jnp.transpose(gate_term.reshape(O, G, C, -1), (0, 2, 1, 3)).reshape(OC, G, 1, -1)
    gate_chip = lax.dynamic_index_in_dim(gate_term, oc, 0, keepdims=False)
    for j in range(1, OC):
        gate_chip = gate_chip + to_oc(
            lax.dynamic_index_in_dim(gate_term, oc ^ j, 0, keepdims=False), j
        )
    grad_gate = jnp.sum(swap_z(gate_chip), axis=0)
    return (image_out[None], text_attn[None], d_attn[None], grad_wo, grad_gate)


def solution(mesh):
    in_specs = (
        P("dp", None, "seq"),
        P("seq"),
        P("seq", None),
        P("dp"),
        P("dp", None),
        P(),
        P(),
        P("dp", "seq", None),
        P("dp", "seq", None),
        P("dp", "seq", None),
        P(),
        P("dp", None),
        P("dp", "seq", None),
    )
    out_specs = (
        P("dp", "seq", None),
        P("dp", "seq", None),
        P("dp", "seq", None),
        P(("dp", "seq"), None),
        P("dp", "seq"),
    )
    return jax.shard_map(
        on_device, mesh=mesh, in_specs=in_specs, out_specs=out_specs, check_vma=False
    )
```

```python
import math
import functools
import jax
import jax.numpy as jnp
from jax import lax
from jax.experimental import pallas as pl
from jax.experimental.pallas import tpu as pltpu
from jax.sharding import PartitionSpec as P

DT5 = 4096
CORES = 2
GROUPS = 4

eps_norm = 1e-06
f32 = jnp.float32
bf16 = jnp.bfloat16


VMEM = pl.BlockSpec(memory_space=pltpu.VMEM)
SMEM = pl.BlockSpec(memory_space=pltpu.SMEM)
ANY = pl.BlockSpec(memory_space=pl.ANY)
TAIL = 128


def params():
    return pltpu.CompilerParams(vmem_limit_bytes=40 * 1024 * 1024)


def cost(flops, bytes_accessed, transcendentals=0):
    return pl.CostEstimate(
        flops=flops, bytes_accessed=bytes_accessed, transcendentals=transcendentals
    )


def pack_kernel(at_ref, k_ref, v_ref, q_ref, *outs):
    for g, out in enumerate(outs):
        width = out.shape[1] // 3
        at = pl.multiple_of(at_ref[g], 128)
        for i, ref in enumerate((k_ref, v_ref, q_ref)):
            out[:, i * width : (i + 1) * width] = ref[:, pl.ds(at, width)]


def pack(at, keys, values, queries, groups):
    rows, width = keys.shape
    shape = jax.ShapeDtypeStruct((rows, 3 * width // groups), bf16)
    return pl.pallas_call(
        pack_kernel,
        out_shape=[shape] * groups,
        in_specs=[SMEM, VMEM, VMEM, VMEM],
        out_specs=[VMEM] * groups,
        compiler_params=params(),
        cost_estimate=cost(0, 12 * rows * width),
    )(at, keys, values, queries)


def split_tail(squares):
    high = squares.astype(bf16).astype(f32)
    low = squares - high
    lane = lax.broadcasted_iota(jnp.int32, (squares.shape[0], TAIL), 1)
    return jnp.where(lane == 0, high, jnp.where(lane == 1, low, 0.0))


def text_kernel(at_ref, states_ref, gain_ref, pick_ref, wq_ref, wk_ref, wv_ref, own_ref, *msgs):
    del at_ref
    picked = jnp.dot(pick_ref[...], states_ref[...], preferred_element_type=f32)
    scaled = (picked * gain_ref[...]).astype(bf16)
    tail = split_tail(jnp.sum(picked * picked, axis=1, keepdims=True))
    rows = own_ref.shape[1]
    width = wq_ref.shape[1]
    for i, w_ref in enumerate((wq_ref, wk_ref, wv_ref)):
        got = jnp.dot(scaled, w_ref[...], preferred_element_type=f32)
        cols = slice(i * width, (i + 1) * width)
        own_ref[0, :, cols] = got[:rows]
        for j, msg in enumerate(msgs):
            msg[0, :, cols] = got[(j + 1) * rows : (j + 2) * rows].astype(bf16)
    own_ref[0, :, 3 * width :] = tail[:rows]
    for j, msg in enumerate(msgs):
        msg[0, :, 3 * width :] = tail[(j + 1) * rows : (j + 2) * rows].astype(bf16)


def text_project(at, states, gain, pick, text_proj, groups, parts):
    slots, depth = states.shape
    rows = pick.shape[0] // parts
    width = text_proj.shape[1] // (3 * groups)
    full = 3 * width + TAIL

    def whole(*shape):
        return pl.BlockSpec(shape, lambda g, at_ref: (0,) * len(shape))

    def weights(i):
        return pl.BlockSpec((depth, width), lambda g, at_ref: (0, i * groups + at_ref[g]))

    block = pl.BlockSpec((1, rows, full), lambda g, at_ref: (g, 0, 0))
    shapes = [jax.ShapeDtypeStruct((groups, rows, full), f32)]
    shapes += [jax.ShapeDtypeStruct((groups, rows, full), bf16)] * (parts - 1)
    return pl.pallas_call(
        text_kernel,
        grid_spec=pltpu.PrefetchScalarGridSpec(
            num_scalar_prefetch=1,
            grid=(groups,),
            in_specs=[
                whole(slots, depth),
                whole(1, depth),
                whole(pick.shape[0], slots),
                weights(0),
                weights(1),
                weights(2),
            ],
            out_specs=[block] * parts,
        ),
        out_shape=shapes,
        compiler_params=params(),
        cost_estimate=cost(
            2 * pick.shape[0] * depth * text_proj.shape[1], 2 * depth * text_proj.shape[1]
        ),
    )(at, states, gain, pick, text_proj, text_proj, text_proj)


def text_sum_kernel(n_got, own_ref, *refs):
    got, outs = refs[:n_got], refs[n_got:]
    for g, out in enumerate(outs):
        total = own_ref[g]
        for ref in got:
            total = total + ref[g].astype(f32)
        width = total.shape[1] - TAIL
        tail = total[:, width:]
        out[:, :width] = total[:, :width].astype(out.dtype)
        out[:, width:] = split_tail(tail[:, 0:1] + tail[:, 1:2]).astype(out.dtype)


def text_sum(own, got):
    groups, rows, full = own.shape
    shapes = [jax.ShapeDtypeStruct((rows, full), f32)]
    shapes += [jax.ShapeDtypeStruct((rows, full), bf16)] * (groups - 1)
    return pl.pallas_call(
        functools.partial(text_sum_kernel, len(got)),
        out_shape=shapes,
        in_specs=[VMEM] * (1 + len(got)),
        out_specs=[VMEM] * groups,
        compiler_params=params(),
        cost_estimate=cost(0, 8 * groups * rows * full),
    )(own, *got)


def text_norm_kernel(features, head_size, gains_ref, own_ref, *refs):
    got, (tq_ref, tkv_ref) = refs[:-2], refs[-2:]
    total = own_ref[...]
    for ref in got:
        total = total + ref[...].astype(f32)
    width = tq_ref.shape[1]
    squares = total[:, 3 * width : 3 * width + 1] + total[:, 3 * width + 1 : 3 * width + 2]
    normed = total[:, : 3 * width] * lax.rsqrt(squares / features + eps_norm)
    for i, out in enumerate((tq_ref, tkv_ref)):
        for head in range(width // head_size):
            cols = slice(head * head_size, (head + 1) * head_size)
            x = normed[:, i * width + head * head_size : i * width + (head + 1) * head_size]
            mean = jnp.mean(x * x, axis=1, keepdims=True)
            out[:, cols] = (x * lax.rsqrt(mean + eps_norm) * gains_ref[i : i + 1, :]).astype(bf16)
    tkv_ref[:, width:] = normed[:, 2 * width :].astype(bf16)


def text_norm(gains, own, got, features):
    rows, full = own.shape
    width = (full - TAIL) // 3
    return pl.pallas_call(
        functools.partial(text_norm_kernel, features, gains.shape[1]),
        out_shape=[
            jax.ShapeDtypeStruct((rows, width), bf16),
            jax.ShapeDtypeStruct((rows, 2 * width), bf16),
        ],
        in_specs=[VMEM] * (2 + len(got)),
        out_specs=[VMEM] * 2,
        compiler_params=params(),
        cost_estimate=cost(0, 8 * rows * full),
    )(gains, own, *got)


def attention_kernel(counts, width, head_size, *refs):
    n_q, n_kv, n_tkv, n_after = counts
    q_refs, refs = refs[:n_q], refs[n_q:]
    kv_refs, refs = refs[:n_kv], refs[n_kv:]
    tkv_refs, refs = refs[:n_tkv], refs[n_tkv:]
    bias_ref, out_refs = refs[0], refs[1 + n_after :]
    factor = head_size ** (-0.5) * math.log2(math.e)
    bias = bias_ref[...]
    nt = (((1,), (1,)), ((), ()))
    for head in range(width // head_size):
        cols = slice(head * head_size, (head + 1) * head_size)
        vcols = slice(width + head * head_size, width + (head + 1) * head_size)
        keys = jnp.concatenate([r[:, cols] for r in kv_refs], axis=0)
        values = jnp.concatenate([r[:, vcols] for r in kv_refs], axis=0)
        tkeys = jnp.concatenate([r[:, cols] for r in tkv_refs], axis=0)
        tvalues = jnp.concatenate([r[:, vcols] for r in tkv_refs], axis=0)
        for q_ref, out_ref in zip(q_refs, out_refs):
            at = q_ref.shape[1] - width + head * head_size
            q = q_ref[:, at : at + head_size]
            s_img = lax.dot_general(q, keys, nt, preferred_element_type=f32)
            s_txt = lax.dot_general(q, tkeys, nt, preferred_element_type=f32) + bias
            top = jnp.maximum(
                jnp.max(s_img, axis=1, keepdims=True), jnp.max(s_txt, axis=1, keepdims=True)
            )
            p_img = jnp.exp2((s_img - top) * factor)
            p_txt = jnp.exp2((s_txt - top) * factor)
            total = jnp.sum(p_img, axis=1, keepdims=True) + jnp.sum(p_txt, axis=1, keepdims=True)
            acc = jnp.dot(p_img.astype(bf16), values, preferred_element_type=f32)
            acc = acc + jnp.dot(p_txt.astype(bf16), tvalues, preferred_element_type=f32)
            out_ref[:, cols] = (acc / total).astype(bf16)


def attention(queries, keyvals, text_keyvals, bias, after, width, head_size):
    args = tuple(queries) + tuple(keyvals) + tuple(text_keyvals) + (bias,)
    counts = (len(queries), len(keyvals), len(text_keyvals), len(after))
    rows = sum(q.shape[0] for q in queries)
    cols = sum(k.shape[0] for k in keyvals) + sum(k.shape[0] for k in text_keyvals)
    return pl.pallas_call(
        functools.partial(attention_kernel, counts, width, head_size),
        out_shape=[jax.ShapeDtypeStruct((q.shape[0], width), bf16) for q in queries],
        in_specs=[VMEM] * len(args) + [ANY] * len(after),
        out_specs=[VMEM] * len(queries),
        compiler_params=params(),
        cost_estimate=cost(
            4 * rows * cols * width,
            4 * (rows + cols) * width,
            rows * cols * width // head_size,
        ),
    )(*args, *after)


def project_kernel(attn_ref, w_ref, gate_ref, d_out_ref, after_ref, out_ref, term_ref):
    del after_ref
    got = lax.dot_general(
        attn_ref[...], w_ref[...], (((1,), (1,)), ((), ())), preferred_element_type=f32
    )
    out_ref[...] = (got * gate_ref[...]).astype(bf16)
    term_ref[...] = jnp.sum(got * d_out_ref[...].astype(f32), axis=0, keepdims=True)


def project(attn, out_weight, gate, d_out, after):
    rows, inner = attn.shape
    model = out_weight.shape[0]
    block = 512
    return pl.pallas_call(
        project_kernel,
        grid=(model // block,),
        out_shape=[
            jax.ShapeDtypeStruct((rows, model), bf16),
            jax.ShapeDtypeStruct((1, model), f32),
        ],
        in_specs=[
            pl.BlockSpec((rows, inner), lambda i: (0, 0)),
            pl.BlockSpec((block, inner), lambda i: (i, 0)),
            pl.BlockSpec((1, block), lambda i: (0, i)),
            pl.BlockSpec((rows, block), lambda i: (0, i)),
            ANY,
        ],
        out_specs=[
            pl.BlockSpec((rows, block), lambda i: (0, i)),
            pl.BlockSpec((1, block), lambda i: (0, i)),
        ],
        compiler_params=params(),
        cost_estimate=cost(2 * rows * inner * model, 2 * inner * model),
    )(attn, out_weight, gate, d_out, after)


def grad_kernel(n_pieces, left_ref, *refs):
    pieces, outs = refs[:n_pieces], refs[n_pieces:]
    rows, width = outs[0].shape
    block = 256
    for start in range(0, width, block):
        cols = slice(start, start + block)
        right = jnp.concatenate([p[:, cols] for p in pieces], axis=0)
        got = jnp.dot(left_ref[...], right, preferred_element_type=f32)
        for g, out in enumerate(outs):
            out[:, cols] = got[g * rows : (g + 1) * rows].astype(out.dtype)


def grad_product(left, pieces, groups):
    total, depth = left.shape
    width = pieces[0].shape[1]
    shapes = [jax.ShapeDtypeStruct((total // groups, width), f32)]
    shapes += [jax.ShapeDtypeStruct((total // groups, width), bf16)] * (groups - 1)
    return pl.pallas_call(
        functools.partial(grad_kernel, len(pieces)),
        out_shape=shapes,
        in_specs=[VMEM] * (1 + len(pieces)),
        out_specs=[VMEM] * groups,
        compiler_params=params(),
        cost_estimate=cost(
            2 * total * depth * width, 2 * (total * depth + depth * width + total * width)
        ),
    )(left, *pieces)


def on_device(
    caption_states,
    caption_gain,
    text_proj,
    caption_len,
    slot_source,
    query_gain,
    key_gain,
    image_q,
    image_k,
    image_v,
    out_weight,
    gate,
    d_out,
):
    n_dp = lax.axis_size("dp")
    n_seq = lax.axis_size("seq")
    G, C = GROUPS, CORES
    O = n_seq // (G * C)
    OC = O * C
    dp = lax.axis_index("dp")
    seq = lax.axis_index("seq")
    z = (seq // C) % G
    oc = (seq // (G * C)) * C + seq % C

    def place(oc_at, z_at):
        return ((oc_at // C) * G + z_at) * C + oc_at % C

    def to_z(x, k):
        perm = [(place(a, b), place(a, b ^ k)) for a in range(OC) for b in range(G)]
        return lax.ppermute(x, "seq", perm)

    def to_oc(x, j):
        perm = [(place(a, b), place(a ^ j, b)) for a in range(OC) for b in range(G)]
        return lax.ppermute(x, "seq", perm)

    def to_dp(x, k):
        return lax.ppermute(x, "dp", [(a, a ^ k) for a in range(n_dp)])

    def part(x, index, size, axis):
        return lax.dynamic_slice_in_dim(x, index * size, size, axis)

    slot_total = slot_source.shape[1]
    slot_local = slot_total // n_seq
    image_local = image_q.shape[1]
    inner_width = image_q.shape[2]
    model_width = out_weight.shape[0]
    head_size = query_gain.shape[0]
    gw = inner_width // G
    far = [2, 3]
    near = [1, 0]
    z_order = z ^ jnp.arange(G, dtype=jnp.int32)
    oc_order = oc ^ jnp.arange(OC, dtype=jnp.int32)

    packed = pack(z_order * gw, image_k[0], image_v[0], image_q[0], G)
    qkv = {0: packed[0]}
    for k in far + near[:1]:
        qkv[k] = to_z(packed[k], k)
    kv_pieces = [qkv[k] for k in range(G)]
    for j in range(1, OC):
        kv_pieces += [to_oc(qkv[k][:, : 2 * gw], j) for k in range(G)]

    sources = slot_source[0].reshape(O, G, C, slot_local)
    sources = jnp.transpose(sources, (0, 2, 1, 3)).reshape(OC, G * slot_local)
    sources = jnp.take(sources, oc_order, axis=0)
    pick = (sources.reshape(-1, 1) == jnp.arange(slot_total, dtype=jnp.int32)).astype(bf16)
    bias = jnp.where(sources.reshape(1, -1) < caption_len[0], 0.0, -1e30).astype(f32)
    partials = text_project(
        z_order, caption_states[0], caption_gain[None], pick, text_proj, G, OC
    )
    got = [to_oc(partials[j], j) for j in range(1, OC)]
    sums = text_sum(partials[0], got)
    got = [to_z(sums[k], k) for k in range(1, G)]
    gains = jnp.stack([query_gain, key_gain])
    text_q, text_kv = text_norm(gains, sums[0], got, DT5)
    text_kvs = [text_kv] + [to_oc(text_kv, j) for j in range(1, OC)]

    gate_row = gate[0]
    gated_grad = (gate_row * d_out[0].astype(f32)).astype(bf16)
    R = model_width // (n_dp * n_seq)
    gg_t = gated_grad.T.reshape(n_dp, O, G, C, R, image_local)
    gg_t = jnp.transpose(gg_t, (0, 1, 3, 2, 4, 5)).reshape(n_dp, OC, G * R, image_local)
    gg_dp = []
    for k in range(n_dp):
        sel = lax.dynamic_index_in_dim(gg_t, dp ^ k, 0, keepdims=False)
        gg_dp.append(sel if k == 0 else to_dp(sel, k))
    gg_left = []
    for j in range(OC):
        sel = [lax.dynamic_index_in_dim(g, oc ^ j, 0, keepdims=False) for g in gg_dp]
        if j:
            sent = to_oc(jnp.stack(sel), j)
            sel = [sent[k] for k in range(n_dp)]
        gg_left += sel
    left = jnp.concatenate(gg_left, axis=1).reshape(G, R, -1)
    left = jnp.take(left, z_order, axis=0).reshape(G * R, -1)
    d_attn = jnp.dot(gated_grad, out_weight, preferred_element_type=f32).astype(bf16)

    first = attention(
        [text_q] + [qkv[k] for k in far],
        kv_pieces, text_kvs, bias, [left, d_attn], gw, head_size,
    )
    second = attention(
        [qkv[k] for k in near], kv_pieces, text_kvs, bias, [first[0]], gw, head_size
    )
    outs = dict(zip(far + near, first[1:] + second))

    attn = jnp.zeros((image_local + slot_local, inner_width), bf16)
    for k in far + near:
        rows = jnp.concatenate([outs[k], part(first[0], z ^ k, slot_local, 0)], axis=0)
        rows = to_z(rows, k) if k else rows
        attn = lax.dynamic_update_slice_in_dim(attn, rows, (z ^ k) * gw, 1)
    image_attn = attn[:image_local]
    own_usable = part(slot_source[0] < caption_len[0], seq, slot_local, 0)
    text_attn = jnp.where(own_usable[:, None], attn[image_local:], jnp.zeros((), bf16))

    attn_dp = [image_attn] + [to_dp(image_attn, k) for k in range(1, n_dp)]
    attn_pieces = list(attn_dp)
    for j in range(1, OC):
        attn_pieces += [to_oc(p, j) for p in attn_dp]

    image_out, gate_term = project(image_attn, out_weight, gate, d_out[0], attn_dp[1])

    grads = grad_product(left, attn_pieces, G)
    grad_wo = grads[0]
    for k in range(1, G):
        grad_wo = grad_wo + to_z(grads[k], k).astype(f32)

    gate_term = jnp.transpose(gate_term.reshape(O, G, C, -1), (0, 2, 1, 3)).reshape(OC, G, 1, -1)
    gate_chip = lax.dynamic_index_in_dim(gate_term, oc, 0, keepdims=False)
    for j in range(1, OC):
        gate_chip = gate_chip + to_oc(
            lax.dynamic_index_in_dim(gate_term, oc ^ j, 0, keepdims=False), j
        )
    grad_gate = lax.dynamic_index_in_dim(gate_chip, z, 0, keepdims=False)
    for k in range(1, G):
        grad_gate = grad_gate + to_z(
            lax.dynamic_index_in_dim(gate_chip, z ^ k, 0, keepdims=False), k
        )
    return (image_out[None], text_attn[None], d_attn[None], grad_wo, grad_gate)


def solution(mesh):
    in_specs = (
        P("dp", None, "seq"),
        P("seq"),
        P("seq", None),
        P("dp"),
        P("dp", None),
        P(),
        P(),
        P("dp", "seq", None),
        P("dp", "seq", None),
        P("dp", "seq", None),
        P(),
        P("dp", None),
        P("dp", "seq", None),
    )
    out_specs = (
        P("dp", "seq", None),
        P("dp", "seq", None),
        P("dp", "seq", None),
        P(("dp", "seq"), None),
        P("dp", "seq"),
    )
    return jax.shard_map(
        on_device, mesh=mesh, in_specs=in_specs, out_specs=out_specs, check_vma=False
    )
```

```python
import math
import functools
import jax
import jax.numpy as jnp
from jax import lax
from jax.experimental import pallas as pl
from jax.experimental.pallas import tpu as pltpu
from jax.sharding import PartitionSpec as P

DT5 = 4096
CORES = 2
GROUPS = 4

eps_norm = 1e-06
f32 = jnp.float32
bf16 = jnp.bfloat16


VMEM = pl.BlockSpec(memory_space=pltpu.VMEM)
SMEM = pl.BlockSpec(memory_space=pltpu.SMEM)
ANY = pl.BlockSpec(memory_space=pl.ANY)
HBM = pl.BlockSpec(memory_space=pltpu.HBM)
TAIL = 128


def params(mib=16):
    return pltpu.CompilerParams(vmem_limit_bytes=mib * 1024 * 1024)


def cost(flops, bytes_accessed, transcendentals=0):
    return pl.CostEstimate(
        flops=flops, bytes_accessed=bytes_accessed, transcendentals=transcendentals
    )


def split_tail(squares):
    high = squares.astype(bf16).astype(f32)
    low = squares - high
    lane = lax.broadcasted_iota(jnp.int32, (squares.shape[0], TAIL), 1)
    return jnp.where(lane == 0, high, jnp.where(lane == 1, low, 0.0))


def text_kernel(
    groups, place_of, meta_ref, len_ref, src_ref, states_ref, gain_ref, w_ref,
    k_ref, v_ref, q_ref, bias_ref, *refs
):
    packed, own_ref, refs = refs[:groups], refs[groups], refs[groups + 1 :]
    msgs, (w_all, sems) = refs[:-2], refs[-2:]
    rows = own_ref.shape[1]
    width = w_all.shape[3]
    slots = states_ref.shape[0]
    slot_local = rows // groups
    copies = []
    for g in range(groups):
        at = pl.multiple_of((meta_ref[0] ^ g) * width, 128)
        for i in range(3):
            cols = pl.ds(pl.multiple_of(at + i * groups * width, 128), width)
            copies.append(pltpu.make_async_copy(w_ref.at[:, cols], w_all.at[g, i], sems.at[g, i]))
            copies[-1].start()
    for g, out in enumerate(packed):
        at = pl.multiple_of((meta_ref[0] ^ g) * width, 128)
        for i, ref in enumerate((k_ref, v_ref, q_ref)):
            out[:, i * width : (i + 1) * width] = ref[:, pl.ds(at, width)]
    oc = meta_ref[1]

    def slot_at(row):
        part = row // rows
        z_at = (row % rows) // slot_local
        return place_of(oc ^ part, z_at) * slot_local + row % slot_local

    iota = functools.partial(lax.broadcasted_iota, jnp.int32, (slots, slots))
    sources = src_ref[...].astype(f32)
    chosen = (iota(1) == slot_at(iota(0))).astype(f32)
    source_col = jnp.sum(chosen * sources, axis=1, keepdims=True)
    pick = (iota(1).astype(f32) == source_col).astype(bf16)
    chosen_t = (iota(0) == slot_at(iota(1))).astype(bf16)
    source_row = jnp.dot(sources.astype(bf16), chosen_t, preferred_element_type=f32)
    bias_ref[...] = jnp.where(source_row < len_ref[0].astype(f32), 0.0, -1e30)

    picked = jnp.dot(pick, states_ref[...], preferred_element_type=f32)
    scaled = (picked * gain_ref[...]).astype(bf16)
    tail = split_tail(jnp.sum(picked * picked, axis=1, keepdims=True))
    for g in range(groups):
        for i in range(3):
            copies[3 * g + i].wait()
            got = jnp.dot(scaled, w_all[g, i], preferred_element_type=f32)
            cols = slice(i * width, (i + 1) * width)
            own_ref[g, :, cols] = got[:rows]
            for j, msg in enumerate(msgs):
                msg[g, :, cols] = got[(j + 1) * rows : (j + 2) * rows].astype(bf16)
        own_ref[g, :, 3 * width :] = tail[:rows]
        for j, msg in enumerate(msgs):
            msg[g, :, 3 * width :] = tail[(j + 1) * rows : (j + 2) * rows].astype(bf16)


def text_project(
    meta, length, sources, states, gain, text_proj, keys, values, queries, groups, parts, place_of
):
    slots, depth = states.shape
    rows = slots // parts
    width = text_proj.shape[1] // (3 * groups)
    full = 3 * width + TAIL
    shapes = [jax.ShapeDtypeStruct((1, slots), f32)]
    shapes += [jax.ShapeDtypeStruct((keys.shape[0], 3 * width), bf16)] * groups
    shapes += [jax.ShapeDtypeStruct((groups, rows, full), f32)]
    shapes += [jax.ShapeDtypeStruct((groups, rows, full), bf16)] * (parts - 1)
    return pl.pallas_call(
        functools.partial(text_kernel, groups, place_of),
        out_shape=shapes,
        in_specs=[SMEM, SMEM, VMEM, VMEM, VMEM, HBM, VMEM, VMEM, VMEM],
        out_specs=[VMEM] * (1 + groups + parts),
        scratch_shapes=[
            pltpu.VMEM((groups, 3, depth, width), bf16),
            pltpu.SemaphoreType.DMA((groups, 3)),
        ],
        compiler_params=params(60),
        cost_estimate=cost(
            2 * slots * depth * text_proj.shape[1], 2 * depth * text_proj.shape[1]
        ),
    )(meta, length, sources, states, gain, text_proj, keys, values, queries)


def text_sum_kernel(n_got, own_ref, *refs):
    got, outs = refs[:n_got], refs[n_got:]
    for g, out in enumerate(outs):
        total = own_ref[g]
        for ref in got:
            total = total + ref[g].astype(f32)
        width = total.shape[1] - TAIL
        tail = total[:, width:]
        out[:, :width] = total[:, :width].astype(out.dtype)
        out[:, width:] = split_tail(tail[:, 0:1] + tail[:, 1:2]).astype(out.dtype)


def text_sum(own, got):
    groups, rows, full = own.shape
    shapes = [jax.ShapeDtypeStruct((rows, full), f32)]
    shapes += [jax.ShapeDtypeStruct((rows, full), bf16)] * (groups - 1)
    return pl.pallas_call(
        functools.partial(text_sum_kernel, len(got)),
        out_shape=shapes,
        in_specs=[VMEM] * (1 + len(got)),
        out_specs=[VMEM] * groups,
        compiler_params=params(),
        cost_estimate=cost(0, 8 * groups * rows * full),
    )(own, *got)


def text_norm_kernel(features, head_size, through_ref, after_ref, qg_ref, kg_ref, own_ref, *refs):
    del through_ref, after_ref
    got, (_, tq_ref, tkv_ref) = refs[:-3], refs[-3:]
    total = own_ref[...]
    for ref in got:
        total = total + ref[...].astype(f32)
    width = tq_ref.shape[1]
    squares = total[:, 3 * width : 3 * width + 1] + total[:, 3 * width + 1 : 3 * width + 2]
    normed = total[:, : 3 * width] * lax.rsqrt(squares / features + eps_norm)
    for i, (out, gain_ref) in enumerate(((tq_ref, qg_ref), (tkv_ref, kg_ref))):
        for head in range(width // head_size):
            cols = slice(head * head_size, (head + 1) * head_size)
            x = normed[:, i * width + head * head_size : i * width + (head + 1) * head_size]
            mean = jnp.mean(x * x, axis=1, keepdims=True)
            out[:, cols] = (x * lax.rsqrt(mean + eps_norm) * gain_ref[...]).astype(bf16)
    tkv_ref[:, width:] = normed[:, 2 * width :].astype(bf16)


def text_norm(through, after, query_gain, key_gain, own, got, features):
    rows, full = own.shape
    width = (full - TAIL) // 3
    return pl.pallas_call(
        functools.partial(text_norm_kernel, features, query_gain.shape[1]),
        out_shape=[
            jax.ShapeDtypeStruct(through.shape, through.dtype),
            jax.ShapeDtypeStruct((rows, width), bf16),
            jax.ShapeDtypeStruct((rows, 2 * width), bf16),
        ],
        in_specs=[ANY] * 2 + [VMEM] * (3 + len(got)),
        out_specs=[ANY] + [VMEM] * 2,
        input_output_aliases={0: 0},
        compiler_params=params(),
        cost_estimate=cost(0, 8 * rows * full),
    )(through, after, query_gain, key_gain, own, *got)


def attention_kernel(counts, width, head_size, *refs):
    n_q, n_kv, n_tkv, n_through = counts
    refs = refs[n_through:]
    q_refs, refs = refs[:n_q], refs[n_q:]
    kv_refs, refs = refs[:n_kv], refs[n_kv:]
    tkv_refs, refs = refs[:n_tkv], refs[n_tkv:]
    bias_ref, out_refs = refs[0], refs[1 + n_through :]
    factor = head_size ** (-0.5) * math.log2(math.e)
    bias = bias_ref[...]
    nt = (((1,), (1,)), ((), ()))
    for head in range(width // head_size):
        cols = slice(head * head_size, (head + 1) * head_size)
        vcols = slice(width + head * head_size, width + (head + 1) * head_size)
        keys = jnp.concatenate([r[:, cols] for r in kv_refs], axis=0)
        values = jnp.concatenate([r[:, vcols] for r in kv_refs], axis=0)
        tkeys = jnp.concatenate([r[:, cols] for r in tkv_refs], axis=0)
        tvalues = jnp.concatenate([r[:, vcols] for r in tkv_refs], axis=0)
        for q_ref, out_ref in zip(q_refs, out_refs):
            at = q_ref.shape[1] - width + head * head_size
            q = q_ref[:, at : at + head_size]
            s_img = lax.dot_general(q, keys, nt, preferred_element_type=f32)
            s_txt = lax.dot_general(q, tkeys, nt, preferred_element_type=f32) + bias
            top = jnp.maximum(
                jnp.max(s_img, axis=1, keepdims=True), jnp.max(s_txt, axis=1, keepdims=True)
            )
            p_img = jnp.exp2((s_img - top) * factor)
            p_txt = jnp.exp2((s_txt - top) * factor)
            total = jnp.sum(p_img, axis=1, keepdims=True) + jnp.sum(p_txt, axis=1, keepdims=True)
            acc = jnp.dot(p_img.astype(bf16), values, preferred_element_type=f32)
            acc = acc + jnp.dot(p_txt.astype(bf16), tvalues, preferred_element_type=f32)
            out_ref[:, cols] = (acc / total).astype(bf16)


def attention(through, queries, keyvals, text_keyvals, bias, width, head_size):
    args = tuple(queries) + tuple(keyvals) + tuple(text_keyvals) + (bias,)
    counts = (len(queries), len(keyvals), len(text_keyvals), len(through))
    rows = sum(q.shape[0] for q in queries)
    cols = sum(k.shape[0] for k in keyvals) + sum(k.shape[0] for k in text_keyvals)
    return pl.pallas_call(
        functools.partial(attention_kernel, counts, width, head_size),
        out_shape=[jax.ShapeDtypeStruct(x.shape, x.dtype) for x in through]
        + [jax.ShapeDtypeStruct((q.shape[0], width), bf16) for q in queries],
        in_specs=[ANY] * len(through) + [VMEM] * len(args),
        out_specs=[ANY] * len(through) + [VMEM] * len(queries),
        input_output_aliases={i: i for i in range(len(through))},
        compiler_params=params(),
        cost_estimate=cost(
            4 * rows * cols * width,
            4 * (rows + cols) * width,
            rows * cols * width // head_size,
        ),
    )(*through, *args)


def assemble_kernel(groups, n_after, meta_ref, slots_ref, *refs):
    pieces, (image_ref, text_ref) = refs[:groups], refs[groups + n_after :]
    rows, width = image_ref.shape[0], pieces[0].shape[1]
    for k, piece in enumerate(pieces):
        at = pl.ds(pl.multiple_of((meta_ref[0] ^ k) * width, 128), width)
        image_ref[:, at] = piece[:rows, :]
        text = piece[rows:, :].astype(f32)
        text_ref[:, at] = jnp.where(slots_ref[...] > 0, text, 0.0).astype(bf16)


def assemble(meta, slots, pieces, after):
    groups = len(pieces)
    text_rows = slots.shape[0]
    rows, width = pieces[0].shape
    return pl.pallas_call(
        functools.partial(assemble_kernel, groups, len(after)),
        out_shape=[
            jax.ShapeDtypeStruct((rows - text_rows, groups * width), bf16),
            jax.ShapeDtypeStruct((text_rows, groups * width), bf16),
        ],
        in_specs=[SMEM] + [VMEM] * (1 + groups) + [ANY] * len(after),
        out_specs=[VMEM] * 2,
        compiler_params=params(),
        cost_estimate=cost(0, 4 * rows * groups * width),
    )(meta, slots, *pieces, *after)


def gated_kernel(n_dp, groups, parts, place_of, meta_ref, gate_ref, d_out_ref, w_ref, after_ref, d_attn_ref, *refs):
    del after_ref
    msgs, (w_all, turned, sems) = refs[:n_dp], refs[n_dp:]
    blocks, block = w_all.shape[:2]
    copies = []
    for i in range(blocks):
        rows = pl.ds(i * block, block)
        copies.append(pltpu.make_async_copy(w_ref.at[rows], w_all.at[i], sems.at[i]))
        copies[-1].start()
    gated = (gate_ref[...] * d_out_ref[...].astype(f32)).astype(bf16)
    turned[...] = gated.astype(f32).T
    rows = msgs[0].shape[2]
    z, oc, dp = meta_ref[0], meta_ref[1], meta_ref[2]
    for k, msg in enumerate(msgs):
        for j in range(parts):
            for g in range(groups):
                at = (dp ^ k) * (groups * parts) + place_of(oc ^ j, z ^ g)
                msg[j, g] = turned[pl.ds(pl.multiple_of(at * rows, 8), rows), :].astype(bf16)
    total = jnp.zeros(d_attn_ref.shape, f32)
    for i in range(blocks):
        copies[i].wait()
        total = total + jnp.dot(
            gated[:, i * block : (i + 1) * block], w_all[i], preferred_element_type=f32
        )
    d_attn_ref[...] = total.astype(bf16)


def gated(meta, gate, d_out, out_weight, after, n_dp, groups, parts, place_of):
    local, model = d_out.shape
    inner = out_weight.shape[1]
    rows = model // (n_dp * groups * parts)
    blocks = 6
    shapes = [jax.ShapeDtypeStruct((local, inner), bf16)]
    shapes += [jax.ShapeDtypeStruct((parts, groups, rows, local), bf16)] * n_dp
    return pl.pallas_call(
        functools.partial(gated_kernel, n_dp, groups, parts, place_of),
        out_shape=shapes,
        in_specs=[SMEM, VMEM, VMEM, HBM, ANY],
        out_specs=[VMEM] * (1 + n_dp),
        scratch_shapes=[
            pltpu.VMEM((blocks, model // blocks, inner), bf16),
            pltpu.VMEM((model, local), f32),
            pltpu.SemaphoreType.DMA((blocks,)),
        ],
        compiler_params=params(56),
        cost_estimate=cost(2 * local * inner * model, 2 * inner * model),
    )(meta, gate, d_out, out_weight, after)


def gather_kernel(n_dp, *refs):
    pieces, outs = refs[:n_dp], refs[n_dp:]
    for j, out in enumerate(outs):
        for k, piece in enumerate(pieces):
            out[k] = piece[j + 1]


def gather_parts(pieces):
    parts = pieces[0].shape[0]
    shape = (len(pieces),) + pieces[0].shape[1:]
    return pl.pallas_call(
        functools.partial(gather_kernel, len(pieces)),
        out_shape=[jax.ShapeDtypeStruct(shape, bf16)] * (parts - 1),
        in_specs=[VMEM] * len(pieces),
        out_specs=[VMEM] * (parts - 1),
        compiler_params=params(),
        cost_estimate=cost(0, 4 * math.prod(shape) * (parts - 1)),
    )(*pieces)


def project_kernel(groups, parts, place_of, meta_ref, attn_ref, w_ref, gate_ref, d_out_ref, after_ref, out_ref, *refs):
    del after_ref
    terms, (w_all, by_place, sems) = refs[:parts], refs[parts:]
    blocks, block = w_all.shape[:2]
    copies = []
    for i in range(blocks):
        rows = pl.ds(i * block, block)
        copies.append(pltpu.make_async_copy(w_ref.at[rows], w_all.at[i], sems.at[i]))
        copies[-1].start()
    sums = []
    for i in range(blocks):
        copies[i].wait()
        cols = slice(i * block, (i + 1) * block)
        got = lax.dot_general(
            attn_ref[...], w_all[i], (((1,), (1,)), ((), ())), preferred_element_type=f32
        )
        out_ref[:, cols] = (got * gate_ref[:, cols]).astype(bf16)
        sums.append(jnp.sum(got * d_out_ref[:, cols].astype(f32), axis=0, keepdims=True))
    sums = jnp.concatenate(sums, axis=1)
    places, width = by_place.shape
    for s in range(places):
        by_place[s : s + 1, :] = sums[:, s * width : (s + 1) * width]
    for j, term in enumerate(terms):
        for g in range(groups):
            at = place_of(meta_ref[1] ^ j, meta_ref[0] ^ g)
            term[g : g + 1, :] = by_place[pl.ds(at, 1), :]


def project(meta, attn, out_weight, gate, d_out, after, groups, parts, place_of):
    rows, inner = attn.shape
    model = out_weight.shape[0]
    blocks = 6
    width = model // (groups * parts)
    shapes = [jax.ShapeDtypeStruct((rows, model), bf16)]
    shapes += [jax.ShapeDtypeStruct((groups, width), f32)] * parts
    return pl.pallas_call(
        functools.partial(project_kernel, groups, parts, place_of),
        out_shape=shapes,
        in_specs=[SMEM, VMEM, HBM, VMEM, VMEM, ANY],
        out_specs=[VMEM] * (1 + parts),
        scratch_shapes=[
            pltpu.VMEM((blocks, model // blocks, inner), bf16),
            pltpu.VMEM((groups * parts, width), f32),
            pltpu.SemaphoreType.DMA((blocks,)),
        ],
        compiler_params=params(56),
        cost_estimate=cost(2 * rows * inner * model, 2 * inner * model),
    )(meta, attn, out_weight, gate, d_out, after)


def gate_kernel(n_got, *refs):
    total = refs[0][...]
    for ref in refs[1 : 1 + n_got]:
        total = total + ref[...]
    for g, out in enumerate(refs[1 + n_got :]):
        out[...] = total[g : g + 1]


def gate_sum(own, got):
    groups, width = own.shape
    return pl.pallas_call(
        functools.partial(gate_kernel, len(got)),
        out_shape=[jax.ShapeDtypeStruct((1, width), f32)] * groups,
        in_specs=[VMEM] * (1 + len(got)),
        out_specs=[VMEM] * groups,
        compiler_params=params(),
        cost_estimate=cost(0, 8 * groups * width),
    )(own, *got)


def grad_kernel(n_left, n_pieces, *refs):
    lefts, pieces, outs = refs[:n_left], refs[n_left : n_left + n_pieces], refs[n_left + n_pieces :]
    rows, width = outs[0].shape
    total = rows * len(outs)
    left = []
    for ref in lefts:
        left += [ref[i].reshape(total, -1) for i in range(ref.shape[0])]
    left = jnp.concatenate(left, axis=1)
    block = 256
    for start in range(0, width, block):
        cols = slice(start, start + block)
        right = jnp.concatenate([p[:, cols] for p in pieces], axis=0)
        got = jnp.dot(left, right, preferred_element_type=f32)
        for g, out in enumerate(outs):
            out[:, cols] = got[g * rows : (g + 1) * rows].astype(out.dtype)


def grad_product(lefts, pieces):
    groups, rows = lefts[0].shape[1:3]
    depth = pieces[0].shape[0] * len(pieces)
    width = pieces[0].shape[1]
    total = groups * rows
    shapes = [jax.ShapeDtypeStruct((rows, width), f32)]
    shapes += [jax.ShapeDtypeStruct((rows, width), bf16)] * (groups - 1)
    return pl.pallas_call(
        functools.partial(grad_kernel, len(lefts), len(pieces)),
        out_shape=shapes,
        in_specs=[VMEM] * (len(lefts) + len(pieces)),
        out_specs=[VMEM] * groups,
        compiler_params=params(),
        cost_estimate=cost(
            2 * total * depth * width, 2 * (total * depth + depth * width + total * width)
        ),
    )(*lefts, *pieces)


def on_device(
    caption_states,
    caption_gain,
    text_proj,
    caption_len,
    slot_source,
    query_gain,
    key_gain,
    image_q,
    image_k,
    image_v,
    out_weight,
    gate,
    d_out,
):
    n_dp = lax.axis_size("dp")
    n_seq = lax.axis_size("seq")
    G, C = GROUPS, CORES
    O = n_seq // (G * C)
    OC = O * C
    dp = lax.axis_index("dp")
    seq = lax.axis_index("seq")
    z = (seq // C) % G
    oc = (seq // (G * C)) * C + seq % C

    def place(oc_at, z_at):
        return ((oc_at // C) * G + z_at) * C + oc_at % C

    def to_z(x, k):
        perm = [(place(a, b), place(a, b ^ k)) for a in range(OC) for b in range(G)]
        return lax.ppermute(x, "seq", perm)

    def to_oc(x, j):
        perm = [(place(a, b), place(a ^ j, b)) for a in range(OC) for b in range(G)]
        return lax.ppermute(x, "seq", perm)

    def to_dp(x, k):
        return lax.ppermute(x, "dp", [(a, a ^ k) for a in range(n_dp)])

    def part(x, index, size, axis):
        return lax.dynamic_slice_in_dim(x, index * size, size, axis)

    slot_total = slot_source.shape[1]
    slot_local = slot_total // n_seq
    image_local = image_q.shape[1]
    inner_width = image_q.shape[2]
    model_width = out_weight.shape[0]
    head_size = query_gain.shape[0]
    gw = inner_width // G
    order = [2, 3, 1]
    meta = jnp.stack([z, oc, dp]).astype(jnp.int32)

    bias, *both = text_project(
        meta, caption_len, slot_source, caption_states[0], caption_gain[None], text_proj,
        image_k[0], image_v[0], image_q[0], G, OC, place,
    )
    packed, partials = both[:G], both[G:]
    qkv = {k: to_z(packed[k], k) for k in order}
    sums = text_sum(partials[0], [to_oc(partials[j], j) for j in range(1, OC)])
    d_attn, *gg = gated(meta, gate, d_out[0], out_weight, sums[0], n_dp, G, OC, place)
    got = [to_z(sums[k], k) for k in order]
    qkv[0], text_q, text_kv = text_norm(
        packed[0], d_attn, query_gain[None], key_gain[None], sums[0], got, DT5
    )
    text_kvs = [text_kv] + [to_oc(text_kv, j) for j in range(1, OC)]
    kv_pieces = [qkv[k] for k in range(G)]
    for j in range(1, OC):
        kv_pieces += [to_oc(qkv[k], j) for k in range(G)]

    queries = [text_q] + [qkv[k] for k in range(G)]
    found = list(attention(gg[1:], queries, kv_pieces, text_kvs, bias, gw, head_size))
    gg, text_out, outs = gg[:1] + found[: n_dp - 1], found[n_dp - 1], found[n_dp:]
    gg_dp = [gg[0]] + [to_dp(gg[k], k) for k in range(1, n_dp)]
    lefts = [g[:1] for g in gg_dp]
    lefts += [to_oc(g, j + 1) for j, g in enumerate(gather_parts(gg_dp))]

    back = []
    for k in range(G):
        rows = jnp.concatenate([outs[k], part(text_out, z ^ k, slot_local, 0)], axis=0)
        back.append(to_z(rows, k) if k else rows)
    own_slots = part(slot_source[0] < caption_len[0], seq, slot_local, 0)
    image_attn, text_attn = assemble(
        meta, own_slots.astype(jnp.int32)[:, None], back, gg_dp[1:]
    )

    attn_dp = [image_attn] + [to_dp(image_attn, k) for k in range(1, n_dp)]
    attn_pieces = list(attn_dp)
    for j in range(1, OC):
        attn_pieces += [to_oc(p, j) for p in attn_dp]

    grads = grad_product(lefts, attn_pieces)
    grad_wo = grads[0]
    for k in order:
        grad_wo = grad_wo + to_z(grads[k], k).astype(f32)

    image_out, *terms = project(
        meta, image_attn, out_weight, gate, d_out[0], grads[0], G, OC, place
    )
    terms = gate_sum(terms[0], [to_oc(terms[j], j) for j in range(1, OC)])
    grad_gate = terms[0]
    for k in order:
        grad_gate = grad_gate + to_z(terms[k], k)
    return (image_out[None], text_attn[None], d_attn[None], grad_wo, grad_gate)


def solution(mesh):
    in_specs = (
        P("dp", None, "seq"),
        P("seq"),
        P("seq", None),
        P("dp"),
        P("dp", None),
        P(),
        P(),
        P("dp", "seq", None),
        P("dp", "seq", None),
        P("dp", "seq", None),
        P(),
        P("dp", None),
        P("dp", "seq", None),
    )
    out_specs = (
        P("dp", "seq", None),
        P("dp", "seq", None),
        P("dp", "seq", None),
        P(("dp", "seq"), None),
        P("dp", "seq"),
    )
    return jax.shard_map(
        on_device, mesh=mesh, in_specs=in_specs, out_specs=out_specs, check_vma=False
    )
```

```python
import math
import functools
import jax
import jax.numpy as jnp
from jax import lax
from jax.experimental import pallas as pl
from jax.experimental.pallas import tpu as pltpu
from jax.sharding import PartitionSpec as P

DT5 = 4096
CORES = 2
GROUPS = 4

eps_norm = 1e-06
f32 = jnp.float32
bf16 = jnp.bfloat16


VMEM = pl.BlockSpec(memory_space=pltpu.VMEM)
SMEM = pl.BlockSpec(memory_space=pltpu.SMEM)
ANY = pl.BlockSpec(memory_space=pl.ANY)


def params(mib=24):
    return pltpu.CompilerParams(vmem_limit_bytes=int(mib * 1024 * 1024))


def cost(flops, bytes_accessed, transcendentals=0):
    return pl.CostEstimate(
        flops=flops, bytes_accessed=bytes_accessed, transcendentals=transcendentals
    )


def split_tail(squares, width):
    high = squares.astype(bf16).astype(f32)
    low = squares - high
    lane = lax.broadcasted_iota(jnp.int32, (squares.shape[0], width), 1)
    return jnp.where(lane == 0, high, jnp.where(lane == 1, low, 0.0))


def joined(tail):
    return tail[:, 0:1] + tail[:, 1:2]


def text_kernel(
    groups, heads, place_of, meta_ref, len_ref, src_ref, states_ref, gain_ref, w_ref, bias_ref, own_ref, *msgs
):
    size = own_ref.shape[2]
    rows = own_ref.shape[1] // (3 * heads + 1)
    width = heads * size
    slots = states_ref.shape[0]
    slot_local = rows // groups

    def slot_at(row):
        z_at = (row % rows) // slot_local
        return place_of(meta_ref[1] ^ (row // rows), z_at) * slot_local + row % slot_local

    iota = functools.partial(lax.broadcasted_iota, jnp.int32, (slots, slots))
    sources = src_ref[...].astype(f32)
    chosen = (iota(1) == slot_at(iota(0))).astype(f32)
    source_col = jnp.sum(chosen * sources, axis=1, keepdims=True)
    pick = (iota(1).astype(f32) == source_col).astype(bf16)
    chosen_t = (iota(0) == slot_at(iota(1))).astype(bf16)
    source_row = jnp.dot(sources.astype(bf16), chosen_t, preferred_element_type=f32)
    bias_ref[...] = jnp.where(source_row < len_ref[0].astype(f32), 0.0, -1e30)

    picked = jnp.dot(pick, states_ref[...], preferred_element_type=f32)
    scaled = (picked * gain_ref[...]).astype(bf16)
    tail = split_tail(jnp.sum(picked * picked, axis=1, keepdims=True), size)
    for g in range(groups):
        for i in range(3):
            at = (i * groups + (meta_ref[0] ^ g)) * width
            got = jnp.dot(
                scaled, w_ref[:, pl.ds(pl.multiple_of(at, 128), width)], preferred_element_type=f32
            )
            for head in range(heads):
                part = got[:, head * size : (head + 1) * size]
                to = slice((i * heads + head) * rows, (i * heads + head + 1) * rows)
                own_ref[g, to, :] = part[:rows]
                for j, msg in enumerate(msgs):
                    msg[g, to, :] = part[(j + 1) * rows : (j + 2) * rows].astype(bf16)
        own_ref[g, 3 * heads * rows :, :] = tail[:rows]
        for j, msg in enumerate(msgs):
            msg[g, 3 * heads * rows :, :] = tail[(j + 1) * rows : (j + 2) * rows].astype(bf16)


def text_project(meta, length, sources, states, gain, text_proj, groups, parts, size, place_of):
    slots, depth = states.shape
    heads = text_proj.shape[1] // (3 * groups * size)
    block = (groups, (3 * heads + 1) * slots // parts, size)
    shapes = [jax.ShapeDtypeStruct((1, slots), f32), jax.ShapeDtypeStruct(block, f32)]
    shapes += [jax.ShapeDtypeStruct(block, bf16)] * (parts - 1)
    return pl.pallas_call(
        functools.partial(text_kernel, groups, heads, place_of),
        out_shape=shapes,
        in_specs=[SMEM, SMEM, VMEM, VMEM, VMEM, VMEM],
        out_specs=[VMEM] * (1 + parts),
        compiler_params=params(),
        cost_estimate=cost(
            2 * slots * depth * text_proj.shape[1], 2 * depth * text_proj.shape[1]
        ),
    )(meta, length, sources, states, gain, text_proj)


def pack_kernel(groups, n_got, meta_ref, k_ref, v_ref, q_ref, *refs):
    part_refs, (own_ref, *outs) = refs[: 1 + n_got], refs[1 + n_got :]
    rows = k_ref.shape[0]
    size = own_ref.shape[1]
    heads = k_ref.shape[1] // (groups * size)
    text_rows = own_ref.shape[0]
    tail_rows = text_rows // (3 * heads + 1)
    for g, out in enumerate(outs):
        for i, ref in enumerate((k_ref, v_ref, q_ref)):
            for head in range(heads):
                at = ((meta_ref[0] ^ g) * heads + head) * size
                to = (i * heads + head) * rows
                out[to : to + rows, :] = ref[:, pl.ds(pl.multiple_of(at, 128), size)]
        total = part_refs[0][g]
        for ref in part_refs[1:]:
            total = total + ref[g].astype(f32)
        tail = split_tail(joined(total[text_rows - tail_rows :]), size)
        total = jnp.concatenate([total[: text_rows - tail_rows], tail], axis=0)
        if g == 0:
            own_ref[...] = total
        else:
            out[3 * heads * rows :, :] = total.astype(bf16)


def pack(meta, keys, values, queries, partials, groups):
    rows = keys.shape[0]
    text_rows, size = partials[0].shape[1:]
    image_rows = 3 * rows * keys.shape[1] // (groups * size)
    shapes = [jax.ShapeDtypeStruct((text_rows, size), f32)]
    shapes += [jax.ShapeDtypeStruct((image_rows, size), bf16)]
    shapes += [jax.ShapeDtypeStruct((image_rows + text_rows, size), bf16)] * (groups - 1)
    return pl.pallas_call(
        functools.partial(pack_kernel, groups, len(partials) - 1),
        out_shape=shapes,
        in_specs=[SMEM] + [VMEM] * (3 + len(partials)),
        out_specs=[VMEM] * (1 + groups),
        compiler_params=params(),
        cost_estimate=cost(0, 12 * keys.size),
    )(meta, keys, values, queries, *partials)


def text_norm_kernel(features, qg_ref, kg_ref, own_ref, *refs):
    got, (tq_ref, tkv_ref) = refs[:-2], refs[-2:]
    size = own_ref.shape[1]
    total = own_ref[...]
    for ref in got:
        total = total + ref[ref.shape[0] - total.shape[0] :, :].astype(f32)
    width = tq_ref.shape[0]
    rows = total.shape[0] - 3 * width
    heads = width // rows
    rate = lax.rsqrt(joined(total[3 * width :]) / features + eps_norm)
    for i in range(3):
        for head in range(heads):
            at = (i * heads + head) * rows
            x = total[at : at + rows] * rate
            if i < 2:
                mean = jnp.sum(x * x, axis=1, keepdims=True) / size
                x = x * lax.rsqrt(mean + eps_norm) * (qg_ref, kg_ref)[i][...]
            if i == 0:
                tq_ref[at : at + rows, :] = x.astype(bf16)
            else:
                tkv_ref[at - width : at - width + rows, :] = x.astype(bf16)


def text_norm(query_gain, key_gain, own, got, features, heads):
    text_rows, size = own.shape
    width = text_rows // (3 * heads + 1) * heads
    return pl.pallas_call(
        functools.partial(text_norm_kernel, features),
        out_shape=[
            jax.ShapeDtypeStruct((width, size), bf16),
            jax.ShapeDtypeStruct((2 * width, size), bf16),
        ],
        in_specs=[VMEM] * (3 + len(got)),
        out_specs=[VMEM] * 2,
        compiler_params=params(),
        cost_estimate=cost(0, 40_000_000),
    )(query_gain, key_gain, own, *got)


def block_kernel(n_got, *refs):
    pieces, text_ref, out_ref = refs[:n_got], refs[n_got], refs[-1]
    rows = (out_ref.shape[0] - text_ref.shape[0]) // n_got
    for k, piece in enumerate(pieces):
        out_ref[k * rows : (k + 1) * rows, :] = piece[:rows, :]
    out_ref[n_got * rows :, :] = text_ref[...]


def block_of(pieces, text_kv, after):
    rows, size = pieces[0].shape
    total = rows // 3 * 2 * len(pieces) + text_kv.shape[0]
    return pl.pallas_call(
        functools.partial(block_kernel, len(pieces)),
        out_shape=jax.ShapeDtypeStruct((total, size), bf16),
        in_specs=[VMEM] * (len(pieces) + 1) + [ANY] * len(after),
        out_specs=VMEM,
        compiler_params=params(),
        cost_estimate=cost(0, 4 * total * size),
    )(*pieces, text_kv, *after)


def attention_kernel(n_pieces, n_blocks, rows, text_rows, *refs):
    pieces, refs = refs[:n_pieces], refs[n_pieces:]
    tq_ref, tkv_ref, refs = refs[0], refs[1], refs[2:]
    blocks, refs = refs[:n_blocks], refs[n_blocks:]
    bias_ref, out_refs, tout_ref = refs[0], refs[1:-1], refs[-1]
    size = tq_ref.shape[1]
    heads = tq_ref.shape[0] // text_rows
    factor = size ** (-0.5) * math.log2(math.e)
    bias = bias_ref[...]
    nt = (((1,), (1,)), ((), ()))
    own = 2 * heads * rows

    def with_ones(values):
        return jnp.concatenate([values, jnp.ones(values.shape, bf16)], axis=1)

    for head in range(heads):
        kv, tkv = [], []
        for i in range(2):
            at = (i * heads + head) * rows
            image = [p[at : at + rows, :] for p in pieces]
            text_at = (i * heads + head) * text_rows
            text = [tkv_ref[text_at : text_at + text_rows, :]]
            for b in blocks:
                image += [b[k * own + at : k * own + at + rows, :] for k in range(n_pieces)]
                start = n_pieces * own + text_at
                text.append(b[start : start + text_rows, :])
            kv.append(jnp.concatenate(image, axis=0))
            tkv.append(jnp.concatenate(text, axis=0))
        keys, values = kv[0], with_ones(kv[1])
        tkeys, tvalues = tkv[0], with_ones(tkv[1])
        cols = slice(head * size, (head + 1) * size)
        q_at = (2 * heads + head) * rows
        work = [(p[q_at : q_at + rows, :], out) for p, out in zip(pieces, out_refs)]
        work.append((tq_ref[head * text_rows : (head + 1) * text_rows, :], tout_ref))
        for q, out_ref in work:
            s_img = lax.dot_general(q, keys, nt, preferred_element_type=f32)
            s_txt = lax.dot_general(q, tkeys, nt, preferred_element_type=f32) + bias
            top = jnp.maximum(
                jnp.max(s_img, axis=1, keepdims=True), jnp.max(s_txt, axis=1, keepdims=True)
            )
            p_img = jnp.exp2((s_img - top) * factor).astype(bf16)
            p_txt = jnp.exp2((s_txt - top) * factor).astype(bf16)
            acc = jnp.dot(p_img, values, preferred_element_type=f32)
            acc = acc + jnp.dot(p_txt, tvalues, preferred_element_type=f32)
            out_ref[:, cols] = (acc[:, :size] / acc[:, size:]).astype(bf16)


def attention(pieces, text_q, text_kv, blocks, bias, rows, text_rows):
    size = text_q.shape[1]
    heads = text_q.shape[0] // text_rows
    queries = len(pieces) * rows + text_rows
    keys = (1 + len(blocks)) * queries
    args = tuple(pieces) + (text_q, text_kv) + tuple(blocks) + (bias,)
    shapes = [jax.ShapeDtypeStruct((rows, heads * size), bf16)] * len(pieces)
    shapes += [jax.ShapeDtypeStruct((text_rows, heads * size), bf16)]
    return pl.pallas_call(
        functools.partial(attention_kernel, len(pieces), len(blocks), rows, text_rows),
        out_shape=shapes,
        in_specs=[VMEM] * len(args),
        out_specs=[VMEM] * len(shapes),
        compiler_params=params(),
        cost_estimate=cost(
            4 * queries * keys * heads * size,
            4 * (queries + keys) * heads * size,
            queries * keys * heads,
        ),
    )(*args)


def gated_kernel(groups, parts, place_of, meta_ref, gate_ref, d_out_ref, *refs):
    msgs, turned = refs[:-1], refs[-1]
    gated = (gate_ref[...] * d_out_ref[...].astype(f32)).astype(bf16)
    turned[...] = gated.astype(f32).T
    rows = msgs[0].shape[2]
    z, oc, dp = meta_ref[0], meta_ref[1], meta_ref[2]
    for k, msg in enumerate(msgs):
        for j in range(parts):
            for g in range(groups):
                at = (dp ^ k) * (groups * parts) + place_of(oc ^ j, z ^ g)
                msg[j, g] = turned[pl.ds(pl.multiple_of(at * rows, 8), rows), :].astype(bf16)


def gated_parts(meta, gate, d_out, n_dp, groups, parts, place_of):
    local, model = d_out.shape
    rows = model // (n_dp * groups * parts)
    return pl.pallas_call(
        functools.partial(gated_kernel, groups, parts, place_of),
        out_shape=[jax.ShapeDtypeStruct((parts, groups, rows, local), bf16)] * n_dp,
        in_specs=[SMEM, VMEM, VMEM],
        out_specs=[VMEM] * n_dp,
        scratch_shapes=[pltpu.VMEM((model, local), f32)],
        compiler_params=params(),
        cost_estimate=cost(0, 4 * local * model),
    )(meta, gate, d_out)


def d_attn_kernel(gate_ref, d_out_ref, w_ref, out_ref):
    block = 512
    total = jnp.zeros(out_ref.shape, f32)
    for at in range(0, w_ref.shape[0], block):
        cols = slice(at, at + block)
        gated = (gate_ref[:, cols] * d_out_ref[:, cols].astype(f32)).astype(bf16)
        total = total + jnp.dot(gated, w_ref[cols, :], preferred_element_type=f32)
    out_ref[...] = total.astype(bf16)


def attn_gradient(gate, d_out, out_weight):
    local, model = d_out.shape
    inner = out_weight.shape[1]
    return pl.pallas_call(
        d_attn_kernel,
        out_shape=jax.ShapeDtypeStruct((local, inner), bf16),
        in_specs=[VMEM] * 3,
        out_specs=VMEM,
        compiler_params=params(),
        cost_estimate=cost(2 * local * inner * model, 2 * inner * model),
    )(gate, d_out, out_weight)


def gather_kernel(n_dp, *refs):
    pieces, outs = refs[:n_dp], refs[n_dp:]
    for j, out in enumerate(outs):
        for k, piece in enumerate(pieces):
            out[k] = piece[j + 1]


def gather_parts(pieces):
    parts = pieces[0].shape[0]
    shape = (len(pieces),) + pieces[0].shape[1:]
    return pl.pallas_call(
        functools.partial(gather_kernel, len(pieces)),
        out_shape=[jax.ShapeDtypeStruct(shape, bf16)] * (parts - 1),
        in_specs=[VMEM] * len(pieces),
        out_specs=[VMEM] * (parts - 1),
        compiler_params=params(),
        cost_estimate=cost(0, 4 * math.prod(shape) * (parts - 1)),
    )(*pieces)


def project_kernel(groups, parts, place_of, meta_ref, attn_ref, w_ref, gate_ref, d_out_ref, after_ref, out_ref, *refs):
    del after_ref
    terms, by_place = refs[:parts], refs[parts]
    block = 512
    sums = []
    for at in range(0, w_ref.shape[0], block):
        cols = slice(at, at + block)
        got = lax.dot_general(
            attn_ref[...], w_ref[cols, :], (((1,), (1,)), ((), ())), preferred_element_type=f32
        )
        out_ref[:, cols] = (got * gate_ref[:, cols]).astype(bf16)
        sums.append(jnp.sum(got * d_out_ref[:, cols].astype(f32), axis=0, keepdims=True))
    sums = jnp.concatenate(sums, axis=1)
    places, width = by_place.shape
    for s in range(places):
        by_place[s : s + 1, :] = sums[:, s * width : (s + 1) * width]
    for j, term in enumerate(terms):
        for g in range(groups):
            at = place_of(meta_ref[1] ^ j, meta_ref[0] ^ g)
            term[g : g + 1, :] = by_place[pl.ds(at, 1), :]


def project(meta, attn, out_weight, gate, d_out, after, groups, parts, place_of):
    rows, inner = attn.shape
    model = out_weight.shape[0]
    width = model // (groups * parts)
    shapes = [jax.ShapeDtypeStruct((rows, model), bf16)]
    shapes += [jax.ShapeDtypeStruct((groups, width), f32)] * parts
    return pl.pallas_call(
        functools.partial(project_kernel, groups, parts, place_of),
        out_shape=shapes,
        in_specs=[SMEM, VMEM, VMEM, VMEM, VMEM, ANY],
        out_specs=[VMEM] * (1 + parts),
        scratch_shapes=[pltpu.VMEM((groups * parts, width), f32)],
        compiler_params=params(),
        cost_estimate=cost(2 * rows * inner * model, 2 * inner * model),
    )(meta, attn, out_weight, gate, d_out, after)


def grad_kernel(n_left, n_pieces, *refs):
    lefts, refs = refs[:n_left], refs[n_left:]
    pieces, outs = refs[:n_pieces], refs[n_pieces:]
    rows, width = outs[0].shape
    total = rows * len(outs)
    left = []
    for ref in lefts:
        left += [ref[i].reshape(total, -1) for i in range(ref.shape[0])]
    left = jnp.concatenate(left, axis=1)
    block = 256
    for start in range(0, width, block):
        cols = slice(start, start + block)
        right = jnp.concatenate([p[:, cols] for p in pieces], axis=0)
        got = jnp.dot(left, right, preferred_element_type=f32)
        for g, out in enumerate(outs):
            out[:, cols] = got[g * rows : (g + 1) * rows].astype(out.dtype)


def grad_product(lefts, pieces):
    groups, rows = lefts[0].shape[1:3]
    depth = pieces[0].shape[0] * len(pieces)
    width = pieces[0].shape[1]
    total = groups * rows
    shapes = [jax.ShapeDtypeStruct((rows, width), f32)]
    shapes += [jax.ShapeDtypeStruct((rows, width), bf16)] * (groups - 1)
    return pl.pallas_call(
        functools.partial(grad_kernel, len(lefts), len(pieces)),
        out_shape=shapes,
        in_specs=[VMEM] * (len(lefts) + len(pieces)),
        out_specs=[VMEM] * groups,
        compiler_params=params(),
        cost_estimate=cost(
            2 * total * depth * width, 2 * (total * depth + depth * width + total * width)
        ),
    )(*lefts, *pieces)


def on_device(
    caption_states,
    caption_gain,
    text_proj,
    caption_len,
    slot_source,
    query_gain,
    key_gain,
    image_q,
    image_k,
    image_v,
    out_weight,
    gate,
    d_out,
):
    n_dp = lax.axis_size("dp")
    n_seq = lax.axis_size("seq")
    G, C = GROUPS, CORES
    O = n_seq // (G * C)
    OC = O * C
    dp = lax.axis_index("dp")
    seq = lax.axis_index("seq")
    z = (seq // C) % G
    oc = (seq // (G * C)) * C + seq % C

    def place(oc_at, z_at):
        return ((oc_at // C) * G + z_at) * C + oc_at % C

    def to_z(x, k):
        perm = [(place(a, b), place(a, b ^ k)) for a in range(OC) for b in range(G)]
        return lax.ppermute(x, "seq", perm)

    def to_oc(x, j):
        perm = [(place(a, b), place(a ^ j, b)) for a in range(OC) for b in range(G)]
        return lax.ppermute(x, "seq", perm)

    def to_dp(x, k):
        return lax.ppermute(x, "dp", [(a, a ^ k) for a in range(n_dp)])

    def part(x, index, size, axis):
        return lax.dynamic_slice_in_dim(x, index * size, size, axis)

    slot_total = slot_source.shape[1]
    slot_local = slot_total // n_seq
    image_local = image_q.shape[1]
    inner_width = image_q.shape[2]
    model_width = out_weight.shape[0]
    head_size = query_gain.shape[0]
    gw = inner_width // G
    order = [2, 3, 1]
    meta = jnp.stack([z, oc, dp]).astype(jnp.int32)

    heads = gw // head_size
    text_rows = G * slot_local
    bias, *partials = text_project(
        meta, caption_len, slot_source, caption_states[0], caption_gain[None], text_proj,
        G, OC, head_size, place,
    )
    partials = [partials[0]] + [to_oc(partials[j], j) for j in range(1, OC)]
    own, *packed = pack(meta, image_k[0], image_v[0], image_q[0], partials, G)
    pieces = {0: packed[0]}
    for k in order:
        pieces[k] = to_z(packed[k], k)
    pieces = [pieces[k] for k in range(G)]
    text_q, text_kv = text_norm(
        query_gain[None], key_gain[None], own, pieces[1:], DT5, heads
    )

    gg = gated_parts(meta, gate, d_out[0], n_dp, G, OC, place)
    gg_dp = [gg[0]] + [to_dp(gg[k], k) for k in range(1, n_dp)]
    lefts = [g[:1] for g in gg_dp]
    lefts += [to_oc(g, j + 1) for j, g in enumerate(gather_parts(gg_dp))]

    block = block_of(pieces, text_kv, gg_dp[1:])
    blocks = [to_oc(block, j) for j in range(1, OC)]
    *outs, text_out = attention(
        pieces, text_q, text_kv, blocks, bias, image_local, text_rows
    )
    d_attn = attn_gradient(gate, d_out[0], out_weight)

    attn = jnp.zeros((image_local + slot_local, inner_width), bf16)
    for k in order + [0]:
        rows = jnp.concatenate([outs[k], part(text_out, z ^ k, slot_local, 0)], axis=0)
        rows = to_z(rows, k) if k else rows
        attn = lax.dynamic_update_slice_in_dim(attn, rows, (z ^ k) * gw, 1)
    image_attn = attn[:image_local]
    own_usable = part(slot_source[0] < caption_len[0], seq, slot_local, 0)
    text_attn = jnp.where(own_usable[:, None], attn[image_local:], jnp.zeros((), bf16))

    pieces = [image_attn] + [to_dp(image_attn, k) for k in range(1, n_dp)]
    pieces = pieces + [to_oc(p, j) for j in range(1, OC) for p in pieces]
    grads = grad_product(lefts, pieces)
    grad_wo = grads[0]
    for k in order:
        grad_wo = grad_wo + to_z(grads[k], k).astype(f32)

    image_out, *terms = project(
        meta, image_attn, out_weight, gate, d_out[0], pieces[n_dp], G, OC, place
    )
    term = terms[0]
    for j in range(1, OC):
        term = term + to_oc(terms[j], j)
    term = term[:2] + to_z(term[2:], 2)
    grad_gate = term[:1] + to_z(term[1:], 1)
    return (image_out[None], text_attn[None], d_attn[None], grad_wo, grad_gate)


def solution(mesh):
    in_specs = (
        P("dp", None, "seq"),
        P("seq"),
        P("seq", None),
        P("dp"),
        P("dp", None),
        P(),
        P(),
        P("dp", "seq", None),
        P("dp", "seq", None),
        P("dp", "seq", None),
        P(),
        P("dp", None),
        P("dp", "seq", None),
    )
    out_specs = (
        P("dp", "seq", None),
        P("dp", "seq", None),
        P("dp", "seq", None),
        P(("dp", "seq"), None),
        P("dp", "seq"),
    )
    return jax.shard_map(
        on_device, mesh=mesh, in_specs=in_specs, out_specs=out_specs, check_vma=False
    )
```

```python
import math
import functools
import jax
import jax.numpy as jnp
from jax import lax
from jax.experimental import pallas as pl
from jax.experimental.pallas import tpu as pltpu
from jax.sharding import PartitionSpec as P

DT5 = 4096
CORES = 2
GROUPS = 4

eps_norm = 1e-06
f32 = jnp.float32
bf16 = jnp.bfloat16
EXTRA = 16


VMEM = pl.BlockSpec(memory_space=pltpu.VMEM)
SMEM = pl.BlockSpec(memory_space=pltpu.SMEM)
ANY = pl.BlockSpec(memory_space=pl.ANY)


def params(mib=24):
    return pltpu.CompilerParams(vmem_limit_bytes=int(mib * 1024 * 1024))


def cost(flops, bytes_accessed, transcendentals=0):
    return pl.CostEstimate(
        flops=flops, bytes_accessed=bytes_accessed, transcendentals=transcendentals
    )


def split_tail(squares, width):
    high = squares.astype(bf16).astype(f32)
    low = squares - high
    lane = lax.broadcasted_iota(jnp.int32, (squares.shape[0], width), 1)
    return jnp.where(lane == 0, high, jnp.where(lane == 1, low, 0.0))


def joined(tail):
    return tail[:, 0:1] + tail[:, 1:2]


def text_kernel(
    groups, heads, place_of, meta_ref, len_ref, src_ref, states_ref, gain_ref, qg_ref, kg_ref,
    w_ref, k_ref, v_ref, q_ref, own_ref, *refs
):
    packed, refs = refs[:groups], refs[groups:]
    msgs, (w_all, w_sems, pack_sems) = refs[:-3], refs[-3:]
    size = own_ref.shape[2]
    rows = (own_ref.shape[1] - EXTRA) // (3 * heads + 1)
    width = heads * size
    slots = states_ref.shape[0]
    slot_local = rows // groups
    copies = []
    for g in range(groups):
        for i in range(3):
            at = (i * groups + (meta_ref[0] ^ g)) * width
            cols = pl.ds(pl.multiple_of(at, 128), width)
            copies.append(pltpu.make_async_copy(w_ref.at[:, cols], w_all.at[g, i], w_sems.at[g, i]))
            copies[-1].start()
    packs = []
    local = k_ref.shape[0]
    for g, out in enumerate(packed):
        for i, ref in enumerate((k_ref, v_ref, q_ref)):
            for head in range(heads):
                at = ((meta_ref[0] ^ g) * heads + head) * size
                source = ref.at[:, pl.ds(pl.multiple_of(at, 128), size)]
                target = out.at[pl.ds((i * heads + head) * local, local), :]
                sem = pack_sems.at[g, i * heads + head]
                packs.append(pltpu.make_async_copy(source, target, sem))
                packs[-1].start()

    def slot_at(row):
        z_at = (row % rows) // slot_local
        return place_of(meta_ref[1] ^ (row // rows), z_at) * slot_local + row % slot_local

    iota = functools.partial(lax.broadcasted_iota, jnp.int32, (slots, slots))
    sources = src_ref[...].astype(f32)
    chosen = (iota(1) == slot_at(iota(0))).astype(f32)
    source_col = jnp.sum(chosen * sources, axis=1, keepdims=True)
    pick = (iota(1).astype(f32) == source_col).astype(bf16)
    chosen_t = (iota(0) == slot_at(iota(1))).astype(bf16)
    source_row = jnp.dot(sources.astype(bf16), chosen_t, preferred_element_type=f32)
    bias = jnp.where(source_row < len_ref[0].astype(f32), 0.0, -1e30)
    end = own_ref.shape[1] - EXTRA
    own_ref[0, end:, :] = jnp.zeros((EXTRA, size), f32)
    own_ref[0, end : end + 1, :] = qg_ref[...]
    own_ref[0, end + 1 : end + 2, :] = kg_ref[...]
    own_ref[0, end + 2 : end + 3, :slots] = bias

    picked = jnp.dot(pick, states_ref[...], preferred_element_type=f32)
    scaled = (picked * gain_ref[...]).astype(bf16)
    tail = split_tail(jnp.sum(picked * picked, axis=1, keepdims=True), size)
    for g in range(groups):
        for i in range(3):
            copies[3 * g + i].wait()
            got = jnp.dot(scaled, w_all[g, i], preferred_element_type=f32)
            for head in range(heads):
                part = got[:, head * size : (head + 1) * size]
                to = slice((i * heads + head) * rows, (i * heads + head + 1) * rows)
                own_ref[g, to, :] = part[:rows]
                for j, msg in enumerate(msgs):
                    msg[g, to, :] = part[(j + 1) * rows : (j + 2) * rows].astype(bf16)
        own_ref[g, 3 * heads * rows : end, :] = tail[:rows]
        for j, msg in enumerate(msgs):
            msg[g, 3 * heads * rows :, :] = tail[(j + 1) * rows : (j + 2) * rows].astype(bf16)
    for copy in packs:
        copy.wait()


def text_project(
    meta, length, sources, states, gain, query_gain, key_gain, text_proj, keys, values, queries,
    groups, parts, place_of
):
    slots, depth = states.shape
    size = query_gain.shape[1]
    local = keys.shape[0]
    heads = text_proj.shape[1] // (3 * groups * size)
    text_rows = (3 * heads + 1) * slots // parts
    shapes = [jax.ShapeDtypeStruct((groups, text_rows + EXTRA, size), f32)]
    for g in range(groups):
        rows = 3 * heads * local + (text_rows if g else 0)
        shapes.append(jax.ShapeDtypeStruct((rows, size), bf16))
    shapes += [jax.ShapeDtypeStruct((groups, text_rows, size), bf16)] * (parts - 1)
    return pl.pallas_call(
        functools.partial(text_kernel, groups, heads, place_of),
        out_shape=shapes,
        in_specs=[SMEM, SMEM] + [VMEM] * 5 + [ANY] * 4,
        out_specs=[VMEM] + [ANY] * groups + [VMEM] * (parts - 1),
        scratch_shapes=[
            pltpu.VMEM((groups, 3, depth, heads * size), bf16),
            pltpu.SemaphoreType.DMA((groups, 3)),
            pltpu.SemaphoreType.DMA((groups, 3 * heads)),
        ],
        compiler_params=params(60),
        cost_estimate=cost(
            2 * slots * depth * text_proj.shape[1], 2 * depth * text_proj.shape[1]
        ),
    )(
        meta, length, sources, states, gain, query_gain, key_gain, text_proj, keys, values, queries
    )


def pack_kernel(n_got, n_out, tail_rows, *refs):
    own_ref, got, refs = refs[0], refs[1 : 1 + n_got], refs[1 + n_got + n_out :]
    kept_ref, outs, (stage, sems) = refs[0], refs[1 : 1 + n_out], refs[1 + n_out :]
    text_rows, size = stage.shape[1:]
    copies = []
    for g in list(range(1, n_out + 1)) + [0]:
        total = own_ref[g, :text_rows, :]
        for ref in got:
            total = total + ref[g].astype(f32)
        tail = split_tail(joined(total[text_rows - tail_rows :]), size)
        total = jnp.concatenate([total[: text_rows - tail_rows], tail], axis=0)
        if g == 0:
            kept_ref[:text_rows, :] = total
            kept_ref[text_rows:, :] = own_ref[0, text_rows:, :]
        else:
            stage[g - 1] = total.astype(bf16)
            start = outs[g - 1].shape[0] - text_rows
            target = outs[g - 1].at[pl.ds(start, text_rows), :]
            copies.append(pltpu.make_async_copy(stage.at[g - 1], target, sems.at[g - 1]))
            copies[-1].start()
    for copy in copies:
        copy.wait()


def pack(own, got, packed, tail_rows):
    groups, rows, size = own.shape
    text_rows = rows - EXTRA
    n = len(packed)
    shapes = [jax.ShapeDtypeStruct((rows, size), f32)]
    shapes += [jax.ShapeDtypeStruct(p.shape, bf16) for p in packed]
    return pl.pallas_call(
        functools.partial(pack_kernel, len(got), n, tail_rows),
        out_shape=shapes,
        in_specs=[VMEM] * (1 + len(got)) + [ANY] * n,
        out_specs=[VMEM] + [ANY] * n,
        input_output_aliases={1 + len(got) + i: 1 + i for i in range(n)},
        scratch_shapes=[pltpu.VMEM((n, text_rows, size), bf16), pltpu.SemaphoreType.DMA((n,))],
        compiler_params=params(60),
        cost_estimate=cost(0, 8 * groups * rows * size),
    )(own, *got, *packed)


def block_kernel(features, heads, n_got, near_ref, own_hbm, *refs):
    got, (out_ref, _, _, own_ref, sems) = refs[:n_got], refs[-5:]
    size = own_ref.shape[1]
    image_rows = near_ref.shape[0]
    copies = [
        pltpu.make_async_copy(own_hbm, own_ref, sems.at[0]),
        pltpu.make_async_copy(near_ref, out_ref.at[pl.ds(0, image_rows), :], sems.at[1]),
    ]
    for copy in copies:
        copy.start()
    kv_rows = image_rows // 3 * 2
    for k, ref in enumerate(got):
        at = image_rows + k * kv_rows
        out_ref[at : at + kv_rows, :] = ref[:kv_rows, :]
    copies[0].wait()
    text_rows = own_ref.shape[0] - EXTRA
    rows = text_rows // (3 * heads + 1)
    total = own_ref[:text_rows, :]
    for ref in got:
        total = total + ref[image_rows:, :].astype(f32)
    rate = lax.rsqrt(joined(total[3 * heads * rows :]) / features + eps_norm)
    end = image_rows + n_got * kv_rows
    for i in range(3):
        for head in range(heads):
            at = (i * heads + head) * rows
            x = total[at : at + rows] * rate
            if i < 2:
                mean = jnp.sum(x * x, axis=1, keepdims=True) / size
                gain = own_ref[text_rows + i : text_rows + i + 1, :]
                x = x * lax.rsqrt(mean + eps_norm) * gain
            out_ref[end + at : end + at + rows, :] = x.astype(bf16)
    bias = own_ref[text_rows + 2 : text_rows + 3, :]
    at = end + 3 * heads * rows
    out_ref[at:, :] = jnp.broadcast_to(bias, (EXTRA, size)).astype(bf16)
    copies[1].wait()


def block_of(near, own, got, after, features, heads):
    image_rows, size = near.shape
    text_rows = own.shape[0] - EXTRA
    total = image_rows + image_rows // 3 * 2 * len(got)
    total += text_rows // (3 * heads + 1) * 3 * heads + EXTRA
    return pl.pallas_call(
        functools.partial(block_kernel, features, heads, len(got)),
        out_shape=[
            jax.ShapeDtypeStruct((total, size), bf16),
            jax.ShapeDtypeStruct(near.shape, bf16),
            jax.ShapeDtypeStruct(own.shape, f32),
        ],
        in_specs=[ANY] * 2 + [VMEM] * len(got) + [ANY] * len(after),
        out_specs=[VMEM, ANY, ANY],
        input_output_aliases={0: 1, 1: 2},
        scratch_shapes=[pltpu.VMEM(own.shape, f32), pltpu.SemaphoreType.DMA((2,))],
        compiler_params=params(),
        cost_estimate=cost(0, 4 * total * size),
    )(near, own, *got, *after)[0]


def attention_kernel(n_far, n_blocks, heads, rows, text_rows, *refs):
    far, refs = refs[:n_far], refs[n_far:]
    blocks, refs = refs[:n_blocks], refs[n_blocks:]
    out_refs, tout_ref = refs[:-1], refs[-1]
    size = blocks[0].shape[1]
    factor = size ** (-0.5) * math.log2(math.e)
    nt = (((1,), (1,)), ((), ()))
    near = 3 * heads * rows
    kv_rows = 2 * heads * rows
    starts = [0] + [near + k * kv_rows for k in range(n_far)]
    text = near + n_far * kv_rows
    end = text + 3 * heads * text_rows
    bias = blocks[0][end : end + EXTRA, :][:1, : n_blocks * text_rows].astype(f32)

    def with_ones(values):
        return jnp.concatenate([values, jnp.ones(values.shape, bf16)], axis=1)

    for head in range(heads):
        kv, tkv = [], []
        for i in range(2):
            at = (i * heads + head) * rows
            text_at = text + ((i + 1) * heads + head) * text_rows
            image = [b[start + at : start + at + rows, :] for b in blocks for start in starts]
            kv.append(jnp.concatenate(image, axis=0))
            tkv.append(jnp.concatenate([b[text_at : text_at + text_rows, :] for b in blocks], axis=0))
        keys, values = kv[0], with_ones(kv[1])
        tkeys, tvalues = tkv[0], with_ones(tkv[1])
        cols = slice(head * size, (head + 1) * size)
        q_at = (2 * heads + head) * rows
        work = [
            (ref[q_at : q_at + rows, :], out) for ref, out in zip((blocks[0],) + far, out_refs)
        ]
        tq_at = text + head * text_rows
        work.append((blocks[0][tq_at : tq_at + text_rows, :], tout_ref))
        for q, out_ref in work:
            s_img = lax.dot_general(q, keys, nt, preferred_element_type=f32)
            s_txt = lax.dot_general(q, tkeys, nt, preferred_element_type=f32) + bias
            top = jnp.maximum(
                jnp.max(s_img, axis=1, keepdims=True), jnp.max(s_txt, axis=1, keepdims=True)
            )
            p_img = jnp.exp2((s_img - top) * factor).astype(bf16)
            p_txt = jnp.exp2((s_txt - top) * factor).astype(bf16)
            acc = jnp.dot(p_img, values, preferred_element_type=f32)
            acc = acc + jnp.dot(p_txt, tvalues, preferred_element_type=f32)
            out_ref[:, cols] = (acc[:, :size] / acc[:, size:]).astype(bf16)


def attention(far, blocks, heads, rows, text_rows):
    size = blocks[0].shape[1]
    queries = (1 + len(far)) * rows + text_rows
    keys = len(blocks) * queries
    shapes = [jax.ShapeDtypeStruct((rows, heads * size), bf16)] * (1 + len(far))
    shapes += [jax.ShapeDtypeStruct((text_rows, heads * size), bf16)]
    return pl.pallas_call(
        functools.partial(
            attention_kernel, len(far), len(blocks), heads, rows, text_rows
        ),
        out_shape=shapes,
        in_specs=[VMEM] * (len(far) + len(blocks)),
        out_specs=[VMEM] * len(shapes),
        compiler_params=params(),
        cost_estimate=cost(
            4 * queries * keys * heads * size,
            4 * (queries + keys) * heads * size,
            queries * keys * heads,
        ),
    )(*far, *blocks)


def gated_kernel(groups, parts, place_of, meta_ref, gate_ref, d_out_ref, *refs):
    msgs, turned = refs[:-1], refs[-1]
    gated = (gate_ref[...] * d_out_ref[...].astype(f32)).astype(bf16)
    turned[...] = gated.astype(f32).T
    rows = msgs[0].shape[2]
    z, oc, dp = meta_ref[0], meta_ref[1], meta_ref[2]
    for k, msg in enumerate(msgs):
        for j in range(parts):
            for g in range(groups):
                at = (dp ^ k) * (groups * parts) + place_of(oc ^ j, z ^ g)
                msg[j, g] = turned[pl.ds(pl.multiple_of(at * rows, 8), rows), :].astype(bf16)


def gated_parts(meta, gate, d_out, n_dp, groups, parts, place_of):
    local, model = d_out.shape
    rows = model // (n_dp * groups * parts)
    return pl.pallas_call(
        functools.partial(gated_kernel, groups, parts, place_of),
        out_shape=[jax.ShapeDtypeStruct((parts, groups, rows, local), bf16)] * n_dp,
        in_specs=[SMEM, VMEM, VMEM],
        out_specs=[VMEM] * n_dp,
        scratch_shapes=[pltpu.VMEM((model, local), f32)],
        compiler_params=params(60),
        cost_estimate=cost(0, 4 * local * model),
    )(meta, gate, d_out)


def d_attn_kernel(gate_ref, d_out_ref, w_ref, after_ref, out_ref):
    del after_ref
    block = 512
    total = jnp.zeros(out_ref.shape, f32)
    for at in range(0, w_ref.shape[0], block):
        cols = slice(at, at + block)
        gated = (gate_ref[:, cols] * d_out_ref[:, cols].astype(f32)).astype(bf16)
        total = total + jnp.dot(gated, w_ref[cols, :], preferred_element_type=f32)
    out_ref[...] = total.astype(bf16)


def attn_gradient(gate, d_out, out_weight, after):
    local, model = d_out.shape
    inner = out_weight.shape[1]
    return pl.pallas_call(
        d_attn_kernel,
        out_shape=jax.ShapeDtypeStruct((local, inner), bf16),
        in_specs=[VMEM] * 3 + [ANY],
        out_specs=VMEM,
        compiler_params=params(),
        cost_estimate=cost(2 * local * inner * model, 2 * inner * model),
    )(gate, d_out, out_weight, after)


def gather_kernel(n_dp, *refs):
    pieces, outs = refs[:n_dp], refs[n_dp:]
    for j, out in enumerate(outs):
        for k, piece in enumerate(pieces):
            out[k] = piece[j + 1]


def gather_parts(pieces):
    parts = pieces[0].shape[0]
    shape = (len(pieces),) + pieces[0].shape[1:]
    return pl.pallas_call(
        functools.partial(gather_kernel, len(pieces)),
        out_shape=[jax.ShapeDtypeStruct(shape, bf16)] * (parts - 1),
        in_specs=[VMEM] * len(pieces),
        out_specs=[VMEM] * (parts - 1),
        compiler_params=params(),
        cost_estimate=cost(0, 4 * math.prod(shape) * (parts - 1)),
    )(*pieces)


def project_kernel(
    groups, parts, place_of, meta_ref, attn_ref, w_ref, gate_ref, d_out_ref, out_ref, term_ref, *refs
):
    sent, by_place = refs[:-1], refs[-1]
    rows = attn_ref.shape[0]
    block = 512
    sums = []
    for at in range(0, w_ref.shape[0], block):
        cols = slice(at, at + block)
        got = lax.dot_general(
            attn_ref[...], w_ref[cols, :], (((1,), (1,)), ((), ())), preferred_element_type=f32
        )
        out_ref[:, cols] = (got * gate_ref[:, cols]).astype(bf16)
        sums.append(jnp.sum(got * d_out_ref[:, cols].astype(f32), axis=0, keepdims=True))
    sums = jnp.concatenate(sums, axis=1)
    places, width = by_place.shape
    for s in range(places):
        by_place[s : s + 1, :] = sums[:, s * width : (s + 1) * width]
    for g in range(groups):
        at = place_of(meta_ref[1], meta_ref[0] ^ g)
        term_ref[g : g + 1, :] = by_place[pl.ds(at, 1), :]
    for j, out in enumerate(sent):
        out[:rows, :] = attn_ref[...]
        line = [
            by_place[pl.ds(place_of(meta_ref[1] ^ (j + 1), meta_ref[0] ^ g), 1), :]
            for g in range(groups)
        ]
        line = jnp.concatenate(line, axis=1)
        line = jnp.concatenate(
            [line, jnp.zeros((1, attn_ref.shape[1] - groups * width), f32)], axis=1
        ) if attn_ref.shape[1] > groups * width else line
        high = line.astype(bf16).astype(f32)
        lines = [high, line - high, jnp.zeros((EXTRA - 2, line.shape[1]), f32)]
        out[rows:, :] = jnp.concatenate(lines, axis=0).astype(bf16)


def project(meta, attn, out_weight, gate, d_out, groups, parts, place_of):
    rows, inner = attn.shape
    model = out_weight.shape[0]
    width = model // (groups * parts)
    shapes = [jax.ShapeDtypeStruct((rows, model), bf16)]
    shapes += [jax.ShapeDtypeStruct((groups, width), f32)]
    shapes += [jax.ShapeDtypeStruct((rows + EXTRA, inner), bf16)] * (parts - 1)
    return pl.pallas_call(
        functools.partial(project_kernel, groups, parts, place_of),
        out_shape=shapes,
        in_specs=[SMEM, VMEM, VMEM, VMEM, VMEM],
        out_specs=[VMEM] * (1 + parts),
        scratch_shapes=[pltpu.VMEM((groups * parts, width), f32)],
        compiler_params=params(),
        cost_estimate=cost(2 * rows * inner * model, 2 * inner * model),
    )(meta, attn, out_weight, gate, d_out)


def grad_kernel(n_left, n_pieces, *refs):
    lefts, refs = refs[:n_left], refs[n_left:]
    pieces, refs = refs[:n_pieces], refs[n_pieces:]
    term_ref, outs, (kept_ref, sent_ref) = refs[0], refs[1:-2], refs[-2:]
    groups, rows, depth = lefts[0].shape[1:]
    width = pieces[0].shape[1]
    left = []
    for ref in lefts:
        left += [ref[i].reshape(groups * rows, depth) for i in range(ref.shape[0])]
    left = jnp.concatenate(left, axis=1)
    block = 256
    for start in range(0, width, block):
        right = jnp.concatenate([p[:depth, start : start + block] for p in pieces], axis=0)
        got = jnp.dot(left, right, preferred_element_type=f32)
        for g, out in enumerate(outs):
            out[:, start : start + block] = got[g * rows : (g + 1) * rows].astype(out.dtype)
    term = term_ref[...]
    size = term.shape[1]
    for p in pieces:
        if p.shape[0] > depth:
            lines = p[depth:, :].astype(f32)
            line = lines[0:1, :] + lines[1:2, :]
            term = term + jnp.concatenate(
                [line[:, g * size : (g + 1) * size] for g in range(groups)], axis=0
            )
    kept_ref[...] = term[: groups // 2]
    sent_ref[...] = term[groups // 2 :]


def grad_product(lefts, pieces, term):
    groups, rows, depth = lefts[0].shape[1:]
    width = pieces[0].shape[1]
    total = groups * rows
    depth = depth * len(pieces)
    shapes = [jax.ShapeDtypeStruct((rows, width), f32)]
    shapes += [jax.ShapeDtypeStruct((rows, width), bf16)] * (groups - 1)
    shapes += [jax.ShapeDtypeStruct((groups // 2, term.shape[1]), f32)] * 2
    return pl.pallas_call(
        functools.partial(grad_kernel, len(lefts), len(pieces)),
        out_shape=shapes,
        in_specs=[VMEM] * (len(lefts) + len(pieces) + 1),
        out_specs=[VMEM] * len(shapes),
        compiler_params=params(),
        cost_estimate=cost(
            2 * total * depth * width, 2 * (total * depth + depth * width + total * width)
        ),
    )(*lefts, *pieces, term)


def on_device(
    caption_states,
    caption_gain,
    text_proj,
    caption_len,
    slot_source,
    query_gain,
    key_gain,
    image_q,
    image_k,
    image_v,
    out_weight,
    gate,
    d_out,
):
    n_dp = lax.axis_size("dp")
    n_seq = lax.axis_size("seq")
    G, C = GROUPS, CORES
    O = n_seq // (G * C)
    OC = O * C
    dp = lax.axis_index("dp")
    seq = lax.axis_index("seq")
    z = (seq // C) % G
    oc = (seq // (G * C)) * C + seq % C

    def place(oc_at, z_at):
        return ((oc_at // C) * G + z_at) * C + oc_at % C

    def to_z(x, k):
        perm = [(place(a, b), place(a, b ^ k)) for a in range(OC) for b in range(G)]
        return lax.ppermute(x, "seq", perm)

    def to_oc(x, j):
        perm = [(place(a, b), place(a ^ j, b)) for a in range(OC) for b in range(G)]
        return lax.ppermute(x, "seq", perm)

    def to_dp(x, k):
        return lax.ppermute(x, "dp", [(a, a ^ k) for a in range(n_dp)])

    def part(x, index, size, axis):
        return lax.dynamic_slice_in_dim(x, index * size, size, axis)

    slot_total = slot_source.shape[1]
    slot_local = slot_total // n_seq
    image_local = image_q.shape[1]
    inner_width = image_q.shape[2]
    model_width = out_weight.shape[0]
    head_size = query_gain.shape[0]
    gw = inner_width // G
    order = [2, 3, 1]
    meta = jnp.stack([z, oc, dp]).astype(jnp.int32)

    heads = gw // head_size
    text_rows = G * slot_local
    own, *rest = text_project(
        meta, caption_len, slot_source, caption_states[0], caption_gain[None],
        query_gain[None], key_gain[None], text_proj, image_k[0], image_v[0], image_q[0],
        G, OC, place,
    )
    packed, sent = rest[:G], rest[G:]
    got = [to_oc(x, j + 1) for j, x in enumerate(sent)]
    own, *messages = pack(own, got, packed[1:], text_rows)
    far = {k: to_z(messages[k - 1], k) for k in order}
    far = [far[k] for k in range(1, G)]

    gg = gated_parts(meta, gate, d_out[0], n_dp, G, OC, place)
    gg_dp = [gg[0]] + [to_dp(gg[k], k) for k in range(1, n_dp)]
    lefts = [g[:1] for g in gg_dp]
    lefts += [to_oc(g, j + 1) for j, g in enumerate(gather_parts(gg_dp))]

    block = block_of(packed[0], own, far, gg_dp[1:], DT5, heads)
    blocks = [block] + [to_oc(block, j) for j in range(1, OC)]
    *outs, text_out = attention(far, blocks, heads, image_local, text_rows)

    attn = jnp.zeros((image_local + slot_local, inner_width), bf16)
    for k in order + [0]:
        rows = jnp.concatenate([outs[k], part(text_out, z ^ k, slot_local, 0)], axis=0)
        rows = to_z(rows, k) if k else rows
        attn = lax.dynamic_update_slice_in_dim(attn, rows, (z ^ k) * gw, 1)
    image_attn = attn[:image_local]
    own_usable = part(slot_source[0] < caption_len[0], seq, slot_local, 0)
    text_attn = jnp.where(own_usable[:, None], attn[image_local:], jnp.zeros((), bf16))

    pieces = [image_attn] + [to_dp(image_attn, k) for k in range(1, n_dp)]
    image_out, term, *sent = project(
        meta, image_attn, out_weight, gate, d_out[0], G, OC, place
    )
    for j in range(1, OC):
        pieces += [to_oc(sent[j - 1], j)] + [to_oc(p, j) for p in pieces[1:n_dp]]
    *grads, kept, sent = grad_product(lefts, pieces, term)
    grad_wo = grads[0]
    for k in order:
        grad_wo = grad_wo + to_z(grads[k], k).astype(f32)
    term = kept + to_z(sent, 2)
    grad_gate = term[:1] + to_z(term[1:], 1)
    d_attn = attn_gradient(gate, d_out[0], out_weight, grads[1])
    return (image_out[None], text_attn[None], d_attn[None], grad_wo, grad_gate)


def solution(mesh):
    in_specs = (
        P("dp", None, "seq"),
        P("seq"),
        P("seq", None),
        P("dp"),
        P("dp", None),
        P(),
        P(),
        P("dp", "seq", None),
        P("dp", "seq", None),
        P("dp", "seq", None),
        P(),
        P("dp", None),
        P("dp", "seq", None),
    )
    out_specs = (
        P("dp", "seq", None),
        P("dp", "seq", None),
        P("dp", "seq", None),
        P(("dp", "seq"), None),
        P("dp", "seq"),
    )
    return jax.shard_map(
        on_device, mesh=mesh, in_specs=in_specs, out_specs=out_specs, check_vma=False
    )
```

```python
import math
import functools
import jax
import jax.numpy as jnp
from jax import lax
from jax.experimental import pallas as pl
from jax.experimental.pallas import tpu as pltpu
from jax.sharding import PartitionSpec as P

DT5 = 4096
CORES = 2
GROUPS = 4

eps_norm = 1e-06
f32 = jnp.float32
bf16 = jnp.bfloat16
EXTRA = 16


VMEM = pl.BlockSpec(memory_space=pltpu.VMEM)
SMEM = pl.BlockSpec(memory_space=pltpu.SMEM)
ANY = pl.BlockSpec(memory_space=pl.ANY)


def params(mib=24):
    return pltpu.CompilerParams(vmem_limit_bytes=int(mib * 1024 * 1024))


def cost(flops, bytes_accessed, transcendentals=0):
    return pl.CostEstimate(
        flops=flops, bytes_accessed=bytes_accessed, transcendentals=transcendentals
    )


def split_tail(squares, width):
    high = squares.astype(bf16).astype(f32)
    low = squares - high
    lane = lax.broadcasted_iota(jnp.int32, (squares.shape[0], width), 1)
    return jnp.where(lane == 0, high, jnp.where(lane == 1, low, 0.0))


def joined(tail):
    return tail[:, 0:1] + tail[:, 1:2]


def text_kernel(
    groups, heads, place_of, meta_ref, len_ref, src_ref, states_ref, gain_ref, qg_ref, kg_ref,
    w_ref, k_ref, v_ref, q_ref, own_ref, *refs
):
    packed, refs = refs[:groups], refs[groups:]
    msgs, (w_all, w_sems) = refs[:-2], refs[-2:]
    size = own_ref.shape[2]
    rows = (own_ref.shape[1] - EXTRA) // (3 * heads + 1)
    width = heads * size
    slots = states_ref.shape[0]
    slot_local = rows // groups
    copies = []
    for g in range(groups):
        for i in range(3):
            at = (i * groups + (meta_ref[0] ^ g)) * width
            cols = pl.ds(pl.multiple_of(at, 128), width)
            copies.append(pltpu.make_async_copy(w_ref.at[:, cols], w_all.at[g, i], w_sems.at[g, i]))
            copies[-1].start()
    local = k_ref.shape[0]
    for g, out in enumerate(packed):
        for i, ref in enumerate((k_ref, v_ref, q_ref)):
            for head in range(heads):
                at = ((meta_ref[0] ^ g) * heads + head) * size
                to = (i * heads + head) * local
                out[to : to + local, :] = ref[:, pl.ds(pl.multiple_of(at, 128), size)]

    def slot_at(row):
        z_at = (row % rows) // slot_local
        return place_of(meta_ref[1] ^ (row // rows), z_at) * slot_local + row % slot_local

    iota = functools.partial(lax.broadcasted_iota, jnp.int32, (slots, slots))
    sources = src_ref[...].astype(f32)
    chosen = (iota(1) == slot_at(iota(0))).astype(f32)
    source_col = jnp.sum(chosen * sources, axis=1, keepdims=True)
    pick = (iota(1).astype(f32) == source_col).astype(bf16)
    chosen_t = (iota(0) == slot_at(iota(1))).astype(bf16)
    source_row = jnp.dot(sources.astype(bf16), chosen_t, preferred_element_type=f32)
    bias = jnp.where(source_row < len_ref[0].astype(f32), 0.0, -1e30)
    end = own_ref.shape[1] - EXTRA
    own_ref[0, end:, :] = jnp.zeros((EXTRA, size), f32)
    own_ref[0, end : end + 1, :] = qg_ref[...]
    own_ref[0, end + 1 : end + 2, :] = kg_ref[...]
    own_ref[0, end + 2 : end + 3, :slots] = bias

    picked = jnp.dot(pick, states_ref[...], preferred_element_type=f32)
    scaled = (picked * gain_ref[...]).astype(bf16)
    tail = split_tail(jnp.sum(picked * picked, axis=1, keepdims=True), size)
    for g in range(groups):
        for i in range(3):
            copies[3 * g + i].wait()
            got = jnp.dot(scaled, w_all[g, i], preferred_element_type=f32)
            for head in range(heads):
                part = got[:, head * size : (head + 1) * size]
                to = slice((i * heads + head) * rows, (i * heads + head + 1) * rows)
                own_ref[g, to, :] = part[:rows]
                for j, msg in enumerate(msgs):
                    msg[g, to, :] = part[(j + 1) * rows : (j + 2) * rows].astype(bf16)
        own_ref[g, 3 * heads * rows : end, :] = tail[:rows]
        for j, msg in enumerate(msgs):
            msg[g, 3 * heads * rows :, :] = tail[(j + 1) * rows : (j + 2) * rows].astype(bf16)


def text_project(
    meta, length, sources, states, gain, query_gain, key_gain, text_proj, keys, values, queries,
    groups, parts, place_of
):
    slots, depth = states.shape
    size = query_gain.shape[1]
    local = keys.shape[0]
    heads = text_proj.shape[1] // (3 * groups * size)
    text_rows = (3 * heads + 1) * slots // parts
    shapes = [jax.ShapeDtypeStruct((groups, text_rows + EXTRA, size), f32)]
    for g in range(groups):
        rows = 3 * heads * local + (text_rows if g else 0)
        shapes.append(jax.ShapeDtypeStruct((rows, size), bf16))
    shapes += [jax.ShapeDtypeStruct((groups, text_rows, size), bf16)] * (parts - 1)
    return pl.pallas_call(
        functools.partial(text_kernel, groups, heads, place_of),
        out_shape=shapes,
        in_specs=[SMEM, SMEM] + [VMEM] * 5 + [ANY] + [VMEM] * 3,
        out_specs=[VMEM] * (groups + parts),
        scratch_shapes=[
            pltpu.VMEM((groups, 3, depth, heads * size), bf16),
            pltpu.SemaphoreType.DMA((groups, 3)),
        ],
        compiler_params=params(60),
        cost_estimate=cost(
            2 * slots * depth * text_proj.shape[1], 2 * depth * text_proj.shape[1]
        ),
    )(
        meta, length, sources, states, gain, query_gain, key_gain, text_proj, keys, values, queries
    )


def pack_kernel(n_got, n_out, tail_rows, *refs):
    own_ref, got, refs = refs[0], refs[1 : 1 + n_got], refs[1 + n_got + n_out :]
    kept_ref, outs, (stage, sems) = refs[0], refs[1 : 1 + n_out], refs[1 + n_out :]
    text_rows, size = stage.shape[1:]
    copies = []
    for g in list(range(1, n_out + 1)) + [0]:
        total = own_ref[g, :text_rows, :]
        for ref in got:
            total = total + ref[g].astype(f32)
        tail = split_tail(joined(total[text_rows - tail_rows :]), size)
        total = jnp.concatenate([total[: text_rows - tail_rows], tail], axis=0)
        if g == 0:
            kept_ref[:text_rows, :] = total
            kept_ref[text_rows:, :] = own_ref[0, text_rows:, :]
        else:
            stage[g - 1] = total.astype(bf16)
            start = outs[g - 1].shape[0] - text_rows
            target = outs[g - 1].at[pl.ds(start, text_rows), :]
            copies.append(pltpu.make_async_copy(stage.at[g - 1], target, sems.at[g - 1]))
            copies[-1].start()
    for copy in copies:
        copy.wait()


def pack(own, got, packed, tail_rows):
    groups, rows, size = own.shape
    text_rows = rows - EXTRA
    n = len(packed)
    shapes = [jax.ShapeDtypeStruct((rows, size), f32)]
    shapes += [jax.ShapeDtypeStruct(p.shape, bf16) for p in packed]
    return pl.pallas_call(
        functools.partial(pack_kernel, len(got), n, tail_rows),
        out_shape=shapes,
        in_specs=[VMEM] * (1 + len(got)) + [ANY] * n,
        out_specs=[VMEM] + [ANY] * n,
        input_output_aliases={1 + len(got) + i: 1 + i for i in range(n)},
        scratch_shapes=[pltpu.VMEM((n, text_rows, size), bf16), pltpu.SemaphoreType.DMA((n,))],
        compiler_params=params(60),
        cost_estimate=cost(0, 8 * groups * rows * size),
    )(own, *got, *packed)


def block_kernel(features, heads, n_got, near_ref, own_hbm, *refs):
    got, (out_ref, _, _, own_ref, sems) = refs[:n_got], refs[-5:]
    size = own_ref.shape[1]
    image_rows = near_ref.shape[0]
    copies = [
        pltpu.make_async_copy(own_hbm, own_ref, sems.at[0]),
        pltpu.make_async_copy(near_ref, out_ref.at[pl.ds(0, image_rows), :], sems.at[1]),
    ]
    for copy in copies:
        copy.start()
    kv_rows = image_rows // 3 * 2
    for k, ref in enumerate(got):
        at = image_rows + k * kv_rows
        out_ref[at : at + kv_rows, :] = ref[:kv_rows, :]
    copies[0].wait()
    text_rows = own_ref.shape[0] - EXTRA
    rows = text_rows // (3 * heads + 1)
    total = own_ref[:text_rows, :]
    for ref in got:
        total = total + ref[image_rows:, :].astype(f32)
    rate = lax.rsqrt(joined(total[3 * heads * rows :]) / features + eps_norm)
    end = image_rows + n_got * kv_rows
    for i in range(3):
        for head in range(heads):
            at = (i * heads + head) * rows
            x = total[at : at + rows] * rate
            if i < 2:
                mean = jnp.sum(x * x, axis=1, keepdims=True) / size
                gain = own_ref[text_rows + i : text_rows + i + 1, :]
                x = x * lax.rsqrt(mean + eps_norm) * gain
            out_ref[end + at : end + at + rows, :] = x.astype(bf16)
    bias = own_ref[text_rows + 2 : text_rows + 3, :]
    at = end + 3 * heads * rows
    out_ref[at:, :] = jnp.broadcast_to(bias, (EXTRA, size)).astype(bf16)
    copies[1].wait()


def block_of(near, own, got, mark, features, heads):
    image_rows, size = near.shape
    text_rows = own.shape[0] - EXTRA
    total = image_rows + image_rows // 3 * 2 * len(got)
    total += text_rows // (3 * heads + 1) * 3 * heads + EXTRA
    return pl.pallas_call(
        functools.partial(block_kernel, features, heads, len(got)),
        out_shape=[
            jax.ShapeDtypeStruct((total, size), bf16),
            jax.ShapeDtypeStruct(near.shape, bf16),
            jax.ShapeDtypeStruct(own.shape, f32),
        ],
        in_specs=[ANY] * 2 + [VMEM] * len(got) + [SMEM],
        out_specs=[VMEM, ANY, ANY],
        input_output_aliases={0: 1, 1: 2},
        scratch_shapes=[pltpu.VMEM(own.shape, f32), pltpu.SemaphoreType.DMA((2,))],
        compiler_params=params(),
        cost_estimate=cost(0, 4 * total * size),
    )(near, own, *got, mark)[0]


def attention_kernel(n_far, n_blocks, heads, rows, text_rows, *refs):
    far, refs = refs[:n_far], refs[n_far:]
    blocks, refs = refs[:n_blocks], refs[n_blocks:]
    out_refs, tout_ref = refs[:-1], refs[-1]
    size = blocks[0].shape[1]
    factor = size ** (-0.5) * math.log2(math.e)
    nt = (((1,), (1,)), ((), ()))
    near = 3 * heads * rows
    kv_rows = 2 * heads * rows
    starts = [0] + [near + k * kv_rows for k in range(n_far)]
    text = near + n_far * kv_rows
    end = text + 3 * heads * text_rows
    bias = blocks[0][end : end + EXTRA, :][:1, : n_blocks * text_rows].astype(f32)

    def with_ones(values):
        return jnp.concatenate([values, jnp.ones(values.shape, bf16)], axis=1)

    for head in range(heads):
        kv, tkv = [], []
        for i in range(2):
            at = (i * heads + head) * rows
            text_at = text + ((i + 1) * heads + head) * text_rows
            image = [b[start + at : start + at + rows, :] for b in blocks for start in starts]
            kv.append(jnp.concatenate(image, axis=0))
            tkv.append(jnp.concatenate([b[text_at : text_at + text_rows, :] for b in blocks], axis=0))
        keys, values = kv[0], with_ones(kv[1])
        tkeys, tvalues = tkv[0], with_ones(tkv[1])
        cols = slice(head * size, (head + 1) * size)
        q_at = (2 * heads + head) * rows
        work = [
            (ref[q_at : q_at + rows, :], out) for ref, out in zip((blocks[0],) + far, out_refs)
        ]
        tq_at = text + head * text_rows
        work.append((blocks[0][tq_at : tq_at + text_rows, :], tout_ref))
        for q, out_ref in work:
            s_img = lax.dot_general(q, keys, nt, preferred_element_type=f32)
            s_txt = lax.dot_general(q, tkeys, nt, preferred_element_type=f32) + bias
            top = jnp.maximum(
                jnp.max(s_img, axis=1, keepdims=True), jnp.max(s_txt, axis=1, keepdims=True)
            )
            p_img = jnp.exp2((s_img - top) * factor).astype(bf16)
            p_txt = jnp.exp2((s_txt - top) * factor).astype(bf16)
            acc = jnp.dot(p_img, values, preferred_element_type=f32)
            acc = acc + jnp.dot(p_txt, tvalues, preferred_element_type=f32)
            out_ref[:, cols] = (acc[:, :size] / acc[:, size:]).astype(bf16)


def attention(far, blocks, heads, rows, text_rows):
    size = blocks[0].shape[1]
    queries = (1 + len(far)) * rows + text_rows
    keys = len(blocks) * queries
    shapes = [jax.ShapeDtypeStruct((rows, heads * size), bf16)] * (1 + len(far))
    shapes += [jax.ShapeDtypeStruct((text_rows, heads * size), bf16)]
    return pl.pallas_call(
        functools.partial(
            attention_kernel, len(far), len(blocks), heads, rows, text_rows
        ),
        out_shape=shapes,
        in_specs=[VMEM] * (len(far) + len(blocks)),
        out_specs=[VMEM] * len(shapes),
        compiler_params=params(),
        cost_estimate=cost(
            4 * queries * keys * heads * size,
            4 * (queries + keys) * heads * size,
            queries * keys * heads,
        ),
    )(*far, *blocks)


def assemble_kernel(groups, n_after, meta_ref, *refs):
    pieces, out_ref = refs[:groups], refs[groups + n_after]
    rows, width = out_ref.shape[0], pieces[0].shape[1]
    for k, piece in enumerate(pieces):
        at = pl.multiple_of((meta_ref[0] ^ k) * width, 128)
        out_ref[:, pl.ds(at, width)] = piece[:rows, :]


def assemble(meta, pieces, after, rows):
    groups, width = len(pieces), pieces[0].shape[1]
    return pl.pallas_call(
        functools.partial(assemble_kernel, groups, len(after)),
        out_shape=jax.ShapeDtypeStruct((rows, groups * width), bf16),
        in_specs=[SMEM] + [VMEM] * groups + [ANY] * len(after),
        out_specs=VMEM,
        compiler_params=params(),
        cost_estimate=cost(0, 4 * rows * groups * width),
    )(meta, *pieces, *after)


def gated_kernel(groups, parts, place_of, meta_ref, gate_ref, d_out_ref, *refs):
    msgs, mark_ref, turned = refs[:-2], refs[-2], refs[-1]
    mark_ref[0] = meta_ref[0]
    gated = (gate_ref[...] * d_out_ref[...].astype(f32)).astype(bf16)
    turned[...] = gated.astype(f32).T
    rows = msgs[0].shape[2]
    z, oc, dp = meta_ref[0], meta_ref[1], meta_ref[2]
    for k, msg in enumerate(msgs):
        for j in range(parts):
            for g in range(groups):
                at = (dp ^ k) * (groups * parts) + place_of(oc ^ j, z ^ g)
                msg[j, g] = turned[pl.ds(pl.multiple_of(at * rows, 8), rows), :].astype(bf16)


def gated_parts(meta, gate, d_out, n_dp, groups, parts, place_of):
    local, model = d_out.shape
    rows = model // (n_dp * groups * parts)
    return pl.pallas_call(
        functools.partial(gated_kernel, groups, parts, place_of),
        out_shape=[jax.ShapeDtypeStruct((parts, groups, rows, local), bf16)] * n_dp
        + [jax.ShapeDtypeStruct((1,), jnp.int32)],
        in_specs=[SMEM, VMEM, VMEM],
        out_specs=[VMEM] * n_dp + [SMEM],
        scratch_shapes=[pltpu.VMEM((model, local), f32)],
        compiler_params=params(60),
        cost_estimate=cost(0, 4 * local * model),
    )(meta, gate, d_out)


def d_attn_kernel(gate_ref, d_out_ref, w_ref, after_ref, out_ref):
    del after_ref
    block = 512
    total = jnp.zeros(out_ref.shape, f32)
    for at in range(0, w_ref.shape[0], block):
        cols = slice(at, at + block)
        gated = (gate_ref[:, cols] * d_out_ref[:, cols].astype(f32)).astype(bf16)
        total = total + jnp.dot(gated, w_ref[cols, :], preferred_element_type=f32)
    out_ref[...] = total.astype(bf16)


def attn_gradient(gate, d_out, out_weight, after):
    local, model = d_out.shape
    inner = out_weight.shape[1]
    return pl.pallas_call(
        d_attn_kernel,
        out_shape=jax.ShapeDtypeStruct((local, inner), bf16),
        in_specs=[VMEM] * 3 + [ANY],
        out_specs=VMEM,
        compiler_params=params(),
        cost_estimate=cost(2 * local * inner * model, 2 * inner * model),
    )(gate, d_out, out_weight, after)


def gather_kernel(n_dp, *refs):
    pieces, outs = refs[:n_dp], refs[n_dp:]
    for j, out in enumerate(outs):
        for k, piece in enumerate(pieces):
            out[k] = piece[j + 1]


def gather_parts(pieces):
    parts = pieces[0].shape[0]
    shape = (len(pieces),) + pieces[0].shape[1:]
    return pl.pallas_call(
        functools.partial(gather_kernel, len(pieces)),
        out_shape=[jax.ShapeDtypeStruct(shape, bf16)] * (parts - 1),
        in_specs=[VMEM] * len(pieces),
        out_specs=[VMEM] * (parts - 1),
        compiler_params=params(),
        cost_estimate=cost(0, 4 * math.prod(shape) * (parts - 1)),
    )(*pieces)


def project_kernel(
    groups, parts, place_of, meta_ref, attn_ref, w_ref, gate_ref, d_out_ref, out_ref, term_ref, *refs
):
    sent, by_place = refs[:-1], refs[-1]
    rows = attn_ref.shape[0]
    block = 512
    sums = []
    for at in range(0, w_ref.shape[0], block):
        cols = slice(at, at + block)
        got = lax.dot_general(
            attn_ref[...], w_ref[cols, :], (((1,), (1,)), ((), ())), preferred_element_type=f32
        )
        out_ref[:, cols] = (got * gate_ref[:, cols]).astype(bf16)
        sums.append(jnp.sum(got * d_out_ref[:, cols].astype(f32), axis=0, keepdims=True))
    sums = jnp.concatenate(sums, axis=1)
    places, width = by_place.shape
    for s in range(places):
        by_place[s : s + 1, :] = sums[:, s * width : (s + 1) * width]
    for g in range(groups):
        at = place_of(meta_ref[1], meta_ref[0] ^ g)
        term_ref[g : g + 1, :] = by_place[pl.ds(at, 1), :]
    for j, out in enumerate(sent):
        out[:rows, :] = attn_ref[...]
        line = [
            by_place[pl.ds(place_of(meta_ref[1] ^ (j + 1), meta_ref[0] ^ g), 1), :]
            for g in range(groups)
        ]
        line = jnp.concatenate(line, axis=1)
        line = jnp.concatenate(
            [line, jnp.zeros((1, attn_ref.shape[1] - groups * width), f32)], axis=1
        ) if attn_ref.shape[1] > groups * width else line
        high = line.astype(bf16).astype(f32)
        lines = [high, line - high, jnp.zeros((EXTRA - 2, line.shape[1]), f32)]
        out[rows:, :] = jnp.concatenate(lines, axis=0).astype(bf16)


def project(meta, attn, out_weight, gate, d_out, groups, parts, place_of):
    rows, inner = attn.shape
    model = out_weight.shape[0]
    width = model // (groups * parts)
    shapes = [jax.ShapeDtypeStruct((rows, model), bf16)]
    shapes += [jax.ShapeDtypeStruct((groups, width), f32)]
    shapes += [jax.ShapeDtypeStruct((rows + EXTRA, inner), bf16)] * (parts - 1)
    return pl.pallas_call(
        functools.partial(project_kernel, groups, parts, place_of),
        out_shape=shapes,
        in_specs=[SMEM, VMEM, VMEM, VMEM, VMEM],
        out_specs=[VMEM] * (1 + parts),
        scratch_shapes=[pltpu.VMEM((groups * parts, width), f32)],
        compiler_params=params(),
        cost_estimate=cost(2 * rows * inner * model, 2 * inner * model),
    )(meta, attn, out_weight, gate, d_out)


def grad_kernel(n_left, n_pieces, *refs):
    lefts, refs = refs[:n_left], refs[n_left:]
    pieces, refs = refs[:n_pieces], refs[n_pieces:]
    term_ref, outs, (kept_ref, sent_ref) = refs[0], refs[1:-2], refs[-2:]
    groups, rows, depth = lefts[0].shape[1:]
    width = pieces[0].shape[1]
    left = []
    for ref in lefts:
        left += [ref[i].reshape(groups * rows, depth) for i in range(ref.shape[0])]
    left = jnp.concatenate(left, axis=1)
    block = 256
    for start in range(0, width, block):
        right = jnp.concatenate([p[:depth, start : start + block] for p in pieces], axis=0)
        got = jnp.dot(left, right, preferred_element_type=f32)
        for g, out in enumerate(outs):
            out[:, start : start + block] = got[g * rows : (g + 1) * rows].astype(out.dtype)
    term = term_ref[...]
    size = term.shape[1]
    for p in pieces:
        if p.shape[0] > depth:
            lines = p[depth:, :].astype(f32)
            line = lines[0:1, :] + lines[1:2, :]
            term = term + jnp.concatenate(
                [line[:, g * size : (g + 1) * size] for g in range(groups)], axis=0
            )
    kept_ref[...] = term[: groups // 2]
    sent_ref[...] = term[groups // 2 :]


def grad_product(lefts, pieces, term):
    groups, rows, depth = lefts[0].shape[1:]
    width = pieces[0].shape[1]
    total = groups * rows
    depth = depth * len(pieces)
    shapes = [jax.ShapeDtypeStruct((rows, width), (f32, bf16)[g % 2]) for g in range(groups)]
    shapes += [jax.ShapeDtypeStruct((groups // 2, term.shape[1]), f32)] * 2
    return pl.pallas_call(
        functools.partial(grad_kernel, len(lefts), len(pieces)),
        out_shape=shapes,
        in_specs=[VMEM] * (len(lefts) + len(pieces) + 1),
        out_specs=[VMEM] * len(shapes),
        compiler_params=params(),
        cost_estimate=cost(
            2 * total * depth * width, 2 * (total * depth + depth * width + total * width)
        ),
    )(*lefts, *pieces, term)


def on_device(
    caption_states,
    caption_gain,
    text_proj,
    caption_len,
    slot_source,
    query_gain,
    key_gain,
    image_q,
    image_k,
    image_v,
    out_weight,
    gate,
    d_out,
):
    n_dp = lax.axis_size("dp")
    n_seq = lax.axis_size("seq")
    G, C = GROUPS, CORES
    O = n_seq // (G * C)
    OC = O * C
    dp = lax.axis_index("dp")
    seq = lax.axis_index("seq")
    z = (seq // C) % G
    oc = (seq // (G * C)) * C + seq % C

    def place(oc_at, z_at):
        return ((oc_at // C) * G + z_at) * C + oc_at % C

    def to_z(x, k):
        perm = [(place(a, b), place(a, b ^ k)) for a in range(OC) for b in range(G)]
        return lax.ppermute(x, "seq", perm)

    def to_oc(x, j):
        perm = [(place(a, b), place(a ^ j, b)) for a in range(OC) for b in range(G)]
        return lax.ppermute(x, "seq", perm)

    def to_dp(x, k):
        return lax.ppermute(x, "dp", [(a, a ^ k) for a in range(n_dp)])

    def part(x, index, size, axis):
        return lax.dynamic_slice_in_dim(x, index * size, size, axis)

    slot_total = slot_source.shape[1]
    slot_local = slot_total // n_seq
    image_local = image_q.shape[1]
    inner_width = image_q.shape[2]
    model_width = out_weight.shape[0]
    head_size = query_gain.shape[0]
    gw = inner_width // G
    order = [2, 3, 1]
    meta = jnp.stack([z, oc, dp]).astype(jnp.int32)

    heads = gw // head_size
    text_rows = G * slot_local
    own, *rest = text_project(
        meta, caption_len, slot_source, caption_states[0], caption_gain[None],
        query_gain[None], key_gain[None], text_proj, image_k[0], image_v[0], image_q[0],
        G, OC, place,
    )
    packed, sent = rest[:G], rest[G:]
    got = [to_oc(x, j + 1) for j, x in enumerate(sent)]
    own, *messages = pack(own, got, packed[1:], text_rows)
    far = {k: to_z(messages[k - 1], k) for k in order}
    far = [far[k] for k in range(1, G)]

    *gg, mark = gated_parts(meta, gate, d_out[0], n_dp, G, OC, place)
    block = block_of(packed[0], own, far, mark, DT5, heads)
    blocks = [block] + [to_oc(block, j) for j in range(1, OC)]
    *outs, text_out = attention(far, blocks, heads, image_local, text_rows)

    back = []
    for k in range(G):
        rows = jnp.concatenate([outs[k], part(text_out, z ^ k, slot_local, 0)], axis=0)
        back.append(to_z(rows, k) if k else rows)
    gg_dp = [gg[0]] + [to_dp(gg[k], k) for k in range(1, n_dp)]
    lefts = [g[:1] for g in gg_dp]
    lefts += [to_oc(g, j + 1) for j, g in enumerate(gather_parts(gg_dp))]
    image_attn = assemble(meta, back, gg_dp[1:], image_local)
    text_attn = jnp.zeros((slot_local, inner_width), bf16)
    own_usable = part(slot_source[0] < caption_len[0], seq, slot_local, 0)
    for k in range(G):
        rows = jnp.where(own_usable[:, None], back[k][image_local:], jnp.zeros((), bf16))
        text_attn = lax.dynamic_update_slice_in_dim(text_attn, rows, (z ^ k) * gw, 1)

    pieces = [image_attn] + [to_dp(image_attn, k) for k in range(1, n_dp)]
    image_out, term, *sent = project(
        meta, image_attn, out_weight, gate, d_out[0], G, OC, place
    )
    for j in range(1, OC):
        pieces += [to_oc(sent[j - 1], j)] + [to_oc(p, j) for p in pieces[1:n_dp]]
    *grads, kept, sent = grad_product(lefts, pieces, term)
    pair = grads[2] + to_z(grads[3], 1).astype(f32)
    grad_wo = grads[0] + to_z(pair.astype(bf16), 2).astype(f32) + to_z(grads[1], 1).astype(f32)
    term = kept + to_z(sent, 2)
    grad_gate = term[:1] + to_z(term[1:], 1)
    d_attn = attn_gradient(gate, d_out[0], out_weight, grads[1])
    return (image_out[None], text_attn[None], d_attn[None], grad_wo, grad_gate)


def solution(mesh):
    in_specs = (
        P("dp", None, "seq"),
        P("seq"),
        P("seq", None),
        P("dp"),
        P("dp", None),
        P(),
        P(),
        P("dp", "seq", None),
        P("dp", "seq", None),
        P("dp", "seq", None),
        P(),
        P("dp", None),
        P("dp", "seq", None),
    )
    out_specs = (
        P("dp", "seq", None),
        P("dp", "seq", None),
        P("dp", "seq", None),
        P(("dp", "seq"), None),
        P("dp", "seq"),
    )
    return jax.shard_map(
        on_device, mesh=mesh, in_specs=in_specs, out_specs=out_specs, check_vma=False
    )
```

```python
import math
import functools
import jax
import jax.numpy as jnp
from jax import lax
from jax.experimental import pallas as pl
from jax.experimental.pallas import tpu as pltpu
from jax.sharding import PartitionSpec as P

DT5 = 4096
CORES = 2
GROUPS = 4

eps_norm = 1e-06
f32 = jnp.float32
bf16 = jnp.bfloat16
EXTRA = 16


VMEM = pl.BlockSpec(memory_space=pltpu.VMEM)
SMEM = pl.BlockSpec(memory_space=pltpu.SMEM)
ANY = pl.BlockSpec(memory_space=pl.ANY)


def params(mib=24):
    return pltpu.CompilerParams(vmem_limit_bytes=int(mib * 1024 * 1024))


def cost(flops, bytes_accessed, transcendentals=0):
    return pl.CostEstimate(
        flops=flops, bytes_accessed=bytes_accessed, transcendentals=transcendentals
    )


def split_tail(squares, width):
    high = squares.astype(bf16).astype(f32)
    low = squares - high
    lane = lax.broadcasted_iota(jnp.int32, (squares.shape[0], width), 1)
    return jnp.where(lane == 0, high, jnp.where(lane == 1, low, 0.0))


def joined(tail):
    return tail[:, 0:1] + tail[:, 1:2]


def text_kernel(
    groups, heads, place_of, meta_ref, len_ref, src_ref, states_ref, gain_ref, qg_ref, kg_ref,
    w_ref, own_ref, *refs
):
    msgs, (w_all, w_sems) = refs[:-2], refs[-2:]
    size = own_ref.shape[2]
    rows = (own_ref.shape[1] - EXTRA) // (3 * heads + 1)
    width = heads * size
    slots = states_ref.shape[0]
    slot_local = rows // groups
    copies = []
    for g in range(groups):
        for i in range(3):
            at = (i * groups + (meta_ref[0] ^ g)) * width
            cols = pl.ds(pl.multiple_of(at, 128), width)
            copies.append(pltpu.make_async_copy(w_ref.at[:, cols], w_all.at[g, i], w_sems.at[g, i]))
            copies[-1].start()
    def slot_at(row):
        z_at = (row % rows) // slot_local
        return place_of(meta_ref[1] ^ (row // rows), z_at) * slot_local + row % slot_local

    iota = functools.partial(lax.broadcasted_iota, jnp.int32, (slots, slots))
    sources = src_ref[...].astype(f32)
    chosen = (iota(1) == slot_at(iota(0))).astype(f32)
    source_col = jnp.sum(chosen * sources, axis=1, keepdims=True)
    pick = (iota(1).astype(f32) == source_col).astype(bf16)
    chosen_t = (iota(0) == slot_at(iota(1))).astype(bf16)
    source_row = jnp.dot(sources.astype(bf16), chosen_t, preferred_element_type=f32)
    bias = jnp.where(source_row < len_ref[0].astype(f32), 0.0, -1e30)
    end = own_ref.shape[1] - EXTRA
    own_ref[0, end:, :] = jnp.zeros((EXTRA, size), f32)
    own_ref[0, end : end + 1, :] = qg_ref[...]
    own_ref[0, end + 1 : end + 2, :] = kg_ref[...]
    own_ref[0, end + 2 : end + 3, :slots] = bias

    picked = jnp.dot(pick, states_ref[...], preferred_element_type=f32)
    scaled = (picked * gain_ref[...]).astype(bf16)
    tail = split_tail(jnp.sum(picked * picked, axis=1, keepdims=True), size)
    for g in range(groups):
        for i in range(3):
            copies[3 * g + i].wait()
            got = jnp.dot(scaled, w_all[g, i], preferred_element_type=f32)
            for head in range(heads):
                part = got[:, head * size : (head + 1) * size]
                to = slice((i * heads + head) * rows, (i * heads + head + 1) * rows)
                own_ref[g, to, :] = part[:rows]
                for j, msg in enumerate(msgs):
                    msg[g, to, :] = part[(j + 1) * rows : (j + 2) * rows].astype(bf16)
        own_ref[g, 3 * heads * rows : end, :] = tail[:rows]
        for j, msg in enumerate(msgs):
            msg[g, 3 * heads * rows :, :] = tail[(j + 1) * rows : (j + 2) * rows].astype(bf16)


def text_project(
    meta, length, sources, states, gain, query_gain, key_gain, text_proj, groups, parts, place_of
):
    slots, depth = states.shape
    size = query_gain.shape[1]
    heads = text_proj.shape[1] // (3 * groups * size)
    text_rows = (3 * heads + 1) * slots // parts
    shapes = [jax.ShapeDtypeStruct((groups, text_rows + EXTRA, size), f32)]
    shapes += [jax.ShapeDtypeStruct((groups, text_rows, size), bf16)] * (parts - 1)
    return pl.pallas_call(
        functools.partial(text_kernel, groups, heads, place_of),
        out_shape=shapes,
        in_specs=[SMEM, SMEM] + [VMEM] * 5 + [ANY],
        out_specs=[VMEM] * parts,
        scratch_shapes=[
            pltpu.VMEM((groups, 3, depth, heads * size), bf16),
            pltpu.SemaphoreType.DMA((groups, 3)),
        ],
        compiler_params=params(60),
        cost_estimate=cost(
            2 * slots * depth * text_proj.shape[1], 2 * depth * text_proj.shape[1]
        ),
    )(meta, length, sources, states, gain, query_gain, key_gain, text_proj)


def pack_kernel(groups, size, meta_ref, k_ref, v_ref, q_ref, *outs):
    rows = k_ref.shape[0]
    heads = k_ref.shape[1] // (groups * size)
    for g, out in enumerate(outs):
        for i, ref in enumerate((k_ref, v_ref, q_ref)):
            for head in range(heads):
                at = ((meta_ref[0] ^ g) * heads + head) * size
                to = (i * heads + head) * rows
                out[to : to + rows, :] = ref[:, pl.ds(pl.multiple_of(at, 128), size)]


def pack(meta, keys, values, queries, groups, size):
    rows, width = keys.shape
    shape = jax.ShapeDtypeStruct((3 * rows * width // (groups * size), size), bf16)
    return pl.pallas_call(
        functools.partial(pack_kernel, groups, size),
        out_shape=[shape] * groups,
        in_specs=[SMEM] + [VMEM] * 3,
        out_specs=[VMEM] * groups,
        compiler_params=params(60),
        cost_estimate=cost(0, 12 * rows * width),
    )(meta, keys, values, queries)


def text_sum_kernel(n_got, tail_rows, own_ref, *refs):
    got, (keep_ref, send_ref) = refs[:n_got], refs[n_got:]
    groups, text_rows, size = got[0].shape
    for g in range(groups):
        total = own_ref[g, :text_rows, :]
        for ref in got:
            total = total + ref[g].astype(f32)
        end = text_rows - tail_rows
        tail = split_tail(joined(total[end:]), size)
        if g % 2 == 0:
            keep_ref[g // 2, :end, :] = total[:end]
            keep_ref[g // 2, end:text_rows, :] = tail
            keep_ref[g // 2, text_rows:, :] = own_ref[g, text_rows:, :]
        else:
            send_ref[g // 2, :end, :] = total[:end].astype(bf16)
            send_ref[g // 2, end:, :] = tail.astype(bf16)


def text_sum(own, got, tail_rows):
    groups, rows, size = own.shape
    return pl.pallas_call(
        functools.partial(text_sum_kernel, len(got), tail_rows),
        out_shape=[
            jax.ShapeDtypeStruct((groups // 2, rows, size), f32),
            jax.ShapeDtypeStruct((groups // 2, rows - EXTRA, size), bf16),
        ],
        in_specs=[VMEM] * (1 + len(got)),
        out_specs=[VMEM] * 2,
        compiler_params=params(),
        cost_estimate=cost(0, 8 * groups * rows * size),
    )(own, *got)


def block_kernel(features, heads, n_far, own_ref, got_ref, mark_ref, *refs):
    del mark_ref
    far, out_ref = refs[:n_far], refs[n_far]
    kv_rows = far[0].shape[0] // 3 * 2
    for k, ref in enumerate(far):
        out_ref[k * kv_rows : (k + 1) * kv_rows, :] = ref[:kv_rows, :]
    size = own_ref.shape[2]
    text_rows = got_ref.shape[1]
    rows = text_rows // (3 * heads + 1)
    total = own_ref[0, :text_rows, :] + got_ref[0].astype(f32)
    rate = lax.rsqrt(joined(total[3 * heads * rows :]) / features + eps_norm)
    start = n_far * kv_rows
    for i in range(3):
        for head in range(heads):
            at = (i * heads + head) * rows
            x = total[at : at + rows] * rate
            if i < 2:
                mean = jnp.sum(x * x, axis=1, keepdims=True) / size
                gain = own_ref[0, text_rows + i : text_rows + i + 1, :]
                x = x * lax.rsqrt(mean + eps_norm) * gain
            out_ref[start + at : start + at + rows, :] = x.astype(bf16)
    bias = own_ref[0, text_rows + 2 : text_rows + 3, :]
    start = start + 3 * heads * rows
    out_ref[start:, :] = jnp.broadcast_to(bias, (EXTRA, size)).astype(bf16)


def block_of(own, got, mark, far, features, heads):
    rows, size = own.shape[1:]
    total = (rows - EXTRA) // (3 * heads + 1) * 3 * heads + EXTRA
    total += far[0].shape[0] // 3 * 2 * len(far)
    return pl.pallas_call(
        functools.partial(block_kernel, features, heads, len(far)),
        out_shape=jax.ShapeDtypeStruct((total, size), bf16),
        in_specs=[VMEM] * 2 + [SMEM] + [VMEM] * len(far),
        out_specs=VMEM,
        compiler_params=params(),
        cost_estimate=cost(0, 4 * total * size),
    )(own, got, mark, *far)


def attention_kernel(n_pieces, n_cores, heads, rows, text_rows, *refs):
    pieces, refs = refs[:n_pieces], refs[n_pieces:]
    nears, refs = refs[: n_cores - 1], refs[n_cores - 1 :]
    blocks, refs = refs[:n_cores], refs[n_cores:]
    out_refs, tout_ref = refs[:-1], refs[-1]
    size = blocks[0].shape[1]
    factor = size ** (-0.5) * math.log2(math.e)
    nt = (((1,), (1,)), ((), ()))
    kv_rows = 2 * heads * rows
    text = (n_pieces - 1) * kv_rows
    end = text + 3 * heads * text_rows
    bias = blocks[0][end : end + EXTRA, :][:1, : n_cores * text_rows].astype(f32)

    def with_ones(values):
        return jnp.concatenate([values, jnp.ones(values.shape, bf16)], axis=1)

    for head in range(heads):
        kv, tkv = [], []
        for i in range(2):
            at = (i * heads + head) * rows
            image = [r[at : at + rows, :] for r in tuple(pieces) + tuple(nears)]
            for b in blocks[1:]:
                starts = [k * kv_rows + at for k in range(n_pieces - 1)]
                image += [b[start : start + rows, :] for start in starts]
            text_at = text + ((i + 1) * heads + head) * text_rows
            kv.append(jnp.concatenate(image, axis=0))
            tkv.append(jnp.concatenate([b[text_at : text_at + text_rows, :] for b in blocks], axis=0))
        keys, values = kv[0], with_ones(kv[1])
        tkeys, tvalues = tkv[0], with_ones(tkv[1])
        cols = slice(head * size, (head + 1) * size)
        q_at = (2 * heads + head) * rows
        work = [(ref[q_at : q_at + rows, :], out) for ref, out in zip(pieces, out_refs)]
        tq_at = text + head * text_rows
        work.append((blocks[0][tq_at : tq_at + text_rows, :], tout_ref))
        for q, out_ref in work:
            s_img = lax.dot_general(q, keys, nt, preferred_element_type=f32)
            s_txt = lax.dot_general(q, tkeys, nt, preferred_element_type=f32) + bias
            top = jnp.maximum(
                jnp.max(s_img, axis=1, keepdims=True), jnp.max(s_txt, axis=1, keepdims=True)
            )
            p_img = jnp.exp2((s_img - top) * factor).astype(bf16)
            p_txt = jnp.exp2((s_txt - top) * factor).astype(bf16)
            acc = jnp.dot(p_img, values, preferred_element_type=f32)
            acc = acc + jnp.dot(p_txt, tvalues, preferred_element_type=f32)
            out_ref[:, cols] = (acc[:, :size] / acc[:, size:]).astype(bf16)


def attention(pieces, nears, blocks, heads, rows, text_rows):
    size = blocks[0].shape[1]
    n = len(pieces)
    queries = n * rows + text_rows
    keys = len(blocks) * queries
    shapes = [jax.ShapeDtypeStruct((rows, heads * size), bf16)] * n
    shapes += [jax.ShapeDtypeStruct((text_rows, heads * size), bf16)]
    return pl.pallas_call(
        functools.partial(attention_kernel, n, len(blocks), heads, rows, text_rows),
        out_shape=shapes,
        in_specs=[VMEM] * (n + len(nears) + len(blocks)),
        out_specs=[VMEM] * len(shapes),
        compiler_params=params(),
        cost_estimate=cost(
            4 * queries * keys * heads * size,
            4 * (queries + keys) * heads * size,
            queries * keys * heads,
        ),
    )(*pieces, *nears, *blocks)


def assemble_kernel(groups, n_after, meta_ref, *refs):
    pieces, out_ref = refs[:groups], refs[groups + n_after]
    rows, width = out_ref.shape[0], pieces[0].shape[1]
    for k, piece in enumerate(pieces):
        at = pl.multiple_of((meta_ref[0] ^ k) * width, 128)
        out_ref[:, pl.ds(at, width)] = piece[:rows, :]


def assemble(meta, pieces, after, rows):
    groups, width = len(pieces), pieces[0].shape[1]
    return pl.pallas_call(
        functools.partial(assemble_kernel, groups, len(after)),
        out_shape=jax.ShapeDtypeStruct((rows, groups * width), bf16),
        in_specs=[SMEM] + [VMEM] * groups + [ANY] * len(after),
        out_specs=VMEM,
        compiler_params=params(),
        cost_estimate=cost(0, 4 * rows * groups * width),
    )(meta, *pieces, *after)


def gated_kernel(groups, parts, place_of, meta_ref, gate_ref, d_out_ref, *refs):
    msgs, mark_ref, turned = refs[:-2], refs[-2], refs[-1]
    mark_ref[0] = meta_ref[0]
    gated = (gate_ref[...] * d_out_ref[...].astype(f32)).astype(bf16)
    turned[...] = gated.astype(f32).T
    rows = msgs[0].shape[2]
    z, oc, dp = meta_ref[0], meta_ref[1], meta_ref[2]
    for k, msg in enumerate(msgs):
        for j in range(parts):
            for g in range(groups):
                at = (dp ^ k) * (groups * parts) + place_of(oc ^ j, z ^ g)
                msg[j, g] = turned[pl.ds(pl.multiple_of(at * rows, 8), rows), :].astype(bf16)


def gated_parts(meta, gate, d_out, n_dp, groups, parts, place_of):
    local, model = d_out.shape
    rows = model // (n_dp * groups * parts)
    return pl.pallas_call(
        functools.partial(gated_kernel, groups, parts, place_of),
        out_shape=[jax.ShapeDtypeStruct((parts, groups, rows, local), bf16)] * n_dp
        + [jax.ShapeDtypeStruct((1,), jnp.int32)],
        in_specs=[SMEM, VMEM, VMEM],
        out_specs=[VMEM] * n_dp + [SMEM],
        scratch_shapes=[pltpu.VMEM((model, local), f32)],
        compiler_params=params(60),
        cost_estimate=cost(0, 4 * local * model),
    )(meta, gate, d_out)


def d_attn_kernel(gate_ref, d_out_ref, w_ref, after_ref, out_ref):
    del after_ref
    block = 512
    total = jnp.zeros(out_ref.shape, f32)
    for at in range(0, w_ref.shape[0], block):
        cols = slice(at, at + block)
        gated = (gate_ref[:, cols] * d_out_ref[:, cols].astype(f32)).astype(bf16)
        total = total + jnp.dot(gated, w_ref[cols, :], preferred_element_type=f32)
    out_ref[...] = total.astype(bf16)


def attn_gradient(gate, d_out, out_weight, after):
    local, model = d_out.shape
    inner = out_weight.shape[1]
    return pl.pallas_call(
        d_attn_kernel,
        out_shape=jax.ShapeDtypeStruct((local, inner), bf16),
        in_specs=[VMEM] * 3 + [ANY],
        out_specs=VMEM,
        compiler_params=params(),
        cost_estimate=cost(2 * local * inner * model, 2 * inner * model),
    )(gate, d_out, out_weight, after)


def gather_kernel(n_dp, *refs):
    pieces, outs = refs[:n_dp], refs[n_dp:]
    for j, out in enumerate(outs):
        for k, piece in enumerate(pieces):
            out[k] = piece[j + 1]


def gather_parts(pieces):
    parts = pieces[0].shape[0]
    shape = (len(pieces),) + pieces[0].shape[1:]
    return pl.pallas_call(
        functools.partial(gather_kernel, len(pieces)),
        out_shape=[jax.ShapeDtypeStruct(shape, bf16)] * (parts - 1),
        in_specs=[VMEM] * len(pieces),
        out_specs=[VMEM] * (parts - 1),
        compiler_params=params(),
        cost_estimate=cost(0, 4 * math.prod(shape) * (parts - 1)),
    )(*pieces)


def project_kernel(
    groups, parts, place_of, meta_ref, attn_ref, w_ref, gate_ref, d_out_ref, out_ref, term_ref, *refs
):
    sent, by_place = refs[:-1], refs[-1]
    rows = attn_ref.shape[0]
    block = 512
    sums = []
    for at in range(0, w_ref.shape[0], block):
        cols = slice(at, at + block)
        got = lax.dot_general(
            attn_ref[...], w_ref[cols, :], (((1,), (1,)), ((), ())), preferred_element_type=f32
        )
        out_ref[:, cols] = (got * gate_ref[:, cols]).astype(bf16)
        sums.append(jnp.sum(got * d_out_ref[:, cols].astype(f32), axis=0, keepdims=True))
    sums = jnp.concatenate(sums, axis=1)
    places, width = by_place.shape
    for s in range(places):
        by_place[s : s + 1, :] = sums[:, s * width : (s + 1) * width]
    for g in range(groups):
        at = place_of(meta_ref[1], meta_ref[0] ^ g)
        term_ref[g : g + 1, :] = by_place[pl.ds(at, 1), :]
    for j, out in enumerate(sent):
        out[:rows, :] = attn_ref[...]
        line = [
            by_place[pl.ds(place_of(meta_ref[1] ^ (j + 1), meta_ref[0] ^ g), 1), :]
            for g in range(groups)
        ]
        line = jnp.concatenate(line, axis=1)
        line = jnp.concatenate(
            [line, jnp.zeros((1, attn_ref.shape[1] - groups * width), f32)], axis=1
        ) if attn_ref.shape[1] > groups * width else line
        high = line.astype(bf16).astype(f32)
        lines = [high, line - high, jnp.zeros((EXTRA - 2, line.shape[1]), f32)]
        out[rows:, :] = jnp.concatenate(lines, axis=0).astype(bf16)


def project(meta, attn, out_weight, gate, d_out, groups, parts, place_of):
    rows, inner = attn.shape
    model = out_weight.shape[0]
    width = model // (groups * parts)
    shapes = [jax.ShapeDtypeStruct((rows, model), bf16)]
    shapes += [jax.ShapeDtypeStruct((groups, width), f32)]
    shapes += [jax.ShapeDtypeStruct((rows + EXTRA, inner), bf16)] * (parts - 1)
    return pl.pallas_call(
        functools.partial(project_kernel, groups, parts, place_of),
        out_shape=shapes,
        in_specs=[SMEM, VMEM, VMEM, VMEM, VMEM],
        out_specs=[VMEM] * (1 + parts),
        scratch_shapes=[pltpu.VMEM((groups * parts, width), f32)],
        compiler_params=params(),
        cost_estimate=cost(2 * rows * inner * model, 2 * inner * model),
    )(meta, attn, out_weight, gate, d_out)


def grad_kernel(n_left, n_pieces, *refs):
    lefts, refs = refs[:n_left], refs[n_left:]
    pieces, refs = refs[:n_pieces], refs[n_pieces:]
    term_ref, outs, (kept_ref, sent_ref) = refs[0], refs[1:-2], refs[-2:]
    groups, rows, depth = lefts[0].shape[1:]
    width = pieces[0].shape[1]
    left = []
    for ref in lefts:
        left += [ref[i].reshape(groups * rows, depth) for i in range(ref.shape[0])]
    left = jnp.concatenate(left, axis=1)
    block = 256
    for start in range(0, width, block):
        right = jnp.concatenate([p[:depth, start : start + block] for p in pieces], axis=0)
        got = jnp.dot(left, right, preferred_element_type=f32)
        for g, out in enumerate(outs):
            out[:, start : start + block] = got[g * rows : (g + 1) * rows].astype(out.dtype)
    term = term_ref[...]
    size = term.shape[1]
    for p in pieces:
        if p.shape[0] > depth:
            lines = p[depth:, :].astype(f32)
            line = lines[0:1, :] + lines[1:2, :]
            term = term + jnp.concatenate(
                [line[:, g * size : (g + 1) * size] for g in range(groups)], axis=0
            )
    kept_ref[...] = term[: groups // 2]
    sent_ref[...] = term[groups // 2 :]


def grad_product(lefts, pieces, term):
    groups, rows, depth = lefts[0].shape[1:]
    width = pieces[0].shape[1]
    total = groups * rows
    depth = depth * len(pieces)
    shapes = [jax.ShapeDtypeStruct((rows, width), (f32, bf16)[g % 2]) for g in range(groups)]
    shapes += [jax.ShapeDtypeStruct((groups // 2, term.shape[1]), f32)] * 2
    return pl.pallas_call(
        functools.partial(grad_kernel, len(lefts), len(pieces)),
        out_shape=shapes,
        in_specs=[VMEM] * (len(lefts) + len(pieces) + 1),
        out_specs=[VMEM] * len(shapes),
        compiler_params=params(),
        cost_estimate=cost(
            2 * total * depth * width, 2 * (total * depth + depth * width + total * width)
        ),
    )(*lefts, *pieces, term)


def pair_kernel(own_ref, got_ref, gate_ref, out_ref, gate_out):
    out_ref[...] = (own_ref[...] + got_ref[...].astype(f32)).astype(bf16)
    gate_out[...] = gate_ref[...]


def pair_sum(own, got, gate):
    return pl.pallas_call(
        pair_kernel,
        out_shape=[
            jax.ShapeDtypeStruct(got.shape, bf16),
            jax.ShapeDtypeStruct(gate.shape, f32),
        ],
        in_specs=[VMEM] * 3,
        out_specs=[VMEM] * 2,
        compiler_params=params(),
        cost_estimate=cost(0, 8 * own.size),
    )(own, got, gate)


def on_device(
    caption_states,
    caption_gain,
    text_proj,
    caption_len,
    slot_source,
    query_gain,
    key_gain,
    image_q,
    image_k,
    image_v,
    out_weight,
    gate,
    d_out,
):
    n_dp = lax.axis_size("dp")
    n_seq = lax.axis_size("seq")
    G, C = GROUPS, CORES
    O = n_seq // (G * C)
    OC = O * C
    dp = lax.axis_index("dp")
    seq = lax.axis_index("seq")
    z = (seq // C) % G
    oc = (seq // (G * C)) * C + seq % C

    def place(oc_at, z_at):
        return ((oc_at // C) * G + z_at) * C + oc_at % C

    def to_z(x, k):
        perm = [(place(a, b), place(a, b ^ k)) for a in range(OC) for b in range(G)]
        return lax.ppermute(x, "seq", perm)

    def to_oc(x, j):
        perm = [(place(a, b), place(a ^ j, b)) for a in range(OC) for b in range(G)]
        return lax.ppermute(x, "seq", perm)

    def to_dp(x, k):
        return lax.ppermute(x, "dp", [(a, a ^ k) for a in range(n_dp)])

    def part(x, index, size, axis):
        return lax.dynamic_slice_in_dim(x, index * size, size, axis)

    slot_total = slot_source.shape[1]
    slot_local = slot_total // n_seq
    image_local = image_q.shape[1]
    inner_width = image_q.shape[2]
    model_width = out_weight.shape[0]
    head_size = query_gain.shape[0]
    gw = inner_width // G
    order = [2, 3, 1]
    meta = jnp.stack([z, oc, dp]).astype(jnp.int32)

    heads = gw // head_size
    text_rows = G * slot_local
    packed = pack(meta, image_k[0], image_v[0], image_q[0], G, head_size)
    images = [packed[0]] + [to_z(packed[k], k) for k in range(1, G)]
    nears = [to_oc(packed[0], j) for j in range(1, OC)]

    own, *sent = text_project(
        meta, caption_len, slot_source, caption_states[0], caption_gain[None],
        query_gain[None], key_gain[None], text_proj, G, OC, place,
    )
    got = [to_oc(x, j + 1) for j, x in enumerate(sent)]
    own, sent = text_sum(own, got, text_rows)
    own, sent = text_sum(own, [to_z(sent, 1)], text_rows)
    got = to_z(sent, 2)

    *gg, mark = gated_parts(meta, gate, d_out[0], n_dp, G, OC, place)
    block = block_of(own, got, mark, images[1:], DT5, heads)
    blocks = [block] + [to_oc(block, j) for j in range(1, OC)]
    *outs, text_out = attention(images, nears, blocks, heads, image_local, text_rows)

    back = []
    for k in range(G):
        rows = jnp.concatenate([outs[k], part(text_out, z ^ k, slot_local, 0)], axis=0)
        back.append(to_z(rows, k) if k else rows)
    gg_dp = [gg[0]] + [to_dp(gg[k], k) for k in range(1, n_dp)]
    lefts = [g[:1] for g in gg_dp]
    lefts += [to_oc(g, j + 1) for j, g in enumerate(gather_parts(gg_dp))]
    image_attn = assemble(meta, back, gg_dp[1:], image_local)
    text_attn = jnp.zeros((slot_local, inner_width), bf16)
    own_usable = part(slot_source[0] < caption_len[0], seq, slot_local, 0)
    for k in range(G):
        rows = jnp.where(own_usable[:, None], back[k][image_local:], jnp.zeros((), bf16))
        text_attn = lax.dynamic_update_slice_in_dim(text_attn, rows, (z ^ k) * gw, 1)

    pieces = [image_attn] + [to_dp(image_attn, k) for k in range(1, n_dp)]
    image_out, term, *sent = project(
        meta, image_attn, out_weight, gate, d_out[0], G, OC, place
    )
    for j in range(1, OC):
        pieces += [to_oc(sent[j - 1], j)] + [to_oc(p, j) for p in pieces[1:n_dp]]
    *grads, kept, sent = grad_product(lefts, pieces, term)
    pair, sent = pair_sum(grads[2], to_z(grads[3], 1), sent)
    grad_wo = grads[0] + to_z(pair, 2).astype(f32) + to_z(grads[1], 1).astype(f32)
    term = kept + to_z(sent, 2)
    grad_gate = term[:1] + to_z(term[1:], 1)
    d_attn = attn_gradient(gate, d_out[0], out_weight, grads[1])
    return (image_out[None], text_attn[None], d_attn[None], grad_wo, grad_gate)


def solution(mesh):
    in_specs = (
        P("dp", None, "seq"),
        P("seq"),
        P("seq", None),
        P("dp"),
        P("dp", None),
        P(),
        P(),
        P("dp", "seq", None),
        P("dp", "seq", None),
        P("dp", "seq", None),
        P(),
        P("dp", None),
        P("dp", "seq", None),
    )
    out_specs = (
        P("dp", "seq", None),
        P("dp", "seq", None),
        P("dp", "seq", None),
        P(("dp", "seq"), None),
        P("dp", "seq"),
    )
    return jax.shard_map(
        on_device, mesh=mesh, in_specs=in_specs, out_specs=out_specs, check_vma=False
    )
```

```python
import math
import functools
import jax
import jax.numpy as jnp
from jax import lax
from jax.experimental import pallas as pl
from jax.experimental.pallas import tpu as pltpu
from jax.sharding import PartitionSpec as P

DT5 = 4096
CORES = 2
GROUPS = 4

eps_norm = 1e-06
f32 = jnp.float32
bf16 = jnp.bfloat16
EXTRA = 16


VMEM = pl.BlockSpec(memory_space=pltpu.VMEM)
SMEM = pl.BlockSpec(memory_space=pltpu.SMEM)
ANY = pl.BlockSpec(memory_space=pl.ANY)


def params(mib=24):
    return pltpu.CompilerParams(vmem_limit_bytes=int(mib * 1024 * 1024))


def cost(flops, bytes_accessed, transcendentals=0):
    return pl.CostEstimate(
        flops=flops, bytes_accessed=bytes_accessed, transcendentals=transcendentals
    )


def split_tail(squares, width):
    high = squares.astype(bf16).astype(f32)
    low = squares - high
    lane = lax.broadcasted_iota(jnp.int32, (squares.shape[0], width), 1)
    return jnp.where(lane == 0, high, jnp.where(lane == 1, low, 0.0))


def joined(tail):
    return tail[:, 0:1] + tail[:, 1:2]


def text_kernel(
    groups, heads, place_of, meta_ref, len_ref, src_ref, states_ref, gain_ref, qg_ref, kg_ref,
    k_ref, v_ref, q_ref, w_ref, own_ref, *refs
):
    packed, refs = refs[:groups], refs[groups:]
    msgs, (w_all, w_sems) = refs[:-2], refs[-2:]
    size = own_ref.shape[2]
    rows = (own_ref.shape[1] - EXTRA) // (3 * heads + 1)
    width = heads * size
    slots = states_ref.shape[0]
    slot_local = rows // groups
    copies = []
    block = w_all.shape[0] // w_sems.shape[0]
    for i in range(w_sems.shape[0]):
        part = pl.ds(i * block, block)
        copies.append(pltpu.make_async_copy(w_ref.at[part], w_all.at[part], w_sems.at[i]))
        copies[-1].start()
    local = k_ref.shape[0]
    for g, out in enumerate(packed):
        for i, ref in enumerate((k_ref, v_ref, q_ref)):
            for head in range(heads):
                at = ((meta_ref[0] ^ g) * heads + head) * size
                to = (i * heads + head) * local
                out[to : to + local, :] = ref[:, pl.ds(pl.multiple_of(at, 128), size)]

    def slot_at(row):
        z_at = (row % rows) // slot_local
        return place_of(meta_ref[1] ^ (row // rows), z_at) * slot_local + row % slot_local

    iota = functools.partial(lax.broadcasted_iota, jnp.int32, (slots, slots))
    sources = src_ref[...].astype(f32)
    chosen = (iota(1) == slot_at(iota(0))).astype(f32)
    source_col = jnp.sum(chosen * sources, axis=1, keepdims=True)
    pick = (iota(1).astype(f32) == source_col).astype(bf16)
    chosen_t = (iota(0) == slot_at(iota(1))).astype(bf16)
    source_row = jnp.dot(sources.astype(bf16), chosen_t, preferred_element_type=f32)
    bias = jnp.where(source_row < len_ref[0].astype(f32), 0.0, -1e30)
    end = own_ref.shape[1] - EXTRA
    own_ref[0, end:, :] = jnp.zeros((EXTRA, size), f32)
    own_ref[0, end : end + 1, :] = qg_ref[...]
    own_ref[0, end + 1 : end + 2, :] = kg_ref[...]
    own_ref[0, end + 2 : end + 3, :slots] = bias

    picked = jnp.dot(pick, states_ref[...], preferred_element_type=f32)
    scaled = (picked * gain_ref[...]).astype(bf16)
    tail = split_tail(jnp.sum(picked * picked, axis=1, keepdims=True), size)
    for copy in copies:
        copy.wait()
    for g in range(groups):
        for i in range(3):
            at = (i * groups + (meta_ref[0] ^ g)) * width
            columns = pl.ds(pl.multiple_of(at, 128), width)
            got = jnp.dot(scaled, w_all[:, columns], preferred_element_type=f32)
            for head in range(heads):
                part = got[:, head * size : (head + 1) * size]
                to = slice((i * heads + head) * rows, (i * heads + head + 1) * rows)
                own_ref[g, to, :] = part[:rows]
                for j, msg in enumerate(msgs):
                    msg[g, to, :] = part[(j + 1) * rows : (j + 2) * rows].astype(bf16)
        own_ref[g, 3 * heads * rows : end, :] = tail[:rows]
        for j, msg in enumerate(msgs):
            msg[g, 3 * heads * rows :, :] = tail[(j + 1) * rows : (j + 2) * rows].astype(bf16)


def text_project(
    meta, length, sources, states, gain, query_gain, key_gain, keys, values, queries, text_proj,
    groups, parts, place_of
):
    slots, depth = states.shape
    size = query_gain.shape[1]
    heads = text_proj.shape[1] // (3 * groups * size)
    text_rows = (3 * heads + 1) * slots // parts
    shapes = [jax.ShapeDtypeStruct((groups, text_rows + EXTRA, size), f32)]
    shapes += [jax.ShapeDtypeStruct((3 * heads * keys.shape[0], size), bf16)] * groups
    shapes += [jax.ShapeDtypeStruct((groups, text_rows, size), bf16)] * (parts - 1)
    return pl.pallas_call(
        functools.partial(text_kernel, groups, heads, place_of),
        out_shape=shapes,
        in_specs=[SMEM, SMEM] + [VMEM] * 8 + [ANY],
        out_specs=[VMEM] * (groups + parts),
        scratch_shapes=[pltpu.VMEM(text_proj.shape, bf16), pltpu.SemaphoreType.DMA((4,))],
        compiler_params=params(60),
        cost_estimate=cost(
            2 * slots * depth * text_proj.shape[1], 2 * depth * text_proj.shape[1]
        ),
    )(
        meta, length, sources, states, gain, query_gain, key_gain, keys, values, queries, text_proj
    )


def text_sum_kernel(n_got, tail_rows, own_ref, *refs):
    got, (keep_ref, send_ref) = refs[:n_got], refs[n_got:]
    groups, text_rows, size = got[0].shape
    for g in range(groups):
        total = own_ref[g, :text_rows, :]
        for ref in got:
            total = total + ref[g].astype(f32)
        end = text_rows - tail_rows
        tail = split_tail(joined(total[end:]), size)
        if g % 2 == 0:
            keep_ref[g // 2, :end, :] = total[:end]
            keep_ref[g // 2, end:text_rows, :] = tail
            keep_ref[g // 2, text_rows:, :] = own_ref[g, text_rows:, :]
        else:
            send_ref[g // 2, :end, :] = total[:end].astype(bf16)
            send_ref[g // 2, end:, :] = tail.astype(bf16)


def text_sum(own, got, tail_rows):
    groups, rows, size = own.shape
    return pl.pallas_call(
        functools.partial(text_sum_kernel, len(got), tail_rows),
        out_shape=[
            jax.ShapeDtypeStruct((groups // 2, rows, size), f32),
            jax.ShapeDtypeStruct((groups // 2, rows - EXTRA, size), bf16),
        ],
        in_specs=[VMEM] * (1 + len(got)),
        out_specs=[VMEM] * 2,
        compiler_params=params(),
        cost_estimate=cost(0, 8 * groups * rows * size),
    )(own, *got)


def block_kernel(features, heads, n_far, own_ref, got_ref, after_ref, *refs):
    del after_ref
    far, out_ref = refs[:n_far], refs[n_far]
    kv_rows = far[0].shape[0] // 3 * 2
    for k, ref in enumerate(far):
        out_ref[k * kv_rows : (k + 1) * kv_rows, :] = ref[:kv_rows, :]
    size = own_ref.shape[2]
    text_rows = got_ref.shape[1]
    rows = text_rows // (3 * heads + 1)
    total = own_ref[0, :text_rows, :] + got_ref[0].astype(f32)
    rate = lax.rsqrt(joined(total[3 * heads * rows :]) / features + eps_norm)
    start = n_far * kv_rows
    for i in range(3):
        for head in range(heads):
            at = (i * heads + head) * rows
            x = total[at : at + rows] * rate
            if i < 2:
                mean = jnp.sum(x * x, axis=1, keepdims=True) / size
                gain = own_ref[0, text_rows + i : text_rows + i + 1, :]
                x = x * lax.rsqrt(mean + eps_norm) * gain
            out_ref[start + at : start + at + rows, :] = x.astype(bf16)
    bias = own_ref[0, text_rows + 2 : text_rows + 3, :]
    start = start + 3 * heads * rows
    out_ref[start:, :] = jnp.broadcast_to(bias, (EXTRA, size)).astype(bf16)


def block_of(own, got, after, far, features, heads):
    rows, size = own.shape[1:]
    total = (rows - EXTRA) // (3 * heads + 1) * 3 * heads + EXTRA
    total += far[0].shape[0] // 3 * 2 * len(far)
    return pl.pallas_call(
        functools.partial(block_kernel, features, heads, len(far)),
        out_shape=jax.ShapeDtypeStruct((total, size), bf16),
        in_specs=[VMEM] * 2 + [ANY] + [VMEM] * len(far),
        out_specs=VMEM,
        compiler_params=params(),
        cost_estimate=cost(0, 4 * total * size),
    )(own, got, after, *far)


def attention_kernel(n_pieces, n_cores, heads, rows, text_rows, *refs):
    pieces, refs = refs[:n_pieces], refs[n_pieces:]
    nears, refs = refs[: n_cores - 1], refs[n_cores - 1 :]
    blocks, refs = refs[:n_cores], refs[n_cores:]
    out_refs, tout_ref = refs[:-1], refs[-1]
    size = blocks[0].shape[1]
    factor = size ** (-0.5) * math.log2(math.e)
    nt = (((1,), (1,)), ((), ()))
    kv_rows = 2 * heads * rows
    text = (n_pieces - 1) * kv_rows
    end = text + 3 * heads * text_rows
    bias = blocks[0][end : end + EXTRA, :][:1, : n_cores * text_rows].astype(f32)

    def with_ones(values):
        return jnp.concatenate([values, jnp.ones(values.shape, bf16)], axis=1)

    for head in range(heads):
        kv, tkv = [], []
        for i in range(2):
            at = (i * heads + head) * rows
            image = [r[at : at + rows, :] for r in tuple(pieces) + tuple(nears)]
            for b in blocks[1:]:
                starts = [k * kv_rows + at for k in range(n_pieces - 1)]
                image += [b[start : start + rows, :] for start in starts]
            text_at = text + ((i + 1) * heads + head) * text_rows
            kv.append(jnp.concatenate(image, axis=0))
            tkv.append(jnp.concatenate([b[text_at : text_at + text_rows, :] for b in blocks], axis=0))
        keys, values = kv[0], with_ones(kv[1])
        tkeys, tvalues = tkv[0], with_ones(tkv[1])
        cols = slice(head * size, (head + 1) * size)
        q_at = (2 * heads + head) * rows
        work = [(ref[q_at : q_at + rows, :], out) for ref, out in zip(pieces, out_refs)]
        tq_at = text + head * text_rows
        work.append((blocks[0][tq_at : tq_at + text_rows, :], tout_ref))
        for q, out_ref in work:
            s_img = lax.dot_general(q, keys, nt, preferred_element_type=f32)
            s_txt = lax.dot_general(q, tkeys, nt, preferred_element_type=f32) + bias
            top = jnp.maximum(
                jnp.max(s_img, axis=1, keepdims=True), jnp.max(s_txt, axis=1, keepdims=True)
            )
            p_img = jnp.exp2((s_img - top) * factor).astype(bf16)
            p_txt = jnp.exp2((s_txt - top) * factor).astype(bf16)
            acc = jnp.dot(p_img, values, preferred_element_type=f32)
            acc = acc + jnp.dot(p_txt, tvalues, preferred_element_type=f32)
            out_ref[:, cols] = (acc[:, :size] / acc[:, size:]).astype(bf16)


def attention(pieces, nears, blocks, heads, rows, text_rows):
    size = blocks[0].shape[1]
    n = len(pieces)
    queries = n * rows + text_rows
    keys = len(blocks) * queries
    shapes = [jax.ShapeDtypeStruct((rows, heads * size), bf16)] * n
    shapes += [jax.ShapeDtypeStruct((text_rows, heads * size), bf16)]
    return pl.pallas_call(
        functools.partial(attention_kernel, n, len(blocks), heads, rows, text_rows),
        out_shape=shapes,
        in_specs=[VMEM] * (n + len(nears) + len(blocks)),
        out_specs=[VMEM] * len(shapes),
        compiler_params=params(),
        cost_estimate=cost(
            4 * queries * keys * heads * size,
            4 * (queries + keys) * heads * size,
            queries * keys * heads,
        ),
    )(*pieces, *nears, *blocks)


def assemble_kernel(groups, n_after, meta_ref, *refs):
    pieces, out_ref = refs[:groups], refs[groups + n_after]
    rows, width = out_ref.shape[0], pieces[0].shape[1]
    for k, piece in enumerate(pieces):
        at = pl.multiple_of((meta_ref[0] ^ k) * width, 128)
        out_ref[:, pl.ds(at, width)] = piece[:rows, :]


def assemble(meta, pieces, after, rows):
    groups, width = len(pieces), pieces[0].shape[1]
    return pl.pallas_call(
        functools.partial(assemble_kernel, groups, len(after)),
        out_shape=jax.ShapeDtypeStruct((rows, groups * width), bf16),
        in_specs=[SMEM] + [VMEM] * groups + [ANY] * len(after),
        out_specs=VMEM,
        compiler_params=params(),
        cost_estimate=cost(0, 4 * rows * groups * width),
    )(meta, *pieces, *after)


def gated_kernel(groups, parts, place_of, meta_ref, gate_ref, d_out_ref, *refs):
    msgs, turned = refs[:-1], refs[-1]
    gated = (gate_ref[...] * d_out_ref[...].astype(f32)).astype(bf16)
    turned[...] = gated.astype(f32).T
    rows = msgs[0].shape[2]
    z, oc, dp = meta_ref[0], meta_ref[1], meta_ref[2]
    for k, msg in enumerate(msgs):
        for j in range(parts):
            for g in range(groups):
                at = (dp ^ k) * (groups * parts) + place_of(oc ^ j, z ^ g)
                msg[j, g] = turned[pl.ds(pl.multiple_of(at * rows, 8), rows), :].astype(bf16)


def gated_parts(meta, gate, d_out, n_dp, groups, parts, place_of):
    local, model = d_out.shape
    rows = model // (n_dp * groups * parts)
    return pl.pallas_call(
        functools.partial(gated_kernel, groups, parts, place_of),
        out_shape=[jax.ShapeDtypeStruct((parts, groups, rows, local), bf16)] * n_dp,
        in_specs=[SMEM, VMEM, VMEM],
        out_specs=[VMEM] * n_dp,
        scratch_shapes=[pltpu.VMEM((model, local), f32)],
        compiler_params=params(60),
        cost_estimate=cost(0, 4 * local * model),
    )(meta, gate, d_out)


def gather_kernel(n_dp, *refs):
    pieces, outs = refs[:n_dp], refs[n_dp:]
    for j, out in enumerate(outs):
        for k, piece in enumerate(pieces):
            out[k] = piece[j + 1]


def gather_parts(pieces):
    parts = pieces[0].shape[0]
    shape = (len(pieces),) + pieces[0].shape[1:]
    return pl.pallas_call(
        functools.partial(gather_kernel, len(pieces)),
        out_shape=[jax.ShapeDtypeStruct(shape, bf16)] * (parts - 1),
        in_specs=[VMEM] * len(pieces),
        out_specs=[VMEM] * (parts - 1),
        compiler_params=params(),
        cost_estimate=cost(0, 4 * math.prod(shape) * (parts - 1)),
    )(*pieces)


def project_kernel(
    groups, parts, place_of, meta_ref, attn_ref, w_ref, gate_ref, d_out_ref, out_ref, d_attn_ref,
    term_ref, *refs
):
    sent, by_place = refs[:-1], refs[-1]
    rows = attn_ref.shape[0]
    block = 512
    sums = []
    for at in range(0, w_ref.shape[0], block):
        cols = slice(at, at + block)
        got = lax.dot_general(
            attn_ref[...], w_ref[cols, :], (((1,), (1,)), ((), ())), preferred_element_type=f32
        )
        out_ref[:, cols] = (got * gate_ref[:, cols]).astype(bf16)
        sums.append(jnp.sum(got * d_out_ref[:, cols].astype(f32), axis=0, keepdims=True))
    total = jnp.zeros(d_attn_ref.shape, f32)
    for at in range(0, w_ref.shape[0], block):
        cols = slice(at, at + block)
        gated = (gate_ref[:, cols] * d_out_ref[:, cols].astype(f32)).astype(bf16)
        total = total + jnp.dot(gated, w_ref[cols, :], preferred_element_type=f32)
    d_attn_ref[...] = total.astype(bf16)
    sums = jnp.concatenate(sums, axis=1)
    places, width = by_place.shape
    for s in range(places):
        by_place[s : s + 1, :] = sums[:, s * width : (s + 1) * width]
    for g in range(groups):
        at = place_of(meta_ref[1], meta_ref[0] ^ g)
        term_ref[g : g + 1, :] = by_place[pl.ds(at, 1), :]
    for j, out in enumerate(sent):
        out[:rows, :] = attn_ref[...]
        line = [
            by_place[pl.ds(place_of(meta_ref[1] ^ (j + 1), meta_ref[0] ^ g), 1), :]
            for g in range(groups)
        ]
        line = jnp.concatenate(line, axis=1)
        line = jnp.concatenate(
            [line, jnp.zeros((1, attn_ref.shape[1] - groups * width), f32)], axis=1
        ) if attn_ref.shape[1] > groups * width else line
        high = line.astype(bf16).astype(f32)
        lines = [high, line - high, jnp.zeros((EXTRA - 2, line.shape[1]), f32)]
        out[rows:, :] = jnp.concatenate(lines, axis=0).astype(bf16)


def project(meta, attn, out_weight, gate, d_out, groups, parts, place_of):
    rows, inner = attn.shape
    model = out_weight.shape[0]
    width = model // (groups * parts)
    shapes = [jax.ShapeDtypeStruct((rows, model), bf16), jax.ShapeDtypeStruct((rows, inner), bf16)]
    shapes += [jax.ShapeDtypeStruct((groups, width), f32)]
    shapes += [jax.ShapeDtypeStruct((rows + EXTRA, inner), bf16)] * (parts - 1)
    return pl.pallas_call(
        functools.partial(project_kernel, groups, parts, place_of),
        out_shape=shapes,
        in_specs=[SMEM, VMEM, VMEM, VMEM, VMEM],
        out_specs=[VMEM] * (2 + parts),
        scratch_shapes=[pltpu.VMEM((groups * parts, width), f32)],
        compiler_params=params(),
        cost_estimate=cost(4 * rows * inner * model, 2 * inner * model),
    )(meta, attn, out_weight, gate, d_out)


def split_gate(gate, size):
    short = -gate.shape[1] % size
    if short:
        gate = jnp.concatenate([gate, jnp.zeros((1, short), f32)], axis=1)
    high = gate.astype(bf16).astype(f32)
    lines = [p[:, at : at + size] for p in (high, gate - high) for at in range(0, gate.shape[1], size)]
    return jnp.concatenate(lines + [jnp.zeros((EXTRA - len(lines), size), f32)], axis=0)


def joined_gate(lines, width):
    n = -(-width // lines.shape[1])
    both = lines[:n] + lines[n : 2 * n]
    return jnp.concatenate([both[i : i + 1] for i in range(n)], axis=1)[:, :width]


def grad_kernel(n_left, n_pieces, *refs):
    lefts, refs = refs[:n_left], refs[n_left:]
    pieces, refs = refs[:n_pieces], refs[n_pieces:]
    term_ref, outs = refs[0], refs[1:]
    groups, rows, depth = lefts[0].shape[1:]
    width = pieces[0].shape[1]
    size = outs[0].shape[1]
    left = []
    for ref in lefts:
        left += [ref[i].reshape(groups * rows, depth) for i in range(ref.shape[0])]
    left = jnp.concatenate(left, axis=1)
    homes = [((outs[0], 0),), ((outs[1], 0), (outs[2], outs[1].shape[0]))]
    homes += [((out, 0),) for out in outs[3:]]
    half = outs[1].shape[0]

    def put(g, at, value):
        out, start = homes[g][-1] if at >= half else homes[g][0]
        out[at - start : at - start + value.shape[0], :] = value.astype(out.dtype)

    block = 256
    for start in range(0, width, block):
        right = jnp.concatenate([p[:depth, start : start + block] for p in pieces], axis=0)
        got = jnp.dot(left, right, preferred_element_type=f32)
        for g in range(groups):
            for at in range(0, block, size):
                put(g, (start + at) // size * rows, got[g * rows : (g + 1) * rows, at : at + size])
    term = term_ref[...]
    each = term.shape[1]
    for p in pieces:
        if p.shape[0] > depth:
            lines = p[depth:, :].astype(f32)
            line = lines[0:1, :] + lines[1:2, :]
            term = term + jnp.concatenate(
                [line[:, g * each : (g + 1) * each] for g in range(groups)], axis=0
            )
    for g in range(groups):
        put(g, width // size * rows, split_gate(term[g : g + 1], size))


def grad_product(lefts, pieces, term):
    groups, rows, depth = lefts[0].shape[1:]
    width = pieces[0].shape[1]
    size = 128
    total = groups * rows
    depth = depth * len(pieces)
    full = width // size * rows + EXTRA
    half = width // size // 2 * rows
    shapes = [(full, f32), (half, bf16), (full - half, bf16), (full, f32), (full, bf16)]
    return pl.pallas_call(
        functools.partial(grad_kernel, len(lefts), len(pieces)),
        out_shape=[jax.ShapeDtypeStruct((n, size), kind) for n, kind in shapes],
        in_specs=[VMEM] * (len(lefts) + len(pieces) + 1),
        out_specs=[VMEM] * len(shapes),
        compiler_params=params(),
        cost_estimate=cost(
            2 * total * depth * width, 2 * (total * depth + depth * width + total * width)
        ),
    )(*lefts, *pieces, term)


def pair_kernel(gate_width, own_ref, got_ref, out_ref):
    total = own_ref[...] + got_ref[...].astype(f32)
    end = total.shape[0] - EXTRA
    out_ref[:end, :] = total[:end].astype(bf16)
    gate = joined_gate(total[end:], gate_width)
    out_ref[end:, :] = split_gate(gate, total.shape[1]).astype(bf16)


def pair_sum(own, got, gate_width):
    return pl.pallas_call(
        functools.partial(pair_kernel, gate_width),
        out_shape=jax.ShapeDtypeStruct(got.shape, bf16),
        in_specs=[VMEM] * 2,
        out_specs=VMEM,
        compiler_params=params(),
        cost_estimate=cost(0, 8 * own.size),
    )(own, got)


def final_kernel(own_ref, far_ref, low_ref, high_ref, out_ref, gate_ref):
    size = own_ref.shape[1]
    rows = out_ref.shape[0]
    half = low_ref.shape[0]

    def total(at, count):
        ref, start = (high_ref, half) if at >= half else (low_ref, 0)
        got = own_ref[at : at + count, :] + far_ref[at : at + count, :].astype(f32)
        return got + ref[at - start : at - start + count, :].astype(f32)

    for i in range(out_ref.shape[1] // size):
        out_ref[:, i * size : (i + 1) * size] = total(i * rows, rows)
    gate_ref[...] = joined_gate(total(own_ref.shape[0] - EXTRA, EXTRA), gate_ref.shape[1])


def final_sum(own, far, low, high, rows, width, gate_width):
    return pl.pallas_call(
        final_kernel,
        out_shape=[
            jax.ShapeDtypeStruct((rows, width), f32),
            jax.ShapeDtypeStruct((1, gate_width), f32),
        ],
        in_specs=[VMEM] * 4,
        out_specs=[VMEM] * 2,
        compiler_params=params(),
        cost_estimate=cost(0, 8 * rows * width),
    )(own, far, low, high)


def on_device(
    caption_states,
    caption_gain,
    text_proj,
    caption_len,
    slot_source,
    query_gain,
    key_gain,
    image_q,
    image_k,
    image_v,
    out_weight,
    gate,
    d_out,
):
    n_dp = lax.axis_size("dp")
    n_seq = lax.axis_size("seq")
    G, C = GROUPS, CORES
    O = n_seq // (G * C)
    OC = O * C
    dp = lax.axis_index("dp")
    seq = lax.axis_index("seq")
    z = (seq // C) % G
    oc = (seq // (G * C)) * C + seq % C

    def place(oc_at, z_at):
        return ((oc_at // C) * G + z_at) * C + oc_at % C

    def to_z(x, k):
        perm = [(place(a, b), place(a, b ^ k)) for a in range(OC) for b in range(G)]
        return lax.ppermute(x, "seq", perm)

    def to_oc(x, j):
        perm = [(place(a, b), place(a ^ j, b)) for a in range(OC) for b in range(G)]
        return lax.ppermute(x, "seq", perm)

    def to_dp(x, k):
        return lax.ppermute(x, "dp", [(a, a ^ k) for a in range(n_dp)])

    def part(x, index, size, axis):
        return lax.dynamic_slice_in_dim(x, index * size, size, axis)

    slot_total = slot_source.shape[1]
    slot_local = slot_total // n_seq
    image_local = image_q.shape[1]
    inner_width = image_q.shape[2]
    model_width = out_weight.shape[0]
    head_size = query_gain.shape[0]
    gw = inner_width // G
    order = [2, 3, 1]
    meta = jnp.stack([z, oc, dp]).astype(jnp.int32)

    heads = gw // head_size
    text_rows = G * slot_local
    own, *rest = text_project(
        meta, caption_len, slot_source, caption_states[0], caption_gain[None],
        query_gain[None], key_gain[None], image_k[0], image_v[0], image_q[0], text_proj,
        G, OC, place,
    )
    packed, sent = rest[:G], rest[G:]
    images = [packed[0]] + [to_z(packed[k], k) for k in range(1, G)]
    nears = [to_oc(packed[0], j) for j in range(1, OC)]
    got = [to_oc(x, j + 1) for j, x in enumerate(sent)]
    own, sent = text_sum(own, got, text_rows)
    own, sent = text_sum(own, [to_z(sent, 1)], text_rows)
    got = to_z(sent, 2)

    gg = gated_parts(meta, gate, d_out[0], n_dp, G, OC, place)
    gg_dp = [gg[0], to_dp(gg[1], 1)]
    block = block_of(own, got, gg_dp[1], images[1:], DT5, heads)
    blocks = [block] + [to_oc(block, j) for j in range(1, OC)]
    *outs, text_out = attention(images, nears, blocks, heads, image_local, text_rows)

    back = []
    for k in range(G):
        rows = jnp.concatenate([outs[k], part(text_out, z ^ k, slot_local, 0)], axis=0)
        back.append(to_z(rows, k) if k else rows)
    gg_dp += [to_dp(gg[k], k) for k in range(2, n_dp)]
    lefts = [g[:1] for g in gg_dp]
    lefts += [to_oc(g, j + 1) for j, g in enumerate(gather_parts(gg_dp))]
    image_attn = assemble(meta, back, gg_dp[1:], image_local)
    text_attn = jnp.zeros((slot_local, inner_width), bf16)
    own_usable = part(slot_source[0] < caption_len[0], seq, slot_local, 0)
    for k in range(G):
        rows = jnp.where(own_usable[:, None], back[k][image_local:], jnp.zeros((), bf16))
        text_attn = lax.dynamic_update_slice_in_dim(text_attn, rows, (z ^ k) * gw, 1)

    pieces = [image_attn] + [to_dp(image_attn, k) for k in range(1, n_dp)]
    image_out, d_attn, term, *sent = project(
        meta, image_attn, out_weight, gate, d_out[0], G, OC, place
    )
    for j in range(1, OC):
        pieces += [to_oc(sent[j - 1], j)] + [to_oc(p, j) for p in pieces[1:n_dp]]
    R = model_width // (n_dp * n_seq)
    gate_width = model_width // n_seq
    own, low, high, own_pair, far = grad_product(lefts, pieces, term)
    pair = pair_sum(own_pair, to_z(far, 1), gate_width)
    grad_wo, grad_gate = final_sum(
        own, to_z(pair, 2), to_z(low, 1), to_z(high, 1), R, inner_width, gate_width
    )
    return (image_out[None], text_attn[None], d_attn[None], grad_wo, grad_gate)


def solution(mesh):
    in_specs = (
        P("dp", None, "seq"),
        P("seq"),
        P("seq", None),
        P("dp"),
        P("dp", None),
        P(),
        P(),
        P("dp", "seq", None),
        P("dp", "seq", None),
        P("dp", "seq", None),
        P(),
        P("dp", None),
        P("dp", "seq", None),
    )
    out_specs = (
        P("dp", "seq", None),
        P("dp", "seq", None),
        P("dp", "seq", None),
        P(("dp", "seq"), None),
        P("dp", "seq"),
    )
    return jax.shard_map(
        on_device, mesh=mesh, in_specs=in_specs, out_specs=out_specs, check_vma=False
    )
```

```python
import math
import functools
import jax
import jax.numpy as jnp
from jax import lax
from jax.experimental import pallas as pl
from jax.experimental.pallas import tpu as pltpu
from jax.sharding import PartitionSpec as P

DT5 = 4096
CORES = 2
GROUPS = 4

eps_norm = 1e-06
f32 = jnp.float32
bf16 = jnp.bfloat16
EXTRA = 16


VMEM = pl.BlockSpec(memory_space=pltpu.VMEM)
SMEM = pl.BlockSpec(memory_space=pltpu.SMEM)
ANY = pl.BlockSpec(memory_space=pl.ANY)


def params(mib=24):
    return pltpu.CompilerParams(vmem_limit_bytes=int(mib * 1024 * 1024))


def cost(flops, bytes_accessed, transcendentals=0):
    return pl.CostEstimate(
        flops=flops, bytes_accessed=bytes_accessed, transcendentals=transcendentals
    )


def split_tail(squares, width):
    high = squares.astype(bf16).astype(f32)
    low = squares - high
    lane = lax.broadcasted_iota(jnp.int32, (squares.shape[0], width), 1)
    return jnp.where(lane == 0, high, jnp.where(lane == 1, low, 0.0))


def joined(tail):
    return tail[:, 0:1] + tail[:, 1:2]


def text_kernel(
    groups, heads, place_of, meta_ref, len_ref, src_ref, states_ref, gain_ref, qg_ref, kg_ref,
    k_ref, v_ref, q_ref, w_ref, own_ref, *refs
):
    packed, refs = refs[:groups], refs[groups:]
    msgs, (w_all, loaded, stage, w_sems, in_sems, out_sems) = refs[:-6], refs[-6:]
    size = own_ref.shape[2]
    rows = (own_ref.shape[1] - EXTRA) // (3 * heads + 1)
    width = heads * size
    slots = states_ref.shape[0]
    slot_local = rows // groups
    copies = []
    block = w_all.shape[0] // w_sems.shape[0]
    for i in range(w_sems.shape[0]):
        part = pl.ds(i * block, block)
        copies.append(pltpu.make_async_copy(w_ref.at[part], w_all.at[part], w_sems.at[i]))
        copies[-1].start()
    loads = []
    for i, ref in enumerate((k_ref, v_ref, q_ref)):
        loads.append(pltpu.make_async_copy(ref, loaded.at[i], in_sems.at[i]))
        loads[-1].start()

    def slot_at(row):
        z_at = (row % rows) // slot_local
        return place_of(meta_ref[1] ^ (row // rows), z_at) * slot_local + row % slot_local

    iota = functools.partial(lax.broadcasted_iota, jnp.int32, (slots, slots))
    sources = src_ref[...].astype(f32)
    chosen = (iota(1) == slot_at(iota(0))).astype(f32)
    source_col = jnp.sum(chosen * sources, axis=1, keepdims=True)
    pick = (iota(1).astype(f32) == source_col).astype(bf16)
    chosen_t = (iota(0) == slot_at(iota(1))).astype(bf16)
    source_row = jnp.dot(sources.astype(bf16), chosen_t, preferred_element_type=f32)
    bias = jnp.where(source_row < len_ref[0].astype(f32), 0.0, -1e30)
    end = own_ref.shape[1] - EXTRA
    own_ref[0, end:, :] = jnp.zeros((EXTRA, size), f32)
    own_ref[0, end : end + 1, :] = qg_ref[...]
    own_ref[0, end + 1 : end + 2, :] = kg_ref[...]
    own_ref[0, end + 2 : end + 3, :slots] = bias

    picked = jnp.dot(pick, states_ref[...], preferred_element_type=f32)
    scaled = (picked * gain_ref[...]).astype(bf16)
    tail = split_tail(jnp.sum(picked * picked, axis=1, keepdims=True), size)
    for copy in loads:
        copy.wait()
    local = loaded.shape[1]
    stores = []
    for g in range(groups):
        for i in range(3):
            for head in range(heads):
                at = ((meta_ref[0] ^ g) * heads + head) * size
                to = (i * heads + head) * local
                stage[g, to : to + local, :] = loaded[i, :, pl.ds(pl.multiple_of(at, 128), size)]
        stores.append(pltpu.make_async_copy(stage.at[g], packed[g], out_sems.at[g]))
        stores[-1].start()
    for copy in copies:
        copy.wait()
    for g in range(groups):
        for i in range(3):
            at = (i * groups + (meta_ref[0] ^ g)) * width
            columns = pl.ds(pl.multiple_of(at, 128), width)
            got = jnp.dot(scaled, w_all[:, columns], preferred_element_type=f32)
            for head in range(heads):
                part = got[:, head * size : (head + 1) * size]
                to = slice((i * heads + head) * rows, (i * heads + head + 1) * rows)
                own_ref[g, to, :] = part[:rows]
                for j, msg in enumerate(msgs):
                    msg[g, to, :] = part[(j + 1) * rows : (j + 2) * rows].astype(bf16)
        own_ref[g, 3 * heads * rows : end, :] = tail[:rows]
        for j, msg in enumerate(msgs):
            msg[g, 3 * heads * rows :, :] = tail[(j + 1) * rows : (j + 2) * rows].astype(bf16)
    for copy in stores:
        copy.wait()


def text_project(
    meta, length, sources, states, gain, query_gain, key_gain, keys, values, queries, text_proj,
    groups, parts, place_of
):
    slots, depth = states.shape
    size = query_gain.shape[1]
    heads = text_proj.shape[1] // (3 * groups * size)
    text_rows = (3 * heads + 1) * slots // parts
    shapes = [jax.ShapeDtypeStruct((groups, text_rows + EXTRA, size), f32)]
    shapes += [jax.ShapeDtypeStruct((3 * heads * keys.shape[0], size), bf16)] * groups
    shapes += [jax.ShapeDtypeStruct((groups, text_rows, size), bf16)] * (parts - 1)
    return pl.pallas_call(
        functools.partial(text_kernel, groups, heads, place_of),
        out_shape=shapes,
        in_specs=[SMEM, SMEM] + [VMEM] * 5 + [ANY] * 4,
        out_specs=[VMEM] + [ANY] * groups + [VMEM] * (parts - 1),
        scratch_shapes=[
            pltpu.VMEM(text_proj.shape, bf16),
            pltpu.VMEM((3,) + keys.shape, bf16),
            pltpu.VMEM((groups, 3 * heads * keys.shape[0], size), bf16),
            pltpu.SemaphoreType.DMA((4,)),
            pltpu.SemaphoreType.DMA((3,)),
            pltpu.SemaphoreType.DMA((groups,)),
        ],
        compiler_params=params(60),
        cost_estimate=cost(
            2 * slots * depth * text_proj.shape[1], 2 * depth * text_proj.shape[1]
        ),
    )(
        meta, length, sources, states, gain, query_gain, key_gain, keys, values, queries, text_proj
    )


def text_sum_kernel(n_got, tail_rows, own_ref, *refs):
    got, (keep_ref, send_ref) = refs[:n_got], refs[n_got:]
    groups, text_rows, size = got[0].shape
    for g in range(groups):
        total = own_ref[g, :text_rows, :]
        for ref in got:
            total = total + ref[g].astype(f32)
        end = text_rows - tail_rows
        tail = split_tail(joined(total[end:]), size)
        if g % 2 == 0:
            keep_ref[g // 2, :end, :] = total[:end]
            keep_ref[g // 2, end:text_rows, :] = tail
            keep_ref[g // 2, text_rows:, :] = own_ref[g, text_rows:, :]
        else:
            send_ref[g // 2, :end, :] = total[:end].astype(bf16)
            send_ref[g // 2, end:, :] = tail.astype(bf16)


def text_sum(own, got, tail_rows):
    groups, rows, size = own.shape
    return pl.pallas_call(
        functools.partial(text_sum_kernel, len(got), tail_rows),
        out_shape=[
            jax.ShapeDtypeStruct((groups // 2, rows, size), f32),
            jax.ShapeDtypeStruct((groups // 2, rows - EXTRA, size), bf16),
        ],
        in_specs=[VMEM] * (1 + len(got)),
        out_specs=[VMEM] * 2,
        compiler_params=params(),
        cost_estimate=cost(0, 8 * groups * rows * size),
    )(own, *got)


def block_kernel(features, heads, n_pieces, own_ref, got_ref, *refs):
    pieces, out_ref = refs[:n_pieces], refs[-1]
    near_rows = pieces[0].shape[0]
    kv_rows = near_rows // 3 * 2
    out_ref[:near_rows, :] = pieces[0][...]
    for k, ref in enumerate(pieces[1:]):
        at = near_rows + k * kv_rows
        out_ref[at : at + kv_rows, :] = ref[:kv_rows, :]
    size = own_ref.shape[2]
    text_rows = got_ref.shape[1]
    rows = text_rows // (3 * heads + 1)
    total = own_ref[0, :text_rows, :] + got_ref[0].astype(f32)
    rate = lax.rsqrt(joined(total[3 * heads * rows :]) / features + eps_norm)
    start = near_rows + (n_pieces - 1) * kv_rows
    for i in range(3):
        for head in range(heads):
            at = (i * heads + head) * rows
            x = total[at : at + rows] * rate
            if i < 2:
                mean = jnp.sum(x * x, axis=1, keepdims=True) / size
                gain = own_ref[0, text_rows + i : text_rows + i + 1, :]
                x = x * lax.rsqrt(mean + eps_norm) * gain
            out_ref[start + at : start + at + rows, :] = x.astype(bf16)
    bias = own_ref[0, text_rows + 2 : text_rows + 3, :]
    start = start + 3 * heads * rows
    out_ref[start:, :] = jnp.broadcast_to(bias, (EXTRA, size)).astype(bf16)


def block_of(own, got, after, pieces, features, heads):
    rows, size = own.shape[1:]
    total = (rows - EXTRA) // (3 * heads + 1) * 3 * heads + EXTRA
    total += pieces[0].shape[0] // 3 * (2 * len(pieces) + 1)
    return pl.pallas_call(
        functools.partial(block_kernel, features, heads, len(pieces)),
        out_shape=jax.ShapeDtypeStruct((total, size), bf16),
        in_specs=[VMEM] * (2 + len(pieces)) + [ANY] * len(after),
        out_specs=VMEM,
        compiler_params=params(),
        cost_estimate=cost(0, 4 * total * size),
    )(own, got, *pieces, *after)


def attention_kernel(n_far, n_cores, heads, rows, text_rows, *refs):
    far, refs = refs[:n_far], refs[n_far:]
    blocks, refs = refs[:n_cores], refs[n_cores:]
    out_refs, tout_ref = refs[:-1], refs[-1]
    size = blocks[0].shape[1]
    factor = size ** (-0.5) * math.log2(math.e)
    nt = (((1,), (1,)), ((), ()))
    kv_rows = 2 * heads * rows
    near_rows = 3 * heads * rows
    starts = [0] + [near_rows + k * kv_rows for k in range(n_far)]
    text = near_rows + n_far * kv_rows
    end = text + 3 * heads * text_rows
    bias = blocks[0][end : end + EXTRA, :][:1, : n_cores * text_rows].astype(f32)

    def with_ones(values):
        return jnp.concatenate([values, jnp.ones(values.shape, bf16)], axis=1)

    for head in range(heads):
        kv, tkv = [], []
        for i in range(2):
            at = (i * heads + head) * rows
            image = [b[start + at : start + at + rows, :] for b in blocks for start in starts]
            text_at = text + ((i + 1) * heads + head) * text_rows
            kv.append(jnp.concatenate(image, axis=0))
            tkv.append(jnp.concatenate([b[text_at : text_at + text_rows, :] for b in blocks], axis=0))
        keys, values = kv[0], with_ones(kv[1])
        tkeys, tvalues = tkv[0], with_ones(tkv[1])
        cols = slice(head * size, (head + 1) * size)
        q_at = (2 * heads + head) * rows
        work = [(ref[q_at : q_at + rows, :], out) for ref, out in zip((blocks[0],) + tuple(far), out_refs)]
        tq_at = text + head * text_rows
        work.append((blocks[0][tq_at : tq_at + text_rows, :], tout_ref))
        for q, out_ref in work:
            s_img = lax.dot_general(q, keys, nt, preferred_element_type=f32)
            s_txt = lax.dot_general(q, tkeys, nt, preferred_element_type=f32) + bias
            top = jnp.maximum(
                jnp.max(s_img, axis=1, keepdims=True), jnp.max(s_txt, axis=1, keepdims=True)
            )
            p_img = jnp.exp2((s_img - top) * factor).astype(bf16)
            p_txt = jnp.exp2((s_txt - top) * factor).astype(bf16)
            acc = jnp.dot(p_img, values, preferred_element_type=f32)
            acc = acc + jnp.dot(p_txt, tvalues, preferred_element_type=f32)
            out_ref[:, cols] = (acc[:, :size] / acc[:, size:]).astype(bf16)


def attention(far, blocks, heads, rows, text_rows):
    size = blocks[0].shape[1]
    n = 1 + len(far)
    queries = n * rows + text_rows
    keys = len(blocks) * queries
    shapes = [jax.ShapeDtypeStruct((rows, heads * size), bf16)] * n
    shapes += [jax.ShapeDtypeStruct((text_rows, heads * size), bf16)]
    return pl.pallas_call(
        functools.partial(attention_kernel, len(far), len(blocks), heads, rows, text_rows),
        out_shape=shapes,
        in_specs=[VMEM] * (len(far) + len(blocks)),
        out_specs=[VMEM] * len(shapes),
        compiler_params=params(),
        cost_estimate=cost(
            4 * queries * keys * heads * size,
            4 * (queries + keys) * heads * size,
            queries * keys * heads,
        ),
    )(*far, *blocks)


def assemble_kernel(groups, n_after, meta_ref, *refs):
    pieces, out_ref = refs[:groups], refs[groups + n_after]
    rows, width = out_ref.shape[0], pieces[0].shape[1]
    for k, piece in enumerate(pieces):
        at = pl.multiple_of((meta_ref[0] ^ k) * width, 128)
        out_ref[:, pl.ds(at, width)] = piece[:rows, :]


def assemble(meta, pieces, after, rows):
    groups, width = len(pieces), pieces[0].shape[1]
    return pl.pallas_call(
        functools.partial(assemble_kernel, groups, len(after)),
        out_shape=jax.ShapeDtypeStruct((rows, groups * width), bf16),
        in_specs=[SMEM] + [VMEM] * groups + [ANY] * len(after),
        out_specs=VMEM,
        compiler_params=params(),
        cost_estimate=cost(0, 4 * rows * groups * width),
    )(meta, *pieces, *after)


def gated_kernel(groups, parts, place_of, meta_ref, gate_ref, d_out_ref, *refs):
    msgs, turned = refs[:-1], refs[-1]
    gated = (gate_ref[...] * d_out_ref[...].astype(f32)).astype(bf16)
    turned[...] = gated.astype(f32).T
    rows = msgs[0].shape[2]
    z, oc, dp = meta_ref[0], meta_ref[1], meta_ref[2]
    for k, msg in enumerate(msgs):
        for j in range(parts):
            for g in range(groups):
                at = (dp ^ k) * (groups * parts) + place_of(oc ^ j, z ^ g)
                msg[j, g] = turned[pl.ds(pl.multiple_of(at * rows, 8), rows), :].astype(bf16)


def gated_parts(meta, gate, d_out, n_dp, groups, parts, place_of):
    local, model = d_out.shape
    rows = model // (n_dp * groups * parts)
    return pl.pallas_call(
        functools.partial(gated_kernel, groups, parts, place_of),
        out_shape=[jax.ShapeDtypeStruct((parts, groups, rows, local), bf16)] * n_dp,
        in_specs=[SMEM, VMEM, VMEM],
        out_specs=[VMEM] * n_dp,
        scratch_shapes=[pltpu.VMEM((model, local), f32)],
        compiler_params=params(60),
        cost_estimate=cost(0, 4 * local * model),
    )(meta, gate, d_out)


def gather_kernel(n_dp, *refs):
    pieces, outs = refs[:n_dp], refs[n_dp:]
    for j, out in enumerate(outs):
        for k, piece in enumerate(pieces):
            out[k] = piece[j + 1]


def gather_parts(pieces):
    parts = pieces[0].shape[0]
    shape = (len(pieces),) + pieces[0].shape[1:]
    return pl.pallas_call(
        functools.partial(gather_kernel, len(pieces)),
        out_shape=[jax.ShapeDtypeStruct(shape, bf16)] * (parts - 1),
        in_specs=[VMEM] * len(pieces),
        out_specs=[VMEM] * (parts - 1),
        compiler_params=params(),
        cost_estimate=cost(0, 4 * math.prod(shape) * (parts - 1)),
    )(*pieces)


def project_kernel(
    groups, parts, place_of, meta_ref, attn_ref, w_ref, gate_ref, d_out_ref, out_ref, d_attn_ref,
    term_ref, *refs
):
    sent, by_place = refs[:-1], refs[-1]
    rows = attn_ref.shape[0]
    block = 512
    sums = []
    for at in range(0, w_ref.shape[0], block):
        cols = slice(at, at + block)
        got = lax.dot_general(
            attn_ref[...], w_ref[cols, :], (((1,), (1,)), ((), ())), preferred_element_type=f32
        )
        out_ref[:, cols] = (got * gate_ref[:, cols]).astype(bf16)
        sums.append(jnp.sum(got * d_out_ref[:, cols].astype(f32), axis=0, keepdims=True))
    total = jnp.zeros(d_attn_ref.shape, f32)
    for at in range(0, w_ref.shape[0], block):
        cols = slice(at, at + block)
        gated = (gate_ref[:, cols] * d_out_ref[:, cols].astype(f32)).astype(bf16)
        total = total + jnp.dot(gated, w_ref[cols, :], preferred_element_type=f32)
    d_attn_ref[...] = total.astype(bf16)
    sums = jnp.concatenate(sums, axis=1)
    places, width = by_place.shape
    for s in range(places):
        by_place[s : s + 1, :] = sums[:, s * width : (s + 1) * width]
    for g in range(groups):
        at = place_of(meta_ref[1], meta_ref[0] ^ g)
        term_ref[g : g + 1, :] = by_place[pl.ds(at, 1), :]
    for j, out in enumerate(sent):
        out[:rows, :] = attn_ref[...]
        line = [
            by_place[pl.ds(place_of(meta_ref[1] ^ (j + 1), meta_ref[0] ^ g), 1), :]
            for g in range(groups)
        ]
        line = jnp.concatenate(line, axis=1)
        line = jnp.concatenate(
            [line, jnp.zeros((1, attn_ref.shape[1] - groups * width), f32)], axis=1
        ) if attn_ref.shape[1] > groups * width else line
        high = line.astype(bf16).astype(f32)
        lines = [high, line - high, jnp.zeros((EXTRA - 2, line.shape[1]), f32)]
        out[rows:, :] = jnp.concatenate(lines, axis=0).astype(bf16)


def project(meta, attn, out_weight, gate, d_out, groups, parts, place_of):
    rows, inner = attn.shape
    model = out_weight.shape[0]
    width = model // (groups * parts)
    shapes = [jax.ShapeDtypeStruct((rows, model), bf16), jax.ShapeDtypeStruct((rows, inner), bf16)]
    shapes += [jax.ShapeDtypeStruct((groups, width), f32)]
    shapes += [jax.ShapeDtypeStruct((rows + EXTRA, inner), bf16)] * (parts - 1)
    return pl.pallas_call(
        functools.partial(project_kernel, groups, parts, place_of),
        out_shape=shapes,
        in_specs=[SMEM, VMEM, VMEM, VMEM, VMEM],
        out_specs=[VMEM] * (2 + parts),
        scratch_shapes=[pltpu.VMEM((groups * parts, width), f32)],
        compiler_params=params(),
        cost_estimate=cost(4 * rows * inner * model, 2 * inner * model),
    )(meta, attn, out_weight, gate, d_out)


def split_gate(gate, size):
    short = -gate.shape[1] % size
    if short:
        gate = jnp.concatenate([gate, jnp.zeros((1, short), f32)], axis=1)
    high = gate.astype(bf16).astype(f32)
    lines = [p[:, at : at + size] for p in (high, gate - high) for at in range(0, gate.shape[1], size)]
    return jnp.concatenate(lines + [jnp.zeros((EXTRA - len(lines), size), f32)], axis=0)


def joined_gate(lines, width):
    n = -(-width // lines.shape[1])
    both = lines[:n] + lines[n : 2 * n]
    return jnp.concatenate([both[i : i + 1] for i in range(n)], axis=1)[:, :width]


def grad_kernel(n_left, n_pieces, *refs):
    lefts, refs = refs[:n_left], refs[n_left:]
    pieces, refs = refs[:n_pieces], refs[n_pieces:]
    term_ref, outs = refs[0], refs[1:]
    groups, rows, depth = lefts[0].shape[1:]
    width = pieces[0].shape[1]
    size = outs[0].shape[1]
    left = []
    for ref in lefts:
        left += [ref[i].reshape(groups * rows, depth) for i in range(ref.shape[0])]
    left = jnp.concatenate(left, axis=1)
    half = outs[1].shape[0]
    homes = [((outs[0], 0),)]
    homes += [((outs[2 * g - 1], 0), (outs[2 * g], half)) for g in range(1, groups)]

    def put(g, at, value):
        out, start = homes[g][-1] if at >= half else homes[g][0]
        out[at - start : at - start + value.shape[0], :] = value.astype(out.dtype)

    block = 256
    for start in range(0, width, block):
        right = jnp.concatenate([p[:depth, start : start + block] for p in pieces], axis=0)
        got = jnp.dot(left, right, preferred_element_type=f32)
        for g in range(groups):
            for at in range(0, block, size):
                put(g, (start + at) // size * rows, got[g * rows : (g + 1) * rows, at : at + size])
    term = term_ref[...]
    each = term.shape[1]
    for p in pieces:
        if p.shape[0] > depth:
            lines = p[depth:, :].astype(f32)
            line = lines[0:1, :] + lines[1:2, :]
            term = term + jnp.concatenate(
                [line[:, g * each : (g + 1) * each] for g in range(groups)], axis=0
            )
    for g in range(groups):
        put(g, width // size * rows, split_gate(term[g : g + 1], size))


def grad_product(lefts, pieces, term):
    groups, rows, depth = lefts[0].shape[1:]
    width = pieces[0].shape[1]
    size = 128
    total = groups * rows
    depth = depth * len(pieces)
    full = width // size * rows + EXTRA
    half = width // size // 2 * rows
    shapes = [(full, f32)]
    for kind in (bf16, f32, bf16):
        shapes += [(half, kind), (full - half, kind)]
    return pl.pallas_call(
        functools.partial(grad_kernel, len(lefts), len(pieces)),
        out_shape=[jax.ShapeDtypeStruct((n, size), kind) for n, kind in shapes],
        in_specs=[VMEM] * (len(lefts) + len(pieces) + 1),
        out_specs=[VMEM] * len(shapes),
        compiler_params=params(),
        cost_estimate=cost(
            2 * total * depth * width, 2 * (total * depth + depth * width + total * width)
        ),
    )(*lefts, *pieces, term)


def pair_kernel(gate_width, own_ref, got_ref, out_ref):
    total = own_ref[...] + got_ref[...].astype(f32)
    if not gate_width:
        out_ref[...] = total.astype(bf16)
    else:
        end = total.shape[0] - EXTRA
        out_ref[:end, :] = total[:end].astype(bf16)
        gate = joined_gate(total[end:], gate_width)
        out_ref[end:, :] = split_gate(gate, total.shape[1]).astype(bf16)


def pair_sum(own, got, gate_width):
    return pl.pallas_call(
        functools.partial(pair_kernel, gate_width),
        out_shape=jax.ShapeDtypeStruct(got.shape, bf16),
        in_specs=[VMEM] * 2,
        out_specs=VMEM,
        compiler_params=params(),
        cost_estimate=cost(0, 8 * own.size),
    )(own, got)


def final_kernel(own_ref, far_low, far_high, near_low, near_high, out_ref, gate_ref):
    size = own_ref.shape[1]
    rows = out_ref.shape[0]
    half = far_low.shape[0]

    def total(at, count):
        refs, start = ((far_high, near_high), half) if at >= half else ((far_low, near_low), 0)
        got = own_ref[at : at + count, :]
        for ref in refs:
            got = got + ref[at - start : at - start + count, :].astype(f32)
        return got

    for i in range(out_ref.shape[1] // size):
        out_ref[:, i * size : (i + 1) * size] = total(i * rows, rows)
    gate_ref[...] = joined_gate(total(own_ref.shape[0] - EXTRA, EXTRA), gate_ref.shape[1])


def final_sum(own, far, near, rows, width, gate_width):
    return pl.pallas_call(
        final_kernel,
        out_shape=[
            jax.ShapeDtypeStruct((rows, width), f32),
            jax.ShapeDtypeStruct((1, gate_width), f32),
        ],
        in_specs=[VMEM] * 5,
        out_specs=[VMEM] * 2,
        compiler_params=params(),
        cost_estimate=cost(0, 8 * rows * width),
    )(own, *far, *near)


def on_device(
    caption_states,
    caption_gain,
    text_proj,
    caption_len,
    slot_source,
    query_gain,
    key_gain,
    image_q,
    image_k,
    image_v,
    out_weight,
    gate,
    d_out,
):
    n_dp = lax.axis_size("dp")
    n_seq = lax.axis_size("seq")
    G, C = GROUPS, CORES
    O = n_seq // (G * C)
    OC = O * C
    dp = lax.axis_index("dp")
    seq = lax.axis_index("seq")
    z = (seq // C) % G
    oc = (seq // (G * C)) * C + seq % C

    def place(oc_at, z_at):
        return ((oc_at // C) * G + z_at) * C + oc_at % C

    def to_z(x, k):
        perm = [(place(a, b), place(a, b ^ k)) for a in range(OC) for b in range(G)]
        return lax.ppermute(x, "seq", perm)

    def to_oc(x, j):
        perm = [(place(a, b), place(a ^ j, b)) for a in range(OC) for b in range(G)]
        return lax.ppermute(x, "seq", perm)

    def to_dp(x, k):
        return lax.ppermute(x, "dp", [(a, a ^ k) for a in range(n_dp)])

    def part(x, index, size, axis):
        return lax.dynamic_slice_in_dim(x, index * size, size, axis)

    slot_total = slot_source.shape[1]
    slot_local = slot_total // n_seq
    image_local = image_q.shape[1]
    inner_width = image_q.shape[2]
    model_width = out_weight.shape[0]
    head_size = query_gain.shape[0]
    gw = inner_width // G
    order = [2, 3, 1]
    meta = jnp.stack([z, oc, dp]).astype(jnp.int32)

    heads = gw // head_size
    text_rows = G * slot_local
    own, *rest = text_project(
        meta, caption_len, slot_source, caption_states[0], caption_gain[None],
        query_gain[None], key_gain[None], image_k[0], image_v[0], image_q[0], text_proj,
        G, OC, place,
    )
    packed, sent = rest[:G], rest[G:]
    images = {0: packed[0]}
    for k in order:
        images[k] = to_z(packed[k], k)
    images = [images[k] for k in range(G)]
    got = [to_oc(x, j + 1) for j, x in enumerate(sent)]
    own, sent = text_sum(own, got, text_rows)
    own, sent = text_sum(own, [to_z(sent, 1)], text_rows)
    got = to_z(sent, 2)

    gg = gated_parts(meta, gate, d_out[0], n_dp, G, OC, place)
    gg_dp = [gg[0], to_dp(gg[1], 1)]
    block = block_of(own, got, gg_dp[1:], images, DT5, heads)
    blocks = [block] + [to_oc(block, j) for j in range(1, OC)]
    *outs, text_out = attention(images[1:], blocks, heads, image_local, text_rows)

    back = {}
    for k in order + [0]:
        rows = jnp.concatenate([outs[k], part(text_out, z ^ k, slot_local, 0)], axis=0)
        back[k] = to_z(rows, k) if k else rows
    back = [back[k] for k in range(G)]
    gg_dp += [to_dp(gg[k], k) for k in range(2, n_dp)]
    lefts = [g[:1] for g in gg_dp]
    lefts += [to_oc(g, j + 1) for j, g in enumerate(gather_parts(gg_dp))]
    image_attn = assemble(meta, back, gg_dp[1:], image_local)
    text_attn = jnp.zeros((slot_local, inner_width), bf16)
    own_usable = part(slot_source[0] < caption_len[0], seq, slot_local, 0)
    for k in range(G):
        rows = jnp.where(own_usable[:, None], back[k][image_local:], jnp.zeros((), bf16))
        text_attn = lax.dynamic_update_slice_in_dim(text_attn, rows, (z ^ k) * gw, 1)

    pieces = [image_attn] + [to_dp(image_attn, k) for k in range(1, n_dp)]
    image_out, d_attn, term, *sent = project(
        meta, image_attn, out_weight, gate, d_out[0], G, OC, place
    )
    for j in range(1, OC):
        pieces += [to_oc(sent[j - 1], j)] + [to_oc(p, j) for p in pieces[1:n_dp]]
    R = model_width // (n_dp * n_seq)
    gate_width = model_width // n_seq
    own, *blocks = grad_product(lefts, pieces, term)
    got = [to_z(x, 1) for x in blocks[4:]]
    pairs = [pair_sum(blocks[2], got[0], 0), pair_sum(blocks[3], got[1], gate_width)]
    far = [to_z(x, 2) for x in pairs]
    near = [to_z(x, 1) for x in blocks[:2]]
    grad_wo, grad_gate = final_sum(own, far, near, R, inner_width, gate_width)
    return (image_out[None], text_attn[None], d_attn[None], grad_wo, grad_gate)


def solution(mesh):
    in_specs = (
        P("dp", None, "seq"),
        P("seq"),
        P("seq", None),
        P("dp"),
        P("dp", None),
        P(),
        P(),
        P("dp", "seq", None),
        P("dp", "seq", None),
        P("dp", "seq", None),
        P(),
        P("dp", None),
        P("dp", "seq", None),
    )
    out_specs = (
        P("dp", "seq", None),
        P("dp", "seq", None),
        P("dp", "seq", None),
        P(("dp", "seq"), None),
        P("dp", "seq"),
    )
    return jax.shard_map(
        on_device, mesh=mesh, in_specs=in_specs, out_specs=out_specs, check_vma=False
    )
```

```python
import math
import functools
import jax
import jax.numpy as jnp
from jax import lax
from jax.experimental import pallas as pl
from jax.experimental.pallas import tpu as pltpu
from jax.sharding import PartitionSpec as P

DT5 = 4096
CORES = 2
GROUPS = 4

eps_norm = 1e-06
f32 = jnp.float32
bf16 = jnp.bfloat16
EXTRA = 16


VMEM = pl.BlockSpec(memory_space=pltpu.VMEM)
SMEM = pl.BlockSpec(memory_space=pltpu.SMEM)
ANY = pl.BlockSpec(memory_space=pl.ANY)


def params(mib=16):
    return pltpu.CompilerParams(vmem_limit_bytes=int(mib * 1024 * 1024))


def cost(flops, bytes_accessed, transcendentals=0):
    return pl.CostEstimate(
        flops=flops, bytes_accessed=bytes_accessed, transcendentals=transcendentals
    )


def split_tail(squares, width):
    high = squares.astype(bf16).astype(f32)
    low = squares - high
    lane = lax.broadcasted_iota(jnp.int32, (squares.shape[0], width), 1)
    return jnp.where(lane == 0, high, jnp.where(lane == 1, low, 0.0))


def joined(tail):
    return tail[:, 0:1] + tail[:, 1:2]


def text_kernel(
    groups, heads, place_of, meta_ref, len_ref, src_ref, states_ref, gain_ref, qg_ref, kg_ref,
    k_ref, v_ref, q_ref, w_ref, own_ref, *refs
):
    packed, refs = refs[:groups], refs[groups:]
    msgs, (w_all, loaded, stage, w_sems, in_sems, out_sems) = refs[:-6], refs[-6:]
    size = own_ref.shape[2]
    rows = (own_ref.shape[1] - EXTRA) // (3 * heads + 1)
    width = heads * size
    slots = states_ref.shape[0]
    slot_local = rows // groups
    copies = []
    block = w_all.shape[0] // w_sems.shape[0]
    for i in range(w_sems.shape[0]):
        part = pl.ds(i * block, block)
        copies.append(pltpu.make_async_copy(w_ref.at[part], w_all.at[part], w_sems.at[i]))
        copies[-1].start()
    loads = []
    for i, ref in enumerate((k_ref, v_ref, q_ref)):
        loads.append(pltpu.make_async_copy(ref, loaded.at[i], in_sems.at[i]))
        loads[-1].start()

    def slot_at(row):
        z_at = (row % rows) // slot_local
        return place_of(meta_ref[1] ^ (row // rows), z_at) * slot_local + row % slot_local

    iota = functools.partial(lax.broadcasted_iota, jnp.int32, (slots, slots))
    sources = src_ref[...].astype(f32)
    chosen = (iota(1) == slot_at(iota(0))).astype(f32)
    source_col = jnp.sum(chosen * sources, axis=1, keepdims=True)
    pick = (iota(1).astype(f32) == source_col).astype(bf16)
    chosen_t = (iota(0) == slot_at(iota(1))).astype(bf16)
    source_row = jnp.dot(sources.astype(bf16), chosen_t, preferred_element_type=f32)
    bias = jnp.where(source_row < len_ref[0].astype(f32), 0.0, -1e30)
    end = own_ref.shape[1] - EXTRA
    own_ref[0, end:, :] = jnp.zeros((EXTRA, size), f32)
    own_ref[0, end : end + 1, :] = qg_ref[...]
    own_ref[0, end + 1 : end + 2, :] = kg_ref[...]
    own_ref[0, end + 2 : end + 3, :slots] = bias

    picked = jnp.dot(pick, states_ref[...], preferred_element_type=f32)
    scaled = (picked * gain_ref[...]).astype(bf16)
    tail = split_tail(jnp.sum(picked * picked, axis=1, keepdims=True), size)
    for copy in loads:
        copy.wait()
    local = loaded.shape[1]
    stores = []
    for g in range(groups):
        for i in range(3):
            for head in range(heads):
                at = ((meta_ref[0] ^ g) * heads + head) * size
                to = (i * heads + head) * local
                stage[g, to : to + local, :] = loaded[i, :, pl.ds(pl.multiple_of(at, 128), size)]
        stores.append(pltpu.make_async_copy(stage.at[g], packed[g], out_sems.at[g]))
        stores[-1].start()
    for copy in copies:
        copy.wait()
    for g in range(groups):
        for i in range(3):
            at = (i * groups + (meta_ref[0] ^ g)) * width
            columns = pl.ds(pl.multiple_of(at, 128), width)
            got = jnp.dot(scaled, w_all[:, columns], preferred_element_type=f32)
            for head in range(heads):
                part = got[:, head * size : (head + 1) * size]
                to = slice((i * heads + head) * rows, (i * heads + head + 1) * rows)
                own_ref[g, to, :] = part[:rows]
                for j, msg in enumerate(msgs):
                    msg[g, to, :] = part[(j + 1) * rows : (j + 2) * rows].astype(bf16)
        own_ref[g, 3 * heads * rows : end, :] = tail[:rows]
        for j, msg in enumerate(msgs):
            msg[g, 3 * heads * rows :, :] = tail[(j + 1) * rows : (j + 2) * rows].astype(bf16)
    for copy in stores:
        copy.wait()


def text_project(
    meta, length, sources, states, gain, query_gain, key_gain, keys, values, queries, text_proj,
    groups, parts, place_of
):
    slots, depth = states.shape
    size = query_gain.shape[1]
    heads = text_proj.shape[1] // (3 * groups * size)
    text_rows = (3 * heads + 1) * slots // parts
    shapes = [jax.ShapeDtypeStruct((groups, text_rows + EXTRA, size), f32)]
    shapes += [jax.ShapeDtypeStruct((3 * heads * keys.shape[0], size), bf16)] * groups
    shapes += [jax.ShapeDtypeStruct((groups, text_rows, size), bf16)] * (parts - 1)
    return pl.pallas_call(
        functools.partial(text_kernel, groups, heads, place_of),
        out_shape=shapes,
        in_specs=[SMEM, SMEM] + [VMEM] * 5 + [ANY] * 4,
        out_specs=[VMEM] + [ANY] * groups + [VMEM] * (parts - 1),
        scratch_shapes=[
            pltpu.VMEM(text_proj.shape, bf16),
            pltpu.VMEM((3,) + keys.shape, bf16),
            pltpu.VMEM((groups, 3 * heads * keys.shape[0], size), bf16),
            pltpu.SemaphoreType.DMA((4,)),
            pltpu.SemaphoreType.DMA((3,)),
            pltpu.SemaphoreType.DMA((groups,)),
        ],
        compiler_params=params(60),
        cost_estimate=cost(
            2 * slots * depth * text_proj.shape[1], 2 * depth * text_proj.shape[1]
        ),
    )(
        meta, length, sources, states, gain, query_gain, key_gain, keys, values, queries, text_proj
    )


def text_sum_kernel(n_got, tail_rows, own_ref, *refs):
    got, (keep_ref, send_ref) = refs[:n_got], refs[n_got:]
    groups, text_rows, size = got[0].shape
    for g in range(groups):
        total = own_ref[g, :text_rows, :]
        for ref in got:
            total = total + ref[g].astype(f32)
        end = text_rows - tail_rows
        tail = split_tail(joined(total[end:]), size)
        if g % 2 == 0:
            keep_ref[g // 2, :end, :] = total[:end]
            keep_ref[g // 2, end:text_rows, :] = tail
            keep_ref[g // 2, text_rows:, :] = own_ref[g, text_rows:, :]
        else:
            send_ref[g // 2, :end, :] = total[:end].astype(bf16)
            send_ref[g // 2, end:, :] = tail.astype(bf16)


def text_sum(own, got, tail_rows):
    groups, rows, size = own.shape
    return pl.pallas_call(
        functools.partial(text_sum_kernel, len(got), tail_rows),
        out_shape=[
            jax.ShapeDtypeStruct((groups // 2, rows, size), f32),
            jax.ShapeDtypeStruct((groups // 2, rows - EXTRA, size), bf16),
        ],
        in_specs=[VMEM] * (1 + len(got)),
        out_specs=[VMEM] * 2,
        compiler_params=params(),
        cost_estimate=cost(0, 8 * groups * rows * size),
    )(own, *got)


def block_kernel(features, heads, n_pieces, own_ref, got_ref, *refs):
    pieces, out_ref = refs[:n_pieces], refs[-1]
    near_rows = pieces[0].shape[0]
    kv_rows = near_rows // 3 * 2
    out_ref[:near_rows, :] = pieces[0][...]
    for k, ref in enumerate(pieces[1:]):
        at = near_rows + k * kv_rows
        out_ref[at : at + kv_rows, :] = ref[:kv_rows, :]
    size = own_ref.shape[2]
    text_rows = got_ref.shape[1]
    rows = text_rows // (3 * heads + 1)
    total = own_ref[0, :text_rows, :] + got_ref[0].astype(f32)
    rate = lax.rsqrt(joined(total[3 * heads * rows :]) / features + eps_norm)
    start = near_rows + (n_pieces - 1) * kv_rows
    for i in range(3):
        for head in range(heads):
            at = (i * heads + head) * rows
            x = total[at : at + rows] * rate
            if i < 2:
                mean = jnp.sum(x * x, axis=1, keepdims=True) / size
                gain = own_ref[0, text_rows + i : text_rows + i + 1, :]
                x = x * lax.rsqrt(mean + eps_norm) * gain
            out_ref[start + at : start + at + rows, :] = x.astype(bf16)
    bias = own_ref[0, text_rows + 2 : text_rows + 3, :]
    start = start + 3 * heads * rows
    out_ref[start:, :] = jnp.broadcast_to(bias, (EXTRA, size)).astype(bf16)


def block_of(own, got, after, pieces, features, heads):
    rows, size = own.shape[1:]
    total = (rows - EXTRA) // (3 * heads + 1) * 3 * heads + EXTRA
    total += pieces[0].shape[0] // 3 * (2 * len(pieces) + 1)
    return pl.pallas_call(
        functools.partial(block_kernel, features, heads, len(pieces)),
        out_shape=jax.ShapeDtypeStruct((total, size), bf16),
        in_specs=[VMEM] * (2 + len(pieces)) + [ANY] * len(after),
        out_specs=VMEM,
        compiler_params=params(),
        cost_estimate=cost(0, 4 * total * size),
    )(own, got, *pieces, *after)


def attention_kernel(n_far, n_cores, heads, rows, text_rows, *refs):
    far, refs = refs[:n_far], refs[n_far:]
    blocks, refs = refs[:n_cores], refs[n_cores:]
    out_refs, tout_ref = refs[:-1], refs[-1]
    size = blocks[0].shape[1]
    factor = size ** (-0.5) * math.log2(math.e)
    nt = (((1,), (1,)), ((), ()))
    kv_rows = 2 * heads * rows
    near_rows = 3 * heads * rows
    starts = [0] + [near_rows + k * kv_rows for k in range(n_far)]
    text = near_rows + n_far * kv_rows
    end = text + 3 * heads * text_rows
    bias = blocks[0][end : end + EXTRA, :][:1, : n_cores * text_rows].astype(f32)

    def with_ones(values):
        return jnp.concatenate([values, jnp.ones(values.shape, bf16)], axis=1)

    for head in range(heads):
        kv, tkv = [], []
        for i in range(2):
            at = (i * heads + head) * rows
            image = [b[start + at : start + at + rows, :] for b in blocks for start in starts]
            text_at = text + ((i + 1) * heads + head) * text_rows
            kv.append(jnp.concatenate(image, axis=0))
            tkv.append(jnp.concatenate([b[text_at : text_at + text_rows, :] for b in blocks], axis=0))
        keys, values = kv[0], with_ones(kv[1])
        tkeys, tvalues = tkv[0], with_ones(tkv[1])
        cols = slice(head * size, (head + 1) * size)
        q_at = (2 * heads + head) * rows
        work = [(ref[q_at : q_at + rows, :], out) for ref, out in zip((blocks[0],) + tuple(far), out_refs)]
        tq_at = text + head * text_rows
        work.append((blocks[0][tq_at : tq_at + text_rows, :], tout_ref))
        for q, out_ref in work:
            s_img = lax.dot_general(q, keys, nt, preferred_element_type=f32)
            s_txt = lax.dot_general(q, tkeys, nt, preferred_element_type=f32) + bias
            top = jnp.maximum(
                jnp.max(s_img, axis=1, keepdims=True), jnp.max(s_txt, axis=1, keepdims=True)
            )
            p_img = jnp.exp2((s_img - top) * factor).astype(bf16)
            p_txt = jnp.exp2((s_txt - top) * factor).astype(bf16)
            acc = jnp.dot(p_img, values, preferred_element_type=f32)
            acc = acc + jnp.dot(p_txt, tvalues, preferred_element_type=f32)
            out_ref[:, cols] = (acc[:, :size] / acc[:, size:]).astype(bf16)


def attention(far, blocks, heads, rows, text_rows):
    size = blocks[0].shape[1]
    n = 1 + len(far)
    queries = n * rows + text_rows
    keys = len(blocks) * queries
    shapes = [jax.ShapeDtypeStruct((rows, heads * size), bf16)] * n
    shapes += [jax.ShapeDtypeStruct((text_rows, heads * size), bf16)]
    return pl.pallas_call(
        functools.partial(attention_kernel, len(far), len(blocks), heads, rows, text_rows),
        out_shape=shapes,
        in_specs=[VMEM] * (len(far) + len(blocks)),
        out_specs=[VMEM] * len(shapes),
        compiler_params=params(),
        cost_estimate=cost(
            4 * queries * keys * heads * size,
            4 * (queries + keys) * heads * size,
            queries * keys * heads,
        ),
    )(*far, *blocks)


def assemble_kernel(places, meta_ref, *refs):
    pieces, out_ref = refs[: len(places)], refs[-1]
    rows, width = out_ref.shape[0], pieces[0].shape[1]
    for k, piece in zip(places, pieces):
        at = pl.multiple_of((meta_ref[0] ^ k) * width, 128)
        out_ref[:, pl.ds(at, width)] = piece[:rows, :]


def assemble(meta, pieces, places, after, rows):
    groups, width = len(pieces), pieces[0].shape[1]
    return pl.pallas_call(
        functools.partial(assemble_kernel, tuple(places)),
        out_shape=jax.ShapeDtypeStruct((rows, groups * width), bf16),
        in_specs=[SMEM] + [VMEM] * groups + [ANY] * len(after),
        out_specs=VMEM,
        compiler_params=params(),
        cost_estimate=cost(0, 4 * rows * groups * width),
    )(meta, *pieces, *after)


def gated_kernel(groups, parts, place_of, meta_ref, gate_ref, d_out_ref, *refs):
    msgs, turned = refs[:-1], refs[-1]
    gated = (gate_ref[...] * d_out_ref[...].astype(f32)).astype(bf16)
    turned[...] = gated.astype(f32).T
    rows = msgs[0].shape[2]
    z, oc, dp = meta_ref[0], meta_ref[1], meta_ref[2]
    for k, msg in enumerate(msgs):
        for j in range(parts):
            for g in range(groups):
                at = (dp ^ k) * (groups * parts) + place_of(oc ^ j, z ^ g)
                msg[j, g] = turned[pl.ds(pl.multiple_of(at * rows, 8), rows), :].astype(bf16)


def gated_parts(meta, gate, d_out, n_dp, groups, parts, place_of):
    local, model = d_out.shape
    rows = model // (n_dp * groups * parts)
    return pl.pallas_call(
        functools.partial(gated_kernel, groups, parts, place_of),
        out_shape=[jax.ShapeDtypeStruct((parts, groups, rows, local), bf16)] * n_dp,
        in_specs=[SMEM, VMEM, VMEM],
        out_specs=[VMEM] * n_dp,
        scratch_shapes=[pltpu.VMEM((model, local), f32)],
        compiler_params=params(60),
        cost_estimate=cost(0, 4 * local * model),
    )(meta, gate, d_out)


def gather_kernel(n_dp, *refs):
    pieces, outs = refs[:n_dp], refs[n_dp:]
    for j, out in enumerate(outs):
        for k, piece in enumerate(pieces):
            out[k] = piece[j + 1]


def gather_parts(pieces):
    parts = pieces[0].shape[0]
    shape = (len(pieces),) + pieces[0].shape[1:]
    return pl.pallas_call(
        functools.partial(gather_kernel, len(pieces)),
        out_shape=[jax.ShapeDtypeStruct(shape, bf16)] * (parts - 1),
        in_specs=[VMEM] * len(pieces),
        out_specs=[VMEM] * (parts - 1),
        compiler_params=params(),
        cost_estimate=cost(0, 4 * math.prod(shape) * (parts - 1)),
    )(*pieces)


def project_kernel(
    groups, parts, place_of, meta_ref, attn_ref, w_ref, gate_ref, d_out_ref, out_ref, d_attn_ref,
    term_ref, *refs
):
    sent, by_place = refs[:-1], refs[-1]
    rows = attn_ref.shape[0]
    block = 512
    sums = []
    for at in range(0, w_ref.shape[0], block):
        cols = slice(at, at + block)
        got = lax.dot_general(
            attn_ref[...], w_ref[cols, :], (((1,), (1,)), ((), ())), preferred_element_type=f32
        )
        out_ref[:, cols] = (got * gate_ref[:, cols]).astype(bf16)
        sums.append(jnp.sum(got * d_out_ref[:, cols].astype(f32), axis=0, keepdims=True))
    total = jnp.zeros(d_attn_ref.shape, f32)
    for at in range(0, w_ref.shape[0], block):
        cols = slice(at, at + block)
        gated = (gate_ref[:, cols] * d_out_ref[:, cols].astype(f32)).astype(bf16)
        total = total + jnp.dot(gated, w_ref[cols, :], preferred_element_type=f32)
    d_attn_ref[...] = total.astype(bf16)
    sums = jnp.concatenate(sums, axis=1)
    places, width = by_place.shape
    for s in range(places):
        by_place[s : s + 1, :] = sums[:, s * width : (s + 1) * width]
    for g in range(groups):
        at = place_of(meta_ref[1], meta_ref[0] ^ g)
        term_ref[g : g + 1, :] = by_place[pl.ds(at, 1), :]
    for j, out in enumerate(sent):
        out[:rows, :] = attn_ref[...]
        line = [
            by_place[pl.ds(place_of(meta_ref[1] ^ (j + 1), meta_ref[0] ^ g), 1), :]
            for g in range(groups)
        ]
        line = jnp.concatenate(line, axis=1)
        line = jnp.concatenate(
            [line, jnp.zeros((1, attn_ref.shape[1] - groups * width), f32)], axis=1
        ) if attn_ref.shape[1] > groups * width else line
        high = line.astype(bf16).astype(f32)
        lines = [high, line - high, jnp.zeros((EXTRA - 2, line.shape[1]), f32)]
        out[rows:, :] = jnp.concatenate(lines, axis=0).astype(bf16)


def project(meta, attn, out_weight, gate, d_out, groups, parts, place_of):
    rows, inner = attn.shape
    model = out_weight.shape[0]
    width = model // (groups * parts)
    shapes = [jax.ShapeDtypeStruct((rows, model), bf16), jax.ShapeDtypeStruct((rows, inner), bf16)]
    shapes += [jax.ShapeDtypeStruct((groups, width), f32)]
    shapes += [jax.ShapeDtypeStruct((rows + EXTRA, inner), bf16)] * (parts - 1)
    return pl.pallas_call(
        functools.partial(project_kernel, groups, parts, place_of),
        out_shape=shapes,
        in_specs=[SMEM, VMEM, VMEM, VMEM, VMEM],
        out_specs=[VMEM] * (2 + parts),
        scratch_shapes=[pltpu.VMEM((groups * parts, width), f32)],
        compiler_params=params(),
        cost_estimate=cost(4 * rows * inner * model, 2 * inner * model),
    )(meta, attn, out_weight, gate, d_out)


def split_gate(gate, size):
    short = -gate.shape[1] % size
    if short:
        gate = jnp.concatenate([gate, jnp.zeros((1, short), f32)], axis=1)
    high = gate.astype(bf16).astype(f32)
    lines = [p[:, at : at + size] for p in (high, gate - high) for at in range(0, gate.shape[1], size)]
    return jnp.concatenate(lines + [jnp.zeros((EXTRA - len(lines), size), f32)], axis=0)


def joined_gate(lines, width):
    n = -(-width // lines.shape[1])
    both = lines[:n] + lines[n : 2 * n]
    return jnp.concatenate([both[i : i + 1] for i in range(n)], axis=1)[:, :width]


def grad_kernel(n_left, n_pieces, *refs):
    lefts, refs = refs[:n_left], refs[n_left:]
    pieces, refs = refs[:n_pieces], refs[n_pieces:]
    term_ref, outs = refs[0], refs[1:]
    groups, rows, depth = lefts[0].shape[1:]
    width = pieces[0].shape[1]
    size = outs[0].shape[1]
    left = []
    for ref in lefts:
        left += [ref[i].reshape(groups * rows, depth) for i in range(ref.shape[0])]
    left = jnp.concatenate(left, axis=1)
    half = outs[1].shape[0]
    homes = [((outs[0], 0),)]
    homes += [((outs[2 * g - 1], 0), (outs[2 * g], half)) for g in range(1, groups)]

    def put(g, at, value):
        out, start = homes[g][-1] if at >= half else homes[g][0]
        out[at - start : at - start + value.shape[0], :] = value.astype(out.dtype)

    block = 256
    for start in range(0, width, block):
        right = jnp.concatenate([p[:depth, start : start + block] for p in pieces], axis=0)
        got = jnp.dot(left, right, preferred_element_type=f32)
        for g in range(groups):
            for at in range(0, block, size):
                put(g, (start + at) // size * rows, got[g * rows : (g + 1) * rows, at : at + size])
    term = term_ref[...]
    each = term.shape[1]
    for p in pieces:
        if p.shape[0] > depth:
            lines = p[depth:, :].astype(f32)
            line = lines[0:1, :] + lines[1:2, :]
            term = term + jnp.concatenate(
                [line[:, g * each : (g + 1) * each] for g in range(groups)], axis=0
            )
    for g in range(groups):
        put(g, width // size * rows, split_gate(term[g : g + 1], size))


def grad_product(lefts, pieces, term):
    groups, rows, depth = lefts[0].shape[1:]
    width = pieces[0].shape[1]
    size = 128
    total = groups * rows
    depth = depth * len(pieces)
    full = width // size * rows + EXTRA
    half = width // size // 2 * rows
    shapes = [(full, f32)]
    for kind in (bf16, f32, bf16):
        shapes += [(half, kind), (full - half, kind)]
    return pl.pallas_call(
        functools.partial(grad_kernel, len(lefts), len(pieces)),
        out_shape=[jax.ShapeDtypeStruct((n, size), kind) for n, kind in shapes],
        in_specs=[VMEM] * (len(lefts) + len(pieces) + 1),
        out_specs=[VMEM] * len(shapes),
        compiler_params=params(),
        cost_estimate=cost(
            2 * total * depth * width, 2 * (total * depth + depth * width + total * width)
        ),
    )(*lefts, *pieces, term)


def pair_kernel(gate_width, n_through, own_ref, got_ref, *refs):
    out_ref = refs[n_through]
    for ref, out in zip(refs[:n_through], refs[n_through + 1 :]):
        out[...] = ref[...]
    total = own_ref[...] + got_ref[...].astype(f32)
    if not gate_width:
        out_ref[...] = total.astype(bf16)
    else:
        end = total.shape[0] - EXTRA
        out_ref[:end, :] = total[:end].astype(bf16)
        gate = joined_gate(total[end:], gate_width)
        out_ref[end:, :] = split_gate(gate, total.shape[1]).astype(bf16)


def pair_sum(own, got, gate_width, through):
    return pl.pallas_call(
        functools.partial(pair_kernel, gate_width, len(through)),
        out_shape=[jax.ShapeDtypeStruct(x.shape, bf16) for x in [got] + through],
        in_specs=[VMEM] * (2 + len(through)),
        out_specs=[VMEM] * (1 + len(through)),
        compiler_params=params(),
        cost_estimate=cost(0, 8 * own.size),
    )(own, got, *through)


def final_kernel(own_ref, far_low, far_high, near_low, near_high, out_ref, gate_ref):
    size = own_ref.shape[1]
    rows = out_ref.shape[0]
    half = far_low.shape[0]

    def total(at, count):
        refs, start = ((far_high, near_high), half) if at >= half else ((far_low, near_low), 0)
        got = own_ref[at : at + count, :]
        for ref in refs:
            got = got + ref[at - start : at - start + count, :].astype(f32)
        return got

    for i in range(out_ref.shape[1] // size):
        out_ref[:, i * size : (i + 1) * size] = total(i * rows, rows)
    gate_ref[...] = joined_gate(total(own_ref.shape[0] - EXTRA, EXTRA), gate_ref.shape[1])


def final_sum(own, far, near, rows, width, gate_width):
    return pl.pallas_call(
        final_kernel,
        out_shape=[
            jax.ShapeDtypeStruct((rows, width), f32),
            jax.ShapeDtypeStruct((1, gate_width), f32),
        ],
        in_specs=[VMEM] * 5,
        out_specs=[VMEM] * 2,
        compiler_params=params(),
        cost_estimate=cost(0, 8 * rows * width),
    )(own, *far, *near)


def on_device(
    caption_states,
    caption_gain,
    text_proj,
    caption_len,
    slot_source,
    query_gain,
    key_gain,
    image_q,
    image_k,
    image_v,
    out_weight,
    gate,
    d_out,
):
    n_dp = lax.axis_size("dp")
    n_seq = lax.axis_size("seq")
    G, C = GROUPS, CORES
    O = n_seq // (G * C)
    OC = O * C
    dp = lax.axis_index("dp")
    seq = lax.axis_index("seq")
    z = (seq // C) % G
    oc = (seq // (G * C)) * C + seq % C

    def place(oc_at, z_at):
        return ((oc_at // C) * G + z_at) * C + oc_at % C

    def to_z(x, k):
        perm = [(place(a, b), place(a, b ^ k)) for a in range(OC) for b in range(G)]
        return lax.ppermute(x, "seq", perm)

    def to_oc(x, j):
        perm = [(place(a, b), place(a ^ j, b)) for a in range(OC) for b in range(G)]
        return lax.ppermute(x, "seq", perm)

    def to_dp(x, k):
        return lax.ppermute(x, "dp", [(a, a ^ k) for a in range(n_dp)])

    def part(x, index, size, axis):
        return lax.dynamic_slice_in_dim(x, index * size, size, axis)

    slot_total = slot_source.shape[1]
    slot_local = slot_total // n_seq
    image_local = image_q.shape[1]
    inner_width = image_q.shape[2]
    model_width = out_weight.shape[0]
    head_size = query_gain.shape[0]
    gw = inner_width // G
    order = [2, 3, 1]
    meta = jnp.stack([z, oc, dp]).astype(jnp.int32)

    heads = gw // head_size
    text_rows = G * slot_local
    own, *rest = text_project(
        meta, caption_len, slot_source, caption_states[0], caption_gain[None],
        query_gain[None], key_gain[None], image_k[0], image_v[0], image_q[0], text_proj,
        G, OC, place,
    )
    packed, sent = rest[:G], rest[G:]
    images = {0: packed[0]}
    for k in order:
        images[k] = to_z(packed[k], k)
    images = [images[k] for k in [0] + order]
    got = [to_oc(x, j + 1) for j, x in enumerate(sent)]
    own, sent = text_sum(own, got, text_rows)
    own, sent = text_sum(own, [to_z(sent, 1)], text_rows)
    got = to_z(sent, 2)

    gg = gated_parts(meta, gate, d_out[0], n_dp, G, OC, place)
    gg_dp = [gg[0], to_dp(gg[1], 1)]
    block = block_of(own, got, gg_dp[1:], images, DT5, heads)
    blocks = [block] + [to_oc(block, j) for j in range(1, OC)]
    *outs, text_out = attention(images[1:], blocks, heads, image_local, text_rows)
    outs = dict(zip([0] + order, outs))

    back = {}
    for k in order + [0]:
        rows = jnp.concatenate([outs[k], part(text_out, z ^ k, slot_local, 0)], axis=0)
        back[k] = to_z(rows, k) if k else rows
    back = [back[k] for k in order + [0]]
    gg_dp += [to_dp(gg[k], k) for k in range(2, n_dp)]
    lefts = [g[:1] for g in gg_dp]
    lefts += [to_oc(g, j + 1) for j, g in enumerate(gather_parts(gg_dp))]
    image_attn = assemble(meta, back, order + [0], gg_dp[1:], image_local)
    text_attn = jnp.zeros((slot_local, inner_width), bf16)
    own_usable = part(slot_source[0] < caption_len[0], seq, slot_local, 0)
    for k, got in zip(order + [0], back):
        rows = jnp.where(own_usable[:, None], got[image_local:], jnp.zeros((), bf16))
        text_attn = lax.dynamic_update_slice_in_dim(text_attn, rows, (z ^ k) * gw, 1)

    pieces = [image_attn] + [to_dp(image_attn, k) for k in range(1, n_dp)]
    image_out, d_attn, term, *sent = project(
        meta, image_attn, out_weight, gate, d_out[0], G, OC, place
    )
    for j in range(1, OC):
        pieces += [to_oc(sent[j - 1], j)] + [to_oc(p, j) for p in pieces[1:n_dp]]
    R = model_width // (n_dp * n_seq)
    gate_width = model_width // n_seq
    own, *blocks = grad_product(lefts, pieces, term)
    got = [to_z(x, 1) for x in blocks[4:]]
    (low,) = pair_sum(blocks[2], got[0], 0, [])
    high, *near = pair_sum(blocks[3], got[1], gate_width, blocks[:2])
    far = [to_z(x, 2) for x in (low, high)]
    near = [to_z(x, 1) for x in near]
    grad_wo, grad_gate = final_sum(own, far, near, R, inner_width, gate_width)
    return (image_out[None], text_attn[None], d_attn[None], grad_wo, grad_gate)


def solution(mesh):
    in_specs = (
        P("dp", None, "seq"),
        P("seq"),
        P("seq", None),
        P("dp"),
        P("dp", None),
        P(),
        P(),
        P("dp", "seq", None),
        P("dp", "seq", None),
        P("dp", "seq", None),
        P(),
        P("dp", None),
        P("dp", "seq", None),
    )
    out_specs = (
        P("dp", "seq", None),
        P("dp", "seq", None),
        P("dp", "seq", None),
        P(("dp", "seq"), None),
        P("dp", "seq"),
    )
    return jax.shard_map(
        on_device, mesh=mesh, in_specs=in_specs, out_specs=out_specs, check_vma=False
    )
```

```python
import math
import functools
import jax
import jax.numpy as jnp
from jax import lax
from jax.experimental import pallas as pl
from jax.experimental.pallas import tpu as pltpu
from jax.sharding import PartitionSpec as P

DT5 = 4096
CORES = 2
GROUPS = 4

eps_norm = 1e-06
f32 = jnp.float32
bf16 = jnp.bfloat16
EXTRA = 16


VMEM = pl.BlockSpec(memory_space=pltpu.VMEM)
SMEM = pl.BlockSpec(memory_space=pltpu.SMEM)
ANY = pl.BlockSpec(memory_space=pl.ANY)


def params(mib=16):
    return pltpu.CompilerParams(vmem_limit_bytes=int(mib * 1024 * 1024))


def cost(flops, bytes_accessed, transcendentals=0):
    return pl.CostEstimate(
        flops=flops, bytes_accessed=bytes_accessed, transcendentals=transcendentals
    )


def split_tail(squares, width):
    high = squares.astype(bf16).astype(f32)
    low = squares - high
    lane = lax.broadcasted_iota(jnp.int32, (squares.shape[0], width), 1)
    return jnp.where(lane == 0, high, jnp.where(lane == 1, low, 0.0))


def joined(tail):
    return tail[:, 0:1] + tail[:, 1:2]


def text_kernel(
    groups, heads, place_of, where, len_ref, src_ref, states_ref, gain_ref, qg_ref, kg_ref,
    k_ref, v_ref, q_ref, w_ref, own_ref, *refs
):
    meta_ref = where()
    packed, refs = refs[:groups], refs[groups:]
    msgs, (w_all, loaded, stage, w_sems, in_sems, out_sems) = refs[:-6], refs[-6:]
    size = own_ref.shape[2]
    rows = (own_ref.shape[1] - EXTRA) // (3 * heads + 1)
    width = heads * size
    slots = states_ref.shape[0]
    slot_local = rows // groups
    copies = []
    block = w_all.shape[0] // w_sems.shape[0]
    for i in range(w_sems.shape[0]):
        part = pl.ds(i * block, block)
        copies.append(pltpu.make_async_copy(w_ref.at[part], w_all.at[part], w_sems.at[i]))
        copies[-1].start()
    loads = []
    for i, ref in enumerate((k_ref, v_ref, q_ref)):
        loads.append(pltpu.make_async_copy(ref, loaded.at[i], in_sems.at[i]))
        loads[-1].start()

    def slot_at(row):
        z_at = (row % rows) // slot_local
        return place_of(meta_ref[1] ^ (row // rows), z_at) * slot_local + row % slot_local

    iota = functools.partial(lax.broadcasted_iota, jnp.int32, (slots, slots))
    sources = src_ref[...].astype(f32)
    chosen = (iota(1) == slot_at(iota(0))).astype(f32)
    source_col = jnp.sum(chosen * sources, axis=1, keepdims=True)
    pick = (iota(1).astype(f32) == source_col).astype(bf16)
    chosen_t = (iota(0) == slot_at(iota(1))).astype(bf16)
    source_row = jnp.dot(sources.astype(bf16), chosen_t, preferred_element_type=f32)
    bias = jnp.where(source_row < len_ref[0].astype(f32), 0.0, -1e30)
    end = own_ref.shape[1] - EXTRA
    own_ref[0, end:, :] = jnp.zeros((EXTRA, size), f32)
    own_ref[0, end : end + 1, :] = qg_ref[...]
    own_ref[0, end + 1 : end + 2, :] = kg_ref[...]
    own_ref[0, end + 2 : end + 3, :slots] = bias

    picked = jnp.dot(pick, states_ref[...], preferred_element_type=f32)
    scaled = (picked * gain_ref[...]).astype(bf16)
    tail = split_tail(jnp.sum(picked * picked, axis=1, keepdims=True), size)
    for copy in loads:
        copy.wait()
    local = loaded.shape[1]
    stores = []
    for g in range(groups):
        for i in range(3):
            for head in range(heads):
                at = ((meta_ref[0] ^ g) * heads + head) * size
                to = (i * heads + head) * local
                stage[g, to : to + local, :] = loaded[i, :, pl.ds(pl.multiple_of(at, 128), size)]
        stores.append(pltpu.make_async_copy(stage.at[g], packed[g], out_sems.at[g]))
        stores[-1].start()
    for copy in copies:
        copy.wait()
    for g in range(groups):
        for i in range(3):
            at = (i * groups + (meta_ref[0] ^ g)) * width
            columns = pl.ds(pl.multiple_of(at, 128), width)
            got = jnp.dot(scaled, w_all[:, columns], preferred_element_type=f32)
            for head in range(heads):
                part = got[:, head * size : (head + 1) * size]
                to = slice((i * heads + head) * rows, (i * heads + head + 1) * rows)
                own_ref[g, to, :] = part[:rows]
                for j, msg in enumerate(msgs):
                    msg[g, to, :] = part[(j + 1) * rows : (j + 2) * rows].astype(bf16)
        own_ref[g, 3 * heads * rows : end, :] = tail[:rows]
        for j, msg in enumerate(msgs):
            msg[g, 3 * heads * rows :, :] = tail[(j + 1) * rows : (j + 2) * rows].astype(bf16)
    for copy in stores:
        copy.wait()


def text_project(
    length, sources, states, gain, query_gain, key_gain, keys, values, queries, text_proj,
    groups, parts, place_of, where
):
    slots, depth = states.shape
    size = query_gain.shape[1]
    heads = text_proj.shape[1] // (3 * groups * size)
    text_rows = (3 * heads + 1) * slots // parts
    shapes = [jax.ShapeDtypeStruct((groups, text_rows + EXTRA, size), f32)]
    shapes += [jax.ShapeDtypeStruct((3 * heads * keys.shape[0], size), bf16)] * groups
    shapes += [jax.ShapeDtypeStruct((groups, text_rows, size), bf16)] * (parts - 1)
    return pl.pallas_call(
        functools.partial(text_kernel, groups, heads, place_of, where),
        out_shape=shapes,
        in_specs=[SMEM] + [VMEM] * 5 + [ANY] * 4,
        out_specs=[VMEM] + [ANY] * groups + [VMEM] * (parts - 1),
        scratch_shapes=[
            pltpu.VMEM(text_proj.shape, bf16),
            pltpu.VMEM((3,) + keys.shape, bf16),
            pltpu.VMEM((groups, 3 * heads * keys.shape[0], size), bf16),
            pltpu.SemaphoreType.DMA((4,)),
            pltpu.SemaphoreType.DMA((3,)),
            pltpu.SemaphoreType.DMA((groups,)),
        ],
        compiler_params=params(60),
        cost_estimate=cost(
            2 * slots * depth * text_proj.shape[1], 2 * depth * text_proj.shape[1]
        ),
    )(
        length, sources, states, gain, query_gain, key_gain, keys, values, queries, text_proj
    )


def text_sum_kernel(n_got, tail_rows, own_ref, *refs):
    got, (keep_ref, send_ref) = refs[:n_got], refs[n_got:]
    groups, text_rows, size = got[0].shape
    for g in range(groups):
        total = own_ref[g, :text_rows, :]
        for ref in got:
            total = total + ref[g].astype(f32)
        end = text_rows - tail_rows
        tail = split_tail(joined(total[end:]), size)
        if g % 2 == 0:
            keep_ref[g // 2, :end, :] = total[:end]
            keep_ref[g // 2, end:text_rows, :] = tail
            keep_ref[g // 2, text_rows:, :] = own_ref[g, text_rows:, :]
        else:
            send_ref[g // 2, :end, :] = total[:end].astype(bf16)
            send_ref[g // 2, end:, :] = tail.astype(bf16)


def text_sum(own, got, tail_rows):
    groups, rows, size = own.shape
    return pl.pallas_call(
        functools.partial(text_sum_kernel, len(got), tail_rows),
        out_shape=[
            jax.ShapeDtypeStruct((groups // 2, rows, size), f32),
            jax.ShapeDtypeStruct((groups // 2, rows - EXTRA, size), bf16),
        ],
        in_specs=[VMEM] * (1 + len(got)),
        out_specs=[VMEM] * 2,
        compiler_params=params(),
        cost_estimate=cost(0, 8 * groups * rows * size),
    )(own, *got)


def block_kernel(features, heads, n_pieces, own_ref, got_ref, *refs):
    pieces, out_ref = refs[:n_pieces], refs[-1]
    near_rows = pieces[0].shape[0]
    kv_rows = near_rows // 3 * 2
    out_ref[:near_rows, :] = pieces[0][...]
    for k, ref in enumerate(pieces[1:]):
        at = near_rows + k * kv_rows
        out_ref[at : at + kv_rows, :] = ref[:kv_rows, :]
    size = own_ref.shape[2]
    text_rows = got_ref.shape[1]
    rows = text_rows // (3 * heads + 1)
    total = own_ref[0, :text_rows, :] + got_ref[0].astype(f32)
    rate = lax.rsqrt(joined(total[3 * heads * rows :]) / features + eps_norm)
    start = near_rows + (n_pieces - 1) * kv_rows
    for i in range(3):
        for head in range(heads):
            at = (i * heads + head) * rows
            x = total[at : at + rows] * rate
            if i < 2:
                mean = jnp.sum(x * x, axis=1, keepdims=True) / size
                gain = own_ref[0, text_rows + i : text_rows + i + 1, :]
                x = x * lax.rsqrt(mean + eps_norm) * gain
            out_ref[start + at : start + at + rows, :] = x.astype(bf16)
    bias = own_ref[0, text_rows + 2 : text_rows + 3, :]
    start = start + 3 * heads * rows
    out_ref[start:, :] = jnp.broadcast_to(bias, (EXTRA, size)).astype(bf16)


def block_of(own, got, after, pieces, features, heads):
    rows, size = own.shape[1:]
    total = (rows - EXTRA) // (3 * heads + 1) * 3 * heads + EXTRA
    total += pieces[0].shape[0] // 3 * (2 * len(pieces) + 1)
    return pl.pallas_call(
        functools.partial(block_kernel, features, heads, len(pieces)),
        out_shape=jax.ShapeDtypeStruct((total, size), bf16),
        in_specs=[VMEM] * (2 + len(pieces)) + [ANY] * len(after),
        out_specs=VMEM,
        compiler_params=params(),
        cost_estimate=cost(0, 4 * total * size),
    )(own, got, *pieces, *after)


def attention_kernel(n_far, n_cores, queries, heads, rows, text_rows, *refs):
    far, refs = refs[: queries[0]], refs[queries[0] :]
    blocks, refs = refs[:n_cores], refs[n_cores + 1 :]
    out_refs, mark_ref = refs[:-1], refs[-1]
    mark_ref[0] = 0
    size = blocks[0].shape[1]
    factor = size ** (-0.5) * math.log2(math.e)
    nt = (((1,), (1,)), ((), ()))
    kv_rows = 2 * heads * rows
    near_rows = 3 * heads * rows
    starts = [0] + [near_rows + k * kv_rows for k in range(n_far)]
    text = near_rows + n_far * kv_rows
    end = text + 3 * heads * text_rows
    bias = blocks[0][end : end + EXTRA, :][:1, : n_cores * text_rows].astype(f32)

    def with_ones(values):
        return jnp.concatenate([values, jnp.ones(values.shape, bf16)], axis=1)

    for head in range(heads):
        kv, tkv = [], []
        for i in range(2):
            at = (i * heads + head) * rows
            image = [b[start + at : start + at + rows, :] for b in blocks for start in starts]
            text_at = text + ((i + 1) * heads + head) * text_rows
            kv.append(jnp.concatenate(image, axis=0))
            tkv.append(jnp.concatenate([b[text_at : text_at + text_rows, :] for b in blocks], axis=0))
        keys, values = kv[0], with_ones(kv[1])
        tkeys, tvalues = tkv[0], with_ones(tkv[1])
        cols = slice(head * size, (head + 1) * size)
        q_at = (2 * heads + head) * rows
        asked = [ref[q_at : q_at + rows, :] for ref in far]
        if queries[1]:
            asked.append(blocks[0][q_at : q_at + rows, :])
        if queries[2]:
            tq_at = text + head * text_rows
            asked.append(blocks[0][tq_at : tq_at + text_rows, :])
        q = jnp.concatenate(asked, axis=0)
        s_img = lax.dot_general(q, keys, nt, preferred_element_type=f32)
        s_txt = lax.dot_general(q, tkeys, nt, preferred_element_type=f32) + bias
        top = jnp.maximum(
            jnp.max(s_img, axis=1, keepdims=True), jnp.max(s_txt, axis=1, keepdims=True)
        )
        p_img = jnp.exp2((s_img - top) * factor).astype(bf16)
        p_txt = jnp.exp2((s_txt - top) * factor).astype(bf16)
        acc = jnp.dot(p_img, values, preferred_element_type=f32)
        acc = acc + jnp.dot(p_txt, tvalues, preferred_element_type=f32)
        done = (acc[:, :size] / acc[:, size:]).astype(bf16)
        at = 0
        for out_ref in out_refs:
            out_ref[:, cols] = done[at : at + out_ref.shape[0]]
            at += out_ref.shape[0]


def attention(far, near, text, blocks, mark, n_far, heads, rows, text_rows):
    size = blocks[0].shape[1]
    counts = [rows] * (len(far) + near) + [text_rows] * text
    queries = sum(counts)
    keys = len(blocks) * ((n_far + 1) * rows + text_rows)
    shapes = [jax.ShapeDtypeStruct((n, heads * size), bf16) for n in counts]
    return pl.pallas_call(
        functools.partial(
            attention_kernel, n_far, len(blocks), (len(far), near, text), heads, rows, text_rows
        ),
        out_shape=shapes + [jax.ShapeDtypeStruct((1,), jnp.int32)],
        in_specs=[VMEM] * (len(far) + len(blocks)) + [SMEM],
        out_specs=[VMEM] * len(shapes) + [SMEM],
        compiler_params=params(),
        cost_estimate=cost(
            4 * queries * keys * heads * size,
            4 * (queries + keys) * heads * size,
            queries * keys * heads,
        ),
    )(*far, *blocks, mark)


def assemble_kernel(places, meta_ref, *refs):
    pieces, out_ref = refs[: len(places)], refs[-1]
    rows, width = out_ref.shape[0], pieces[0].shape[1]
    for k, piece in zip(places, pieces):
        at = pl.multiple_of((meta_ref[0] ^ k) * width, 128)
        out_ref[:, pl.ds(at, width)] = piece[:rows, :]


def assemble(meta, pieces, places, after, rows):
    groups, width = len(pieces), pieces[0].shape[1]
    return pl.pallas_call(
        functools.partial(assemble_kernel, tuple(places)),
        out_shape=jax.ShapeDtypeStruct((rows, groups * width), bf16),
        in_specs=[SMEM] + [VMEM] * groups + [ANY] * len(after),
        out_specs=VMEM,
        compiler_params=params(),
        cost_estimate=cost(0, 4 * rows * groups * width),
    )(meta, *pieces, *after)


def gated_kernel(groups, parts, place_of, meta_ref, gate_ref, d_out_ref, *refs):
    msgs, turned = refs[:-1], refs[-1]
    gated = (gate_ref[...] * d_out_ref[...].astype(f32)).astype(bf16)
    turned[...] = gated.astype(f32).T
    rows = msgs[0].shape[2]
    z, oc, dp = meta_ref[0], meta_ref[1], meta_ref[2]
    for k, msg in enumerate(msgs):
        for j in range(parts):
            for g in range(groups):
                at = (dp ^ k) * (groups * parts) + place_of(oc ^ j, z ^ g)
                msg[j, g] = turned[pl.ds(pl.multiple_of(at * rows, 8), rows), :].astype(bf16)


def gated_parts(meta, gate, d_out, n_dp, groups, parts, place_of):
    local, model = d_out.shape
    rows = model // (n_dp * groups * parts)
    return pl.pallas_call(
        functools.partial(gated_kernel, groups, parts, place_of),
        out_shape=[jax.ShapeDtypeStruct((parts, groups, rows, local), bf16)] * n_dp,
        in_specs=[SMEM, VMEM, VMEM],
        out_specs=[VMEM] * n_dp,
        scratch_shapes=[pltpu.VMEM((model, local), f32)],
        compiler_params=params(60),
        cost_estimate=cost(0, 4 * local * model),
    )(meta, gate, d_out)


def gather_kernel(n_dp, *refs):
    pieces, outs = refs[:n_dp], refs[n_dp:]
    for j, out in enumerate(outs):
        for k, piece in enumerate(pieces):
            out[k] = piece[j + 1]


def gather_parts(pieces):
    parts = pieces[0].shape[0]
    shape = (len(pieces),) + pieces[0].shape[1:]
    return pl.pallas_call(
        functools.partial(gather_kernel, len(pieces)),
        out_shape=[jax.ShapeDtypeStruct(shape, bf16)] * (parts - 1),
        in_specs=[VMEM] * len(pieces),
        out_specs=[VMEM] * (parts - 1),
        compiler_params=params(),
        cost_estimate=cost(0, 4 * math.prod(shape) * (parts - 1)),
    )(*pieces)


def project_kernel(
    groups, parts, place_of, meta_ref, attn_ref, w_ref, gate_ref, d_out_ref, out_ref, d_attn_ref,
    term_ref, *refs
):
    sent, by_place = refs[:-1], refs[-1]
    rows = attn_ref.shape[0]
    block = 512
    sums = []
    for at in range(0, w_ref.shape[0], block):
        cols = slice(at, at + block)
        got = lax.dot_general(
            attn_ref[...], w_ref[cols, :], (((1,), (1,)), ((), ())), preferred_element_type=f32
        )
        out_ref[:, cols] = (got * gate_ref[:, cols]).astype(bf16)
        sums.append(jnp.sum(got * d_out_ref[:, cols].astype(f32), axis=0, keepdims=True))
    total = jnp.zeros(d_attn_ref.shape, f32)
    for at in range(0, w_ref.shape[0], block):
        cols = slice(at, at + block)
        gated = (gate_ref[:, cols] * d_out_ref[:, cols].astype(f32)).astype(bf16)
        total = total + jnp.dot(gated, w_ref[cols, :], preferred_element_type=f32)
    d_attn_ref[...] = total.astype(bf16)
    sums = jnp.concatenate(sums, axis=1)
    places, width = by_place.shape
    for s in range(places):
        by_place[s : s + 1, :] = sums[:, s * width : (s + 1) * width]
    for g in range(groups):
        at = place_of(meta_ref[1], meta_ref[0] ^ g)
        term_ref[g : g + 1, :] = by_place[pl.ds(at, 1), :]
    for j, out in enumerate(sent):
        out[:rows, :] = attn_ref[...]
        line = [
            by_place[pl.ds(place_of(meta_ref[1] ^ (j + 1), meta_ref[0] ^ g), 1), :]
            for g in range(groups)
        ]
        line = jnp.concatenate(line, axis=1)
        line = jnp.concatenate(
            [line, jnp.zeros((1, attn_ref.shape[1] - groups * width), f32)], axis=1
        ) if attn_ref.shape[1] > groups * width else line
        high = line.astype(bf16).astype(f32)
        lines = [high, line - high, jnp.zeros((EXTRA - 2, line.shape[1]), f32)]
        out[rows:, :] = jnp.concatenate(lines, axis=0).astype(bf16)


def project(meta, attn, out_weight, gate, d_out, groups, parts, place_of):
    rows, inner = attn.shape
    model = out_weight.shape[0]
    width = model // (groups * parts)
    shapes = [jax.ShapeDtypeStruct((rows, model), bf16), jax.ShapeDtypeStruct((rows, inner), bf16)]
    shapes += [jax.ShapeDtypeStruct((groups, width), f32)]
    shapes += [jax.ShapeDtypeStruct((rows + EXTRA, inner), bf16)] * (parts - 1)
    return pl.pallas_call(
        functools.partial(project_kernel, groups, parts, place_of),
        out_shape=shapes,
        in_specs=[SMEM, VMEM, VMEM, VMEM, VMEM],
        out_specs=[VMEM] * (2 + parts),
        scratch_shapes=[pltpu.VMEM((groups * parts, width), f32)],
        compiler_params=params(),
        cost_estimate=cost(4 * rows * inner * model, 2 * inner * model),
    )(meta, attn, out_weight, gate, d_out)


def split_gate(gate, size):
    short = -gate.shape[1] % size
    if short:
        gate = jnp.concatenate([gate, jnp.zeros((1, short), f32)], axis=1)
    high = gate.astype(bf16).astype(f32)
    lines = [p[:, at : at + size] for p in (high, gate - high) for at in range(0, gate.shape[1], size)]
    return jnp.concatenate(lines + [jnp.zeros((EXTRA - len(lines), size), f32)], axis=0)


def joined_gate(lines, width):
    n = -(-width // lines.shape[1])
    both = lines[:n] + lines[n : 2 * n]
    return jnp.concatenate([both[i : i + 1] for i in range(n)], axis=1)[:, :width]


def grad_kernel(n_left, n_pieces, *refs):
    lefts, refs = refs[:n_left], refs[n_left:]
    pieces, refs = refs[:n_pieces], refs[n_pieces:]
    term_ref, outs = refs[0], refs[1:]
    groups, rows, depth = lefts[0].shape[1:]
    width = pieces[0].shape[1]
    size = outs[0].shape[1]
    left = []
    for ref in lefts:
        left += [ref[i].reshape(groups * rows, depth) for i in range(ref.shape[0])]
    left = jnp.concatenate(left, axis=1)
    half = outs[1].shape[0]
    homes = [((outs[0], 0),)]
    homes += [((outs[2 * g - 1], 0), (outs[2 * g], half)) for g in range(1, groups)]

    def put(g, at, value):
        out, start = homes[g][-1] if at >= half else homes[g][0]
        out[at - start : at - start + value.shape[0], :] = value.astype(out.dtype)

    block = 256
    for start in range(0, width, block):
        right = jnp.concatenate([p[:depth, start : start + block] for p in pieces], axis=0)
        got = jnp.dot(left, right, preferred_element_type=f32)
        for g in range(groups):
            for at in range(0, block, size):
                put(g, (start + at) // size * rows, got[g * rows : (g + 1) * rows, at : at + size])
    term = term_ref[...]
    each = term.shape[1]
    for p in pieces:
        if p.shape[0] > depth:
            lines = p[depth:, :].astype(f32)
            line = lines[0:1, :] + lines[1:2, :]
            term = term + jnp.concatenate(
                [line[:, g * each : (g + 1) * each] for g in range(groups)], axis=0
            )
    for g in range(groups):
        put(g, width // size * rows, split_gate(term[g : g + 1], size))


def grad_product(lefts, pieces, term):
    groups, rows, depth = lefts[0].shape[1:]
    width = pieces[0].shape[1]
    size = 128
    total = groups * rows
    depth = depth * len(pieces)
    full = width // size * rows + EXTRA
    half = width // size // 2 * rows
    shapes = [(full, f32)]
    for kind in (bf16, f32, bf16):
        shapes += [(half, kind), (full - half, kind)]
    return pl.pallas_call(
        functools.partial(grad_kernel, len(lefts), len(pieces)),
        out_shape=[jax.ShapeDtypeStruct((n, size), kind) for n, kind in shapes],
        in_specs=[VMEM] * (len(lefts) + len(pieces) + 1),
        out_specs=[VMEM] * len(shapes),
        compiler_params=params(),
        cost_estimate=cost(
            2 * total * depth * width, 2 * (total * depth + depth * width + total * width)
        ),
    )(*lefts, *pieces, term)


def pair_kernel(gate_width, n_through, own_ref, got_ref, *refs):
    out_ref = refs[n_through]
    for ref, out in zip(refs[:n_through], refs[n_through + 1 :]):
        out[...] = ref[...]
    total = own_ref[...] + got_ref[...].astype(f32)
    if not gate_width:
        out_ref[...] = total.astype(bf16)
    else:
        end = total.shape[0] - EXTRA
        out_ref[:end, :] = total[:end].astype(bf16)
        gate = joined_gate(total[end:], gate_width)
        out_ref[end:, :] = split_gate(gate, total.shape[1]).astype(bf16)


def pair_sum(own, got, gate_width, through):
    return pl.pallas_call(
        functools.partial(pair_kernel, gate_width, len(through)),
        out_shape=[jax.ShapeDtypeStruct(x.shape, bf16) for x in [got] + through],
        in_specs=[VMEM] * (2 + len(through)),
        out_specs=[VMEM] * (1 + len(through)),
        compiler_params=params(),
        cost_estimate=cost(0, 8 * own.size),
    )(own, got, *through)


def final_kernel(own_ref, far_low, far_high, near_low, near_high, out_ref, gate_ref):
    size = own_ref.shape[1]
    rows = out_ref.shape[0]
    half = far_low.shape[0]

    def total(at, count):
        refs, start = ((far_high, near_high), half) if at >= half else ((far_low, near_low), 0)
        got = own_ref[at : at + count, :]
        for ref in refs:
            got = got + ref[at - start : at - start + count, :].astype(f32)
        return got

    for i in range(out_ref.shape[1] // size):
        out_ref[:, i * size : (i + 1) * size] = total(i * rows, rows)
    gate_ref[...] = joined_gate(total(own_ref.shape[0] - EXTRA, EXTRA), gate_ref.shape[1])


def final_sum(own, far, near, rows, width, gate_width):
    return pl.pallas_call(
        final_kernel,
        out_shape=[
            jax.ShapeDtypeStruct((rows, width), f32),
            jax.ShapeDtypeStruct((1, gate_width), f32),
        ],
        in_specs=[VMEM] * 5,
        out_specs=[VMEM] * 2,
        compiler_params=params(),
        cost_estimate=cost(0, 8 * rows * width),
    )(own, *far, *near)


def on_device(
    caption_states,
    caption_gain,
    text_proj,
    caption_len,
    slot_source,
    query_gain,
    key_gain,
    image_q,
    image_k,
    image_v,
    out_weight,
    gate,
    d_out,
):
    n_dp = lax.axis_size("dp")
    n_seq = lax.axis_size("seq")
    G, C = GROUPS, CORES
    O = n_seq // (G * C)
    OC = O * C
    dp = lax.axis_index("dp")
    seq = lax.axis_index("seq")

    def where():
        at = lax.axis_index("seq")
        return (at // C) % G, (at // (G * C)) * C + at % C

    z, oc = where()

    def place(oc_at, z_at):
        return ((oc_at // C) * G + z_at) * C + oc_at % C

    def to_z(x, k):
        perm = [(place(a, b), place(a, b ^ k)) for a in range(OC) for b in range(G)]
        return lax.ppermute(x, "seq", perm)

    def to_oc(x, j):
        perm = [(place(a, b), place(a ^ j, b)) for a in range(OC) for b in range(G)]
        return lax.ppermute(x, "seq", perm)

    def to_dp(x, k):
        return lax.ppermute(x, "dp", [(a, a ^ k) for a in range(n_dp)])

    def part(x, index, size, axis):
        return lax.dynamic_slice_in_dim(x, index * size, size, axis)

    slot_total = slot_source.shape[1]
    slot_local = slot_total // n_seq
    image_local = image_q.shape[1]
    inner_width = image_q.shape[2]
    model_width = out_weight.shape[0]
    head_size = query_gain.shape[0]
    gw = inner_width // G
    order = [2, 3, 1]
    meta = jnp.stack([z, oc, dp]).astype(jnp.int32)

    heads = gw // head_size
    text_rows = G * slot_local
    own, *rest = text_project(
        caption_len, slot_source, caption_states[0], caption_gain[None],
        query_gain[None], key_gain[None], image_k[0], image_v[0], image_q[0], text_proj,
        G, OC, place, where,
    )
    packed, sent = rest[:G], rest[G:]
    images = {0: packed[0]}
    for k in order:
        images[k] = to_z(packed[k], k)
    images = [images[k] for k in [0] + order]
    got = [to_oc(x, j + 1) for j, x in enumerate(sent)]
    own, sent = text_sum(own, got, text_rows)
    own, sent = text_sum(own, [to_z(sent, 1)], text_rows)
    got = to_z(sent, 2)

    gg = gated_parts(meta, gate, d_out[0], n_dp, G, OC, place)
    gg_dp = [gg[0], to_dp(gg[1], 1)]
    block = block_of(own, got, gg_dp[1:], images, DT5, heads)
    blocks = [block] + [to_oc(block, j) for j in range(1, OC)]
    far = images[1:]
    *first, text_out, mark = attention(
        far[:2], 0, 1, blocks, caption_len, len(far), heads, image_local, text_rows
    )
    *second, _ = attention(
        far[2:], 1, 0, blocks, mark, len(far), heads, image_local, text_rows
    )
    outs = dict(zip(order + [0], first + second))

    back = {}
    for k in order + [0]:
        rows = jnp.concatenate([outs[k], part(text_out, z ^ k, slot_local, 0)], axis=0)
        back[k] = to_z(rows, k) if k else rows
    back = [back[k] for k in order + [0]]
    gg_dp += [to_dp(gg[k], k) for k in range(2, n_dp)]
    lefts = [g[:1] for g in gg_dp]
    lefts += [to_oc(g, j + 1) for j, g in enumerate(gather_parts(gg_dp))]
    image_attn = assemble(meta, back, order + [0], gg_dp[1:], image_local)
    text_attn = jnp.zeros((slot_local, inner_width), bf16)
    own_usable = part(slot_source[0] < caption_len[0], seq, slot_local, 0)
    for k, got in zip(order + [0], back):
        rows = jnp.where(own_usable[:, None], got[image_local:], jnp.zeros((), bf16))
        text_attn = lax.dynamic_update_slice_in_dim(text_attn, rows, (z ^ k) * gw, 1)

    pieces = [image_attn] + [to_dp(image_attn, k) for k in range(1, n_dp)]
    image_out, d_attn, term, *sent = project(
        meta, image_attn, out_weight, gate, d_out[0], G, OC, place
    )
    for j in range(1, OC):
        pieces += [to_oc(sent[j - 1], j)] + [to_oc(p, j) for p in pieces[1:n_dp]]
    R = model_width // (n_dp * n_seq)
    gate_width = model_width // n_seq
    own, *blocks = grad_product(lefts, pieces, term)
    got = [to_z(x, 1) for x in blocks[4:]]
    (low,) = pair_sum(blocks[2], got[0], 0, [])
    high, *near = pair_sum(blocks[3], got[1], gate_width, blocks[:2])
    far = [to_z(x, 2) for x in (low, high)]
    near = [to_z(x, 1) for x in near]
    grad_wo, grad_gate = final_sum(own, far, near, R, inner_width, gate_width)
    return (image_out[None], text_attn[None], d_attn[None], grad_wo, grad_gate)


def solution(mesh):
    in_specs = (
        P("dp", None, "seq"),
        P("seq"),
        P("seq", None),
        P("dp"),
        P("dp", None),
        P(),
        P(),
        P("dp", "seq", None),
        P("dp", "seq", None),
        P("dp", "seq", None),
        P(),
        P("dp", None),
        P("dp", "seq", None),
    )
    out_specs = (
        P("dp", "seq", None),
        P("dp", "seq", None),
        P("dp", "seq", None),
        P(("dp", "seq"), None),
        P("dp", "seq"),
    )
    return jax.shard_map(
        on_device, mesh=mesh, in_specs=in_specs, out_specs=out_specs, check_vma=False
    )
```

```python
import math
import functools
import jax
import jax.numpy as jnp
from jax import lax
from jax.experimental import pallas as pl
from jax.experimental.pallas import tpu as pltpu
from jax.sharding import PartitionSpec as P

DT5 = 4096
CORES = 2
GROUPS = 4

eps_norm = 1e-06
f32 = jnp.float32
bf16 = jnp.bfloat16
EXTRA = 16


VMEM = pl.BlockSpec(memory_space=pltpu.VMEM)
SMEM = pl.BlockSpec(memory_space=pltpu.SMEM)
ANY = pl.BlockSpec(memory_space=pl.ANY)


def params(mib=16):
    return pltpu.CompilerParams(vmem_limit_bytes=int(mib * 1024 * 1024))


def cost(flops, bytes_accessed, transcendentals=0):
    return pl.CostEstimate(
        flops=flops, bytes_accessed=bytes_accessed, transcendentals=transcendentals
    )


def split_tail(squares, width):
    high = squares.astype(bf16).astype(f32)
    low = squares - high
    lane = lax.broadcasted_iota(jnp.int32, (squares.shape[0], width), 1)
    return jnp.where(lane == 0, high, jnp.where(lane == 1, low, 0.0))


def joined(tail):
    return tail[:, 0:1] + tail[:, 1:2]


def text_kernel(
    groups, heads, place_of, where, len_ref, src_ref, states_ref, gain_ref, qg_ref, kg_ref,
    k_ref, v_ref, q_ref, w_ref, own_ref, *refs
):
    meta_ref = where()
    packed, refs = refs[:groups], refs[groups:]
    msgs, (w_all, loaded, stage, w_sems, in_sems, out_sems) = refs[:-6], refs[-6:]
    size = own_ref.shape[2]
    rows = (own_ref.shape[1] - EXTRA) // (3 * heads + 1)
    width = heads * size
    slots = states_ref.shape[0]
    slot_local = rows // groups
    copies = []
    block = w_all.shape[0] // w_sems.shape[0]
    for i in range(w_sems.shape[0]):
        part = pl.ds(i * block, block)
        copies.append(pltpu.make_async_copy(w_ref.at[part], w_all.at[part], w_sems.at[i]))
        copies[-1].start()
    loads = []
    for i, ref in enumerate((k_ref, v_ref, q_ref)):
        loads.append(pltpu.make_async_copy(ref, loaded.at[i], in_sems.at[i]))
        loads[-1].start()

    def slot_at(row):
        z_at = (row % rows) // slot_local
        return place_of(meta_ref[1] ^ (row // rows), z_at) * slot_local + row % slot_local

    iota = functools.partial(lax.broadcasted_iota, jnp.int32, (slots, slots))
    sources = src_ref[...].astype(f32)
    chosen = (iota(1) == slot_at(iota(0))).astype(f32)
    source_col = jnp.sum(chosen * sources, axis=1, keepdims=True)
    pick = (iota(1).astype(f32) == source_col).astype(bf16)
    chosen_t = (iota(0) == slot_at(iota(1))).astype(bf16)
    source_row = jnp.dot(sources.astype(bf16), chosen_t, preferred_element_type=f32)
    bias = jnp.where(source_row < len_ref[0].astype(f32), 0.0, -1e30)
    end = own_ref.shape[1] - EXTRA
    own_ref[0, end:, :] = jnp.zeros((EXTRA, size), f32)
    own_ref[0, end : end + 1, :] = qg_ref[...]
    own_ref[0, end + 1 : end + 2, :] = kg_ref[...]
    own_ref[0, end + 2 : end + 3, :slots] = bias

    picked = jnp.dot(pick, states_ref[...], preferred_element_type=f32)
    scaled = (picked * gain_ref[...]).astype(bf16)
    tail = split_tail(jnp.sum(picked * picked, axis=1, keepdims=True), size)
    for copy in loads:
        copy.wait()
    local = loaded.shape[1]
    stores = []
    for g in range(groups):
        for i in range(3):
            for head in range(heads):
                at = ((meta_ref[0] ^ g) * heads + head) * size
                to = (i * heads + head) * local
                stage[g, to : to + local, :] = loaded[i, :, pl.ds(pl.multiple_of(at, 128), size)]
        stores.append(pltpu.make_async_copy(stage.at[g], packed[g], out_sems.at[g]))
        stores[-1].start()
    for copy in copies:
        copy.wait()
    for g in range(groups):
        for i in range(3):
            at = (i * groups + (meta_ref[0] ^ g)) * width
            columns = pl.ds(pl.multiple_of(at, 128), width)
            got = jnp.dot(scaled, w_all[:, columns], preferred_element_type=f32)
            for head in range(heads):
                part = got[:, head * size : (head + 1) * size]
                to = slice((i * heads + head) * rows, (i * heads + head + 1) * rows)
                own_ref[g, to, :] = part[:rows]
                for j, msg in enumerate(msgs):
                    msg[g, to, :] = part[(j + 1) * rows : (j + 2) * rows].astype(bf16)
        own_ref[g, 3 * heads * rows : end, :] = tail[:rows]
        for j, msg in enumerate(msgs):
            msg[g, 3 * heads * rows :, :] = tail[(j + 1) * rows : (j + 2) * rows].astype(bf16)
    for copy in stores:
        copy.wait()


def text_project(
    length, sources, states, gain, query_gain, key_gain, keys, values, queries, text_proj,
    groups, parts, place_of, where
):
    slots, depth = states.shape
    size = query_gain.shape[1]
    heads = text_proj.shape[1] // (3 * groups * size)
    text_rows = (3 * heads + 1) * slots // parts
    shapes = [jax.ShapeDtypeStruct((groups, text_rows + EXTRA, size), f32)]
    shapes += [jax.ShapeDtypeStruct((3 * heads * keys.shape[0], size), bf16)] * groups
    shapes += [jax.ShapeDtypeStruct((groups, text_rows, size), bf16)] * (parts - 1)
    return pl.pallas_call(
        functools.partial(text_kernel, groups, heads, place_of, where),
        out_shape=shapes,
        in_specs=[SMEM] + [VMEM] * 5 + [ANY] * 4,
        out_specs=[VMEM] + [ANY] * groups + [VMEM] * (parts - 1),
        scratch_shapes=[
            pltpu.VMEM(text_proj.shape, bf16),
            pltpu.VMEM((3,) + keys.shape, bf16),
            pltpu.VMEM((groups, 3 * heads * keys.shape[0], size), bf16),
            pltpu.SemaphoreType.DMA((4,)),
            pltpu.SemaphoreType.DMA((3,)),
            pltpu.SemaphoreType.DMA((groups,)),
        ],
        compiler_params=params(60),
        cost_estimate=cost(
            2 * slots * depth * text_proj.shape[1], 2 * depth * text_proj.shape[1]
        ),
    )(
        length, sources, states, gain, query_gain, key_gain, keys, values, queries, text_proj
    )


def text_sum_kernel(n_got, tail_rows, own_ref, *refs):
    got, (keep_ref, send_ref) = refs[:n_got], refs[n_got:]
    groups, text_rows, size = got[0].shape
    for g in range(groups):
        total = own_ref[g, :text_rows, :]
        for ref in got:
            total = total + ref[g].astype(f32)
        end = text_rows - tail_rows
        tail = split_tail(joined(total[end:]), size)
        if g % 2 == 0:
            keep_ref[g // 2, :end, :] = total[:end]
            keep_ref[g // 2, end:text_rows, :] = tail
            keep_ref[g // 2, text_rows:, :] = own_ref[g, text_rows:, :]
        else:
            send_ref[g // 2, :end, :] = total[:end].astype(bf16)
            send_ref[g // 2, end:, :] = tail.astype(bf16)


def text_sum(own, got, tail_rows):
    groups, rows, size = own.shape
    return pl.pallas_call(
        functools.partial(text_sum_kernel, len(got), tail_rows),
        out_shape=[
            jax.ShapeDtypeStruct((groups // 2, rows, size), f32),
            jax.ShapeDtypeStruct((groups // 2, rows - EXTRA, size), bf16),
        ],
        in_specs=[VMEM] * (1 + len(got)),
        out_specs=[VMEM] * 2,
        compiler_params=params(),
        cost_estimate=cost(0, 8 * groups * rows * size),
    )(own, *got)


def block_kernel(features, heads, n_pieces, own_ref, got_ref, *refs):
    pieces, (out_ref, first_ref, second_ref) = refs[:n_pieces], refs[-3:]
    near_rows = pieces[0].shape[0]
    kv_rows = near_rows // 3 * 2
    out_ref[:near_rows, :] = pieces[0][...]
    for k, ref in enumerate(pieces[1:]):
        at = near_rows + k * kv_rows
        out_ref[at : at + kv_rows, :] = ref[:kv_rows, :]
    q_rows = near_rows - kv_rows
    first_ref[:q_rows, :] = pieces[1][kv_rows:, :]
    first_ref[q_rows:, :] = pieces[2][kv_rows:, :]
    second_ref[...] = pieces[3][kv_rows:, :]
    size = own_ref.shape[2]
    text_rows = got_ref.shape[1]
    rows = text_rows // (3 * heads + 1)
    total = own_ref[0, :text_rows, :] + got_ref[0].astype(f32)
    rate = lax.rsqrt(joined(total[3 * heads * rows :]) / features + eps_norm)
    start = near_rows + (n_pieces - 1) * kv_rows
    for i in range(3):
        for head in range(heads):
            at = (i * heads + head) * rows
            x = total[at : at + rows] * rate
            if i < 2:
                mean = jnp.sum(x * x, axis=1, keepdims=True) / size
                gain = own_ref[0, text_rows + i : text_rows + i + 1, :]
                x = x * lax.rsqrt(mean + eps_norm) * gain
            out_ref[start + at : start + at + rows, :] = x.astype(bf16)
    bias = own_ref[0, text_rows + 2 : text_rows + 3, :]
    start = start + 3 * heads * rows
    out_ref[start:, :] = jnp.broadcast_to(bias, (EXTRA, size)).astype(bf16)


def block_of(own, got, after, pieces, features, heads):
    rows, size = own.shape[1:]
    total = (rows - EXTRA) // (3 * heads + 1) * 3 * heads + EXTRA
    q_rows = pieces[0].shape[0] // 3
    total += q_rows * (2 * len(pieces) + 1)
    return pl.pallas_call(
        functools.partial(block_kernel, features, heads, len(pieces)),
        out_shape=[jax.ShapeDtypeStruct((n, size), bf16) for n in (total, 2 * q_rows, q_rows)],
        in_specs=[VMEM] * (2 + len(pieces)) + [ANY] * len(after),
        out_specs=[VMEM] * 3,
        compiler_params=params(),
        cost_estimate=cost(0, 4 * total * size),
    )(own, got, *pieces, *after)


def attention_kernel(n_far, n_cores, n_after, queries, heads, rows, text_rows, *refs):
    far_ref, blocks = refs[0], refs[1 : 1 + n_cores]
    out_refs = refs[1 + n_cores + n_after :]
    size = blocks[0].shape[1]
    factor = size ** (-0.5) * math.log2(math.e)
    nt = (((1,), (1,)), ((), ()))
    kv_rows = 2 * heads * rows
    near_rows = 3 * heads * rows
    starts = [0] + [near_rows + k * kv_rows for k in range(n_far)]
    text = near_rows + n_far * kv_rows
    end = text + 3 * heads * text_rows
    bias = blocks[0][end : end + EXTRA, :][:1, : n_cores * text_rows].astype(f32)

    def with_ones(values):
        return jnp.concatenate([values, jnp.ones(values.shape, bf16)], axis=1)

    for head in range(heads):
        kv, tkv = [], []
        for i in range(2):
            at = (i * heads + head) * rows
            image = [b[start + at : start + at + rows, :] for b in blocks for start in starts]
            text_at = text + ((i + 1) * heads + head) * text_rows
            kv.append(jnp.concatenate(image, axis=0))
            tkv.append(jnp.concatenate([b[text_at : text_at + text_rows, :] for b in blocks], axis=0))
        keys, values = kv[0], with_ones(kv[1])
        tkeys, tvalues = tkv[0], with_ones(tkv[1])
        cols = slice(head * size, (head + 1) * size)
        q_at = (2 * heads + head) * rows
        asked = [
            far_ref[(k * heads + head) * rows : (k * heads + head + 1) * rows, :]
            for k in range(queries[0])
        ]
        if queries[1]:
            asked.append(blocks[0][q_at : q_at + rows, :])
        if queries[2]:
            tq_at = text + head * text_rows
            asked.append(blocks[0][tq_at : tq_at + text_rows, :])
        q = jnp.concatenate(asked, axis=0)
        s_img = lax.dot_general(q, keys, nt, preferred_element_type=f32)
        s_txt = lax.dot_general(q, tkeys, nt, preferred_element_type=f32) + bias
        top = jnp.maximum(
            jnp.max(s_img, axis=1, keepdims=True), jnp.max(s_txt, axis=1, keepdims=True)
        )
        p_img = jnp.exp2((s_img - top) * factor).astype(bf16)
        p_txt = jnp.exp2((s_txt - top) * factor).astype(bf16)
        acc = jnp.dot(p_img, values, preferred_element_type=f32)
        acc = acc + jnp.dot(p_txt, tvalues, preferred_element_type=f32)
        done = (acc[:, :size] / acc[:, size:]).astype(bf16)
        at = 0
        for out_ref in out_refs:
            out_ref[:, cols] = done[at : at + out_ref.shape[0]]
            at += out_ref.shape[0]


def attention(far, near, text, blocks, after, n_far, heads, rows, text_rows):
    size = blocks[0].shape[1]
    asked = far.shape[0] // (heads * rows)
    counts = [rows] * (asked + near) + [text_rows] * text
    queries = sum(counts)
    keys = len(blocks) * ((n_far + 1) * rows + text_rows)
    shapes = [jax.ShapeDtypeStruct((n, heads * size), bf16) for n in counts]
    return pl.pallas_call(
        functools.partial(
            attention_kernel,
            n_far,
            len(blocks),
            len(after),
            (asked, near, text),
            heads,
            rows,
            text_rows,
        ),
        out_shape=shapes,
        in_specs=[VMEM] * (1 + len(blocks)) + [ANY] * len(after),
        out_specs=[VMEM] * len(shapes),
        compiler_params=params(),
        cost_estimate=cost(
            4 * queries * keys * heads * size,
            4 * (queries + keys) * heads * size,
            queries * keys * heads,
        ),
    )(far, *blocks, *after)


def assemble_kernel(places, where, *refs):
    pieces, out_ref = refs[: len(places)], refs[-1]
    z = where()[0]
    rows, width = out_ref.shape[0], pieces[0].shape[1]
    for k, piece in zip(places, pieces):
        at = pl.multiple_of((z ^ k) * width, 128)
        out_ref[:, pl.ds(at, width)] = piece[:rows, :]


def assemble(where, pieces, places, after, rows):
    groups, width = len(pieces), pieces[0].shape[1]
    return pl.pallas_call(
        functools.partial(assemble_kernel, tuple(places), where),
        out_shape=jax.ShapeDtypeStruct((rows, groups * width), bf16),
        in_specs=[VMEM] * groups + [ANY] * len(after),
        out_specs=VMEM,
        compiler_params=params(),
        cost_estimate=cost(0, 4 * rows * groups * width),
    )(*pieces, *after)


def gated_kernel(groups, parts, place_of, meta_ref, gate_ref, d_out_ref, *refs):
    msgs, turned = refs[:-1], refs[-1]
    gated = (gate_ref[...] * d_out_ref[...].astype(f32)).astype(bf16)
    turned[...] = gated.astype(f32).T
    rows = msgs[0].shape[2]
    z, oc, dp = meta_ref[0], meta_ref[1], meta_ref[2]
    for k, msg in enumerate(msgs):
        for j in range(parts):
            for g in range(groups):
                at = (dp ^ k) * (groups * parts) + place_of(oc ^ j, z ^ g)
                msg[j, g] = turned[pl.ds(pl.multiple_of(at * rows, 8), rows), :].astype(bf16)


def gated_parts(meta, gate, d_out, n_dp, groups, parts, place_of):
    local, model = d_out.shape
    rows = model // (n_dp * groups * parts)
    return pl.pallas_call(
        functools.partial(gated_kernel, groups, parts, place_of),
        out_shape=[jax.ShapeDtypeStruct((parts, groups, rows, local), bf16)] * n_dp,
        in_specs=[SMEM, VMEM, VMEM],
        out_specs=[VMEM] * n_dp,
        scratch_shapes=[pltpu.VMEM((model, local), f32)],
        compiler_params=params(60),
        cost_estimate=cost(0, 4 * local * model),
    )(meta, gate, d_out)


def gather_kernel(n_dp, *refs):
    pieces, outs = refs[:n_dp], refs[n_dp:]
    for j, out in enumerate(outs):
        for k, piece in enumerate(pieces):
            out[k] = piece[j + 1]


def gather_parts(pieces):
    parts = pieces[0].shape[0]
    shape = (len(pieces),) + pieces[0].shape[1:]
    return pl.pallas_call(
        functools.partial(gather_kernel, len(pieces)),
        out_shape=[jax.ShapeDtypeStruct(shape, bf16)] * (parts - 1),
        in_specs=[VMEM] * len(pieces),
        out_specs=[VMEM] * (parts - 1),
        compiler_params=params(),
        cost_estimate=cost(0, 4 * math.prod(shape) * (parts - 1)),
    )(*pieces)


def project_kernel(
    groups, parts, place_of, meta_ref, attn_ref, w_ref, gate_ref, d_out_ref, out_ref, d_attn_ref,
    term_ref, *refs
):
    sent, by_place = refs[:-1], refs[-1]
    rows = attn_ref.shape[0]
    block = 512
    sums = []
    for at in range(0, w_ref.shape[0], block):
        cols = slice(at, at + block)
        got = lax.dot_general(
            attn_ref[...], w_ref[cols, :], (((1,), (1,)), ((), ())), preferred_element_type=f32
        )
        out_ref[:, cols] = (got * gate_ref[:, cols]).astype(bf16)
        sums.append(jnp.sum(got * d_out_ref[:, cols].astype(f32), axis=0, keepdims=True))
    total = jnp.zeros(d_attn_ref.shape, f32)
    for at in range(0, w_ref.shape[0], block):
        cols = slice(at, at + block)
        gated = (gate_ref[:, cols] * d_out_ref[:, cols].astype(f32)).astype(bf16)
        total = total + jnp.dot(gated, w_ref[cols, :], preferred_element_type=f32)
    d_attn_ref[...] = total.astype(bf16)
    sums = jnp.concatenate(sums, axis=1)
    places, width = by_place.shape
    for s in range(places):
        by_place[s : s + 1, :] = sums[:, s * width : (s + 1) * width]
    for g in range(groups):
        at = place_of(meta_ref[1], meta_ref[0] ^ g)
        term_ref[g : g + 1, :] = by_place[pl.ds(at, 1), :]
    for j, out in enumerate(sent):
        out[:rows, :] = attn_ref[...]
        line = [
            by_place[pl.ds(place_of(meta_ref[1] ^ (j + 1), meta_ref[0] ^ g), 1), :]
            for g in range(groups)
        ]
        line = jnp.concatenate(line, axis=1)
        line = jnp.concatenate(
            [line, jnp.zeros((1, attn_ref.shape[1] - groups * width), f32)], axis=1
        ) if attn_ref.shape[1] > groups * width else line
        high = line.astype(bf16).astype(f32)
        lines = [high, line - high, jnp.zeros((EXTRA - 2, line.shape[1]), f32)]
        out[rows:, :] = jnp.concatenate(lines, axis=0).astype(bf16)


def project(meta, attn, out_weight, gate, d_out, groups, parts, place_of):
    rows, inner = attn.shape
    model = out_weight.shape[0]
    width = model // (groups * parts)
    shapes = [jax.ShapeDtypeStruct((rows, model), bf16), jax.ShapeDtypeStruct((rows, inner), bf16)]
    shapes += [jax.ShapeDtypeStruct((groups, width), f32)]
    shapes += [jax.ShapeDtypeStruct((rows + EXTRA, inner), bf16)] * (parts - 1)
    return pl.pallas_call(
        functools.partial(project_kernel, groups, parts, place_of),
        out_shape=shapes,
        in_specs=[SMEM, VMEM, VMEM, VMEM, VMEM],
        out_specs=[VMEM] * (2 + parts),
        scratch_shapes=[pltpu.VMEM((groups * parts, width), f32)],
        compiler_params=params(),
        cost_estimate=cost(4 * rows * inner * model, 2 * inner * model),
    )(meta, attn, out_weight, gate, d_out)


def split_gate(gate, size):
    short = -gate.shape[1] % size
    if short:
        gate = jnp.concatenate([gate, jnp.zeros((1, short), f32)], axis=1)
    high = gate.astype(bf16).astype(f32)
    lines = [p[:, at : at + size] for p in (high, gate - high) for at in range(0, gate.shape[1], size)]
    return jnp.concatenate(lines + [jnp.zeros((EXTRA - len(lines), size), f32)], axis=0)


def joined_gate(lines, width):
    n = -(-width // lines.shape[1])
    both = lines[:n] + lines[n : 2 * n]
    return jnp.concatenate([both[i : i + 1] for i in range(n)], axis=1)[:, :width]


def grad_kernel(n_left, n_pieces, *refs):
    lefts, refs = refs[:n_left], refs[n_left:]
    pieces, refs = refs[:n_pieces], refs[n_pieces:]
    term_ref, outs = refs[0], refs[1:]
    groups, rows, depth = lefts[0].shape[1:]
    width = pieces[0].shape[1]
    size = outs[0].shape[1]
    left = []
    for ref in lefts:
        left += [ref[i].reshape(groups * rows, depth) for i in range(ref.shape[0])]
    left = jnp.concatenate(left, axis=1)
    half = outs[1].shape[0]
    homes = [((outs[0], 0),)]
    homes += [((outs[2 * g - 1], 0), (outs[2 * g], half)) for g in range(1, groups)]

    def put(g, at, value):
        out, start = homes[g][-1] if at >= half else homes[g][0]
        out[at - start : at - start + value.shape[0], :] = value.astype(out.dtype)

    block = 256
    for start in range(0, width, block):
        right = jnp.concatenate([p[:depth, start : start + block] for p in pieces], axis=0)
        got = jnp.dot(left, right, preferred_element_type=f32)
        for g in range(groups):
            for at in range(0, block, size):
                put(g, (start + at) // size * rows, got[g * rows : (g + 1) * rows, at : at + size])
    term = term_ref[...]
    each = term.shape[1]
    for p in pieces:
        if p.shape[0] > depth:
            lines = p[depth:, :].astype(f32)
            line = lines[0:1, :] + lines[1:2, :]
            term = term + jnp.concatenate(
                [line[:, g * each : (g + 1) * each] for g in range(groups)], axis=0
            )
    for g in range(groups):
        put(g, width // size * rows, split_gate(term[g : g + 1], size))


def grad_product(lefts, pieces, term):
    groups, rows, depth = lefts[0].shape[1:]
    width = pieces[0].shape[1]
    size = 128
    total = groups * rows
    depth = depth * len(pieces)
    full = width // size * rows + EXTRA
    half = width // size // 2 * rows
    shapes = [(full, f32)]
    for kind in (bf16, f32, bf16):
        shapes += [(half, kind), (full - half, kind)]
    return pl.pallas_call(
        functools.partial(grad_kernel, len(lefts), len(pieces)),
        out_shape=[jax.ShapeDtypeStruct((n, size), kind) for n, kind in shapes],
        in_specs=[VMEM] * (len(lefts) + len(pieces) + 1),
        out_specs=[VMEM] * len(shapes),
        compiler_params=params(),
        cost_estimate=cost(
            2 * total * depth * width, 2 * (total * depth + depth * width + total * width)
        ),
    )(*lefts, *pieces, term)


def pair_kernel(gate_width, n_through, own_ref, got_ref, *refs):
    out_ref = refs[n_through]
    for ref, out in zip(refs[:n_through], refs[n_through + 1 :]):
        out[...] = ref[...]
    total = own_ref[...] + got_ref[...].astype(f32)
    if not gate_width:
        out_ref[...] = total.astype(bf16)
    else:
        end = total.shape[0] - EXTRA
        out_ref[:end, :] = total[:end].astype(bf16)
        gate = joined_gate(total[end:], gate_width)
        out_ref[end:, :] = split_gate(gate, total.shape[1]).astype(bf16)


def pair_sum(own, got, gate_width, through):
    return pl.pallas_call(
        functools.partial(pair_kernel, gate_width, len(through)),
        out_shape=[jax.ShapeDtypeStruct(x.shape, bf16) for x in [got] + through],
        in_specs=[VMEM] * (2 + len(through)),
        out_specs=[VMEM] * (1 + len(through)),
        compiler_params=params(),
        cost_estimate=cost(0, 8 * own.size),
    )(own, got, *through)


def final_kernel(own_ref, far_low, far_high, near_low, near_high, out_ref, gate_ref):
    size = own_ref.shape[1]
    rows = out_ref.shape[0]
    half = far_low.shape[0]

    def total(at, count):
        refs, start = ((far_high, near_high), half) if at >= half else ((far_low, near_low), 0)
        got = own_ref[at : at + count, :]
        for ref in refs:
            got = got + ref[at - start : at - start + count, :].astype(f32)
        return got

    for i in range(out_ref.shape[1] // size):
        out_ref[:, i * size : (i + 1) * size] = total(i * rows, rows)
    gate_ref[...] = joined_gate(total(own_ref.shape[0] - EXTRA, EXTRA), gate_ref.shape[1])


def final_sum(own, far, near, rows, width, gate_width):
    return pl.pallas_call(
        final_kernel,
        out_shape=[
            jax.ShapeDtypeStruct((rows, width), f32),
            jax.ShapeDtypeStruct((1, gate_width), f32),
        ],
        in_specs=[VMEM] * 5,
        out_specs=[VMEM] * 2,
        compiler_params=params(),
        cost_estimate=cost(0, 8 * rows * width),
    )(own, *far, *near)


def on_device(
    caption_states,
    caption_gain,
    text_proj,
    caption_len,
    slot_source,
    query_gain,
    key_gain,
    image_q,
    image_k,
    image_v,
    out_weight,
    gate,
    d_out,
):
    n_dp = lax.axis_size("dp")
    n_seq = lax.axis_size("seq")
    G, C = GROUPS, CORES
    O = n_seq // (G * C)
    OC = O * C
    dp = lax.axis_index("dp")
    seq = lax.axis_index("seq")

    def where():
        at = lax.axis_index("seq")
        return (at // C) % G, (at // (G * C)) * C + at % C

    z, oc = where()

    def place(oc_at, z_at):
        return ((oc_at // C) * G + z_at) * C + oc_at % C

    def to_z(x, k):
        perm = [(place(a, b), place(a, b ^ k)) for a in range(OC) for b in range(G)]
        return lax.ppermute(x, "seq", perm)

    def to_oc(x, j):
        perm = [(place(a, b), place(a ^ j, b)) for a in range(OC) for b in range(G)]
        return lax.ppermute(x, "seq", perm)

    def to_dp(x, k):
        return lax.ppermute(x, "dp", [(a, a ^ k) for a in range(n_dp)])

    def part(x, index, size, axis):
        return lax.dynamic_slice_in_dim(x, index * size, size, axis)

    slot_total = slot_source.shape[1]
    slot_local = slot_total // n_seq
    image_local = image_q.shape[1]
    inner_width = image_q.shape[2]
    model_width = out_weight.shape[0]
    head_size = query_gain.shape[0]
    gw = inner_width // G
    order = [2, 3, 1]
    meta = jnp.stack([z, oc, dp]).astype(jnp.int32)

    heads = gw // head_size
    text_rows = G * slot_local
    own, *rest = text_project(
        caption_len, slot_source, caption_states[0], caption_gain[None],
        query_gain[None], key_gain[None], image_k[0], image_v[0], image_q[0], text_proj,
        G, OC, place, where,
    )
    packed, sent = rest[:G], rest[G:]
    images = {0: packed[0]}
    for k in order:
        images[k] = to_z(packed[k], k)
    images = [images[k] for k in [0] + order]
    got = [to_oc(x, j + 1) for j, x in enumerate(sent)]
    own, sent = text_sum(own, got, text_rows)
    own, sent = text_sum(own, [to_z(sent, 1)], text_rows)
    got = to_z(sent, 2)

    gg = gated_parts(meta, gate, d_out[0], n_dp, G, OC, place)
    gg_dp = [gg[0], to_dp(gg[1], 1)]
    block, far_first, far_second = block_of(own, got, gg_dp[1:], images, DT5, heads)
    blocks = [block] + [to_oc(block, j) for j in range(1, OC)]
    *first, text_out = attention(
        far_first, 0, 1, blocks, [], G - 1, heads, image_local, text_rows
    )
    second = attention(
        far_second, 1, 0, blocks, [text_out], G - 1, heads, image_local, text_rows
    )
    second = list(second)
    outs = dict(zip(order + [0], first + second))

    back = {}
    for k in order + [0]:
        rows = jnp.concatenate([outs[k], part(text_out, z ^ k, slot_local, 0)], axis=0)
        back[k] = to_z(rows, k) if k else rows
    back = [back[k] for k in order + [0]]
    gg_dp += [to_dp(gg[k], k) for k in range(2, n_dp)]
    lefts = [g[:1] for g in gg_dp]
    lefts += [to_oc(g, j + 1) for j, g in enumerate(gather_parts(gg_dp))]
    image_attn = assemble(where, back, order + [0], gg_dp[1:], image_local)
    text_attn = jnp.zeros((slot_local, inner_width), bf16)
    own_usable = part(slot_source[0] < caption_len[0], seq, slot_local, 0)
    for k, got in zip(order + [0], back):
        rows = jnp.where(own_usable[:, None], got[image_local:], jnp.zeros((), bf16))
        text_attn = lax.dynamic_update_slice_in_dim(text_attn, rows, (z ^ k) * gw, 1)

    pieces = [image_attn] + [to_dp(image_attn, k) for k in range(1, n_dp)]
    image_out, d_attn, term, *sent = project(
        meta, image_attn, out_weight, gate, d_out[0], G, OC, place
    )
    for j in range(1, OC):
        pieces += [to_oc(sent[j - 1], j)] + [to_oc(p, j) for p in pieces[1:n_dp]]
    R = model_width // (n_dp * n_seq)
    gate_width = model_width // n_seq
    own, *blocks = grad_product(lefts, pieces, term)
    got = [to_z(x, 1) for x in blocks[4:]]
    (low,) = pair_sum(blocks[2], got[0], 0, [])
    high, *near = pair_sum(blocks[3], got[1], gate_width, blocks[:2])
    far = [to_z(x, 2) for x in (low, high)]
    near = [to_z(x, 1) for x in near]
    grad_wo, grad_gate = final_sum(own, far, near, R, inner_width, gate_width)
    return (image_out[None], text_attn[None], d_attn[None], grad_wo, grad_gate)


def solution(mesh):
    in_specs = (
        P("dp", None, "seq"),
        P("seq"),
        P("seq", None),
        P("dp"),
        P("dp", None),
        P(),
        P(),
        P("dp", "seq", None),
        P("dp", "seq", None),
        P("dp", "seq", None),
        P(),
        P("dp", None),
        P("dp", "seq", None),
    )
    out_specs = (
        P("dp", "seq", None),
        P("dp", "seq", None),
        P("dp", "seq", None),
        P(("dp", "seq"), None),
        P("dp", "seq"),
    )
    return jax.shard_map(
        on_device, mesh=mesh, in_specs=in_specs, out_specs=out_specs, check_vma=False
    )
```

```python
import math
import functools
import jax
import jax.numpy as jnp
from jax import lax
from jax.experimental import pallas as pl
from jax.experimental.pallas import tpu as pltpu
from jax.sharding import PartitionSpec as P

DT5 = 4096
CORES = 2
GROUPS = 4

eps_norm = 1e-06
f32 = jnp.float32
bf16 = jnp.bfloat16
EXTRA = 16


VMEM = pl.BlockSpec(memory_space=pltpu.VMEM)
SMEM = pl.BlockSpec(memory_space=pltpu.SMEM)
ANY = pl.BlockSpec(memory_space=pl.ANY)


def params(mib=16):
    return pltpu.CompilerParams(vmem_limit_bytes=int(mib * 1024 * 1024))


def cost(flops, bytes_accessed, transcendentals=0):
    return pl.CostEstimate(
        flops=flops, bytes_accessed=bytes_accessed, transcendentals=transcendentals
    )


def split_tail(squares, width):
    high = squares.astype(bf16).astype(f32)
    low = squares - high
    lane = lax.broadcasted_iota(jnp.int32, (squares.shape[0], width), 1)
    return jnp.where(lane == 0, high, jnp.where(lane == 1, low, 0.0))


def joined(tail):
    return tail[:, 0:1] + tail[:, 1:2]


def text_kernel(
    groups, heads, place_of, where, len_ref, src_ref, states_ref, gain_ref, qg_ref, kg_ref,
    k_ref, v_ref, q_ref, w_ref, own_ref, *refs
):
    meta_ref = where()
    packed, refs = refs[:groups], refs[groups:]
    msgs, (w_all, loaded, stage, w_sems, in_sems, out_sems) = refs[:-6], refs[-6:]
    size = own_ref.shape[2]
    rows = (own_ref.shape[1] - EXTRA) // (3 * heads + 1)
    width = heads * size
    slots = states_ref.shape[0]
    slot_local = rows // groups
    copies = []
    block = w_all.shape[0] // w_sems.shape[0]
    for i in range(w_sems.shape[0]):
        part = pl.ds(i * block, block)
        copies.append(pltpu.make_async_copy(w_ref.at[part], w_all.at[part], w_sems.at[i]))
        copies[-1].start()
    loads = []
    for i, ref in enumerate((k_ref, v_ref, q_ref)):
        loads.append(pltpu.make_async_copy(ref, loaded.at[i], in_sems.at[i]))
        loads[-1].start()

    def slot_at(row):
        z_at = (row % rows) // slot_local
        return place_of(meta_ref[1] ^ (row // rows), z_at) * slot_local + row % slot_local

    iota = functools.partial(lax.broadcasted_iota, jnp.int32, (slots, slots))
    sources = src_ref[...].astype(f32)
    chosen = (iota(1) == slot_at(iota(0))).astype(f32)
    source_col = jnp.sum(chosen * sources, axis=1, keepdims=True)
    pick = (iota(1).astype(f32) == source_col).astype(bf16)
    chosen_t = (iota(0) == slot_at(iota(1))).astype(bf16)
    source_row = jnp.dot(sources.astype(bf16), chosen_t, preferred_element_type=f32)
    bias = jnp.where(source_row < len_ref[0].astype(f32), 0.0, -1e30)
    end = own_ref.shape[1] - EXTRA
    own_ref[0, end:, :] = jnp.zeros((EXTRA, size), f32)
    own_ref[0, end : end + 1, :] = qg_ref[...]
    own_ref[0, end + 1 : end + 2, :] = kg_ref[...]
    own_ref[0, end + 2 : end + 3, :slots] = bias

    picked = jnp.dot(pick, states_ref[...], preferred_element_type=f32)
    scaled = (picked * gain_ref[...]).astype(bf16)
    tail = split_tail(jnp.sum(picked * picked, axis=1, keepdims=True), size)
    for copy in loads:
        copy.wait()
    local = loaded.shape[1]
    stores = []
    for g in range(groups):
        for i in range(3):
            for head in range(heads):
                at = ((meta_ref[0] ^ g) * heads + head) * size
                to = (i * heads + head) * local
                stage[g, to : to + local, :] = loaded[i, :, pl.ds(pl.multiple_of(at, 128), size)]
        stores.append(pltpu.make_async_copy(stage.at[g], packed[g], out_sems.at[g]))
        stores[-1].start()
    for copy in copies:
        copy.wait()
    for g in range(groups):
        for i in range(3):
            at = (i * groups + (meta_ref[0] ^ g)) * width
            columns = pl.ds(pl.multiple_of(at, 128), width)
            got = jnp.dot(scaled, w_all[:, columns], preferred_element_type=f32)
            for head in range(heads):
                part = got[:, head * size : (head + 1) * size]
                to = slice((i * heads + head) * rows, (i * heads + head + 1) * rows)
                own_ref[g, to, :] = part[:rows]
                for j, msg in enumerate(msgs):
                    msg[g, to, :] = part[(j + 1) * rows : (j + 2) * rows].astype(bf16)
        own_ref[g, 3 * heads * rows : end, :] = tail[:rows]
        for j, msg in enumerate(msgs):
            msg[g, 3 * heads * rows :, :] = tail[(j + 1) * rows : (j + 2) * rows].astype(bf16)
    for copy in stores:
        copy.wait()


def text_project(
    length, sources, states, gain, query_gain, key_gain, keys, values, queries, text_proj,
    groups, parts, place_of, where
):
    slots, depth = states.shape
    size = query_gain.shape[1]
    heads = text_proj.shape[1] // (3 * groups * size)
    text_rows = (3 * heads + 1) * slots // parts
    shapes = [jax.ShapeDtypeStruct((groups, text_rows + EXTRA, size), f32)]
    shapes += [jax.ShapeDtypeStruct((3 * heads * keys.shape[0], size), bf16)] * groups
    shapes += [jax.ShapeDtypeStruct((groups, text_rows, size), bf16)] * (parts - 1)
    return pl.pallas_call(
        functools.partial(text_kernel, groups, heads, place_of, where),
        out_shape=shapes,
        in_specs=[SMEM] + [VMEM] * 5 + [ANY] * 4,
        out_specs=[VMEM] + [ANY] * groups + [VMEM] * (parts - 1),
        scratch_shapes=[
            pltpu.VMEM(text_proj.shape, bf16),
            pltpu.VMEM((3,) + keys.shape, bf16),
            pltpu.VMEM((groups, 3 * heads * keys.shape[0], size), bf16),
            pltpu.SemaphoreType.DMA((4,)),
            pltpu.SemaphoreType.DMA((3,)),
            pltpu.SemaphoreType.DMA((groups,)),
        ],
        compiler_params=params(60),
        cost_estimate=cost(
            2 * slots * depth * text_proj.shape[1], 2 * depth * text_proj.shape[1]
        ),
    )(
        length, sources, states, gain, query_gain, key_gain, keys, values, queries, text_proj
    )


def text_sum_kernel(n_got, tail_rows, own_ref, *refs):
    got, (keep_ref, send_ref) = refs[:n_got], refs[n_got:]
    groups, text_rows, size = got[0].shape
    for g in range(groups):
        total = own_ref[g, :text_rows, :]
        for ref in got:
            total = total + ref[g].astype(f32)
        end = text_rows - tail_rows
        tail = split_tail(joined(total[end:]), size)
        if g % 2 == 0:
            keep_ref[g // 2, :end, :] = total[:end]
            keep_ref[g // 2, end:text_rows, :] = tail
            keep_ref[g // 2, text_rows:, :] = own_ref[g, text_rows:, :]
        else:
            send_ref[g // 2, :end, :] = total[:end].astype(bf16)
            send_ref[g // 2, end:, :] = tail.astype(bf16)


def text_sum(own, got, tail_rows):
    groups, rows, size = own.shape
    return pl.pallas_call(
        functools.partial(text_sum_kernel, len(got), tail_rows),
        out_shape=[
            jax.ShapeDtypeStruct((groups // 2, rows, size), f32),
            jax.ShapeDtypeStruct((groups // 2, rows - EXTRA, size), bf16),
        ],
        in_specs=[VMEM] * (1 + len(got)),
        out_specs=[VMEM] * 2,
        compiler_params=params(),
        cost_estimate=cost(0, 8 * groups * rows * size),
    )(own, *got)


def block_kernel(features, heads, n_pieces, own_ref, got_ref, *refs):
    pieces, out_ref = refs[:n_pieces], refs[-1]
    each = pieces[0].shape[0]
    for k, ref in enumerate(pieces):
        out_ref[k * each : (k + 1) * each, :] = ref[...]
    size = own_ref.shape[2]
    text_rows = got_ref.shape[1]
    rows = text_rows // (3 * heads + 1)
    total = own_ref[0, :text_rows, :] + got_ref[0].astype(f32)
    rate = lax.rsqrt(joined(total[3 * heads * rows :]) / features + eps_norm)
    start = n_pieces * each
    for i in range(3):
        for head in range(heads):
            at = (i * heads + head) * rows
            x = total[at : at + rows] * rate
            if i < 2:
                mean = jnp.sum(x * x, axis=1, keepdims=True) / size
                gain = own_ref[0, text_rows + i : text_rows + i + 1, :]
                x = x * lax.rsqrt(mean + eps_norm) * gain
            out_ref[start + at : start + at + rows, :] = x.astype(bf16)
    bias = own_ref[0, text_rows + 2 : text_rows + 3, :]
    start = start + 3 * heads * rows
    out_ref[start:, :] = jnp.broadcast_to(bias, (EXTRA, size)).astype(bf16)


def block_of(own, got, after, pieces, features, heads):
    rows, size = own.shape[1:]
    total = (rows - EXTRA) // (3 * heads + 1) * 3 * heads + EXTRA
    total += pieces[0].shape[0] * len(pieces)
    return pl.pallas_call(
        functools.partial(block_kernel, features, heads, len(pieces)),
        out_shape=jax.ShapeDtypeStruct((total, size), bf16),
        in_specs=[VMEM] * (2 + len(pieces)) + [ANY] * len(after),
        out_specs=VMEM,
        compiler_params=params(),
        cost_estimate=cost(0, 4 * total * size),
    )(own, got, *pieces, *after)


def attention_kernel(n_pieces, n_cores, n_after, asked_of, heads, rows, text_rows, *refs):
    blocks, out_refs = refs[:n_cores], refs[n_cores + n_after :]
    size = blocks[0].shape[1]
    factor = size ** (-0.5) * math.log2(math.e)
    nt = (((1,), (1,)), ((), ()))
    each = 3 * heads * rows
    starts = [k * each for k in range(n_pieces)]
    text = n_pieces * each
    end = text + 3 * heads * text_rows
    bias = blocks[0][end : end + EXTRA, :][:1, : n_cores * text_rows].astype(f32)

    def with_ones(values):
        return jnp.concatenate([values, jnp.ones(values.shape, bf16)], axis=1)

    for head in range(heads):
        kv, tkv = [], []
        for i in range(2):
            at = (i * heads + head) * rows
            image = [b[start + at : start + at + rows, :] for b in blocks for start in starts]
            text_at = text + ((i + 1) * heads + head) * text_rows
            kv.append(jnp.concatenate(image, axis=0))
            tkv.append(jnp.concatenate([b[text_at : text_at + text_rows, :] for b in blocks], axis=0))
        keys, values = kv[0], with_ones(kv[1])
        tkeys, tvalues = tkv[0], with_ones(tkv[1])
        cols = slice(head * size, (head + 1) * size)
        q_at = (2 * heads + head) * rows
        asked = []
        for k in asked_of:
            if k < n_pieces:
                asked.append(blocks[0][starts[k] + q_at : starts[k] + q_at + rows, :])
            else:
                tq_at = text + head * text_rows
                asked.append(blocks[0][tq_at : tq_at + text_rows, :])
        q = jnp.concatenate(asked, axis=0)
        s_img = lax.dot_general(q, keys, nt, preferred_element_type=f32)
        s_txt = lax.dot_general(q, tkeys, nt, preferred_element_type=f32) + bias
        top = jnp.maximum(
            jnp.max(s_img, axis=1, keepdims=True), jnp.max(s_txt, axis=1, keepdims=True)
        )
        p_img = jnp.exp2((s_img - top) * factor).astype(bf16)
        p_txt = jnp.exp2((s_txt - top) * factor).astype(bf16)
        acc = jnp.dot(p_img, values, preferred_element_type=f32)
        acc = acc + jnp.dot(p_txt, tvalues, preferred_element_type=f32)
        done = (acc[:, :size] / acc[:, size:]).astype(bf16)
        at = 0
        for out_ref in out_refs:
            out_ref[:, cols] = done[at : at + out_ref.shape[0]]
            at += out_ref.shape[0]


def attention(blocks, asked_of, after, n_pieces, heads, rows, text_rows):
    size = blocks[0].shape[1]
    counts = [rows if k < n_pieces else text_rows for k in asked_of]
    queries = sum(counts)
    keys = len(blocks) * (n_pieces * rows + text_rows)
    shapes = [jax.ShapeDtypeStruct((n, heads * size), bf16) for n in counts]
    return pl.pallas_call(
        functools.partial(
            attention_kernel,
            n_pieces,
            len(blocks),
            len(after),
            tuple(asked_of),
            heads,
            rows,
            text_rows,
        ),
        out_shape=shapes,
        in_specs=[VMEM] * len(blocks) + [ANY] * len(after),
        out_specs=[VMEM] * len(shapes),
        compiler_params=params(),
        cost_estimate=cost(
            4 * queries * keys * heads * size,
            4 * (queries + keys) * heads * size,
            queries * keys * heads,
        ),
    )(*blocks, *after)


def assemble_kernel(places, where, *refs):
    pieces, out_ref = refs[: len(places)], refs[-1]
    z = where()[0]
    rows, width = out_ref.shape[0], pieces[0].shape[1]
    for k, piece in zip(places, pieces):
        at = pl.multiple_of((z ^ k) * width, 128)
        out_ref[:, pl.ds(at, width)] = piece[:rows, :]


def assemble(where, pieces, places, after, rows):
    groups, width = len(pieces), pieces[0].shape[1]
    return pl.pallas_call(
        functools.partial(assemble_kernel, tuple(places), where),
        out_shape=jax.ShapeDtypeStruct((rows, groups * width), bf16),
        in_specs=[VMEM] * groups + [ANY] * len(after),
        out_specs=VMEM,
        compiler_params=params(),
        cost_estimate=cost(0, 4 * rows * groups * width),
    )(*pieces, *after)


def gated_kernel(groups, parts, place_of, meta_ref, gate_ref, d_out_ref, *refs):
    msgs, turned = refs[:-1], refs[-1]
    gated = (gate_ref[...] * d_out_ref[...].astype(f32)).astype(bf16)
    turned[...] = gated.astype(f32).T
    rows = msgs[0].shape[2]
    z, oc, dp = meta_ref[0], meta_ref[1], meta_ref[2]
    for k, msg in enumerate(msgs):
        for j in range(parts):
            for g in range(groups):
                at = (dp ^ k) * (groups * parts) + place_of(oc ^ j, z ^ g)
                msg[j, g] = turned[pl.ds(pl.multiple_of(at * rows, 8), rows), :].astype(bf16)


def gated_parts(meta, gate, d_out, n_dp, groups, parts, place_of):
    local, model = d_out.shape
    rows = model // (n_dp * groups * parts)
    return pl.pallas_call(
        functools.partial(gated_kernel, groups, parts, place_of),
        out_shape=[jax.ShapeDtypeStruct((parts, groups, rows, local), bf16)] * n_dp,
        in_specs=[SMEM, VMEM, VMEM],
        out_specs=[VMEM] * n_dp,
        scratch_shapes=[pltpu.VMEM((model, local), f32)],
        compiler_params=params(60),
        cost_estimate=cost(0, 4 * local * model),
    )(meta, gate, d_out)


def gather_kernel(n_dp, *refs):
    pieces, outs = refs[:n_dp], refs[n_dp:]
    for j, out in enumerate(outs):
        for k, piece in enumerate(pieces):
            out[k] = piece[j + 1]


def gather_parts(pieces):
    parts = pieces[0].shape[0]
    shape = (len(pieces),) + pieces[0].shape[1:]
    return pl.pallas_call(
        functools.partial(gather_kernel, len(pieces)),
        out_shape=[jax.ShapeDtypeStruct(shape, bf16)] * (parts - 1),
        in_specs=[VMEM] * len(pieces),
        out_specs=[VMEM] * (parts - 1),
        compiler_params=params(),
        cost_estimate=cost(0, 4 * math.prod(shape) * (parts - 1)),
    )(*pieces)


def project_kernel(
    groups, parts, place_of, meta_ref, attn_ref, w_ref, gate_ref, d_out_ref, out_ref, d_attn_ref,
    term_ref, *refs
):
    sent, by_place = refs[:-1], refs[-1]
    rows = attn_ref.shape[0]
    block = 512
    sums = []
    for at in range(0, w_ref.shape[0], block):
        cols = slice(at, at + block)
        got = lax.dot_general(
            attn_ref[...], w_ref[cols, :], (((1,), (1,)), ((), ())), preferred_element_type=f32
        )
        out_ref[:, cols] = (got * gate_ref[:, cols]).astype(bf16)
        sums.append(jnp.sum(got * d_out_ref[:, cols].astype(f32), axis=0, keepdims=True))
    total = jnp.zeros(d_attn_ref.shape, f32)
    for at in range(0, w_ref.shape[0], block):
        cols = slice(at, at + block)
        gated = (gate_ref[:, cols] * d_out_ref[:, cols].astype(f32)).astype(bf16)
        total = total + jnp.dot(gated, w_ref[cols, :], preferred_element_type=f32)
    d_attn_ref[...] = total.astype(bf16)
    sums = jnp.concatenate(sums, axis=1)
    places, width = by_place.shape
    for s in range(places):
        by_place[s : s + 1, :] = sums[:, s * width : (s + 1) * width]
    for g in range(groups):
        at = place_of(meta_ref[1], meta_ref[0] ^ g)
        term_ref[g : g + 1, :] = by_place[pl.ds(at, 1), :]
    for j, out in enumerate(sent):
        out[:rows, :] = attn_ref[...]
        line = [
            by_place[pl.ds(place_of(meta_ref[1] ^ (j + 1), meta_ref[0] ^ g), 1), :]
            for g in range(groups)
        ]
        line = jnp.concatenate(line, axis=1)
        line = jnp.concatenate(
            [line, jnp.zeros((1, attn_ref.shape[1] - groups * width), f32)], axis=1
        ) if attn_ref.shape[1] > groups * width else line
        high = line.astype(bf16).astype(f32)
        lines = [high, line - high, jnp.zeros((EXTRA - 2, line.shape[1]), f32)]
        out[rows:, :] = jnp.concatenate(lines, axis=0).astype(bf16)


def project(meta, attn, out_weight, gate, d_out, groups, parts, place_of):
    rows, inner = attn.shape
    model = out_weight.shape[0]
    width = model // (groups * parts)
    shapes = [jax.ShapeDtypeStruct((rows, model), bf16), jax.ShapeDtypeStruct((rows, inner), bf16)]
    shapes += [jax.ShapeDtypeStruct((groups, width), f32)]
    shapes += [jax.ShapeDtypeStruct((rows + EXTRA, inner), bf16)] * (parts - 1)
    return pl.pallas_call(
        functools.partial(project_kernel, groups, parts, place_of),
        out_shape=shapes,
        in_specs=[SMEM, VMEM, VMEM, VMEM, VMEM],
        out_specs=[VMEM] * (2 + parts),
        scratch_shapes=[pltpu.VMEM((groups * parts, width), f32)],
        compiler_params=params(),
        cost_estimate=cost(4 * rows * inner * model, 2 * inner * model),
    )(meta, attn, out_weight, gate, d_out)


def split_gate(gate, size):
    short = -gate.shape[1] % size
    if short:
        gate = jnp.concatenate([gate, jnp.zeros((1, short), f32)], axis=1)
    high = gate.astype(bf16).astype(f32)
    lines = [p[:, at : at + size] for p in (high, gate - high) for at in range(0, gate.shape[1], size)]
    return jnp.concatenate(lines + [jnp.zeros((EXTRA - len(lines), size), f32)], axis=0)


def joined_gate(lines, width):
    n = -(-width // lines.shape[1])
    both = lines[:n] + lines[n : 2 * n]
    return jnp.concatenate([both[i : i + 1] for i in range(n)], axis=1)[:, :width]


def grad_kernel(n_left, n_pieces, *refs):
    lefts, refs = refs[:n_left], refs[n_left:]
    pieces, refs = refs[:n_pieces], refs[n_pieces:]
    term_ref, outs = refs[0], refs[1:]
    groups, rows, depth = lefts[0].shape[1:]
    width = pieces[0].shape[1]
    size = outs[0].shape[1]
    left = []
    for ref in lefts:
        left += [ref[i].reshape(groups * rows, depth) for i in range(ref.shape[0])]
    left = jnp.concatenate(left, axis=1)
    half = outs[1].shape[0]
    homes = [((outs[0], 0),)]
    homes += [((outs[2 * g - 1], 0), (outs[2 * g], half)) for g in range(1, groups)]

    def put(g, at, value):
        out, start = homes[g][-1] if at >= half else homes[g][0]
        out[at - start : at - start + value.shape[0], :] = value.astype(out.dtype)

    block = 256
    for start in range(0, width, block):
        right = jnp.concatenate([p[:depth, start : start + block] for p in pieces], axis=0)
        got = jnp.dot(left, right, preferred_element_type=f32)
        for g in range(groups):
            for at in range(0, block, size):
                put(g, (start + at) // size * rows, got[g * rows : (g + 1) * rows, at : at + size])
    term = term_ref[...]
    each = term.shape[1]
    for p in pieces:
        if p.shape[0] > depth:
            lines = p[depth:, :].astype(f32)
            line = lines[0:1, :] + lines[1:2, :]
            term = term + jnp.concatenate(
                [line[:, g * each : (g + 1) * each] for g in range(groups)], axis=0
            )
    for g in range(groups):
        put(g, width // size * rows, split_gate(term[g : g + 1], size))


def grad_product(lefts, pieces, term):
    groups, rows, depth = lefts[0].shape[1:]
    width = pieces[0].shape[1]
    size = 128
    total = groups * rows
    depth = depth * len(pieces)
    full = width // size * rows + EXTRA
    half = width // size // 2 * rows
    shapes = [(full, f32)]
    for kind in (bf16, f32, bf16):
        shapes += [(half, kind), (full - half, kind)]
    return pl.pallas_call(
        functools.partial(grad_kernel, len(lefts), len(pieces)),
        out_shape=[jax.ShapeDtypeStruct((n, size), kind) for n, kind in shapes],
        in_specs=[VMEM] * (len(lefts) + len(pieces) + 1),
        out_specs=[VMEM] * len(shapes),
        compiler_params=params(),
        cost_estimate=cost(
            2 * total * depth * width, 2 * (total * depth + depth * width + total * width)
        ),
    )(*lefts, *pieces, term)


def pair_kernel(gate_width, n_through, own_ref, got_ref, *refs):
    out_ref = refs[n_through]
    for ref, out in zip(refs[:n_through], refs[n_through + 1 :]):
        out[...] = ref[...]
    total = own_ref[...] + got_ref[...].astype(f32)
    if not gate_width:
        out_ref[...] = total.astype(bf16)
    else:
        end = total.shape[0] - EXTRA
        out_ref[:end, :] = total[:end].astype(bf16)
        gate = joined_gate(total[end:], gate_width)
        out_ref[end:, :] = split_gate(gate, total.shape[1]).astype(bf16)


def pair_sum(own, got, gate_width, through):
    return pl.pallas_call(
        functools.partial(pair_kernel, gate_width, len(through)),
        out_shape=[jax.ShapeDtypeStruct(x.shape, bf16) for x in [got] + through],
        in_specs=[VMEM] * (2 + len(through)),
        out_specs=[VMEM] * (1 + len(through)),
        compiler_params=params(),
        cost_estimate=cost(0, 8 * own.size),
    )(own, got, *through)


def final_kernel(own_ref, far_low, far_high, near_low, near_high, out_ref, gate_ref):
    size = own_ref.shape[1]
    rows = out_ref.shape[0]
    half = far_low.shape[0]

    def total(at, count):
        refs, start = ((far_high, near_high), half) if at >= half else ((far_low, near_low), 0)
        got = own_ref[at : at + count, :]
        for ref in refs:
            got = got + ref[at - start : at - start + count, :].astype(f32)
        return got

    for i in range(out_ref.shape[1] // size):
        out_ref[:, i * size : (i + 1) * size] = total(i * rows, rows)
    gate_ref[...] = joined_gate(total(own_ref.shape[0] - EXTRA, EXTRA), gate_ref.shape[1])


def final_sum(own, far, near, rows, width, gate_width):
    return pl.pallas_call(
        final_kernel,
        out_shape=[
            jax.ShapeDtypeStruct((rows, width), f32),
            jax.ShapeDtypeStruct((1, gate_width), f32),
        ],
        in_specs=[VMEM] * 5,
        out_specs=[VMEM] * 2,
        compiler_params=params(),
        cost_estimate=cost(0, 8 * rows * width),
    )(own, *far, *near)


def on_device(
    caption_states,
    caption_gain,
    text_proj,
    caption_len,
    slot_source,
    query_gain,
    key_gain,
    image_q,
    image_k,
    image_v,
    out_weight,
    gate,
    d_out,
):
    n_dp = lax.axis_size("dp")
    n_seq = lax.axis_size("seq")
    G, C = GROUPS, CORES
    O = n_seq // (G * C)
    OC = O * C
    dp = lax.axis_index("dp")
    seq = lax.axis_index("seq")

    def where():
        at = lax.axis_index("seq")
        return (at // C) % G, (at // (G * C)) * C + at % C

    z, oc = where()

    def place(oc_at, z_at):
        return ((oc_at // C) * G + z_at) * C + oc_at % C

    def to_z(x, k):
        perm = [(place(a, b), place(a, b ^ k)) for a in range(OC) for b in range(G)]
        return lax.ppermute(x, "seq", perm)

    def to_oc(x, j):
        perm = [(place(a, b), place(a ^ j, b)) for a in range(OC) for b in range(G)]
        return lax.ppermute(x, "seq", perm)

    def to_dp(x, k):
        return lax.ppermute(x, "dp", [(a, a ^ k) for a in range(n_dp)])

    def part(x, index, size, axis):
        return lax.dynamic_slice_in_dim(x, index * size, size, axis)

    slot_total = slot_source.shape[1]
    slot_local = slot_total // n_seq
    image_local = image_q.shape[1]
    inner_width = image_q.shape[2]
    model_width = out_weight.shape[0]
    head_size = query_gain.shape[0]
    gw = inner_width // G
    order = [2, 3, 1]
    meta = jnp.stack([z, oc, dp]).astype(jnp.int32)

    heads = gw // head_size
    text_rows = G * slot_local
    own, *rest = text_project(
        caption_len, slot_source, caption_states[0], caption_gain[None],
        query_gain[None], key_gain[None], image_k[0], image_v[0], image_q[0], text_proj,
        G, OC, place, where,
    )
    packed, sent = rest[:G], rest[G:]
    images = {0: packed[0]}
    for k in order:
        images[k] = to_z(packed[k], k)
    images = [images[k] for k in [0] + order]
    got = [to_oc(x, j + 1) for j, x in enumerate(sent)]
    own, sent = text_sum(own, got, text_rows)
    own, sent = text_sum(own, [to_z(sent, 1)], text_rows)
    got = to_z(sent, 2)

    gg = gated_parts(meta, gate, d_out[0], n_dp, G, OC, place)
    gg_dp = [gg[0], to_dp(gg[1], 1)]
    block = block_of(own, got, gg_dp[1:], images, DT5, heads)
    blocks = [block] + [to_oc(block, j) for j in range(1, OC)]
    *first, text_out = attention(
        blocks, [1, 2, G], [], G, heads, image_local, text_rows
    )
    second = attention(
        blocks, [3, 0], [text_out], G, heads, image_local, text_rows
    )
    outs = dict(zip(order + [0], first + list(second)))

    back = {}
    for k in order + [0]:
        rows = jnp.concatenate([outs[k], part(text_out, z ^ k, slot_local, 0)], axis=0)
        back[k] = to_z(rows, k) if k else rows
    back = [back[k] for k in order + [0]]
    gg_dp += [to_dp(gg[k], k) for k in range(2, n_dp)]
    lefts = [g[:1] for g in gg_dp]
    lefts += [to_oc(g, j + 1) for j, g in enumerate(gather_parts(gg_dp))]
    image_attn = assemble(where, back, order + [0], gg_dp[1:], image_local)
    text_attn = jnp.zeros((slot_local, inner_width), bf16)
    own_usable = part(slot_source[0] < caption_len[0], seq, slot_local, 0)
    for k, got in zip(order + [0], back):
        rows = jnp.where(own_usable[:, None], got[image_local:], jnp.zeros((), bf16))
        text_attn = lax.dynamic_update_slice_in_dim(text_attn, rows, (z ^ k) * gw, 1)

    pieces = [image_attn] + [to_dp(image_attn, k) for k in range(1, n_dp)]
    image_out, d_attn, term, *sent = project(
        meta, image_attn, out_weight, gate, d_out[0], G, OC, place
    )
    for j in range(1, OC):
        pieces += [to_oc(sent[j - 1], j)] + [to_oc(p, j) for p in pieces[1:n_dp]]
    R = model_width // (n_dp * n_seq)
    gate_width = model_width // n_seq
    own, *blocks = grad_product(lefts, pieces, term)
    got = [to_z(x, 1) for x in blocks[4:]]
    (low,) = pair_sum(blocks[2], got[0], 0, [])
    high, *near = pair_sum(blocks[3], got[1], gate_width, blocks[:2])
    far = [to_z(x, 2) for x in (low, high)]
    near = [to_z(x, 1) for x in near]
    grad_wo, grad_gate = final_sum(own, far, near, R, inner_width, gate_width)
    return (image_out[None], text_attn[None], d_attn[None], grad_wo, grad_gate)


def solution(mesh):
    in_specs = (
        P("dp", None, "seq"),
        P("seq"),
        P("seq", None),
        P("dp"),
        P("dp", None),
        P(),
        P(),
        P("dp", "seq", None),
        P("dp", "seq", None),
        P("dp", "seq", None),
        P(),
        P("dp", None),
        P("dp", "seq", None),
    )
    out_specs = (
        P("dp", "seq", None),
        P("dp", "seq", None),
        P("dp", "seq", None),
        P(("dp", "seq"), None),
        P("dp", "seq"),
    )
    return jax.shard_map(
        on_device, mesh=mesh, in_specs=in_specs, out_specs=out_specs, check_vma=False
    )
```

```python
import math
import functools
import jax
import jax.numpy as jnp
from jax import lax
from jax.experimental import pallas as pl
from jax.experimental.pallas import tpu as pltpu
from jax.sharding import PartitionSpec as P

DT5 = 4096
CORES = 2
GROUPS = 4

eps_norm = 1e-06
f32 = jnp.float32
bf16 = jnp.bfloat16
EXTRA = 16


VMEM = pl.BlockSpec(memory_space=pltpu.VMEM)
SMEM = pl.BlockSpec(memory_space=pltpu.SMEM)
ANY = pl.BlockSpec(memory_space=pl.ANY)


def params(mib=16):
    return pltpu.CompilerParams(vmem_limit_bytes=int(mib * 1024 * 1024))


def cost(flops, bytes_accessed, transcendentals=0):
    return pl.CostEstimate(
        flops=flops, bytes_accessed=bytes_accessed, transcendentals=transcendentals
    )


def split_tail(squares, width):
    high = squares.astype(bf16).astype(f32)
    low = squares - high
    lane = lax.broadcasted_iota(jnp.int32, (squares.shape[0], width), 1)
    return jnp.where(lane == 0, high, jnp.where(lane == 1, low, 0.0))


def joined(tail):
    return tail[:, 0:1] + tail[:, 1:2]


def text_kernel(
    groups, heads, place_of, where, len_ref, src_ref, states_ref, gain_ref, qg_ref, kg_ref,
    k_ref, v_ref, q_ref, w_ref, own_ref, *refs
):
    meta_ref = where()
    packed, refs = refs[:groups], refs[groups:]
    msgs, (w_all, sums, loaded, stage, w_sems, in_sems, out_sems) = refs[:-7], refs[-7:]
    size = own_ref.shape[2]
    rows = (own_ref.shape[1] - EXTRA) // (3 * heads + 1)
    width = heads * size
    slots = states_ref.shape[0]
    slot_local = rows // groups
    copies = []
    block = w_all.shape[0] // w_sems.shape[0]
    for i in range(w_sems.shape[0]):
        part = pl.ds(i * block, block)
        copies.append(pltpu.make_async_copy(w_ref.at[part], w_all.at[part], w_sems.at[i]))
        copies[-1].start()
    loads = []
    for i, ref in enumerate((k_ref, v_ref, q_ref)):
        loads.append(pltpu.make_async_copy(ref, loaded.at[i], in_sems.at[i]))
        loads[-1].start()

    def slot_at(row):
        z_at = (row % rows) // slot_local
        return place_of(meta_ref[1] ^ (row // rows), z_at) * slot_local + row % slot_local

    iota = functools.partial(lax.broadcasted_iota, jnp.int32, (slots, slots))
    sources = src_ref[...].astype(f32)
    chosen = (iota(1) == slot_at(iota(0))).astype(f32)
    source_col = jnp.sum(chosen * sources, axis=1, keepdims=True)
    pick = (iota(1).astype(f32) == source_col).astype(bf16)
    chosen_t = (iota(0) == slot_at(iota(1))).astype(bf16)
    source_row = jnp.dot(sources.astype(bf16), chosen_t, preferred_element_type=f32)
    bias = jnp.where(source_row < len_ref[0].astype(f32), 0.0, -1e30)
    end = own_ref.shape[1] - EXTRA
    own_ref[0, end:, :] = jnp.zeros((EXTRA, size), f32)
    own_ref[0, end : end + 1, :] = qg_ref[...]
    own_ref[0, end + 1 : end + 2, :] = kg_ref[...]
    own_ref[0, end + 2 : end + 3, :slots] = bias

    picked = jnp.dot(pick, states_ref[...], preferred_element_type=f32)
    scaled = (picked * gain_ref[...]).astype(bf16)
    tail = split_tail(jnp.sum(picked * picked, axis=1, keepdims=True), size)
    for copy in loads:
        copy.wait()
    local = loaded.shape[1]
    stores = []
    for g in range(groups):
        for i in range(3):
            for head in range(heads):
                at = ((meta_ref[0] ^ g) * heads + head) * size
                to = (i * heads + head) * local
                stage[g, to : to + local, :] = loaded[i, :, pl.ds(pl.multiple_of(at, 128), size)]
        stores.append(pltpu.make_async_copy(stage.at[g], packed[g], out_sems.at[g]))
        stores[-1].start()
    def product(part, g, i):
        at = (i * groups + (meta_ref[0] ^ g)) * width
        columns = pl.ds(pl.multiple_of(at, 128), width)
        rows_of = slice(part * block, (part + 1) * block)
        return jnp.dot(scaled[:, rows_of], w_all[rows_of, columns], preferred_element_type=f32)

    copies[0].wait()
    for g in range(groups):
        for i in range(3):
            sums[3 * g + i] = product(0, g, i)
    copies[1].wait()
    for g in range(groups):
        for i in range(3):
            got = sums[3 * g + i] + product(1, g, i)
            for head in range(heads):
                part = got[:, head * size : (head + 1) * size]
                to = slice((i * heads + head) * rows, (i * heads + head + 1) * rows)
                own_ref[g, to, :] = part[:rows]
                for j, msg in enumerate(msgs):
                    msg[g, to, :] = part[(j + 1) * rows : (j + 2) * rows].astype(bf16)
        own_ref[g, 3 * heads * rows : end, :] = tail[:rows]
        for j, msg in enumerate(msgs):
            msg[g, 3 * heads * rows :, :] = tail[(j + 1) * rows : (j + 2) * rows].astype(bf16)
    for copy in stores:
        copy.wait()


def text_project(
    length, sources, states, gain, query_gain, key_gain, keys, values, queries, text_proj,
    groups, parts, place_of, where
):
    slots, depth = states.shape
    size = query_gain.shape[1]
    heads = text_proj.shape[1] // (3 * groups * size)
    text_rows = (3 * heads + 1) * slots // parts
    shapes = [jax.ShapeDtypeStruct((groups, text_rows + EXTRA, size), f32)]
    shapes += [jax.ShapeDtypeStruct((3 * heads * keys.shape[0], size), bf16)] * groups
    shapes += [jax.ShapeDtypeStruct((groups, text_rows, size), bf16)] * (parts - 1)
    return pl.pallas_call(
        functools.partial(text_kernel, groups, heads, place_of, where),
        out_shape=shapes,
        in_specs=[SMEM] + [VMEM] * 5 + [ANY] * 4,
        out_specs=[VMEM] + [ANY] * groups + [VMEM] * (parts - 1),
        scratch_shapes=[
            pltpu.VMEM(text_proj.shape, bf16),
            pltpu.VMEM((3 * groups, slots, heads * size), f32),
            pltpu.VMEM((3,) + keys.shape, bf16),
            pltpu.VMEM((groups, 3 * heads * keys.shape[0], size), bf16),
            pltpu.SemaphoreType.DMA((2,)),
            pltpu.SemaphoreType.DMA((3,)),
            pltpu.SemaphoreType.DMA((groups,)),
        ],
        compiler_params=params(60),
        cost_estimate=cost(
            2 * slots * depth * text_proj.shape[1], 2 * depth * text_proj.shape[1]
        ),
    )(
        length, sources, states, gain, query_gain, key_gain, keys, values, queries, text_proj
    )


def text_sum_kernel(n_got, tail_rows, own_ref, *refs):
    got, (keep_ref, send_ref) = refs[:n_got], refs[n_got:]
    groups, text_rows, size = got[0].shape
    for g in range(groups):
        total = own_ref[g, :text_rows, :]
        for ref in got:
            total = total + ref[g].astype(f32)
        end = text_rows - tail_rows
        tail = split_tail(joined(total[end:]), size)
        if g % 2 == 0:
            keep_ref[g // 2, :end, :] = total[:end]
            keep_ref[g // 2, end:text_rows, :] = tail
            keep_ref[g // 2, text_rows:, :] = own_ref[g, text_rows:, :]
        else:
            send_ref[g // 2, :end, :] = total[:end].astype(bf16)
            send_ref[g // 2, end:, :] = tail.astype(bf16)


def text_sum(own, got, tail_rows):
    groups, rows, size = own.shape
    return pl.pallas_call(
        functools.partial(text_sum_kernel, len(got), tail_rows),
        out_shape=[
            jax.ShapeDtypeStruct((groups // 2, rows, size), f32),
            jax.ShapeDtypeStruct((groups // 2, rows - EXTRA, size), bf16),
        ],
        in_specs=[VMEM] * (1 + len(got)),
        out_specs=[VMEM] * 2,
        compiler_params=params(),
        cost_estimate=cost(0, 8 * groups * rows * size),
    )(own, *got)


def block_kernel(features, heads, n_pieces, own_ref, got_ref, *refs):
    pieces, out_ref = refs[:n_pieces], refs[-1]
    each = pieces[0].shape[0]
    for k, ref in enumerate(pieces):
        out_ref[k * each : (k + 1) * each, :] = ref[...]
    size = own_ref.shape[2]
    text_rows = got_ref.shape[1]
    rows = text_rows // (3 * heads + 1)
    total = own_ref[0, :text_rows, :] + got_ref[0].astype(f32)
    rate = lax.rsqrt(joined(total[3 * heads * rows :]) / features + eps_norm)
    start = n_pieces * each
    for i in range(3):
        for head in range(heads):
            at = (i * heads + head) * rows
            x = total[at : at + rows] * rate
            if i < 2:
                mean = jnp.sum(x * x, axis=1, keepdims=True) / size
                gain = own_ref[0, text_rows + i : text_rows + i + 1, :]
                x = x * lax.rsqrt(mean + eps_norm) * gain
            out_ref[start + at : start + at + rows, :] = x.astype(bf16)
    bias = own_ref[0, text_rows + 2 : text_rows + 3, :]
    start = start + 3 * heads * rows
    out_ref[start:, :] = jnp.broadcast_to(bias, (EXTRA, size)).astype(bf16)


def block_of(own, got, after, pieces, features, heads):
    rows, size = own.shape[1:]
    total = (rows - EXTRA) // (3 * heads + 1) * 3 * heads + EXTRA
    total += pieces[0].shape[0] * len(pieces)
    return pl.pallas_call(
        functools.partial(block_kernel, features, heads, len(pieces)),
        out_shape=jax.ShapeDtypeStruct((total, size), bf16),
        in_specs=[VMEM] * (2 + len(pieces)) + [ANY] * len(after),
        out_specs=VMEM,
        compiler_params=params(),
        cost_estimate=cost(0, 4 * total * size),
    )(own, got, *pieces, *after)


def attention_kernel(n_pieces, n_cores, n_after, asked_of, heads, rows, text_rows, *refs):
    blocks, out_refs = refs[:n_cores], refs[n_cores + n_after :]
    size = blocks[0].shape[1]
    factor = size ** (-0.5) * math.log2(math.e)
    nt = (((1,), (1,)), ((), ()))
    each = 3 * heads * rows
    starts = [k * each for k in range(n_pieces)]
    text = n_pieces * each
    end = text + 3 * heads * text_rows
    bias = blocks[0][end : end + EXTRA, :][:1, : n_cores * text_rows].astype(f32)

    def with_ones(values):
        return jnp.concatenate([values, jnp.ones(values.shape, bf16)], axis=1)

    for head in range(heads):
        kv, tkv = [], []
        for i in range(2):
            at = (i * heads + head) * rows
            image = [b[start + at : start + at + rows, :] for b in blocks for start in starts]
            text_at = text + ((i + 1) * heads + head) * text_rows
            kv.append(jnp.concatenate(image, axis=0))
            tkv.append(jnp.concatenate([b[text_at : text_at + text_rows, :] for b in blocks], axis=0))
        keys, values = kv[0], with_ones(kv[1])
        tkeys, tvalues = tkv[0], with_ones(tkv[1])
        cols = slice(head * size, (head + 1) * size)
        q_at = (2 * heads + head) * rows
        asked = []
        for k in asked_of:
            if k < n_pieces:
                asked.append(blocks[0][starts[k] + q_at : starts[k] + q_at + rows, :])
            else:
                tq_at = text + head * text_rows
                asked.append(blocks[0][tq_at : tq_at + text_rows, :])
        q = jnp.concatenate(asked, axis=0)
        s_img = lax.dot_general(q, keys, nt, preferred_element_type=f32)
        s_txt = lax.dot_general(q, tkeys, nt, preferred_element_type=f32) + bias
        top = jnp.maximum(
            jnp.max(s_img, axis=1, keepdims=True), jnp.max(s_txt, axis=1, keepdims=True)
        )
        p_img = jnp.exp2((s_img - top) * factor).astype(bf16)
        p_txt = jnp.exp2((s_txt - top) * factor).astype(bf16)
        acc = jnp.dot(p_img, values, preferred_element_type=f32)
        acc = acc + jnp.dot(p_txt, tvalues, preferred_element_type=f32)
        done = (acc[:, :size] / acc[:, size:]).astype(bf16)
        at = 0
        for out_ref in out_refs:
            out_ref[:, cols] = done[at : at + out_ref.shape[0]]
            at += out_ref.shape[0]


def attention(blocks, asked_of, after, n_pieces, heads, rows, text_rows):
    size = blocks[0].shape[1]
    counts = [rows if k < n_pieces else text_rows for k in asked_of]
    queries = sum(counts)
    keys = len(blocks) * (n_pieces * rows + text_rows)
    shapes = [jax.ShapeDtypeStruct((n, heads * size), bf16) for n in counts]
    return pl.pallas_call(
        functools.partial(
            attention_kernel,
            n_pieces,
            len(blocks),
            len(after),
            tuple(asked_of),
            heads,
            rows,
            text_rows,
        ),
        out_shape=shapes,
        in_specs=[VMEM] * len(blocks) + [ANY] * len(after),
        out_specs=[VMEM] * len(shapes),
        compiler_params=params(),
        cost_estimate=cost(
            4 * queries * keys * heads * size,
            4 * (queries + keys) * heads * size,
            queries * keys * heads,
        ),
    )(*blocks, *after)


def assemble_kernel(places, where, *refs):
    pieces, out_ref = refs[: len(places)], refs[-1]
    z = where()[0]
    rows, width = out_ref.shape[0], pieces[0].shape[1]
    for k, piece in zip(places, pieces):
        at = pl.multiple_of((z ^ k) * width, 128)
        out_ref[:, pl.ds(at, width)] = piece[:rows, :]


def assemble(where, pieces, places, after, rows):
    groups, width = len(pieces), pieces[0].shape[1]
    return pl.pallas_call(
        functools.partial(assemble_kernel, tuple(places), where),
        out_shape=jax.ShapeDtypeStruct((rows, groups * width), bf16),
        in_specs=[VMEM] * groups + [ANY] * len(after),
        out_specs=VMEM,
        compiler_params=params(),
        cost_estimate=cost(0, 4 * rows * groups * width),
    )(*pieces, *after)


def gated_kernel(groups, parts, place_of, meta_ref, gate_ref, d_out_ref, *refs):
    msgs, turned = refs[:-1], refs[-1]
    gated = (gate_ref[...] * d_out_ref[...].astype(f32)).astype(bf16)
    turned[...] = gated.astype(f32).T
    rows = msgs[0].shape[2]
    z, oc, dp = meta_ref[0], meta_ref[1], meta_ref[2]
    for k, msg in enumerate(msgs):
        for j in range(parts):
            for g in range(groups):
                at = (dp ^ k) * (groups * parts) + place_of(oc ^ j, z ^ g)
                msg[j, g] = turned[pl.ds(pl.multiple_of(at * rows, 8), rows), :].astype(bf16)


def gated_parts(meta, gate, d_out, n_dp, groups, parts, place_of):
    local, model = d_out.shape
    rows = model // (n_dp * groups * parts)
    return pl.pallas_call(
        functools.partial(gated_kernel, groups, parts, place_of),
        out_shape=[jax.ShapeDtypeStruct((parts, groups, rows, local), bf16)] * n_dp,
        in_specs=[SMEM, VMEM, VMEM],
        out_specs=[VMEM] * n_dp,
        scratch_shapes=[pltpu.VMEM((model, local), f32)],
        compiler_params=params(60),
        cost_estimate=cost(0, 4 * local * model),
    )(meta, gate, d_out)


def gather_kernel(n_dp, *refs):
    pieces, outs = refs[:n_dp], refs[n_dp:]
    for j, out in enumerate(outs):
        for k, piece in enumerate(pieces):
            out[k] = piece[j + 1]


def gather_parts(pieces):
    parts = pieces[0].shape[0]
    shape = (len(pieces),) + pieces[0].shape[1:]
    return pl.pallas_call(
        functools.partial(gather_kernel, len(pieces)),
        out_shape=[jax.ShapeDtypeStruct(shape, bf16)] * (parts - 1),
        in_specs=[VMEM] * len(pieces),
        out_specs=[VMEM] * (parts - 1),
        compiler_params=params(),
        cost_estimate=cost(0, 4 * math.prod(shape) * (parts - 1)),
    )(*pieces)


def project_kernel(
    groups, parts, place_of, meta_ref, attn_ref, w_ref, gate_ref, d_out_ref, out_ref, d_attn_ref,
    term_ref, *refs
):
    sent, by_place = refs[:-1], refs[-1]
    rows = attn_ref.shape[0]
    block = 512
    sums = []
    for at in range(0, w_ref.shape[0], block):
        cols = slice(at, at + block)
        got = lax.dot_general(
            attn_ref[...], w_ref[cols, :], (((1,), (1,)), ((), ())), preferred_element_type=f32
        )
        out_ref[:, cols] = (got * gate_ref[:, cols]).astype(bf16)
        sums.append(jnp.sum(got * d_out_ref[:, cols].astype(f32), axis=0, keepdims=True))
    total = jnp.zeros(d_attn_ref.shape, f32)
    for at in range(0, w_ref.shape[0], block):
        cols = slice(at, at + block)
        gated = (gate_ref[:, cols] * d_out_ref[:, cols].astype(f32)).astype(bf16)
        total = total + jnp.dot(gated, w_ref[cols, :], preferred_element_type=f32)
    d_attn_ref[...] = total.astype(bf16)
    sums = jnp.concatenate(sums, axis=1)
    places, width = by_place.shape
    for s in range(places):
        by_place[s : s + 1, :] = sums[:, s * width : (s + 1) * width]
    for g in range(groups):
        at = place_of(meta_ref[1], meta_ref[0] ^ g)
        term_ref[g : g + 1, :] = by_place[pl.ds(at, 1), :]
    for j, out in enumerate(sent):
        out[:rows, :] = attn_ref[...]
        line = [
            by_place[pl.ds(place_of(meta_ref[1] ^ (j + 1), meta_ref[0] ^ g), 1), :]
            for g in range(groups)
        ]
        line = jnp.concatenate(line, axis=1)
        line = jnp.concatenate(
            [line, jnp.zeros((1, attn_ref.shape[1] - groups * width), f32)], axis=1
        ) if attn_ref.shape[1] > groups * width else line
        high = line.astype(bf16).astype(f32)
        lines = [high, line - high, jnp.zeros((EXTRA - 2, line.shape[1]), f32)]
        out[rows:, :] = jnp.concatenate(lines, axis=0).astype(bf16)


def project(meta, attn, out_weight, gate, d_out, groups, parts, place_of):
    rows, inner = attn.shape
    model = out_weight.shape[0]
    width = model // (groups * parts)
    shapes = [jax.ShapeDtypeStruct((rows, model), bf16), jax.ShapeDtypeStruct((rows, inner), bf16)]
    shapes += [jax.ShapeDtypeStruct((groups, width), f32)]
    shapes += [jax.ShapeDtypeStruct((rows + EXTRA, inner), bf16)] * (parts - 1)
    return pl.pallas_call(
        functools.partial(project_kernel, groups, parts, place_of),
        out_shape=shapes,
        in_specs=[SMEM, VMEM, VMEM, VMEM, VMEM],
        out_specs=[VMEM] * (2 + parts),
        scratch_shapes=[pltpu.VMEM((groups * parts, width), f32)],
        compiler_params=params(),
        cost_estimate=cost(4 * rows * inner * model, 2 * inner * model),
    )(meta, attn, out_weight, gate, d_out)


def split_gate(gate, size):
    short = -gate.shape[1] % size
    if short:
        gate = jnp.concatenate([gate, jnp.zeros((1, short), f32)], axis=1)
    high = gate.astype(bf16).astype(f32)
    lines = [p[:, at : at + size] for p in (high, gate - high) for at in range(0, gate.shape[1], size)]
    return jnp.concatenate(lines + [jnp.zeros((EXTRA - len(lines), size), f32)], axis=0)


def joined_gate(lines, width):
    n = -(-width // lines.shape[1])
    both = lines[:n] + lines[n : 2 * n]
    return jnp.concatenate([both[i : i + 1] for i in range(n)], axis=1)[:, :width]


def grad_kernel(n_left, n_pieces, *refs):
    lefts, refs = refs[:n_left], refs[n_left:]
    pieces, refs = refs[:n_pieces], refs[n_pieces:]
    term_ref, outs = refs[0], refs[1:]
    groups, rows, depth = lefts[0].shape[1:]
    width = pieces[0].shape[1]
    size = outs[0].shape[1]
    left = []
    for ref in lefts:
        left += [ref[i].reshape(groups * rows, depth) for i in range(ref.shape[0])]
    left = jnp.concatenate(left, axis=1)
    half = outs[1].shape[0]
    homes = [((outs[0], 0),)]
    homes += [((outs[2 * g - 1], 0), (outs[2 * g], half)) for g in range(1, groups)]

    def put(g, at, value):
        out, start = homes[g][-1] if at >= half else homes[g][0]
        out[at - start : at - start + value.shape[0], :] = value.astype(out.dtype)

    block = 256
    for start in range(0, width, block):
        right = jnp.concatenate([p[:depth, start : start + block] for p in pieces], axis=0)
        got = jnp.dot(left, right, preferred_element_type=f32)
        for g in range(groups):
            for at in range(0, block, size):
                put(g, (start + at) // size * rows, got[g * rows : (g + 1) * rows, at : at + size])
    term = term_ref[...]
    each = term.shape[1]
    for p in pieces:
        if p.shape[0] > depth:
            lines = p[depth:, :].astype(f32)
            line = lines[0:1, :] + lines[1:2, :]
            term = term + jnp.concatenate(
                [line[:, g * each : (g + 1) * each] for g in range(groups)], axis=0
            )
    for g in range(groups):
        put(g, width // size * rows, split_gate(term[g : g + 1], size))


def grad_product(lefts, pieces, term):
    groups, rows, depth = lefts[0].shape[1:]
    width = pieces[0].shape[1]
    size = 128
    total = groups * rows
    depth = depth * len(pieces)
    full = width // size * rows + EXTRA
    half = width // size // 2 * rows
    shapes = [(full, f32)]
    for kind in (bf16, f32, bf16):
        shapes += [(half, kind), (full - half, kind)]
    return pl.pallas_call(
        functools.partial(grad_kernel, len(lefts), len(pieces)),
        out_shape=[jax.ShapeDtypeStruct((n, size), kind) for n, kind in shapes],
        in_specs=[VMEM] * (len(lefts) + len(pieces) + 1),
        out_specs=[VMEM] * len(shapes),
        compiler_params=params(),
        cost_estimate=cost(
            2 * total * depth * width, 2 * (total * depth + depth * width + total * width)
        ),
    )(*lefts, *pieces, term)


def pair_kernel(gate_width, n_through, own_ref, got_ref, *refs):
    out_ref = refs[n_through]
    for ref, out in zip(refs[:n_through], refs[n_through + 1 :]):
        out[...] = ref[...]
    total = own_ref[...] + got_ref[...].astype(f32)
    if not gate_width:
        out_ref[...] = total.astype(bf16)
    else:
        end = total.shape[0] - EXTRA
        out_ref[:end, :] = total[:end].astype(bf16)
        gate = joined_gate(total[end:], gate_width)
        out_ref[end:, :] = split_gate(gate, total.shape[1]).astype(bf16)


def pair_sum(own, got, gate_width, through):
    return pl.pallas_call(
        functools.partial(pair_kernel, gate_width, len(through)),
        out_shape=[jax.ShapeDtypeStruct(x.shape, bf16) for x in [got] + through],
        in_specs=[VMEM] * (2 + len(through)),
        out_specs=[VMEM] * (1 + len(through)),
        compiler_params=params(),
        cost_estimate=cost(0, 8 * own.size),
    )(own, got, *through)


def final_kernel(own_ref, far_low, far_high, near_low, near_high, out_ref, gate_ref):
    size = own_ref.shape[1]
    rows = out_ref.shape[0]
    half = far_low.shape[0]

    def total(at, count):
        refs, start = ((far_high, near_high), half) if at >= half else ((far_low, near_low), 0)
        got = own_ref[at : at + count, :]
        for ref in refs:
            got = got + ref[at - start : at - start + count, :].astype(f32)
        return got

    for i in range(out_ref.shape[1] // size):
        out_ref[:, i * size : (i + 1) * size] = total(i * rows, rows)
    gate_ref[...] = joined_gate(total(own_ref.shape[0] - EXTRA, EXTRA), gate_ref.shape[1])


def final_sum(own, far, near, rows, width, gate_width):
    return pl.pallas_call(
        final_kernel,
        out_shape=[
            jax.ShapeDtypeStruct((rows, width), f32),
            jax.ShapeDtypeStruct((1, gate_width), f32),
        ],
        in_specs=[VMEM] * 5,
        out_specs=[VMEM] * 2,
        compiler_params=params(),
        cost_estimate=cost(0, 8 * rows * width),
    )(own, *far, *near)


def on_device(
    caption_states,
    caption_gain,
    text_proj,
    caption_len,
    slot_source,
    query_gain,
    key_gain,
    image_q,
    image_k,
    image_v,
    out_weight,
    gate,
    d_out,
):
    n_dp = lax.axis_size("dp")
    n_seq = lax.axis_size("seq")
    G, C = GROUPS, CORES
    O = n_seq // (G * C)
    OC = O * C
    dp = lax.axis_index("dp")
    seq = lax.axis_index("seq")

    def where():
        at = lax.axis_index("seq")
        return (at // C) % G, (at // (G * C)) * C + at % C

    z, oc = where()

    def place(oc_at, z_at):
        return ((oc_at // C) * G + z_at) * C + oc_at % C

    def to_z(x, k):
        perm = [(place(a, b), place(a, b ^ k)) for a in range(OC) for b in range(G)]
        return lax.ppermute(x, "seq", perm)

    def to_oc(x, j):
        perm = [(place(a, b), place(a ^ j, b)) for a in range(OC) for b in range(G)]
        return lax.ppermute(x, "seq", perm)

    def to_dp(x, k):
        return lax.ppermute(x, "dp", [(a, a ^ k) for a in range(n_dp)])

    def part(x, index, size, axis):
        return lax.dynamic_slice_in_dim(x, index * size, size, axis)

    slot_total = slot_source.shape[1]
    slot_local = slot_total // n_seq
    image_local = image_q.shape[1]
    inner_width = image_q.shape[2]
    model_width = out_weight.shape[0]
    head_size = query_gain.shape[0]
    gw = inner_width // G
    order = [2, 3, 1]
    meta = jnp.stack([z, oc, dp]).astype(jnp.int32)

    heads = gw // head_size
    text_rows = G * slot_local
    own, *rest = text_project(
        caption_len, slot_source, caption_states[0], caption_gain[None],
        query_gain[None], key_gain[None], image_k[0], image_v[0], image_q[0], text_proj,
        G, OC, place, where,
    )
    packed, sent = rest[:G], rest[G:]
    images = {0: packed[0]}
    for k in order:
        images[k] = to_z(packed[k], k)
    images = [images[k] for k in [0] + order]
    got = [to_oc(x, j + 1) for j, x in enumerate(sent)]
    own, sent = text_sum(own, got, text_rows)
    own, sent = text_sum(own, [to_z(sent, 1)], text_rows)
    got = to_z(sent, 2)

    gg = gated_parts(meta, gate, d_out[0], n_dp, G, OC, place)
    gg_dp = [gg[0], to_dp(gg[1], 1)]
    block = block_of(own, got, gg_dp[1:], images, DT5, heads)
    blocks = [block] + [to_oc(block, j) for j in range(1, OC)]
    *first, text_out = attention(
        blocks, [1, 2, G], [], G, heads, image_local, text_rows
    )
    second = attention(
        blocks, [3, 0], [text_out], G, heads, image_local, text_rows
    )
    outs = dict(zip(order + [0], first + list(second)))

    back = {}
    for k in order + [0]:
        rows = jnp.concatenate([outs[k], part(text_out, z ^ k, slot_local, 0)], axis=0)
        back[k] = to_z(rows, k) if k else rows
    back = [back[k] for k in order + [0]]
    gg_dp += [to_dp(gg[k], k) for k in range(2, n_dp)]
    dp_order = [0] + list(range(n_dp - 1, 0, -1))
    lefts = [gg_dp[k][:1] for k in dp_order]
    lefts += [to_oc(g, j + 1) for j, g in enumerate(gather_parts([gg_dp[k] for k in dp_order]))]
    image_attn = assemble(where, back, order + [0], gg_dp[1:], image_local)
    text_attn = jnp.zeros((slot_local, inner_width), bf16)
    own_usable = part(slot_source[0] < caption_len[0], seq, slot_local, 0)
    for k, got in zip(order + [0], back):
        rows = jnp.where(own_usable[:, None], got[image_local:], jnp.zeros((), bf16))
        text_attn = lax.dynamic_update_slice_in_dim(text_attn, rows, (z ^ k) * gw, 1)

    pieces = [image_attn] + [to_dp(image_attn, k) for k in dp_order[1:]]
    image_out, d_attn, term, *sent = project(
        meta, image_attn, out_weight, gate, d_out[0], G, OC, place
    )
    for j in range(1, OC):
        pieces += [to_oc(sent[j - 1], j)] + [to_oc(p, j) for p in pieces[1:n_dp]]
    R = model_width // (n_dp * n_seq)
    gate_width = model_width // n_seq
    own, *blocks = grad_product(lefts, pieces, term)
    got = [to_z(x, 1) for x in blocks[4:]]
    (low,) = pair_sum(blocks[2], got[0], 0, [])
    high, *near = pair_sum(blocks[3], got[1], gate_width, blocks[:2])
    far = [to_z(x, 2) for x in (low, high)]
    near = [to_z(x, 1) for x in near]
    grad_wo, grad_gate = final_sum(own, far, near, R, inner_width, gate_width)
    return (image_out[None], text_attn[None], d_attn[None], grad_wo, grad_gate)


def solution(mesh):
    in_specs = (
        P("dp", None, "seq"),
        P("seq"),
        P("seq", None),
        P("dp"),
        P("dp", None),
        P(),
        P(),
        P("dp", "seq", None),
        P("dp", "seq", None),
        P("dp", "seq", None),
        P(),
        P("dp", None),
        P("dp", "seq", None),
    )
    out_specs = (
        P("dp", "seq", None),
        P("dp", "seq", None),
        P("dp", "seq", None),
        P(("dp", "seq"), None),
        P("dp", "seq"),
    )
    return jax.shard_map(
        on_device, mesh=mesh, in_specs=in_specs, out_specs=out_specs, check_vma=False
    )
```

```python
import math
import functools
import jax
import jax.numpy as jnp
from jax import lax
from jax.experimental import pallas as pl
from jax.experimental.pallas import tpu as pltpu
from jax.sharding import PartitionSpec as P

DT5 = 4096
CORES = 2
GROUPS = 4

eps_norm = 1e-06
f32 = jnp.float32
bf16 = jnp.bfloat16
EXTRA = 16


VMEM = pl.BlockSpec(memory_space=pltpu.VMEM)
SMEM = pl.BlockSpec(memory_space=pltpu.SMEM)
ANY = pl.BlockSpec(memory_space=pl.ANY)


def params(mib=16):
    return pltpu.CompilerParams(vmem_limit_bytes=int(mib * 1024 * 1024))


def cost(flops, bytes_accessed, transcendentals=0):
    return pl.CostEstimate(
        flops=flops, bytes_accessed=bytes_accessed, transcendentals=transcendentals
    )


def split_tail(squares, width):
    high = squares.astype(bf16).astype(f32)
    low = squares - high
    lane = lax.broadcasted_iota(jnp.int32, (squares.shape[0], width), 1)
    return jnp.where(lane == 0, high, jnp.where(lane == 1, low, 0.0))


def joined(tail):
    return tail[:, 0:1] + tail[:, 1:2]


def text_kernel(
    groups, heads, place_of, where, len_ref, src_ref, states_ref, gain_ref, qg_ref, kg_ref,
    k_ref, v_ref, q_ref, w_ref, own_ref, *refs
):
    meta_ref = where()
    packed, refs = refs[:groups], refs[groups:]
    msgs, (w_all, sums, loaded, stage, w_sems, in_sems, out_sems) = refs[:-7], refs[-7:]
    size = own_ref.shape[2]
    rows = (own_ref.shape[1] - EXTRA) // (3 * heads + 1)
    width = heads * size
    slots = states_ref.shape[0]
    slot_local = rows // groups
    copies = []
    block = w_all.shape[0] // w_sems.shape[0]
    for i in range(w_sems.shape[0]):
        part = pl.ds(i * block, block)
        copies.append(pltpu.make_async_copy(w_ref.at[part], w_all.at[part], w_sems.at[i]))
        copies[-1].start()
    loads = []
    for i, ref in enumerate((k_ref, v_ref, q_ref)):
        loads.append(pltpu.make_async_copy(ref, loaded.at[i], in_sems.at[i]))
        loads[-1].start()

    def slot_at(row):
        z_at = (row % rows) // slot_local
        return place_of(meta_ref[1] ^ (row // rows), z_at) * slot_local + row % slot_local

    iota = functools.partial(lax.broadcasted_iota, jnp.int32, (slots, slots))
    sources = src_ref[...].astype(f32)
    chosen = (iota(1) == slot_at(iota(0))).astype(f32)
    source_col = jnp.sum(chosen * sources, axis=1, keepdims=True)
    pick = (iota(1).astype(f32) == source_col).astype(bf16)
    chosen_t = (iota(0) == slot_at(iota(1))).astype(bf16)
    source_row = jnp.dot(sources.astype(bf16), chosen_t, preferred_element_type=f32)
    bias = jnp.where(source_row < len_ref[0].astype(f32), 0.0, -1e30)
    end = own_ref.shape[1] - EXTRA
    own_ref[0, end:, :] = jnp.zeros((EXTRA, size), f32)
    own_ref[0, end : end + 1, :] = qg_ref[...]
    own_ref[0, end + 1 : end + 2, :] = kg_ref[...]
    own_ref[0, end + 2 : end + 3, :slots] = bias

    picked = jnp.dot(pick, states_ref[...], preferred_element_type=f32)
    scaled = (picked * gain_ref[...]).astype(bf16)
    tail = split_tail(jnp.sum(picked * picked, axis=1, keepdims=True), size)
    for copy in loads:
        copy.wait()
    local = loaded.shape[1]
    stores = []
    for g in range(groups):
        for i in range(3):
            for head in range(heads):
                at = ((meta_ref[0] ^ g) * heads + head) * size
                to = (i * heads + head) * local
                stage[g, to : to + local, :] = loaded[i, :, pl.ds(pl.multiple_of(at, 128), size)]
        stores.append(pltpu.make_async_copy(stage.at[g], packed[g], out_sems.at[g]))
        stores[-1].start()
    def product(part, g, i):
        at = (i * groups + (meta_ref[0] ^ g)) * width
        columns = pl.ds(pl.multiple_of(at, 128), width)
        rows_of = slice(part * block, (part + 1) * block)
        return jnp.dot(scaled[:, rows_of], w_all[rows_of, columns], preferred_element_type=f32)

    copies[0].wait()
    for g in range(groups):
        for i in range(3):
            sums[3 * g + i] = product(0, g, i)
    copies[1].wait()
    for g in range(groups):
        for i in range(3):
            got = sums[3 * g + i] + product(1, g, i)
            for head in range(heads):
                part = got[:, head * size : (head + 1) * size]
                to = slice((i * heads + head) * rows, (i * heads + head + 1) * rows)
                own_ref[g, to, :] = part[:rows]
                for j, msg in enumerate(msgs):
                    msg[g, to, :] = part[(j + 1) * rows : (j + 2) * rows].astype(bf16)
        own_ref[g, 3 * heads * rows : end, :] = tail[:rows]
        for j, msg in enumerate(msgs):
            msg[g, 3 * heads * rows :, :] = tail[(j + 1) * rows : (j + 2) * rows].astype(bf16)
    for copy in stores:
        copy.wait()


def text_project(
    length, sources, states, gain, query_gain, key_gain, keys, values, queries, text_proj,
    groups, parts, place_of, where
):
    slots, depth = states.shape
    size = query_gain.shape[1]
    heads = text_proj.shape[1] // (3 * groups * size)
    text_rows = (3 * heads + 1) * slots // parts
    shapes = [jax.ShapeDtypeStruct((groups, text_rows + EXTRA, size), f32)]
    shapes += [jax.ShapeDtypeStruct((3 * heads * keys.shape[0], size), bf16)] * groups
    shapes += [jax.ShapeDtypeStruct((groups, text_rows, size), bf16)] * (parts - 1)
    return pl.pallas_call(
        functools.partial(text_kernel, groups, heads, place_of, where),
        out_shape=shapes,
        in_specs=[SMEM] + [VMEM] * 5 + [ANY] * 4,
        out_specs=[VMEM] + [ANY] * groups + [VMEM] * (parts - 1),
        scratch_shapes=[
            pltpu.VMEM(text_proj.shape, bf16),
            pltpu.VMEM((3 * groups, slots, heads * size), f32),
            pltpu.VMEM((3,) + keys.shape, bf16),
            pltpu.VMEM((groups, 3 * heads * keys.shape[0], size), bf16),
            pltpu.SemaphoreType.DMA((2,)),
            pltpu.SemaphoreType.DMA((3,)),
            pltpu.SemaphoreType.DMA((groups,)),
        ],
        compiler_params=params(60),
        cost_estimate=cost(
            2 * slots * depth * text_proj.shape[1], 2 * depth * text_proj.shape[1]
        ),
    )(
        length, sources, states, gain, query_gain, key_gain, keys, values, queries, text_proj
    )


def text_sum_kernel(n_got, tail_rows, own_ref, *refs):
    got, (keep_ref, send_ref) = refs[:n_got], refs[n_got:]
    groups, text_rows, size = got[0].shape
    for g in range(groups):
        total = own_ref[g, :text_rows, :]
        for ref in got:
            total = total + ref[g].astype(f32)
        end = text_rows - tail_rows
        tail = split_tail(joined(total[end:]), size)
        if g % 2 == 0:
            keep_ref[g // 2, :end, :] = total[:end]
            keep_ref[g // 2, end:text_rows, :] = tail
            keep_ref[g // 2, text_rows:, :] = own_ref[g, text_rows:, :]
        else:
            send_ref[g // 2, :end, :] = total[:end].astype(bf16)
            send_ref[g // 2, end:, :] = tail.astype(bf16)


def text_sum(own, got, tail_rows):
    groups, rows, size = own.shape
    return pl.pallas_call(
        functools.partial(text_sum_kernel, len(got), tail_rows),
        out_shape=[
            jax.ShapeDtypeStruct((groups // 2, rows, size), f32),
            jax.ShapeDtypeStruct((groups // 2, rows - EXTRA, size), bf16),
        ],
        in_specs=[VMEM] * (1 + len(got)),
        out_specs=[VMEM] * 2,
        compiler_params=params(),
        cost_estimate=cost(0, 8 * groups * rows * size),
    )(own, *got)


def block_kernel(features, heads, n_pieces, own_ref, got_ref, *refs):
    pieces, out_ref = refs[:n_pieces], refs[-1]
    each = pieces[0].shape[0]
    for k, ref in enumerate(pieces):
        out_ref[k * each : (k + 1) * each, :] = ref[...]
    size = own_ref.shape[2]
    text_rows = got_ref.shape[1]
    rows = text_rows // (3 * heads + 1)
    total = own_ref[0, :text_rows, :] + got_ref[0].astype(f32)
    rate = lax.rsqrt(joined(total[3 * heads * rows :]) / features + eps_norm)
    start = n_pieces * each
    for i in range(3):
        for head in range(heads):
            at = (i * heads + head) * rows
            x = total[at : at + rows] * rate
            if i < 2:
                mean = jnp.sum(x * x, axis=1, keepdims=True) / size
                gain = own_ref[0, text_rows + i : text_rows + i + 1, :]
                x = x * lax.rsqrt(mean + eps_norm) * gain
            out_ref[start + at : start + at + rows, :] = x.astype(bf16)
    bias = own_ref[0, text_rows + 2 : text_rows + 3, :]
    start = start + 3 * heads * rows
    out_ref[start:, :] = jnp.broadcast_to(bias, (EXTRA, size)).astype(bf16)


def block_of(own, got, after, pieces, features, heads):
    rows, size = own.shape[1:]
    total = (rows - EXTRA) // (3 * heads + 1) * 3 * heads + EXTRA
    total += pieces[0].shape[0] * len(pieces)
    return pl.pallas_call(
        functools.partial(block_kernel, features, heads, len(pieces)),
        out_shape=jax.ShapeDtypeStruct((total, size), bf16),
        in_specs=[VMEM] * (2 + len(pieces)) + [ANY] * len(after),
        out_specs=VMEM,
        compiler_params=params(),
        cost_estimate=cost(0, 4 * total * size),
    )(own, got, *pieces, *after)


def attention_kernel(n_pieces, n_cores, n_after, asked_of, heads, rows, text_rows, *refs):
    blocks, out_refs = refs[:n_cores], refs[n_cores + n_after :]
    size = blocks[0].shape[1]
    factor = size ** (-0.5) * math.log2(math.e)
    nt = (((1,), (1,)), ((), ()))
    each = 3 * heads * rows
    starts = [k * each for k in range(n_pieces)]
    text = n_pieces * each
    end = text + 3 * heads * text_rows
    bias = blocks[0][end : end + EXTRA, :][:1, : n_cores * text_rows].astype(f32)

    def with_ones(values):
        return jnp.concatenate([values, jnp.ones(values.shape, bf16)], axis=1)

    for head in range(heads):
        kv, tkv = [], []
        for i in range(2):
            at = (i * heads + head) * rows
            image = [b[start + at : start + at + rows, :] for b in blocks for start in starts]
            text_at = text + ((i + 1) * heads + head) * text_rows
            kv.append(jnp.concatenate(image, axis=0))
            tkv.append(jnp.concatenate([b[text_at : text_at + text_rows, :] for b in blocks], axis=0))
        keys, values = kv[0], with_ones(kv[1])
        tkeys, tvalues = tkv[0], with_ones(tkv[1])
        cols = slice(head * size, (head + 1) * size)
        q_at = (2 * heads + head) * rows
        asked = []
        for k in asked_of:
            if k < n_pieces:
                asked.append(blocks[0][starts[k] + q_at : starts[k] + q_at + rows, :])
            else:
                tq_at = text + head * text_rows
                asked.append(blocks[0][tq_at : tq_at + text_rows, :])
        q = jnp.concatenate(asked, axis=0)
        s_img = lax.dot_general(q, keys, nt, preferred_element_type=f32)
        s_txt = lax.dot_general(q, tkeys, nt, preferred_element_type=f32) + bias
        top = jnp.maximum(
            jnp.max(s_img, axis=1, keepdims=True), jnp.max(s_txt, axis=1, keepdims=True)
        )
        p_img = jnp.exp2((s_img - top) * factor).astype(bf16)
        p_txt = jnp.exp2((s_txt - top) * factor).astype(bf16)
        acc = jnp.dot(p_img, values, preferred_element_type=f32)
        acc = acc + jnp.dot(p_txt, tvalues, preferred_element_type=f32)
        done = (acc[:, :size] / acc[:, size:]).astype(bf16)
        at = 0
        for out_ref in out_refs:
            out_ref[:, cols] = done[at : at + out_ref.shape[0]]
            at += out_ref.shape[0]


def attention(blocks, asked_of, after, n_pieces, heads, rows, text_rows):
    size = blocks[0].shape[1]
    counts = [rows if k < n_pieces else text_rows for k in asked_of]
    queries = sum(counts)
    keys = len(blocks) * (n_pieces * rows + text_rows)
    shapes = [jax.ShapeDtypeStruct((n, heads * size), bf16) for n in counts]
    return pl.pallas_call(
        functools.partial(
            attention_kernel,
            n_pieces,
            len(blocks),
            len(after),
            tuple(asked_of),
            heads,
            rows,
            text_rows,
        ),
        out_shape=shapes,
        in_specs=[VMEM] * len(blocks) + [ANY] * len(after),
        out_specs=[VMEM] * len(shapes),
        compiler_params=params(),
        cost_estimate=cost(
            4 * queries * keys * heads * size,
            4 * (queries + keys) * heads * size,
            queries * keys * heads,
        ),
    )(*blocks, *after)


def assemble_kernel(places, where, *refs):
    pieces, out_ref = refs[: len(places)], refs[-1]
    z = where()[0]
    rows, width = out_ref.shape[0], pieces[0].shape[1]
    for k, piece in zip(places, pieces):
        at = pl.multiple_of((z ^ k) * width, 128)
        out_ref[:, pl.ds(at, width)] = piece[:rows, :]


def assemble(where, pieces, places, after, rows):
    groups, width = len(pieces), pieces[0].shape[1]
    return pl.pallas_call(
        functools.partial(assemble_kernel, tuple(places), where),
        out_shape=jax.ShapeDtypeStruct((rows, groups * width), bf16),
        in_specs=[VMEM] * groups + [ANY] * len(after),
        out_specs=VMEM,
        compiler_params=params(),
        cost_estimate=cost(0, 4 * rows * groups * width),
    )(*pieces, *after)


def gated_kernel(groups, parts, place_of, meta_ref, gate_ref, d_out_ref, *refs):
    msgs, turned = refs[:-1], refs[-1]
    gated = (gate_ref[...] * d_out_ref[...].astype(f32)).astype(bf16)
    turned[...] = gated.astype(f32).T
    rows = msgs[0].shape[2]
    z, oc, dp = meta_ref[0], meta_ref[1], meta_ref[2]
    for k, msg in enumerate(msgs):
        for j in range(parts):
            for g in range(groups):
                at = (dp ^ k) * (groups * parts) + place_of(oc ^ j, z ^ g)
                msg[j, g] = turned[pl.ds(pl.multiple_of(at * rows, 8), rows), :].astype(bf16)


def gated_parts(meta, gate, d_out, n_dp, groups, parts, place_of):
    local, model = d_out.shape
    rows = model // (n_dp * groups * parts)
    return pl.pallas_call(
        functools.partial(gated_kernel, groups, parts, place_of),
        out_shape=[jax.ShapeDtypeStruct((parts, groups, rows, local), bf16)] * n_dp,
        in_specs=[SMEM, VMEM, VMEM],
        out_specs=[VMEM] * n_dp,
        scratch_shapes=[pltpu.VMEM((model, local), f32)],
        compiler_params=params(60),
        cost_estimate=cost(0, 4 * local * model),
    )(meta, gate, d_out)


def gather_kernel(n_dp, *refs):
    pieces, outs = refs[:n_dp], refs[n_dp:]
    for j, out in enumerate(outs):
        for k, piece in enumerate(pieces):
            out[k] = piece[j]


def gather_parts(pieces):
    parts = pieces[0].shape[0]
    shape = (len(pieces),) + pieces[0].shape[1:]
    return pl.pallas_call(
        functools.partial(gather_kernel, len(pieces)),
        out_shape=[jax.ShapeDtypeStruct(shape, bf16)] * parts,
        in_specs=[VMEM] * len(pieces),
        out_specs=[VMEM] * parts,
        compiler_params=params(),
        cost_estimate=cost(0, 4 * math.prod(shape) * parts),
    )(*pieces)


def project_kernel(
    groups, parts, place_of, meta_ref, attn_ref, w_ref, gate_ref, d_out_ref, out_ref, d_attn_ref,
    term_ref, *refs
):
    sent, by_place = refs[:-1], refs[-1]
    rows = attn_ref.shape[0]
    block = 512
    sums = []
    for at in range(0, w_ref.shape[0], block):
        cols = slice(at, at + block)
        got = lax.dot_general(
            attn_ref[...], w_ref[cols, :], (((1,), (1,)), ((), ())), preferred_element_type=f32
        )
        out_ref[:, cols] = (got * gate_ref[:, cols]).astype(bf16)
        sums.append(jnp.sum(got * d_out_ref[:, cols].astype(f32), axis=0, keepdims=True))
    total = jnp.zeros(d_attn_ref.shape, f32)
    for at in range(0, w_ref.shape[0], block):
        cols = slice(at, at + block)
        gated = (gate_ref[:, cols] * d_out_ref[:, cols].astype(f32)).astype(bf16)
        total = total + jnp.dot(gated, w_ref[cols, :], preferred_element_type=f32)
    d_attn_ref[...] = total.astype(bf16)
    sums = jnp.concatenate(sums, axis=1)
    places, width = by_place.shape
    for s in range(places):
        by_place[s : s + 1, :] = sums[:, s * width : (s + 1) * width]
    for g in range(groups):
        at = place_of(meta_ref[1], meta_ref[0] ^ g)
        term_ref[g : g + 1, :] = by_place[pl.ds(at, 1), :]
    for j, out in enumerate(sent):
        out[:rows, :] = attn_ref[...]
        line = [
            by_place[pl.ds(place_of(meta_ref[1] ^ (j + 1), meta_ref[0] ^ g), 1), :]
            for g in range(groups)
        ]
        line = jnp.concatenate(line, axis=1)
        line = jnp.concatenate(
            [line, jnp.zeros((1, attn_ref.shape[1] - groups * width), f32)], axis=1
        ) if attn_ref.shape[1] > groups * width else line
        high = line.astype(bf16).astype(f32)
        lines = [high, line - high, jnp.zeros((EXTRA - 2, line.shape[1]), f32)]
        out[rows:, :] = jnp.concatenate(lines, axis=0).astype(bf16)


def project(meta, attn, out_weight, gate, d_out, groups, parts, place_of):
    rows, inner = attn.shape
    model = out_weight.shape[0]
    width = model // (groups * parts)
    shapes = [jax.ShapeDtypeStruct((rows, model), bf16), jax.ShapeDtypeStruct((rows, inner), bf16)]
    shapes += [jax.ShapeDtypeStruct((groups, width), f32)]
    shapes += [jax.ShapeDtypeStruct((rows + EXTRA, inner), bf16)] * (parts - 1)
    return pl.pallas_call(
        functools.partial(project_kernel, groups, parts, place_of),
        out_shape=shapes,
        in_specs=[SMEM, VMEM, VMEM, VMEM, VMEM],
        out_specs=[VMEM] * (2 + parts),
        scratch_shapes=[pltpu.VMEM((groups * parts, width), f32)],
        compiler_params=params(),
        cost_estimate=cost(4 * rows * inner * model, 2 * inner * model),
    )(meta, attn, out_weight, gate, d_out)


def split_gate(gate, size):
    short = -gate.shape[1] % size
    if short:
        gate = jnp.concatenate([gate, jnp.zeros((1, short), f32)], axis=1)
    high = gate.astype(bf16).astype(f32)
    lines = [p[:, at : at + size] for p in (high, gate - high) for at in range(0, gate.shape[1], size)]
    return jnp.concatenate(lines + [jnp.zeros((EXTRA - len(lines), size), f32)], axis=0)


def joined_gate(lines, width):
    n = -(-width // lines.shape[1])
    both = lines[:n] + lines[n : 2 * n]
    return jnp.concatenate([both[i : i + 1] for i in range(n)], axis=1)[:, :width]


def grad_kernel(n_left, n_pieces, *refs):
    lefts, refs = refs[:n_left], refs[n_left:]
    pieces, refs = refs[:n_pieces], refs[n_pieces:]
    term_ref, outs = refs[0], refs[1:]
    groups, rows, depth = lefts[0].shape[1:]
    width = pieces[0].shape[1]
    size = outs[0].shape[1]
    left = []
    for ref in lefts:
        left += [ref[i].reshape(groups * rows, depth) for i in range(ref.shape[0])]
    left = jnp.concatenate(left, axis=1)
    half = outs[1].shape[0]
    homes = [((outs[0], 0),)]
    homes += [((outs[2 * g - 1], 0), (outs[2 * g], half)) for g in range(1, groups)]

    def put(g, at, value):
        out, start = homes[g][-1] if at >= half else homes[g][0]
        out[at - start : at - start + value.shape[0], :] = value.astype(out.dtype)

    block = 256
    for start in range(0, width, block):
        right = jnp.concatenate([p[:depth, start : start + block] for p in pieces], axis=0)
        got = jnp.dot(left, right, preferred_element_type=f32)
        for g in range(groups):
            for at in range(0, block, size):
                put(g, (start + at) // size * rows, got[g * rows : (g + 1) * rows, at : at + size])
    term = term_ref[...]
    each = term.shape[1]
    for p in pieces:
        if p.shape[0] > depth:
            lines = p[depth:, :].astype(f32)
            line = lines[0:1, :] + lines[1:2, :]
            term = term + jnp.concatenate(
                [line[:, g * each : (g + 1) * each] for g in range(groups)], axis=0
            )
    for g in range(groups):
        put(g, width // size * rows, split_gate(term[g : g + 1], size))


def grad_product(lefts, pieces, term):
    groups, rows, depth = lefts[0].shape[1:]
    width = pieces[0].shape[1]
    size = 128
    total = groups * rows
    depth = depth * len(pieces)
    full = width // size * rows + EXTRA
    half = width // size // 2 * rows
    shapes = [(full, f32)]
    for kind in (bf16, f32, bf16):
        shapes += [(half, kind), (full - half, kind)]
    return pl.pallas_call(
        functools.partial(grad_kernel, len(lefts), len(pieces)),
        out_shape=[jax.ShapeDtypeStruct((n, size), kind) for n, kind in shapes],
        in_specs=[VMEM] * (len(lefts) + len(pieces) + 1),
        out_specs=[VMEM] * len(shapes),
        compiler_params=params(),
        cost_estimate=cost(
            2 * total * depth * width, 2 * (total * depth + depth * width + total * width)
        ),
    )(*lefts, *pieces, term)


def pair_kernel(gate_width, n_through, own_ref, got_ref, *refs):
    out_ref = refs[n_through]
    for ref, out in zip(refs[:n_through], refs[n_through + 1 :]):
        out[...] = ref[...]
    total = own_ref[...] + got_ref[...].astype(f32)
    if not gate_width:
        out_ref[...] = total.astype(bf16)
    else:
        end = total.shape[0] - EXTRA
        out_ref[:end, :] = total[:end].astype(bf16)
        gate = joined_gate(total[end:], gate_width)
        out_ref[end:, :] = split_gate(gate, total.shape[1]).astype(bf16)


def pair_sum(own, got, gate_width, through):
    return pl.pallas_call(
        functools.partial(pair_kernel, gate_width, len(through)),
        out_shape=[jax.ShapeDtypeStruct(x.shape, bf16) for x in [got] + through],
        in_specs=[VMEM] * (2 + len(through)),
        out_specs=[VMEM] * (1 + len(through)),
        compiler_params=params(),
        cost_estimate=cost(0, 8 * own.size),
    )(own, got, *through)


def final_kernel(own_ref, far_low, far_high, near_low, near_high, out_ref, gate_ref):
    size = own_ref.shape[1]
    rows = out_ref.shape[0]
    half = far_low.shape[0]

    def total(at, count):
        refs, start = ((far_high, near_high), half) if at >= half else ((far_low, near_low), 0)
        got = own_ref[at : at + count, :]
        for ref in refs:
            got = got + ref[at - start : at - start + count, :].astype(f32)
        return got

    for i in range(out_ref.shape[1] // size):
        out_ref[:, i * size : (i + 1) * size] = total(i * rows, rows)
    gate_ref[...] = joined_gate(total(own_ref.shape[0] - EXTRA, EXTRA), gate_ref.shape[1])


def final_sum(own, far, near, rows, width, gate_width):
    return pl.pallas_call(
        final_kernel,
        out_shape=[
            jax.ShapeDtypeStruct((rows, width), f32),
            jax.ShapeDtypeStruct((1, gate_width), f32),
        ],
        in_specs=[VMEM] * 5,
        out_specs=[VMEM] * 2,
        compiler_params=params(),
        cost_estimate=cost(0, 8 * rows * width),
    )(own, *far, *near)


def on_device(
    caption_states,
    caption_gain,
    text_proj,
    caption_len,
    slot_source,
    query_gain,
    key_gain,
    image_q,
    image_k,
    image_v,
    out_weight,
    gate,
    d_out,
):
    n_dp = lax.axis_size("dp")
    n_seq = lax.axis_size("seq")
    G, C = GROUPS, CORES
    O = n_seq // (G * C)
    OC = O * C
    dp = lax.axis_index("dp")
    seq = lax.axis_index("seq")

    def where():
        at = lax.axis_index("seq")
        return (at // C) % G, (at // (G * C)) * C + at % C

    z, oc = where()

    def place(oc_at, z_at):
        return ((oc_at // C) * G + z_at) * C + oc_at % C

    def to_z(x, k):
        perm = [(place(a, b), place(a, b ^ k)) for a in range(OC) for b in range(G)]
        return lax.ppermute(x, "seq", perm)

    def to_oc(x, j):
        perm = [(place(a, b), place(a ^ j, b)) for a in range(OC) for b in range(G)]
        return lax.ppermute(x, "seq", perm)

    def to_dp(x, k):
        return lax.ppermute(x, "dp", [(a, a ^ k) for a in range(n_dp)])

    def part(x, index, size, axis):
        return lax.dynamic_slice_in_dim(x, index * size, size, axis)

    slot_total = slot_source.shape[1]
    slot_local = slot_total // n_seq
    image_local = image_q.shape[1]
    inner_width = image_q.shape[2]
    model_width = out_weight.shape[0]
    head_size = query_gain.shape[0]
    gw = inner_width // G
    order = [2, 3, 1]
    meta = jnp.stack([z, oc, dp]).astype(jnp.int32)

    heads = gw // head_size
    text_rows = G * slot_local
    own, *rest = text_project(
        caption_len, slot_source, caption_states[0], caption_gain[None],
        query_gain[None], key_gain[None], image_k[0], image_v[0], image_q[0], text_proj,
        G, OC, place, where,
    )
    packed, sent = rest[:G], rest[G:]
    images = {0: packed[0]}
    for k in order:
        images[k] = to_z(packed[k], k)
    images = [images[k] for k in [0] + order]
    got = [to_oc(x, j + 1) for j, x in enumerate(sent)]
    own, sent = text_sum(own, got, text_rows)
    own, sent = text_sum(own, [to_z(sent, 1)], text_rows)
    got = to_z(sent, 2)

    gg = gated_parts(meta, gate, d_out[0], n_dp, G, OC, place)
    gg_dp = [gg[0], to_dp(gg[1], 1)]
    block = block_of(own, got, gg_dp[1:], images, DT5, heads)
    blocks = [block] + [to_oc(block, j) for j in range(1, OC)]
    *first, text_out = attention(
        blocks, [1, 2, G], [], G, heads, image_local, text_rows
    )
    second = attention(
        blocks, [3, 0], [text_out], G, heads, image_local, text_rows
    )
    outs = dict(zip(order + [0], first + list(second)))

    back = {}
    for k in order + [0]:
        rows = jnp.concatenate([outs[k], part(text_out, z ^ k, slot_local, 0)], axis=0)
        back[k] = to_z(rows, k) if k else rows
    back = [back[k] for k in order + [0]]
    gg_dp += [to_dp(gg[k], k) for k in range(2, n_dp)]
    dp_order = [0] + list(range(n_dp - 1, 0, -1))
    lefts = gather_parts([gg_dp[k] for k in dp_order])
    lefts = [to_oc(g, j) if j else g for j, g in enumerate(lefts)]
    image_attn = assemble(where, back, order + [0], gg_dp[1:], image_local)
    text_attn = jnp.zeros((slot_local, inner_width), bf16)
    own_usable = part(slot_source[0] < caption_len[0], seq, slot_local, 0)
    for k, got in zip(order + [0], back):
        rows = jnp.where(own_usable[:, None], got[image_local:], jnp.zeros((), bf16))
        text_attn = lax.dynamic_update_slice_in_dim(text_attn, rows, (z ^ k) * gw, 1)

    pieces = [image_attn] + [to_dp(image_attn, k) for k in dp_order[1:]]
    image_out, d_attn, term, *sent = project(
        meta, image_attn, out_weight, gate, d_out[0], G, OC, place
    )
    for j in range(1, OC):
        pieces += [to_oc(sent[j - 1], j)] + [to_oc(p, j) for p in pieces[1:n_dp]]
    R = model_width // (n_dp * n_seq)
    gate_width = model_width // n_seq
    own, *blocks = grad_product(lefts, pieces, term)
    got = [to_z(x, 1) for x in blocks[4:]]
    (low,) = pair_sum(blocks[2], got[0], 0, [])
    high, *near = pair_sum(blocks[3], got[1], gate_width, blocks[:2])
    far = [to_z(x, 2) for x in (low, high)]
    near = [to_z(x, 1) for x in near]
    grad_wo, grad_gate = final_sum(own, far, near, R, inner_width, gate_width)
    return (image_out[None], text_attn[None], d_attn[None], grad_wo, grad_gate)


def solution(mesh):
    in_specs = (
        P("dp", None, "seq"),
        P("seq"),
        P("seq", None),
        P("dp"),
        P("dp", None),
        P(),
        P(),
        P("dp", "seq", None),
        P("dp", "seq", None),
        P("dp", "seq", None),
        P(),
        P("dp", None),
        P("dp", "seq", None),
    )
    out_specs = (
        P("dp", "seq", None),
        P("dp", "seq", None),
        P("dp", "seq", None),
        P(("dp", "seq"), None),
        P("dp", "seq"),
    )
    return jax.shard_map(
        on_device, mesh=mesh, in_specs=in_specs, out_specs=out_specs, check_vma=False
    )
```

```python
import math
import functools
import jax
import jax.numpy as jnp
from jax import lax
from jax.experimental import pallas as pl
from jax.experimental.pallas import tpu as pltpu
from jax.sharding import PartitionSpec as P

DT5 = 4096
CORES = 2
GROUPS = 4

eps_norm = 1e-06
f32 = jnp.float32
bf16 = jnp.bfloat16
EXTRA = 16


VMEM = pl.BlockSpec(memory_space=pltpu.VMEM)
SMEM = pl.BlockSpec(memory_space=pltpu.SMEM)
ANY = pl.BlockSpec(memory_space=pl.ANY)


def params(mib=16):
    return pltpu.CompilerParams(vmem_limit_bytes=int(mib * 1024 * 1024))


def cost(flops, bytes_accessed, transcendentals=0):
    return pl.CostEstimate(
        flops=flops, bytes_accessed=bytes_accessed, transcendentals=transcendentals
    )


def split_tail(squares, width):
    high = squares.astype(bf16).astype(f32)
    low = squares - high
    lane = lax.broadcasted_iota(jnp.int32, (squares.shape[0], width), 1)
    return jnp.where(lane == 0, high, jnp.where(lane == 1, low, 0.0))


def joined(tail):
    return tail[:, 0:1] + tail[:, 1:2]


def text_kernel(
    groups, heads, place_of, where, len_ref, src_ref, states_ref, gain_ref, qg_ref, kg_ref,
    k_ref, v_ref, q_ref, w_ref, own_ref, *refs
):
    meta_ref = where()
    packed, refs = refs[:groups], refs[groups:]
    msgs, (w_all, sums, loaded, stage, w_sems, in_sems, out_sems) = refs[:-7], refs[-7:]
    size = own_ref.shape[2]
    rows = (own_ref.shape[1] - EXTRA) // (3 * heads + 1)
    width = heads * size
    slots = states_ref.shape[0]
    slot_local = rows // groups
    copies = []
    block = w_all.shape[0] // w_sems.shape[0]
    for i in range(w_sems.shape[0]):
        part = pl.ds(i * block, block)
        copies.append(pltpu.make_async_copy(w_ref.at[part], w_all.at[part], w_sems.at[i]))
        copies[-1].start()
    loads = []
    for i, ref in enumerate((k_ref, v_ref, q_ref)):
        loads.append(pltpu.make_async_copy(ref, loaded.at[i], in_sems.at[i]))
        loads[-1].start()

    def slot_at(row):
        z_at = (row % rows) // slot_local
        return place_of(meta_ref[1] ^ (row // rows), z_at) * slot_local + row % slot_local

    iota = functools.partial(lax.broadcasted_iota, jnp.int32, (slots, slots))
    sources = src_ref[...].astype(f32)
    chosen = (iota(1) == slot_at(iota(0))).astype(f32)
    source_col = jnp.sum(chosen * sources, axis=1, keepdims=True)
    pick = (iota(1).astype(f32) == source_col).astype(bf16)
    chosen_t = (iota(0) == slot_at(iota(1))).astype(bf16)
    source_row = jnp.dot(sources.astype(bf16), chosen_t, preferred_element_type=f32)
    bias = jnp.where(source_row < len_ref[0].astype(f32), 0.0, -1e30)
    end = own_ref.shape[1] - EXTRA
    own_ref[0, end:, :] = jnp.zeros((EXTRA, size), f32)
    own_ref[0, end : end + 1, :] = qg_ref[...]
    own_ref[0, end + 1 : end + 2, :] = kg_ref[...]
    own_ref[0, end + 2 : end + 3, :slots] = bias

    picked = jnp.dot(pick, states_ref[...], preferred_element_type=f32)
    scaled = (picked * gain_ref[...]).astype(bf16)
    tail = split_tail(jnp.sum(picked * picked, axis=1, keepdims=True), size)
    for copy in loads:
        copy.wait()
    local = loaded.shape[1]
    stores = []
    for g in range(groups):
        for i in range(3):
            for head in range(heads):
                at = ((meta_ref[0] ^ g) * heads + head) * size
                to = (i * heads + head) * local
                stage[g, to : to + local, :] = loaded[i, :, pl.ds(pl.multiple_of(at, 128), size)]
        stores.append(pltpu.make_async_copy(stage.at[g], packed[g], out_sems.at[g]))
        stores[-1].start()
    def product(part, g, i):
        at = (i * groups + (meta_ref[0] ^ g)) * width
        columns = pl.ds(pl.multiple_of(at, 128), width)
        rows_of = slice(part * block, (part + 1) * block)
        return jnp.dot(scaled[:, rows_of], w_all[rows_of, columns], preferred_element_type=f32)

    copies[0].wait()
    for g in range(groups):
        for i in range(3):
            sums[3 * g + i] = product(0, g, i)
    copies[1].wait()
    for g in range(groups):
        for i in range(3):
            got = sums[3 * g + i] + product(1, g, i)
            for head in range(heads):
                part = got[:, head * size : (head + 1) * size]
                to = slice((i * heads + head) * rows, (i * heads + head + 1) * rows)
                own_ref[g, to, :] = part[:rows]
                for j, msg in enumerate(msgs):
                    msg[g, to, :] = part[(j + 1) * rows : (j + 2) * rows].astype(bf16)
        own_ref[g, 3 * heads * rows : end, :] = tail[:rows]
        for j, msg in enumerate(msgs):
            msg[g, 3 * heads * rows :, :] = tail[(j + 1) * rows : (j + 2) * rows].astype(bf16)
    for copy in stores:
        copy.wait()


def text_project(
    length, sources, states, gain, query_gain, key_gain, keys, values, queries, text_proj,
    groups, parts, place_of, where
):
    slots, depth = states.shape
    size = query_gain.shape[1]
    heads = text_proj.shape[1] // (3 * groups * size)
    text_rows = (3 * heads + 1) * slots // parts
    shapes = [jax.ShapeDtypeStruct((groups, text_rows + EXTRA, size), f32)]
    shapes += [jax.ShapeDtypeStruct((3 * heads * keys.shape[0], size), bf16)] * groups
    shapes += [jax.ShapeDtypeStruct((groups, text_rows, size), bf16)] * (parts - 1)
    return pl.pallas_call(
        functools.partial(text_kernel, groups, heads, place_of, where),
        out_shape=shapes,
        in_specs=[SMEM] + [VMEM] * 5 + [ANY] * 4,
        out_specs=[VMEM] + [ANY] * groups + [VMEM] * (parts - 1),
        scratch_shapes=[
            pltpu.VMEM(text_proj.shape, bf16),
            pltpu.VMEM((3 * groups, slots, heads * size), f32),
            pltpu.VMEM((3,) + keys.shape, bf16),
            pltpu.VMEM((groups, 3 * heads * keys.shape[0], size), bf16),
            pltpu.SemaphoreType.DMA((2,)),
            pltpu.SemaphoreType.DMA((3,)),
            pltpu.SemaphoreType.DMA((groups,)),
        ],
        compiler_params=params(60),
        cost_estimate=cost(
            2 * slots * depth * text_proj.shape[1], 2 * depth * text_proj.shape[1]
        ),
    )(
        length, sources, states, gain, query_gain, key_gain, keys, values, queries, text_proj
    )


def text_sum_kernel(n_got, tail_rows, own_ref, *refs):
    got, (keep_ref, send_ref) = refs[:n_got], refs[n_got:]
    groups, text_rows, size = got[0].shape
    for g in range(groups):
        total = own_ref[g, :text_rows, :]
        for ref in got:
            total = total + ref[g].astype(f32)
        end = text_rows - tail_rows
        tail = split_tail(joined(total[end:]), size)
        if g % 2 == 0:
            keep_ref[g // 2, :end, :] = total[:end]
            keep_ref[g // 2, end:text_rows, :] = tail
            keep_ref[g // 2, text_rows:, :] = own_ref[g, text_rows:, :]
        else:
            send_ref[g // 2, :end, :] = total[:end].astype(bf16)
            send_ref[g // 2, end:, :] = tail.astype(bf16)


def text_sum(own, got, tail_rows):
    groups, rows, size = own.shape
    return pl.pallas_call(
        functools.partial(text_sum_kernel, len(got), tail_rows),
        out_shape=[
            jax.ShapeDtypeStruct((groups // 2, rows, size), f32),
            jax.ShapeDtypeStruct((groups // 2, rows - EXTRA, size), bf16),
        ],
        in_specs=[VMEM] * (1 + len(got)),
        out_specs=[VMEM] * 2,
        compiler_params=params(),
        cost_estimate=cost(0, 8 * groups * rows * size),
    )(own, *got)


def block_kernel(features, heads, n_pieces, own_ref, got_ref, *refs):
    pieces, out_ref = refs[:n_pieces], refs[-1]
    each = pieces[0].shape[0]
    for k, ref in enumerate(pieces):
        out_ref[k * each : (k + 1) * each, :] = ref[...]
    size = own_ref.shape[2]
    text_rows = got_ref.shape[1]
    rows = text_rows // (3 * heads + 1)
    total = own_ref[0, :text_rows, :] + got_ref[0].astype(f32)
    rate = lax.rsqrt(joined(total[3 * heads * rows :]) / features + eps_norm)
    start = n_pieces * each
    for i in range(3):
        for head in range(heads):
            at = (i * heads + head) * rows
            x = total[at : at + rows] * rate
            if i < 2:
                mean = jnp.sum(x * x, axis=1, keepdims=True) / size
                gain = own_ref[0, text_rows + i : text_rows + i + 1, :]
                x = x * lax.rsqrt(mean + eps_norm) * gain
            out_ref[start + at : start + at + rows, :] = x.astype(bf16)
    bias = own_ref[0, text_rows + 2 : text_rows + 3, :]
    start = start + 3 * heads * rows
    out_ref[start:, :] = jnp.broadcast_to(bias, (EXTRA, size)).astype(bf16)


def block_of(own, got, after, pieces, features, heads):
    rows, size = own.shape[1:]
    total = (rows - EXTRA) // (3 * heads + 1) * 3 * heads + EXTRA
    total += pieces[0].shape[0] * len(pieces)
    return pl.pallas_call(
        functools.partial(block_kernel, features, heads, len(pieces)),
        out_shape=jax.ShapeDtypeStruct((total, size), bf16),
        in_specs=[VMEM] * (2 + len(pieces)) + [ANY] * len(after),
        out_specs=VMEM,
        compiler_params=params(),
        cost_estimate=cost(0, 4 * total * size),
    )(own, got, *pieces, *after)


def attention_kernel(n_pieces, n_cores, n_after, asked_of, heads, rows, text_rows, *refs):
    blocks, out_refs = refs[:n_cores], refs[n_cores + n_after :]
    size = blocks[0].shape[1]
    factor = size ** (-0.5) * math.log2(math.e)
    nt = (((1,), (1,)), ((), ()))
    each = 3 * heads * rows
    starts = [k * each for k in range(n_pieces)]
    text = n_pieces * each
    end = text + 3 * heads * text_rows
    bias = blocks[0][end : end + EXTRA, :][:1, : n_cores * text_rows].astype(f32)

    def with_ones(values):
        return jnp.concatenate([values, jnp.ones(values.shape, bf16)], axis=1)

    for head in range(heads):
        kv, tkv = [], []
        for i in range(2):
            at = (i * heads + head) * rows
            image = [b[start + at : start + at + rows, :] for b in blocks for start in starts]
            text_at = text + ((i + 1) * heads + head) * text_rows
            kv.append(jnp.concatenate(image, axis=0))
            tkv.append(jnp.concatenate([b[text_at : text_at + text_rows, :] for b in blocks], axis=0))
        keys, values = kv[0], with_ones(kv[1])
        tkeys, tvalues = tkv[0], with_ones(tkv[1])
        cols = slice(head * size, (head + 1) * size)
        q_at = (2 * heads + head) * rows
        asked = []
        for k in asked_of:
            if k < n_pieces:
                asked.append(blocks[0][starts[k] + q_at : starts[k] + q_at + rows, :])
            else:
                tq_at = text + head * text_rows
                asked.append(blocks[0][tq_at : tq_at + text_rows, :])
        q = jnp.concatenate(asked, axis=0)
        s_img = lax.dot_general(q, keys, nt, preferred_element_type=f32)
        s_txt = lax.dot_general(q, tkeys, nt, preferred_element_type=f32) + bias
        top = jnp.maximum(
            jnp.max(s_img, axis=1, keepdims=True), jnp.max(s_txt, axis=1, keepdims=True)
        )
        p_img = jnp.exp2((s_img - top) * factor).astype(bf16)
        p_txt = jnp.exp2((s_txt - top) * factor).astype(bf16)
        acc = jnp.dot(p_img, values, preferred_element_type=f32)
        acc = acc + jnp.dot(p_txt, tvalues, preferred_element_type=f32)
        done = (acc[:, :size] / acc[:, size:]).astype(bf16)
        at = 0
        for out_ref in out_refs:
            out_ref[:, cols] = done[at : at + out_ref.shape[0]]
            at += out_ref.shape[0]


def attention(blocks, asked_of, after, n_pieces, heads, rows, text_rows):
    size = blocks[0].shape[1]
    counts = [rows if k < n_pieces else text_rows for k in asked_of]
    queries = sum(counts)
    keys = len(blocks) * (n_pieces * rows + text_rows)
    shapes = [jax.ShapeDtypeStruct((n, heads * size), bf16) for n in counts]
    return pl.pallas_call(
        functools.partial(
            attention_kernel,
            n_pieces,
            len(blocks),
            len(after),
            tuple(asked_of),
            heads,
            rows,
            text_rows,
        ),
        out_shape=shapes,
        in_specs=[VMEM] * len(blocks) + [ANY] * len(after),
        out_specs=[VMEM] * len(shapes),
        compiler_params=params(),
        cost_estimate=cost(
            4 * queries * keys * heads * size,
            4 * (queries + keys) * heads * size,
            queries * keys * heads,
        ),
    )(*blocks, *after)


def assemble_kernel(places, where, *refs):
    pieces, out_ref = refs[: len(places)], refs[-1]
    z = where()[0]
    rows, width = out_ref.shape[0], pieces[0].shape[1]
    for k, piece in zip(places, pieces):
        at = pl.multiple_of((z ^ k) * width, 128)
        out_ref[:, pl.ds(at, width)] = piece[:rows, :]


def assemble(where, pieces, places, after, rows):
    groups, width = len(pieces), pieces[0].shape[1]
    return pl.pallas_call(
        functools.partial(assemble_kernel, tuple(places), where),
        out_shape=jax.ShapeDtypeStruct((rows, groups * width), bf16),
        in_specs=[VMEM] * groups + [ANY] * len(after),
        out_specs=VMEM,
        compiler_params=params(),
        cost_estimate=cost(0, 4 * rows * groups * width),
    )(*pieces, *after)


def gated_kernel(groups, parts, place_of, meta_ref, gate_ref, d_out_ref, *refs):
    msgs, turned = refs[:-1], refs[-1]
    gated = (gate_ref[...] * d_out_ref[...].astype(f32)).astype(bf16)
    turned[...] = gated.astype(f32).T
    rows = msgs[0].shape[2]
    z, oc, dp = meta_ref[0], meta_ref[1], meta_ref[2]
    for k, msg in enumerate(msgs):
        for j in range(parts):
            for g in range(groups):
                at = (dp ^ k) * (groups * parts) + place_of(oc ^ j, z ^ g)
                msg[j, g] = turned[pl.ds(pl.multiple_of(at * rows, 8), rows), :].astype(bf16)


def gated_parts(meta, gate, d_out, n_dp, groups, parts, place_of):
    local, model = d_out.shape
    rows = model // (n_dp * groups * parts)
    return pl.pallas_call(
        functools.partial(gated_kernel, groups, parts, place_of),
        out_shape=[jax.ShapeDtypeStruct((parts, groups, rows, local), bf16)] * n_dp,
        in_specs=[SMEM, VMEM, VMEM],
        out_specs=[VMEM] * n_dp,
        scratch_shapes=[pltpu.VMEM((model, local), f32)],
        compiler_params=params(60),
        cost_estimate=cost(0, 4 * local * model),
    )(meta, gate, d_out)


def gather_kernel(n_dp, *refs):
    pieces, outs = refs[:n_dp], refs[n_dp:]
    for j, out in enumerate(outs):
        for k, piece in enumerate(pieces):
            out[k] = piece[j]


def gather_parts(pieces):
    parts = pieces[0].shape[0]
    shape = (len(pieces),) + pieces[0].shape[1:]
    return pl.pallas_call(
        functools.partial(gather_kernel, len(pieces)),
        out_shape=[jax.ShapeDtypeStruct(shape, bf16)] * parts,
        in_specs=[VMEM] * len(pieces),
        out_specs=[VMEM] * parts,
        compiler_params=params(),
        cost_estimate=cost(0, 4 * math.prod(shape) * parts),
    )(*pieces)


def project_kernel(
    groups, parts, place_of, meta_ref, attn_ref, w_ref, gate_ref, d_out_ref, out_ref, d_attn_ref,
    term_ref, *refs
):
    sent, by_place = refs[:-1], refs[-1]
    rows = attn_ref.shape[0]
    block = 512
    sums = []
    for at in range(0, w_ref.shape[0], block):
        cols = slice(at, at + block)
        got = lax.dot_general(
            attn_ref[...], w_ref[cols, :], (((1,), (1,)), ((), ())), preferred_element_type=f32
        )
        out_ref[:, cols] = (got * gate_ref[:, cols]).astype(bf16)
        sums.append(jnp.sum(got * d_out_ref[:, cols].astype(f32), axis=0, keepdims=True))
    total = jnp.zeros(d_attn_ref.shape, f32)
    for at in range(0, w_ref.shape[0], block):
        cols = slice(at, at + block)
        gated = (gate_ref[:, cols] * d_out_ref[:, cols].astype(f32)).astype(bf16)
        total = total + jnp.dot(gated, w_ref[cols, :], preferred_element_type=f32)
    d_attn_ref[...] = total.astype(bf16)
    sums = jnp.concatenate(sums, axis=1)
    places, width = by_place.shape
    for s in range(places):
        by_place[s : s + 1, :] = sums[:, s * width : (s + 1) * width]
    for g in range(groups):
        at = place_of(meta_ref[1], meta_ref[0] ^ g)
        term_ref[g : g + 1, :] = by_place[pl.ds(at, 1), :]
    for j, out in enumerate(sent):
        out[:rows, :] = attn_ref[...]
        line = [
            by_place[pl.ds(place_of(meta_ref[1] ^ (j + 1), meta_ref[0] ^ g), 1), :]
            for g in range(groups)
        ]
        line = jnp.concatenate(line, axis=1)
        line = jnp.concatenate(
            [line, jnp.zeros((1, attn_ref.shape[1] - groups * width), f32)], axis=1
        ) if attn_ref.shape[1] > groups * width else line
        high = line.astype(bf16).astype(f32)
        lines = [high, line - high, jnp.zeros((EXTRA - 2, line.shape[1]), f32)]
        out[rows:, :] = jnp.concatenate(lines, axis=0).astype(bf16)


def project(meta, attn, out_weight, gate, d_out, groups, parts, place_of):
    rows, inner = attn.shape
    model = out_weight.shape[0]
    width = model // (groups * parts)
    shapes = [jax.ShapeDtypeStruct((rows, model), bf16), jax.ShapeDtypeStruct((rows, inner), bf16)]
    shapes += [jax.ShapeDtypeStruct((groups, width), f32)]
    shapes += [jax.ShapeDtypeStruct((rows + EXTRA, inner), bf16)] * (parts - 1)
    return pl.pallas_call(
        functools.partial(project_kernel, groups, parts, place_of),
        out_shape=shapes,
        in_specs=[SMEM, VMEM, VMEM, VMEM, VMEM],
        out_specs=[VMEM] * (2 + parts),
        scratch_shapes=[pltpu.VMEM((groups * parts, width), f32)],
        compiler_params=params(),
        cost_estimate=cost(4 * rows * inner * model, 2 * inner * model),
    )(meta, attn, out_weight, gate, d_out)


def split_gate(gate, size):
    short = -gate.shape[1] % size
    if short:
        gate = jnp.concatenate([gate, jnp.zeros((1, short), f32)], axis=1)
    high = gate.astype(bf16).astype(f32)
    lines = [p[:, at : at + size] for p in (high, gate - high) for at in range(0, gate.shape[1], size)]
    return jnp.concatenate(lines + [jnp.zeros((EXTRA - len(lines), size), f32)], axis=0)


def joined_gate(lines, width):
    n = -(-width // lines.shape[1])
    both = lines[:n] + lines[n : 2 * n]
    return jnp.concatenate([both[i : i + 1] for i in range(n)], axis=1)[:, :width]


def grad_kernel(n_left, n_pieces, *refs):
    lefts, refs = refs[:n_left], refs[n_left:]
    pieces, refs = refs[:n_pieces], refs[n_pieces:]
    term_ref, outs = refs[0], refs[1:]
    groups, rows, depth = lefts[0].shape[1:]
    width = pieces[0].shape[1]
    size = outs[0].shape[1]
    left = []
    for ref in lefts:
        left += [ref[i].reshape(groups * rows, depth) for i in range(ref.shape[0])]
    left = jnp.concatenate(left, axis=1)
    half = outs[1].shape[0]
    homes = [((outs[0], 0),)]
    homes += [((outs[2 * g - 1], 0), (outs[2 * g], half)) for g in range(1, groups)]

    def put(g, at, value):
        out, start = homes[g][-1] if at >= half else homes[g][0]
        out[at - start : at - start + value.shape[0], :] = value.astype(out.dtype)

    block = 256
    for start in range(0, width, block):
        right = jnp.concatenate([p[:depth, start : start + block] for p in pieces], axis=0)
        got = jnp.dot(left, right, preferred_element_type=f32)
        for g in range(groups):
            for at in range(0, block, size):
                put(g, (start + at) // size * rows, got[g * rows : (g + 1) * rows, at : at + size])
    term = term_ref[...]
    each = term.shape[1]
    for p in pieces:
        if p.shape[0] > depth:
            lines = p[depth:, :].astype(f32)
            line = lines[0:1, :] + lines[1:2, :]
            term = term + jnp.concatenate(
                [line[:, g * each : (g + 1) * each] for g in range(groups)], axis=0
            )
    for g in range(groups):
        put(g, width // size * rows, split_gate(term[g : g + 1], size))


def grad_product(lefts, pieces, term):
    groups, rows, depth = lefts[0].shape[1:]
    width = pieces[0].shape[1]
    size = 128
    total = groups * rows
    depth = depth * len(pieces)
    full = width // size * rows + EXTRA
    half = width // size // 2 * rows
    shapes = [(full, f32)]
    for kind in (bf16, f32, bf16):
        shapes += [(half, kind), (full - half, kind)]
    return pl.pallas_call(
        functools.partial(grad_kernel, len(lefts), len(pieces)),
        out_shape=[jax.ShapeDtypeStruct((n, size), kind) for n, kind in shapes],
        in_specs=[VMEM] * (len(lefts) + len(pieces) + 1),
        out_specs=[VMEM] * len(shapes),
        compiler_params=params(),
        cost_estimate=cost(
            2 * total * depth * width, 2 * (total * depth + depth * width + total * width)
        ),
    )(*lefts, *pieces, term)


def pair_kernel(gate_width, n_through, own_ref, got_ref, *refs):
    out_ref = refs[n_through]
    for ref, out in zip(refs[:n_through], refs[n_through + 1 :]):
        out[...] = ref[...]
    total = own_ref[...] + got_ref[...].astype(f32)
    if not gate_width:
        out_ref[...] = total.astype(bf16)
    else:
        end = total.shape[0] - EXTRA
        out_ref[:end, :] = total[:end].astype(bf16)
        gate = joined_gate(total[end:], gate_width)
        out_ref[end:, :] = split_gate(gate, total.shape[1]).astype(bf16)


def pair_sum(own, got, gate_width, through):
    return pl.pallas_call(
        functools.partial(pair_kernel, gate_width, len(through)),
        out_shape=[jax.ShapeDtypeStruct(x.shape, bf16) for x in [got] + through],
        in_specs=[VMEM] * (2 + len(through)),
        out_specs=[VMEM] * (1 + len(through)),
        compiler_params=params(),
        cost_estimate=cost(0, 8 * own.size),
    )(own, got, *through)


def final_kernel(own_ref, far_low, far_high, near_low, near_high, out_ref, gate_ref):
    size = own_ref.shape[1]
    rows = out_ref.shape[0]
    half = far_low.shape[0]

    def total(at, count):
        refs, start = ((far_high, near_high), half) if at >= half else ((far_low, near_low), 0)
        got = own_ref[at : at + count, :]
        for ref in refs:
            got = got + ref[at - start : at - start + count, :].astype(f32)
        return got

    for i in range(out_ref.shape[1] // size):
        out_ref[:, i * size : (i + 1) * size] = total(i * rows, rows)
    gate_ref[...] = joined_gate(total(own_ref.shape[0] - EXTRA, EXTRA), gate_ref.shape[1])


def final_sum(own, far, near, rows, width, gate_width):
    return pl.pallas_call(
        final_kernel,
        out_shape=[
            jax.ShapeDtypeStruct((rows, width), f32),
            jax.ShapeDtypeStruct((1, gate_width), f32),
        ],
        in_specs=[VMEM] * 5,
        out_specs=[VMEM] * 2,
        compiler_params=params(),
        cost_estimate=cost(0, 8 * rows * width),
    )(own, *far, *near)


def on_device(
    caption_states,
    caption_gain,
    text_proj,
    caption_len,
    slot_source,
    query_gain,
    key_gain,
    image_q,
    image_k,
    image_v,
    out_weight,
    gate,
    d_out,
):
    n_dp = lax.axis_size("dp")
    n_seq = lax.axis_size("seq")
    G, C = GROUPS, CORES
    O = n_seq // (G * C)
    OC = O * C
    dp = lax.axis_index("dp")
    seq = lax.axis_index("seq")

    def where():
        at = lax.axis_index("seq")
        return (at // C) % G, (at // (G * C)) * C + at % C

    z, oc = where()

    def place(oc_at, z_at):
        return ((oc_at // C) * G + z_at) * C + oc_at % C

    def to_z(x, k):
        perm = [(place(a, b), place(a, b ^ k)) for a in range(OC) for b in range(G)]
        return lax.ppermute(x, "seq", perm)

    def to_oc(x, j):
        perm = [(place(a, b), place(a ^ j, b)) for a in range(OC) for b in range(G)]
        return lax.ppermute(x, "seq", perm)

    def to_dp(x, k):
        return lax.ppermute(x, "dp", [(a, a ^ k) for a in range(n_dp)])

    def part(x, index, size, axis):
        return lax.dynamic_slice_in_dim(x, index * size, size, axis)

    slot_total = slot_source.shape[1]
    slot_local = slot_total // n_seq
    image_local = image_q.shape[1]
    inner_width = image_q.shape[2]
    model_width = out_weight.shape[0]
    head_size = query_gain.shape[0]
    gw = inner_width // G
    order = [2, 3, 1]
    meta = jnp.stack([z, oc, dp]).astype(jnp.int32)

    heads = gw // head_size
    text_rows = G * slot_local
    own, *rest = text_project(
        caption_len, slot_source, caption_states[0], caption_gain[None],
        query_gain[None], key_gain[None], image_k[0], image_v[0], image_q[0], text_proj,
        G, OC, place, where,
    )
    packed, sent = rest[:G], rest[G:]
    images = {0: packed[0]}
    for k in order:
        images[k] = to_z(packed[k], k)
    images = [images[k] for k in [0] + order]
    got = [to_oc(x, j + 1) for j, x in enumerate(sent)]
    own, sent = text_sum(own, got, text_rows)
    own, sent = text_sum(own, [to_z(sent, 1)], text_rows)
    got = to_z(sent, 2)

    gg = gated_parts(meta, gate, d_out[0], n_dp, G, OC, place)
    gg_dp = [gg[0], to_dp(gg[1], 1)]
    block = block_of(own, got, gg_dp[1:], images, DT5, heads)
    blocks = [block] + [to_oc(block, j) for j in range(1, OC)]
    *first, text_out = attention(
        blocks, [1, 2, 3, G], [], G, heads, image_local, text_rows
    )
    second = attention(
        blocks, [0], [text_out], G, heads, image_local, text_rows
    )
    outs = dict(zip(order + [0], first + list(second)))

    back = {}
    for k in order + [0]:
        rows = jnp.concatenate([outs[k], part(text_out, z ^ k, slot_local, 0)], axis=0)
        back[k] = to_z(rows, k) if k else rows
    back = [back[k] for k in order + [0]]
    gg_dp += [to_dp(gg[k], k) for k in range(2, n_dp)]
    dp_order = [0] + list(range(n_dp - 1, 0, -1))
    lefts = gather_parts([gg_dp[k] for k in dp_order])
    lefts = [to_oc(g, j) if j else g for j, g in enumerate(lefts)]
    image_attn = assemble(where, back, order + [0], gg_dp[1:], image_local)
    text_attn = jnp.zeros((slot_local, inner_width), bf16)
    own_usable = part(slot_source[0] < caption_len[0], seq, slot_local, 0)
    for k, got in zip(order + [0], back):
        rows = jnp.where(own_usable[:, None], got[image_local:], jnp.zeros((), bf16))
        text_attn = lax.dynamic_update_slice_in_dim(text_attn, rows, (z ^ k) * gw, 1)

    pieces = [image_attn] + [to_dp(image_attn, k) for k in dp_order[1:]]
    image_out, d_attn, term, *sent = project(
        meta, image_attn, out_weight, gate, d_out[0], G, OC, place
    )
    for j in range(1, OC):
        pieces += [to_oc(sent[j - 1], j)] + [to_oc(p, j) for p in pieces[1:n_dp]]
    R = model_width // (n_dp * n_seq)
    gate_width = model_width // n_seq
    own, *blocks = grad_product(lefts, pieces, term)
    got = [to_z(x, 1) for x in blocks[4:]]
    (low,) = pair_sum(blocks[2], got[0], 0, [])
    high, *near = pair_sum(blocks[3], got[1], gate_width, blocks[:2])
    far = [to_z(x, 2) for x in (low, high)]
    near = [to_z(x, 1) for x in near]
    grad_wo, grad_gate = final_sum(own, far, near, R, inner_width, gate_width)
    return (image_out[None], text_attn[None], d_attn[None], grad_wo, grad_gate)


def solution(mesh):
    in_specs = (
        P("dp", None, "seq"),
        P("seq"),
        P("seq", None),
        P("dp"),
        P("dp", None),
        P(),
        P(),
        P("dp", "seq", None),
        P("dp", "seq", None),
        P("dp", "seq", None),
        P(),
        P("dp", None),
        P("dp", "seq", None),
    )
    out_specs = (
        P("dp", "seq", None),
        P("dp", "seq", None),
        P("dp", "seq", None),
        P(("dp", "seq"), None),
        P("dp", "seq"),
    )
    return jax.shard_map(
        on_device, mesh=mesh, in_specs=in_specs, out_specs=out_specs, check_vma=False
    )
```

```python
import math
import functools
import jax
import jax.numpy as jnp
from jax import lax
from jax.experimental import pallas as pl
from jax.experimental.pallas import tpu as pltpu
from jax.sharding import PartitionSpec as P

DT5 = 4096
CORES = 2
GROUPS = 4

eps_norm = 1e-06
f32 = jnp.float32
bf16 = jnp.bfloat16
EXTRA = 16


VMEM = pl.BlockSpec(memory_space=pltpu.VMEM)
SMEM = pl.BlockSpec(memory_space=pltpu.SMEM)
ANY = pl.BlockSpec(memory_space=pl.ANY)


def params(mib=16):
    return pltpu.CompilerParams(vmem_limit_bytes=int(mib * 1024 * 1024))


def cost(flops, bytes_accessed, transcendentals=0):
    return pl.CostEstimate(
        flops=flops, bytes_accessed=bytes_accessed, transcendentals=transcendentals
    )


def split_tail(squares, width):
    high = squares.astype(bf16).astype(f32)
    low = squares - high
    lane = lax.broadcasted_iota(jnp.int32, (squares.shape[0], width), 1)
    return jnp.where(lane == 0, high, jnp.where(lane == 1, low, 0.0))


def joined(tail):
    return tail[:, 0:1] + tail[:, 1:2]


def text_kernel(
    groups, heads, place_of, where, len_ref, src_ref, states_ref, gain_ref, qg_ref, kg_ref,
    k_ref, v_ref, q_ref, w_ref, own_ref, *refs
):
    meta_ref = where()
    packed, refs = refs[:groups], refs[groups:]
    msgs, (w_all, sums, loaded, stage, w_sems, in_sems, out_sems) = refs[:-7], refs[-7:]
    size = own_ref.shape[2]
    rows = (own_ref.shape[1] - EXTRA) // (3 * heads + 1)
    width = heads * size
    slots = states_ref.shape[0]
    slot_local = rows // groups
    copies = []
    block = w_all.shape[0] // w_sems.shape[0]
    for i in range(w_sems.shape[0]):
        part = pl.ds(i * block, block)
        copies.append(pltpu.make_async_copy(w_ref.at[part], w_all.at[part], w_sems.at[i]))
        copies[-1].start()
    loads = []
    for i, ref in enumerate((k_ref, v_ref, q_ref)):
        loads.append(pltpu.make_async_copy(ref, loaded.at[i], in_sems.at[i]))
        loads[-1].start()

    def slot_at(row):
        z_at = (row % rows) // slot_local
        return place_of(meta_ref[1] ^ (row // rows), z_at) * slot_local + row % slot_local

    iota = functools.partial(lax.broadcasted_iota, jnp.int32, (slots, slots))
    sources = src_ref[...].astype(f32)
    chosen = (iota(1) == slot_at(iota(0))).astype(f32)
    source_col = jnp.sum(chosen * sources, axis=1, keepdims=True)
    pick = (iota(1).astype(f32) == source_col).astype(bf16)
    chosen_t = (iota(0) == slot_at(iota(1))).astype(bf16)
    source_row = jnp.dot(sources.astype(bf16), chosen_t, preferred_element_type=f32)
    bias = jnp.where(source_row < len_ref[0].astype(f32), 0.0, -1e30)
    end = own_ref.shape[1] - EXTRA
    own_ref[0, end:, :] = jnp.zeros((EXTRA, size), f32)
    own_ref[0, end : end + 1, :] = qg_ref[...]
    own_ref[0, end + 1 : end + 2, :] = kg_ref[...]
    own_ref[0, end + 2 : end + 3, :slots] = bias

    picked = jnp.dot(pick, states_ref[...], preferred_element_type=f32)
    scaled = (picked * gain_ref[...]).astype(bf16)
    tail = split_tail(jnp.sum(picked * picked, axis=1, keepdims=True), size)
    for copy in loads:
        copy.wait()
    local = loaded.shape[1]
    stores = []
    for g in range(groups):
        for i in range(3):
            for head in range(heads):
                at = ((meta_ref[0] ^ g) * heads + head) * size
                to = (i * heads + head) * local
                stage[g, to : to + local, :] = loaded[i, :, pl.ds(pl.multiple_of(at, 128), size)]
        stores.append(pltpu.make_async_copy(stage.at[g], packed[g], out_sems.at[g]))
        stores[-1].start()
    def product(part, g, i):
        at = (i * groups + (meta_ref[0] ^ g)) * width
        columns = pl.ds(pl.multiple_of(at, 128), width)
        rows_of = slice(part * block, (part + 1) * block)
        return jnp.dot(scaled[:, rows_of], w_all[rows_of, columns], preferred_element_type=f32)

    copies[0].wait()
    for g in range(groups):
        for i in range(3):
            sums[3 * g + i] = product(0, g, i)
    copies[1].wait()
    for g in range(groups):
        for i in range(3):
            got = sums[3 * g + i] + product(1, g, i)
            for head in range(heads):
                part = got[:, head * size : (head + 1) * size]
                to = slice((i * heads + head) * rows, (i * heads + head + 1) * rows)
                own_ref[g, to, :] = part[:rows]
                for j, msg in enumerate(msgs):
                    msg[g, to, :] = part[(j + 1) * rows : (j + 2) * rows].astype(bf16)
        own_ref[g, 3 * heads * rows : end, :] = tail[:rows]
        for j, msg in enumerate(msgs):
            msg[g, 3 * heads * rows :, :] = tail[(j + 1) * rows : (j + 2) * rows].astype(bf16)
    for copy in stores:
        copy.wait()


def text_project(
    length, sources, states, gain, query_gain, key_gain, keys, values, queries, text_proj,
    groups, parts, place_of, where
):
    slots, depth = states.shape
    size = query_gain.shape[1]
    heads = text_proj.shape[1] // (3 * groups * size)
    text_rows = (3 * heads + 1) * slots // parts
    shapes = [jax.ShapeDtypeStruct((groups, text_rows + EXTRA, size), f32)]
    shapes += [jax.ShapeDtypeStruct((3 * heads * keys.shape[0], size), bf16)] * groups
    shapes += [jax.ShapeDtypeStruct((groups, text_rows, size), bf16)] * (parts - 1)
    return pl.pallas_call(
        functools.partial(text_kernel, groups, heads, place_of, where),
        out_shape=shapes,
        in_specs=[SMEM] + [VMEM] * 5 + [ANY] * 4,
        out_specs=[VMEM] + [ANY] * groups + [VMEM] * (parts - 1),
        scratch_shapes=[
            pltpu.VMEM(text_proj.shape, bf16),
            pltpu.VMEM((3 * groups, slots, heads * size), f32),
            pltpu.VMEM((3,) + keys.shape, bf16),
            pltpu.VMEM((groups, 3 * heads * keys.shape[0], size), bf16),
            pltpu.SemaphoreType.DMA((2,)),
            pltpu.SemaphoreType.DMA((3,)),
            pltpu.SemaphoreType.DMA((groups,)),
        ],
        compiler_params=params(60),
        cost_estimate=cost(
            2 * slots * depth * text_proj.shape[1], 2 * depth * text_proj.shape[1]
        ),
    )(
        length, sources, states, gain, query_gain, key_gain, keys, values, queries, text_proj
    )


def text_sum_kernel(n_got, tail_rows, n_through, own_ref, *refs):
    got, refs = refs[:n_got], refs[n_got:]
    for ref, out in zip(refs[:n_through], refs[n_through + 2 :]):
        out[...] = ref[...]
    keep_ref, send_ref = refs[n_through : n_through + 2]
    groups, text_rows, size = got[0].shape
    for g in range(groups):
        total = own_ref[g, :text_rows, :]
        for ref in got:
            total = total + ref[g].astype(f32)
        end = text_rows - tail_rows
        tail = split_tail(joined(total[end:]), size)
        if g % 2 == 0:
            keep_ref[g // 2, :end, :] = total[:end]
            keep_ref[g // 2, end:text_rows, :] = tail
            keep_ref[g // 2, text_rows:, :] = own_ref[g, text_rows:, :]
        else:
            send_ref[g // 2, :end, :] = total[:end].astype(bf16)
            send_ref[g // 2, end:, :] = tail.astype(bf16)


def text_sum(own, got, tail_rows, through=()):
    groups, rows, size = own.shape
    return pl.pallas_call(
        functools.partial(text_sum_kernel, len(got), tail_rows, len(through)),
        out_shape=[
            jax.ShapeDtypeStruct((groups // 2, rows, size), f32),
            jax.ShapeDtypeStruct((groups // 2, rows - EXTRA, size), bf16),
        ]
        + [jax.ShapeDtypeStruct(x.shape, x.dtype) for x in through],
        in_specs=[VMEM] * (1 + len(got) + len(through)),
        out_specs=[VMEM] * (2 + len(through)),
        compiler_params=params(),
        cost_estimate=cost(0, 8 * groups * rows * size),
    )(own, *got, *through)


def block_kernel(features, heads, n_pieces, own_ref, got_ref, *refs):
    pieces, out_ref = refs[:n_pieces], refs[-1]
    each = pieces[0].shape[0]
    for k, ref in enumerate(pieces):
        out_ref[k * each : (k + 1) * each, :] = ref[...]
    size = own_ref.shape[2]
    text_rows = got_ref.shape[1]
    rows = text_rows // (3 * heads + 1)
    total = own_ref[0, :text_rows, :] + got_ref[0].astype(f32)
    rate = lax.rsqrt(joined(total[3 * heads * rows :]) / features + eps_norm)
    start = n_pieces * each
    for i in range(3):
        for head in range(heads):
            at = (i * heads + head) * rows
            x = total[at : at + rows] * rate
            if i < 2:
                mean = jnp.sum(x * x, axis=1, keepdims=True) / size
                gain = own_ref[0, text_rows + i : text_rows + i + 1, :]
                x = x * lax.rsqrt(mean + eps_norm) * gain
            out_ref[start + at : start + at + rows, :] = x.astype(bf16)
    bias = own_ref[0, text_rows + 2 : text_rows + 3, :]
    start = start + 3 * heads * rows
    out_ref[start:, :] = jnp.broadcast_to(bias, (EXTRA, size)).astype(bf16)


def block_of(own, got, after, pieces, features, heads):
    rows, size = own.shape[1:]
    total = (rows - EXTRA) // (3 * heads + 1) * 3 * heads + EXTRA
    total += pieces[0].shape[0] * len(pieces)
    return pl.pallas_call(
        functools.partial(block_kernel, features, heads, len(pieces)),
        out_shape=jax.ShapeDtypeStruct((total, size), bf16),
        in_specs=[VMEM] * (2 + len(pieces)) + [ANY] * len(after),
        out_specs=VMEM,
        compiler_params=params(),
        cost_estimate=cost(0, 4 * total * size),
    )(own, got, *pieces, *after)


def attention_kernel(n_pieces, n_cores, n_after, asked_of, heads, rows, text_rows, *refs):
    blocks, out_refs = refs[:n_cores], refs[n_cores + n_after :]
    size = blocks[0].shape[1]
    factor = size ** (-0.5) * math.log2(math.e)
    nt = (((1,), (1,)), ((), ()))
    each = 3 * heads * rows
    starts = [k * each for k in range(n_pieces)]
    text = n_pieces * each
    end = text + 3 * heads * text_rows
    bias = blocks[0][end : end + EXTRA, :][:1, : n_cores * text_rows].astype(f32)

    def with_ones(values):
        return jnp.concatenate([values, jnp.ones(values.shape, bf16)], axis=1)

    for head in range(heads):
        kv, tkv = [], []
        for i in range(2):
            at = (i * heads + head) * rows
            image = [b[start + at : start + at + rows, :] for b in blocks for start in starts]
            text_at = text + ((i + 1) * heads + head) * text_rows
            kv.append(jnp.concatenate(image, axis=0))
            tkv.append(jnp.concatenate([b[text_at : text_at + text_rows, :] for b in blocks], axis=0))
        keys, values = kv[0], with_ones(kv[1])
        tkeys, tvalues = tkv[0], with_ones(tkv[1])
        cols = slice(head * size, (head + 1) * size)
        q_at = (2 * heads + head) * rows
        asked = []
        for k in asked_of:
            if k < n_pieces:
                asked.append(blocks[0][starts[k] + q_at : starts[k] + q_at + rows, :])
            else:
                tq_at = text + head * text_rows
                asked.append(blocks[0][tq_at : tq_at + text_rows, :])
        q = jnp.concatenate(asked, axis=0)
        s_img = lax.dot_general(q, keys, nt, preferred_element_type=f32)
        s_txt = lax.dot_general(q, tkeys, nt, preferred_element_type=f32) + bias
        top = jnp.maximum(
            jnp.max(s_img, axis=1, keepdims=True), jnp.max(s_txt, axis=1, keepdims=True)
        )
        p_img = jnp.exp2((s_img - top) * factor).astype(bf16)
        p_txt = jnp.exp2((s_txt - top) * factor).astype(bf16)
        acc = jnp.dot(p_img, values, preferred_element_type=f32)
        acc = acc + jnp.dot(p_txt, tvalues, preferred_element_type=f32)
        done = (acc[:, :size] / acc[:, size:]).astype(bf16)
        at = 0
        for out_ref in out_refs:
            out_ref[:, cols] = done[at : at + out_ref.shape[0]]
            at += out_ref.shape[0]


def attention(blocks, asked_of, after, n_pieces, heads, rows, text_rows):
    size = blocks[0].shape[1]
    counts = [rows if k < n_pieces else text_rows for k in asked_of]
    queries = sum(counts)
    keys = len(blocks) * (n_pieces * rows + text_rows)
    shapes = [jax.ShapeDtypeStruct((n, heads * size), bf16) for n in counts]
    return pl.pallas_call(
        functools.partial(
            attention_kernel,
            n_pieces,
            len(blocks),
            len(after),
            tuple(asked_of),
            heads,
            rows,
            text_rows,
        ),
        out_shape=shapes,
        in_specs=[VMEM] * len(blocks) + [ANY] * len(after),
        out_specs=[VMEM] * len(shapes),
        compiler_params=params(),
        cost_estimate=cost(
            4 * queries * keys * heads * size,
            4 * (queries + keys) * heads * size,
            queries * keys * heads,
        ),
    )(*blocks, *after)


def assemble_kernel(places, where, *refs):
    pieces, out_ref = refs[: len(places)], refs[-1]
    z = where()[0]
    rows, width = out_ref.shape[0], pieces[0].shape[1]
    for k, piece in zip(places, pieces):
        at = pl.multiple_of((z ^ k) * width, 128)
        out_ref[:, pl.ds(at, width)] = piece[:rows, :]


def assemble(where, pieces, places, after, rows):
    groups, width = len(pieces), pieces[0].shape[1]
    return pl.pallas_call(
        functools.partial(assemble_kernel, tuple(places), where),
        out_shape=jax.ShapeDtypeStruct((rows, groups * width), bf16),
        in_specs=[VMEM] * groups + [ANY] * len(after),
        out_specs=VMEM,
        compiler_params=params(),
        cost_estimate=cost(0, 4 * rows * groups * width),
    )(*pieces, *after)


def gated_kernel(groups, parts, place_of, meta_ref, gate_ref, d_out_ref, *refs):
    msgs, turned = refs[:-1], refs[-1]
    gated = (gate_ref[...] * d_out_ref[...].astype(f32)).astype(bf16)
    turned[...] = gated.astype(f32).T
    rows = msgs[0].shape[2]
    z, oc, dp = meta_ref[0], meta_ref[1], meta_ref[2]
    for k, msg in enumerate(msgs):
        for j in range(parts):
            for g in range(groups):
                at = (dp ^ k) * (groups * parts) + place_of(oc ^ j, z ^ g)
                msg[j, g] = turned[pl.ds(pl.multiple_of(at * rows, 8), rows), :].astype(bf16)


def gated_parts(meta, gate, d_out, n_dp, groups, parts, place_of):
    local, model = d_out.shape
    rows = model // (n_dp * groups * parts)
    return pl.pallas_call(
        functools.partial(gated_kernel, groups, parts, place_of),
        out_shape=[jax.ShapeDtypeStruct((parts, groups, rows, local), bf16)] * n_dp,
        in_specs=[SMEM, VMEM, VMEM],
        out_specs=[VMEM] * n_dp,
        scratch_shapes=[pltpu.VMEM((model, local), f32)],
        compiler_params=params(60),
        cost_estimate=cost(0, 4 * local * model),
    )(meta, gate, d_out)


def gather_kernel(n_dp, *refs):
    pieces, outs = refs[:n_dp], refs[n_dp:]
    for j, out in enumerate(outs):
        for k, piece in enumerate(pieces):
            out[k] = piece[j]


def gather_parts(pieces):
    parts = pieces[0].shape[0]
    shape = (len(pieces),) + pieces[0].shape[1:]
    return pl.pallas_call(
        functools.partial(gather_kernel, len(pieces)),
        out_shape=[jax.ShapeDtypeStruct(shape, bf16)] * parts,
        in_specs=[VMEM] * len(pieces),
        out_specs=[VMEM] * parts,
        compiler_params=params(),
        cost_estimate=cost(0, 4 * math.prod(shape) * parts),
    )(*pieces)


def project_kernel(
    groups, parts, place_of, meta_ref, attn_ref, w_ref, gate_ref, d_out_ref, out_ref, d_attn_ref,
    term_ref, *refs
):
    sent, by_place = refs[:-1], refs[-1]
    rows = attn_ref.shape[0]
    block = 512
    sums = []
    for at in range(0, w_ref.shape[0], block):
        cols = slice(at, at + block)
        got = lax.dot_general(
            attn_ref[...], w_ref[cols, :], (((1,), (1,)), ((), ())), preferred_element_type=f32
        )
        out_ref[:, cols] = (got * gate_ref[:, cols]).astype(bf16)
        sums.append(jnp.sum(got * d_out_ref[:, cols].astype(f32), axis=0, keepdims=True))
    total = jnp.zeros(d_attn_ref.shape, f32)
    for at in range(0, w_ref.shape[0], block):
        cols = slice(at, at + block)
        gated = (gate_ref[:, cols] * d_out_ref[:, cols].astype(f32)).astype(bf16)
        total = total + jnp.dot(gated, w_ref[cols, :], preferred_element_type=f32)
    d_attn_ref[...] = total.astype(bf16)
    sums = jnp.concatenate(sums, axis=1)
    places, width = by_place.shape
    for s in range(places):
        by_place[s : s + 1, :] = sums[:, s * width : (s + 1) * width]
    for g in range(groups):
        at = place_of(meta_ref[1], meta_ref[0] ^ g)
        term_ref[g : g + 1, :] = by_place[pl.ds(at, 1), :]
    for j, out in enumerate(sent):
        out[:rows, :] = attn_ref[...]
        line = [
            by_place[pl.ds(place_of(meta_ref[1] ^ (j + 1), meta_ref[0] ^ g), 1), :]
            for g in range(groups)
        ]
        line = jnp.concatenate(line, axis=1)
        line = jnp.concatenate(
            [line, jnp.zeros((1, attn_ref.shape[1] - groups * width), f32)], axis=1
        ) if attn_ref.shape[1] > groups * width else line
        high = line.astype(bf16).astype(f32)
        lines = [high, line - high, jnp.zeros((EXTRA - 2, line.shape[1]), f32)]
        out[rows:, :] = jnp.concatenate(lines, axis=0).astype(bf16)


def project(meta, attn, out_weight, gate, d_out, groups, parts, place_of):
    rows, inner = attn.shape
    model = out_weight.shape[0]
    width = model // (groups * parts)
    shapes = [jax.ShapeDtypeStruct((rows, model), bf16), jax.ShapeDtypeStruct((rows, inner), bf16)]
    shapes += [jax.ShapeDtypeStruct((groups, width), f32)]
    shapes += [jax.ShapeDtypeStruct((rows + EXTRA, inner), bf16)] * (parts - 1)
    return pl.pallas_call(
        functools.partial(project_kernel, groups, parts, place_of),
        out_shape=shapes,
        in_specs=[SMEM, VMEM, VMEM, VMEM, VMEM],
        out_specs=[VMEM] * (2 + parts),
        scratch_shapes=[pltpu.VMEM((groups * parts, width), f32)],
        compiler_params=params(),
        cost_estimate=cost(4 * rows * inner * model, 2 * inner * model),
    )(meta, attn, out_weight, gate, d_out)


def split_gate(gate, size):
    short = -gate.shape[1] % size
    if short:
        gate = jnp.concatenate([gate, jnp.zeros((1, short), f32)], axis=1)
    high = gate.astype(bf16).astype(f32)
    lines = [p[:, at : at + size] for p in (high, gate - high) for at in range(0, gate.shape[1], size)]
    return jnp.concatenate(lines + [jnp.zeros((EXTRA - len(lines), size), f32)], axis=0)


def joined_gate(lines, width):
    n = -(-width // lines.shape[1])
    both = lines[:n] + lines[n : 2 * n]
    return jnp.concatenate([both[i : i + 1] for i in range(n)], axis=1)[:, :width]


def grad_kernel(n_left, n_pieces, *refs):
    lefts, refs = refs[:n_left], refs[n_left:]
    pieces, refs = refs[:n_pieces], refs[n_pieces:]
    term_ref, outs = refs[0], refs[1:]
    groups, rows, depth = lefts[0].shape[1:]
    width = pieces[0].shape[1]
    size = outs[0].shape[1]
    left = []
    for ref in lefts:
        left += [ref[i].reshape(groups * rows, depth) for i in range(ref.shape[0])]
    left = jnp.concatenate(left, axis=1)
    half = outs[1].shape[0]
    homes = [((outs[0], 0),)]
    homes += [((outs[2 * g - 1], 0), (outs[2 * g], half)) for g in range(1, groups)]

    def put(g, at, value):
        out, start = homes[g][-1] if at >= half else homes[g][0]
        out[at - start : at - start + value.shape[0], :] = value.astype(out.dtype)

    block = 256
    for start in range(0, width, block):
        right = jnp.concatenate([p[:depth, start : start + block] for p in pieces], axis=0)
        got = jnp.dot(left, right, preferred_element_type=f32)
        for g in range(groups):
            for at in range(0, block, size):
                put(g, (start + at) // size * rows, got[g * rows : (g + 1) * rows, at : at + size])
    term = term_ref[...]
    each = term.shape[1]
    for p in pieces:
        if p.shape[0] > depth:
            lines = p[depth:, :].astype(f32)
            line = lines[0:1, :] + lines[1:2, :]
            term = term + jnp.concatenate(
                [line[:, g * each : (g + 1) * each] for g in range(groups)], axis=0
            )
    for g in range(groups):
        put(g, width // size * rows, split_gate(term[g : g + 1], size))


def grad_product(lefts, pieces, term):
    groups, rows, depth = lefts[0].shape[1:]
    width = pieces[0].shape[1]
    size = 128
    total = groups * rows
    depth = depth * len(pieces)
    full = width // size * rows + EXTRA
    half = width // size // 2 * rows
    shapes = [(full, f32)]
    for kind in (bf16, f32, bf16):
        shapes += [(half, kind), (full - half, kind)]
    return pl.pallas_call(
        functools.partial(grad_kernel, len(lefts), len(pieces)),
        out_shape=[jax.ShapeDtypeStruct((n, size), kind) for n, kind in shapes],
        in_specs=[VMEM] * (len(lefts) + len(pieces) + 1),
        out_specs=[VMEM] * len(shapes),
        compiler_params=params(),
        cost_estimate=cost(
            2 * total * depth * width, 2 * (total * depth + depth * width + total * width)
        ),
    )(*lefts, *pieces, term)


def pair_kernel(gate_width, n_through, own_ref, got_ref, *refs):
    out_ref = refs[n_through]
    for ref, out in zip(refs[:n_through], refs[n_through + 1 :]):
        out[...] = ref[...]
    total = own_ref[...] + got_ref[...].astype(f32)
    if not gate_width:
        out_ref[...] = total.astype(bf16)
    else:
        end = total.shape[0] - EXTRA
        out_ref[:end, :] = total[:end].astype(bf16)
        gate = joined_gate(total[end:], gate_width)
        out_ref[end:, :] = split_gate(gate, total.shape[1]).astype(bf16)


def pair_sum(own, got, gate_width, through):
    return pl.pallas_call(
        functools.partial(pair_kernel, gate_width, len(through)),
        out_shape=[jax.ShapeDtypeStruct(x.shape, bf16) for x in [got] + through],
        in_specs=[VMEM] * (2 + len(through)),
        out_specs=[VMEM] * (1 + len(through)),
        compiler_params=params(),
        cost_estimate=cost(0, 8 * own.size),
    )(own, got, *through)


def final_kernel(own_ref, far_low, far_high, near_low, near_high, out_ref, gate_ref):
    size = own_ref.shape[1]
    rows = out_ref.shape[0]
    half = far_low.shape[0]

    def total(at, count):
        refs, start = ((far_high, near_high), half) if at >= half else ((far_low, near_low), 0)
        got = own_ref[at : at + count, :]
        for ref in refs:
            got = got + ref[at - start : at - start + count, :].astype(f32)
        return got

    for i in range(out_ref.shape[1] // size):
        out_ref[:, i * size : (i + 1) * size] = total(i * rows, rows)
    gate_ref[...] = joined_gate(total(own_ref.shape[0] - EXTRA, EXTRA), gate_ref.shape[1])


def final_sum(own, far, near, rows, width, gate_width):
    return pl.pallas_call(
        final_kernel,
        out_shape=[
            jax.ShapeDtypeStruct((rows, width), f32),
            jax.ShapeDtypeStruct((1, gate_width), f32),
        ],
        in_specs=[VMEM] * 5,
        out_specs=[VMEM] * 2,
        compiler_params=params(),
        cost_estimate=cost(0, 8 * rows * width),
    )(own, *far, *near)


def on_device(
    caption_states,
    caption_gain,
    text_proj,
    caption_len,
    slot_source,
    query_gain,
    key_gain,
    image_q,
    image_k,
    image_v,
    out_weight,
    gate,
    d_out,
):
    n_dp = lax.axis_size("dp")
    n_seq = lax.axis_size("seq")
    G, C = GROUPS, CORES
    O = n_seq // (G * C)
    OC = O * C
    dp = lax.axis_index("dp")
    seq = lax.axis_index("seq")

    def where():
        at = lax.axis_index("seq")
        return (at // C) % G, (at // (G * C)) * C + at % C

    z, oc = where()

    def place(oc_at, z_at):
        return ((oc_at // C) * G + z_at) * C + oc_at % C

    def to_z(x, k):
        perm = [(place(a, b), place(a, b ^ k)) for a in range(OC) for b in range(G)]
        return lax.ppermute(x, "seq", perm)

    def to_oc(x, j):
        perm = [(place(a, b), place(a ^ j, b)) for a in range(OC) for b in range(G)]
        return lax.ppermute(x, "seq", perm)

    def to_dp(x, k):
        return lax.ppermute(x, "dp", [(a, a ^ k) for a in range(n_dp)])

    def part(x, index, size, axis):
        return lax.dynamic_slice_in_dim(x, index * size, size, axis)

    slot_total = slot_source.shape[1]
    slot_local = slot_total // n_seq
    image_local = image_q.shape[1]
    inner_width = image_q.shape[2]
    model_width = out_weight.shape[0]
    head_size = query_gain.shape[0]
    gw = inner_width // G
    order = [2, 3, 1]
    meta = jnp.stack([z, oc, dp]).astype(jnp.int32)

    heads = gw // head_size
    text_rows = G * slot_local
    own, *rest = text_project(
        caption_len, slot_source, caption_states[0], caption_gain[None],
        query_gain[None], key_gain[None], image_k[0], image_v[0], image_q[0], text_proj,
        G, OC, place, where,
    )
    packed, sent = rest[:G], rest[G:]
    images = {0: packed[0]}
    for k in order:
        images[k] = to_z(packed[k], k)
    images = [images[k] for k in [0] + order]
    got = [to_oc(x, j + 1) for j, x in enumerate(sent)]
    own, sent = text_sum(own, got, text_rows)
    own, sent, images[0] = text_sum(own, [to_z(sent, 1)], text_rows, [packed[0]])
    got = to_z(sent, 2)

    gg = gated_parts(meta, gate, d_out[0], n_dp, G, OC, place)
    gg_dp = [gg[0], to_dp(gg[1], 1)]
    block = block_of(own, got, gg_dp[1:], images, DT5, heads)
    blocks = [block] + [to_oc(block, j) for j in range(1, OC)]
    *first, text_out = attention(
        blocks, [1, 2, 3, G], [], G, heads, image_local, text_rows
    )
    second = attention(
        blocks, [0], [text_out], G, heads, image_local, text_rows
    )
    outs = dict(zip(order + [0], first + list(second)))

    back = {}
    for k in order + [0]:
        rows = jnp.concatenate([outs[k], part(text_out, z ^ k, slot_local, 0)], axis=0)
        back[k] = to_z(rows, k) if k else rows
    back = [back[k] for k in order + [0]]
    gg_dp += [to_dp(gg[k], k) for k in range(2, n_dp)]
    dp_order = [0] + list(range(n_dp - 1, 0, -1))
    lefts = gather_parts([gg_dp[k] for k in dp_order])
    lefts = [to_oc(g, j) if j else g for j, g in enumerate(lefts)]
    image_attn = assemble(where, back, order + [0], gg_dp[1:], image_local)
    text_attn = jnp.zeros((slot_local, inner_width), bf16)
    own_usable = part(slot_source[0] < caption_len[0], seq, slot_local, 0)
    for k, got in zip(order + [0], back):
        rows = jnp.where(own_usable[:, None], got[image_local:], jnp.zeros((), bf16))
        text_attn = lax.dynamic_update_slice_in_dim(text_attn, rows, (z ^ k) * gw, 1)

    pieces = [image_attn] + [to_dp(image_attn, k) for k in dp_order[1:]]
    image_out, d_attn, term, *sent = project(
        meta, image_attn, out_weight, gate, d_out[0], G, OC, place
    )
    for j in range(1, OC):
        pieces += [to_oc(sent[j - 1], j)] + [to_oc(p, j) for p in pieces[1:n_dp]]
    R = model_width // (n_dp * n_seq)
    gate_width = model_width // n_seq
    own, *blocks = grad_product(lefts, pieces, term)
    got = [to_z(x, 1) for x in blocks[4:]]
    (low,) = pair_sum(blocks[2], got[0], 0, [])
    high, *near = pair_sum(blocks[3], got[1], gate_width, blocks[:2])
    far = [to_z(x, 2) for x in (low, high)]
    near = [to_z(x, 1) for x in near]
    grad_wo, grad_gate = final_sum(own, far, near, R, inner_width, gate_width)
    return (image_out[None], text_attn[None], d_attn[None], grad_wo, grad_gate)


def solution(mesh):
    in_specs = (
        P("dp", None, "seq"),
        P("seq"),
        P("seq", None),
        P("dp"),
        P("dp", None),
        P(),
        P(),
        P("dp", "seq", None),
        P("dp", "seq", None),
        P("dp", "seq", None),
        P(),
        P("dp", None),
        P("dp", "seq", None),
    )
    out_specs = (
        P("dp", "seq", None),
        P("dp", "seq", None),
        P("dp", "seq", None),
        P(("dp", "seq"), None),
        P("dp", "seq"),
    )
    return jax.shard_map(
        on_device, mesh=mesh, in_specs=in_specs, out_specs=out_specs, check_vma=False
    )
```

```python
import math
import functools
import jax
import jax.numpy as jnp
from jax import lax
from jax.experimental import pallas as pl
from jax.experimental.pallas import tpu as pltpu
from jax.sharding import PartitionSpec as P

DT5 = 4096
CORES = 2
GROUPS = 4

eps_norm = 1e-06
f32 = jnp.float32
bf16 = jnp.bfloat16
EXTRA = 16


VMEM = pl.BlockSpec(memory_space=pltpu.VMEM)
SMEM = pl.BlockSpec(memory_space=pltpu.SMEM)
ANY = pl.BlockSpec(memory_space=pl.ANY)


def params(mib=16):
    return pltpu.CompilerParams(vmem_limit_bytes=int(mib * 1024 * 1024))


def cost(flops, bytes_accessed, transcendentals=0):
    return pl.CostEstimate(
        flops=flops, bytes_accessed=bytes_accessed, transcendentals=transcendentals
    )


def split_tail(squares, width):
    high = squares.astype(bf16).astype(f32)
    low = squares - high
    lane = lax.broadcasted_iota(jnp.int32, (squares.shape[0], width), 1)
    return jnp.where(lane == 0, high, jnp.where(lane == 1, low, 0.0))


def joined(tail):
    return tail[:, 0:1] + tail[:, 1:2]


def text_kernel(
    groups, heads, place_of, where, len_ref, src_ref, states_ref, gain_ref, qg_ref, kg_ref,
    k_ref, v_ref, q_ref, w_ref, own_ref, *refs
):
    meta_ref = where()
    packed, refs = refs[:groups], refs[groups:]
    msgs, (w_all, sums, loaded, stage, w_sems, in_sems, out_sems) = refs[:-7], refs[-7:]
    size = own_ref.shape[2]
    rows = (own_ref.shape[1] - EXTRA) // (3 * heads + 1)
    width = heads * size
    slots = states_ref.shape[0]
    slot_local = rows // groups
    copies = []
    block = w_all.shape[0] // w_sems.shape[0]
    for i in range(w_sems.shape[0]):
        part = pl.ds(i * block, block)
        copies.append(pltpu.make_async_copy(w_ref.at[part], w_all.at[part], w_sems.at[i]))
        copies[-1].start()
    loads = []
    for i, ref in enumerate((k_ref, v_ref, q_ref)):
        loads.append(pltpu.make_async_copy(ref, loaded.at[i], in_sems.at[i]))
        loads[-1].start()

    def slot_at(row):
        z_at = (row % rows) // slot_local
        return place_of(meta_ref[1] ^ (row // rows), z_at) * slot_local + row % slot_local

    iota = functools.partial(lax.broadcasted_iota, jnp.int32, (slots, slots))
    sources = src_ref[...].astype(f32)
    chosen = (iota(1) == slot_at(iota(0))).astype(f32)
    source_col = jnp.sum(chosen * sources, axis=1, keepdims=True)
    pick = (iota(1).astype(f32) == source_col).astype(bf16)
    chosen_t = (iota(0) == slot_at(iota(1))).astype(bf16)
    source_row = jnp.dot(sources.astype(bf16), chosen_t, preferred_element_type=f32)
    bias = jnp.where(source_row < len_ref[0].astype(f32), 0.0, -1e30)
    end = own_ref.shape[1] - EXTRA
    own_ref[0, end:, :] = jnp.zeros((EXTRA, size), f32)
    own_ref[0, end : end + 1, :] = qg_ref[...]
    own_ref[0, end + 1 : end + 2, :] = kg_ref[...]
    own_ref[0, end + 2 : end + 3, :slots] = bias

    picked = jnp.dot(pick, states_ref[...], preferred_element_type=f32)
    scaled = (picked * gain_ref[...]).astype(bf16)
    tail = split_tail(jnp.sum(picked * picked, axis=1, keepdims=True), size)
    for copy in loads:
        copy.wait()
    local = loaded.shape[1]
    stores = []
    for g in range(groups):
        for i in range(3):
            for head in range(heads):
                at = ((meta_ref[0] ^ g) * heads + head) * size
                to = (i * heads + head) * local
                stage[g, to : to + local, :] = loaded[i, :, pl.ds(pl.multiple_of(at, 128), size)]
        stores.append(pltpu.make_async_copy(stage.at[g], packed[g], out_sems.at[g]))
        stores[-1].start()
    def product(part, g, i):
        at = (i * groups + (meta_ref[0] ^ g)) * width
        columns = pl.ds(pl.multiple_of(at, 128), width)
        rows_of = slice(part * block, (part + 1) * block)
        return jnp.dot(scaled[:, rows_of], w_all[rows_of, columns], preferred_element_type=f32)

    copies[0].wait()
    for g in range(groups):
        for i in range(3):
            sums[3 * g + i] = product(0, g, i)
    copies[1].wait()
    for g in range(groups):
        for i in range(3):
            got = sums[3 * g + i] + product(1, g, i)
            for head in range(heads):
                part = got[:, head * size : (head + 1) * size]
                to = slice((i * heads + head) * rows, (i * heads + head + 1) * rows)
                own_ref[g, to, :] = part[:rows]
                for j, msg in enumerate(msgs):
                    msg[g, to, :] = part[(j + 1) * rows : (j + 2) * rows].astype(bf16)
        own_ref[g, 3 * heads * rows : end, :] = tail[:rows]
        for j, msg in enumerate(msgs):
            msg[g, 3 * heads * rows :, :] = tail[(j + 1) * rows : (j + 2) * rows].astype(bf16)
    for copy in stores:
        copy.wait()


def text_project(
    length, sources, states, gain, query_gain, key_gain, keys, values, queries, text_proj,
    groups, parts, place_of, where
):
    slots, depth = states.shape
    size = query_gain.shape[1]
    heads = text_proj.shape[1] // (3 * groups * size)
    text_rows = (3 * heads + 1) * slots // parts
    shapes = [jax.ShapeDtypeStruct((groups, text_rows + EXTRA, size), f32)]
    shapes += [jax.ShapeDtypeStruct((3 * heads * keys.shape[0], size), bf16)] * groups
    shapes += [jax.ShapeDtypeStruct((groups, text_rows, size), bf16)] * (parts - 1)
    return pl.pallas_call(
        functools.partial(text_kernel, groups, heads, place_of, where),
        out_shape=shapes,
        in_specs=[SMEM] + [VMEM] * 5 + [ANY] * 4,
        out_specs=[VMEM] + [ANY] * groups + [VMEM] * (parts - 1),
        scratch_shapes=[
            pltpu.VMEM(text_proj.shape, bf16),
            pltpu.VMEM((3 * groups, slots, heads * size), f32),
            pltpu.VMEM((3,) + keys.shape, bf16),
            pltpu.VMEM((groups, 3 * heads * keys.shape[0], size), bf16),
            pltpu.SemaphoreType.DMA((2,)),
            pltpu.SemaphoreType.DMA((3,)),
            pltpu.SemaphoreType.DMA((groups,)),
        ],
        compiler_params=params(60),
        cost_estimate=cost(
            2 * slots * depth * text_proj.shape[1], 2 * depth * text_proj.shape[1]
        ),
    )(
        length, sources, states, gain, query_gain, key_gain, keys, values, queries, text_proj
    )


def text_sum_kernel(n_got, tail_rows, n_through, own_ref, *refs):
    got, refs = refs[:n_got], refs[n_got:]
    for ref, out in zip(refs[:n_through], refs[n_through + 2 :]):
        out[...] = ref[...]
    keep_ref, send_ref = refs[n_through : n_through + 2]
    groups, text_rows, size = got[0].shape
    for g in range(groups):
        total = own_ref[g, :text_rows, :]
        for ref in got:
            total = total + ref[g].astype(f32)
        end = text_rows - tail_rows
        tail = split_tail(joined(total[end:]), size)
        if g % 2 == 0:
            keep_ref[g // 2, :end, :] = total[:end]
            keep_ref[g // 2, end:text_rows, :] = tail
            keep_ref[g // 2, text_rows:, :] = own_ref[g, text_rows:, :]
        else:
            send_ref[g // 2, :end, :] = total[:end].astype(bf16)
            send_ref[g // 2, end:, :] = tail.astype(bf16)


def text_sum(own, got, tail_rows, through=()):
    groups, rows, size = own.shape
    return pl.pallas_call(
        functools.partial(text_sum_kernel, len(got), tail_rows, len(through)),
        out_shape=[
            jax.ShapeDtypeStruct((groups // 2, rows, size), f32),
            jax.ShapeDtypeStruct((groups // 2, rows - EXTRA, size), bf16),
        ]
        + [jax.ShapeDtypeStruct(x.shape, x.dtype) for x in through],
        in_specs=[VMEM] * (1 + len(got) + len(through)),
        out_specs=[VMEM] * (2 + len(through)),
        compiler_params=params(),
        cost_estimate=cost(0, 8 * groups * rows * size),
    )(own, *got, *through)


def block_kernel(features, heads, n_pieces, own_ref, got_ref, *refs):
    pieces, out_ref = refs[:n_pieces], refs[-1]
    each = pieces[0].shape[0]
    for k, ref in enumerate(pieces):
        out_ref[k * each : (k + 1) * each, :] = ref[...]
    size = own_ref.shape[2]
    text_rows = got_ref.shape[1]
    rows = text_rows // (3 * heads + 1)
    total = own_ref[0, :text_rows, :] + got_ref[0].astype(f32)
    rate = lax.rsqrt(joined(total[3 * heads * rows :]) / features + eps_norm)
    start = n_pieces * each
    for i in range(3):
        for head in range(heads):
            at = (i * heads + head) * rows
            x = total[at : at + rows] * rate
            if i < 2:
                mean = jnp.sum(x * x, axis=1, keepdims=True) / size
                gain = own_ref[0, text_rows + i : text_rows + i + 1, :]
                x = x * lax.rsqrt(mean + eps_norm) * gain
            out_ref[start + at : start + at + rows, :] = x.astype(bf16)
    bias = own_ref[0, text_rows + 2 : text_rows + 3, :]
    start = start + 3 * heads * rows
    out_ref[start:, :] = jnp.broadcast_to(bias, (EXTRA, size)).astype(bf16)


def block_of(own, got, after, pieces, features, heads):
    rows, size = own.shape[1:]
    total = (rows - EXTRA) // (3 * heads + 1) * 3 * heads + EXTRA
    total += pieces[0].shape[0] * len(pieces)
    return pl.pallas_call(
        functools.partial(block_kernel, features, heads, len(pieces)),
        out_shape=jax.ShapeDtypeStruct((total, size), bf16),
        in_specs=[VMEM] * (2 + len(pieces)) + [ANY] * len(after),
        out_specs=VMEM,
        compiler_params=params(),
        cost_estimate=cost(0, 4 * total * size),
    )(own, got, *pieces, *after)


def attention_kernel(n_pieces, n_cores, n_after, asked_of, heads, rows, text_rows, *refs):
    blocks, out_refs = refs[:n_cores], refs[n_cores + n_after :]
    size = blocks[0].shape[1]
    factor = size ** (-0.5) * math.log2(math.e)
    nt = (((1,), (1,)), ((), ()))
    each = 3 * heads * rows
    starts = [k * each for k in range(n_pieces)]
    text = n_pieces * each
    end = text + 3 * heads * text_rows
    bias = blocks[0][end : end + EXTRA, :][:1, : n_cores * text_rows].astype(f32)

    def with_ones(values):
        return jnp.concatenate([values, jnp.ones(values.shape, bf16)], axis=1)

    for head in range(heads):
        kv, tkv = [], []
        for i in range(2):
            at = (i * heads + head) * rows
            image = [b[start + at : start + at + rows, :] for b in blocks for start in starts]
            text_at = text + ((i + 1) * heads + head) * text_rows
            kv.append(jnp.concatenate(image, axis=0))
            tkv.append(jnp.concatenate([b[text_at : text_at + text_rows, :] for b in blocks], axis=0))
        keys, values = kv[0], with_ones(kv[1])
        tkeys, tvalues = tkv[0], with_ones(tkv[1])
        cols = slice(head * size, (head + 1) * size)
        q_at = (2 * heads + head) * rows
        asked = []
        for k in asked_of:
            if k < n_pieces:
                asked.append(blocks[0][starts[k] + q_at : starts[k] + q_at + rows, :])
            else:
                tq_at = text + head * text_rows
                asked.append(blocks[0][tq_at : tq_at + text_rows, :])
        q = jnp.concatenate(asked, axis=0)
        s_img = lax.dot_general(q, keys, nt, preferred_element_type=f32)
        s_txt = lax.dot_general(q, tkeys, nt, preferred_element_type=f32) + bias
        top = jnp.maximum(
            jnp.max(s_img, axis=1, keepdims=True), jnp.max(s_txt, axis=1, keepdims=True)
        )
        p_img = jnp.exp2((s_img - top) * factor).astype(bf16)
        p_txt = jnp.exp2((s_txt - top) * factor).astype(bf16)
        acc = jnp.dot(p_img, values, preferred_element_type=f32)
        acc = acc + jnp.dot(p_txt, tvalues, preferred_element_type=f32)
        done = (acc[:, :size] / acc[:, size:]).astype(bf16)
        at = 0
        for out_ref in out_refs:
            out_ref[:, cols] = done[at : at + out_ref.shape[0]]
            at += out_ref.shape[0]


def attention(blocks, asked_of, after, n_pieces, heads, rows, text_rows):
    size = blocks[0].shape[1]
    counts = [rows if k < n_pieces else text_rows for k in asked_of]
    queries = sum(counts)
    keys = len(blocks) * (n_pieces * rows + text_rows)
    shapes = [jax.ShapeDtypeStruct((n, heads * size), bf16) for n in counts]
    return pl.pallas_call(
        functools.partial(
            attention_kernel,
            n_pieces,
            len(blocks),
            len(after),
            tuple(asked_of),
            heads,
            rows,
            text_rows,
        ),
        out_shape=shapes,
        in_specs=[VMEM] * len(blocks) + [ANY] * len(after),
        out_specs=[VMEM] * len(shapes),
        compiler_params=params(),
        cost_estimate=cost(
            4 * queries * keys * heads * size,
            4 * (queries + keys) * heads * size,
            queries * keys * heads,
        ),
    )(*blocks, *after)


def assemble_kernel(places, where, *refs):
    pieces, out_ref = refs[: len(places)], refs[-1]
    z = where()[0]
    rows, width = out_ref.shape[0], pieces[0].shape[1]
    for k, piece in zip(places, pieces):
        at = pl.multiple_of((z ^ k) * width, 128)
        out_ref[:, pl.ds(at, width)] = piece[:rows, :]


def assemble(where, pieces, places, after, rows):
    groups, width = len(pieces), pieces[0].shape[1]
    return pl.pallas_call(
        functools.partial(assemble_kernel, tuple(places), where),
        out_shape=jax.ShapeDtypeStruct((rows, groups * width), bf16),
        in_specs=[VMEM] * groups + [ANY] * len(after),
        out_specs=VMEM,
        compiler_params=params(),
        cost_estimate=cost(0, 4 * rows * groups * width),
    )(*pieces, *after)


def gated_kernel(groups, parts, place_of, meta_ref, gate_ref, d_out_ref, *refs):
    msgs, turned = refs[:-1], refs[-1]
    gated = (gate_ref[...] * d_out_ref[...].astype(f32)).astype(bf16)
    turned[...] = gated.astype(f32).T
    rows = msgs[0].shape[2]
    z, oc, dp = meta_ref[0], meta_ref[1], meta_ref[2]
    for k, msg in enumerate(msgs):
        for j in range(parts):
            for g in range(groups):
                at = (dp ^ k) * (groups * parts) + place_of(oc ^ j, z ^ g)
                msg[j, g] = turned[pl.ds(pl.multiple_of(at * rows, 8), rows), :].astype(bf16)


def gated_parts(meta, gate, d_out, n_dp, groups, parts, place_of):
    local, model = d_out.shape
    rows = model // (n_dp * groups * parts)
    return pl.pallas_call(
        functools.partial(gated_kernel, groups, parts, place_of),
        out_shape=[jax.ShapeDtypeStruct((parts, groups, rows, local), bf16)] * n_dp,
        in_specs=[SMEM, VMEM, VMEM],
        out_specs=[VMEM] * n_dp,
        scratch_shapes=[pltpu.VMEM((model, local), f32)],
        compiler_params=params(60),
        cost_estimate=cost(0, 4 * local * model),
    )(meta, gate, d_out)


def gather_kernel(n_dp, *refs):
    pieces, outs = refs[:n_dp], refs[n_dp:]
    for j, out in enumerate(outs):
        for k, piece in enumerate(pieces):
            out[k] = piece[j]


def gather_parts(pieces):
    parts = pieces[0].shape[0]
    shape = (len(pieces),) + pieces[0].shape[1:]
    return pl.pallas_call(
        functools.partial(gather_kernel, len(pieces)),
        out_shape=[jax.ShapeDtypeStruct(shape, bf16)] * parts,
        in_specs=[VMEM] * len(pieces),
        out_specs=[VMEM] * parts,
        compiler_params=params(),
        cost_estimate=cost(0, 4 * math.prod(shape) * parts),
    )(*pieces)


def project_kernel(
    groups, parts, place_of, meta_ref, attn_ref, w_ref, gate_ref, d_out_ref, out_ref, d_attn_ref,
    term_ref, *refs
):
    sent, by_place = refs[:-1], refs[-1]
    rows = attn_ref.shape[0]
    block = 512
    sums = []
    for at in range(0, w_ref.shape[0], block):
        cols = slice(at, at + block)
        got = lax.dot_general(
            attn_ref[...], w_ref[cols, :], (((1,), (1,)), ((), ())), preferred_element_type=f32
        )
        out_ref[:, cols] = (got * gate_ref[:, cols]).astype(bf16)
        sums.append(jnp.sum(got * d_out_ref[:, cols].astype(f32), axis=0, keepdims=True))
    total = jnp.zeros(d_attn_ref.shape, f32)
    for at in range(0, w_ref.shape[0], block):
        cols = slice(at, at + block)
        gated = (gate_ref[:, cols] * d_out_ref[:, cols].astype(f32)).astype(bf16)
        total = total + jnp.dot(gated, w_ref[cols, :], preferred_element_type=f32)
    d_attn_ref[...] = total.astype(bf16)
    sums = jnp.concatenate(sums, axis=1)
    places, width = by_place.shape
    for s in range(places):
        by_place[s : s + 1, :] = sums[:, s * width : (s + 1) * width]
    for g in range(groups):
        at = place_of(meta_ref[1], meta_ref[0] ^ g)
        term_ref[g : g + 1, :] = by_place[pl.ds(at, 1), :]
    for j, out in enumerate(sent):
        out[:rows, :] = attn_ref[...]
        line = [
            by_place[pl.ds(place_of(meta_ref[1] ^ (j + 1), meta_ref[0] ^ g), 1), :]
            for g in range(groups)
        ]
        line = jnp.concatenate(line, axis=1)
        line = jnp.concatenate(
            [line, jnp.zeros((1, attn_ref.shape[1] - groups * width), f32)], axis=1
        ) if attn_ref.shape[1] > groups * width else line
        high = line.astype(bf16).astype(f32)
        lines = [high, line - high, jnp.zeros((EXTRA - 2, line.shape[1]), f32)]
        out[rows:, :] = jnp.concatenate(lines, axis=0).astype(bf16)


def project(meta, attn, out_weight, gate, d_out, groups, parts, place_of):
    rows, inner = attn.shape
    model = out_weight.shape[0]
    width = model // (groups * parts)
    shapes = [jax.ShapeDtypeStruct((rows, model), bf16), jax.ShapeDtypeStruct((rows, inner), bf16)]
    shapes += [jax.ShapeDtypeStruct((groups, width), f32)]
    shapes += [jax.ShapeDtypeStruct((rows + EXTRA, inner), bf16)] * (parts - 1)
    return pl.pallas_call(
        functools.partial(project_kernel, groups, parts, place_of),
        out_shape=shapes,
        in_specs=[SMEM, VMEM, VMEM, VMEM, VMEM],
        out_specs=[VMEM] * (2 + parts),
        scratch_shapes=[pltpu.VMEM((groups * parts, width), f32)],
        compiler_params=params(),
        cost_estimate=cost(4 * rows * inner * model, 2 * inner * model),
    )(meta, attn, out_weight, gate, d_out)


def split_gate(gate, size):
    short = -gate.shape[1] % size
    if short:
        gate = jnp.concatenate([gate, jnp.zeros((1, short), f32)], axis=1)
    high = gate.astype(bf16).astype(f32)
    lines = [p[:, at : at + size] for p in (high, gate - high) for at in range(0, gate.shape[1], size)]
    return jnp.concatenate(lines + [jnp.zeros((EXTRA - len(lines), size), f32)], axis=0)


def joined_gate(lines, width):
    n = -(-width // lines.shape[1])
    both = lines[:n] + lines[n : 2 * n]
    return jnp.concatenate([both[i : i + 1] for i in range(n)], axis=1)[:, :width]


def grad_kernel(n_left, n_pieces, *refs):
    lefts, refs = refs[:n_left], refs[n_left:]
    pieces, refs = refs[:n_pieces], refs[n_pieces:]
    term_ref, outs = refs[0], refs[1:]
    groups, rows, depth = lefts[0].shape[1:]
    width = pieces[0].shape[1]
    size = outs[0].shape[1]
    left = []
    for ref in lefts:
        left += [ref[i].reshape(groups * rows, depth) for i in range(ref.shape[0])]
    left = jnp.concatenate(left, axis=1)
    half = outs[1].shape[0]
    homes = [((outs[0], 0),)]
    homes += [((outs[2 * g - 1], 0), (outs[2 * g], half)) for g in range(1, groups)]

    def put(g, at, value):
        out, start = homes[g][-1] if at >= half else homes[g][0]
        out[at - start : at - start + value.shape[0], :] = value.astype(out.dtype)

    block = 256
    for start in range(0, width, block):
        right = jnp.concatenate([p[:depth, start : start + block] for p in pieces], axis=0)
        got = jnp.dot(left, right, preferred_element_type=f32)
        for g in range(groups):
            for at in range(0, block, size):
                put(g, (start + at) // size * rows, got[g * rows : (g + 1) * rows, at : at + size])
    term = term_ref[...]
    each = term.shape[1]
    for p in pieces:
        if p.shape[0] > depth:
            lines = p[depth:, :].astype(f32)
            line = lines[0:1, :] + lines[1:2, :]
            term = term + jnp.concatenate(
                [line[:, g * each : (g + 1) * each] for g in range(groups)], axis=0
            )
    for g in range(groups):
        put(g, width // size * rows, split_gate(term[g : g + 1], size))


def grad_product(lefts, pieces, term):
    groups, rows, depth = lefts[0].shape[1:]
    width = pieces[0].shape[1]
    size = 128
    total = groups * rows
    depth = depth * len(pieces)
    full = width // size * rows + EXTRA
    half = width // size // 2 * rows
    shapes = [(full, f32)]
    for kind in (bf16, f32, bf16):
        shapes += [(half, kind), (full - half, kind)]
    return pl.pallas_call(
        functools.partial(grad_kernel, len(lefts), len(pieces)),
        out_shape=[jax.ShapeDtypeStruct((n, size), kind) for n, kind in shapes],
        in_specs=[VMEM] * (len(lefts) + len(pieces) + 1),
        out_specs=[VMEM] * len(shapes),
        compiler_params=params(),
        cost_estimate=cost(
            2 * total * depth * width, 2 * (total * depth + depth * width + total * width)
        ),
    )(*lefts, *pieces, term)


def pair_kernel(gate_width, n_through, own_ref, got_ref, *refs):
    out_ref = refs[n_through]
    for ref, out in zip(refs[:n_through], refs[n_through + 1 :]):
        out[...] = ref[...]
    total = own_ref[...] + got_ref[...].astype(f32)
    if not gate_width:
        out_ref[...] = total.astype(bf16)
    else:
        end = total.shape[0] - EXTRA
        out_ref[:end, :] = total[:end].astype(bf16)
        gate = joined_gate(total[end:], gate_width)
        out_ref[end:, :] = split_gate(gate, total.shape[1]).astype(bf16)


def pair_sum(own, got, gate_width, through):
    return pl.pallas_call(
        functools.partial(pair_kernel, gate_width, len(through)),
        out_shape=[jax.ShapeDtypeStruct(x.shape, bf16) for x in [got] + through],
        in_specs=[VMEM] * (2 + len(through)),
        out_specs=[VMEM] * (1 + len(through)),
        compiler_params=params(),
        cost_estimate=cost(0, 8 * own.size),
    )(own, got, *through)


def final_kernel(own_ref, far_low, far_high, near_low, near_high, out_ref, gate_ref):
    size = own_ref.shape[1]
    rows = out_ref.shape[0]
    half = far_low.shape[0]

    def total(at, count):
        refs, start = ((far_high, near_high), half) if at >= half else ((far_low, near_low), 0)
        got = own_ref[at : at + count, :]
        for ref in refs:
            got = got + ref[at - start : at - start + count, :].astype(f32)
        return got

    for i in range(out_ref.shape[1] // size):
        out_ref[:, i * size : (i + 1) * size] = total(i * rows, rows)
    gate_ref[...] = joined_gate(total(own_ref.shape[0] - EXTRA, EXTRA), gate_ref.shape[1])


def final_sum(own, far, near, rows, width, gate_width):
    return pl.pallas_call(
        final_kernel,
        out_shape=[
            jax.ShapeDtypeStruct((rows, width), f32),
            jax.ShapeDtypeStruct((1, gate_width), f32),
        ],
        in_specs=[VMEM] * 5,
        out_specs=[VMEM] * 2,
        compiler_params=params(),
        cost_estimate=cost(0, 8 * rows * width),
    )(own, *far, *near)


def on_device(
    caption_states,
    caption_gain,
    text_proj,
    caption_len,
    slot_source,
    query_gain,
    key_gain,
    image_q,
    image_k,
    image_v,
    out_weight,
    gate,
    d_out,
):
    n_dp = lax.axis_size("dp")
    n_seq = lax.axis_size("seq")
    G, C = GROUPS, CORES
    O = n_seq // (G * C)
    OC = O * C
    dp = lax.axis_index("dp")
    seq = lax.axis_index("seq")

    def where():
        at = lax.axis_index("seq")
        return (at // C) % G, (at // (G * C)) * C + at % C

    z, oc = where()

    def place(oc_at, z_at):
        return ((oc_at // C) * G + z_at) * C + oc_at % C

    def to_z(x, k):
        perm = [(place(a, b), place(a, b ^ k)) for a in range(OC) for b in range(G)]
        return lax.ppermute(x, "seq", perm)

    def to_oc(x, j):
        perm = [(place(a, b), place(a ^ j, b)) for a in range(OC) for b in range(G)]
        return lax.ppermute(x, "seq", perm)

    def to_dp(x, k):
        return lax.ppermute(x, "dp", [(a, a ^ k) for a in range(n_dp)])

    def part(x, index, size, axis):
        return lax.dynamic_slice_in_dim(x, index * size, size, axis)

    slot_total = slot_source.shape[1]
    slot_local = slot_total // n_seq
    image_local = image_q.shape[1]
    inner_width = image_q.shape[2]
    model_width = out_weight.shape[0]
    head_size = query_gain.shape[0]
    gw = inner_width // G
    order = [2, 3, 1]
    meta = jnp.stack([z, oc, dp]).astype(jnp.int32)

    heads = gw // head_size
    text_rows = G * slot_local
    own, *rest = text_project(
        caption_len, slot_source, caption_states[0], caption_gain[None],
        query_gain[None], key_gain[None], image_k[0], image_v[0], image_q[0], text_proj,
        G, OC, place, where,
    )
    packed, sent = rest[:G], rest[G:]
    images = {0: packed[0]}
    for k in order:
        images[k] = to_z(packed[k], k)
    images = [images[k] for k in [0] + order]
    got = [to_oc(x, j + 1) for j, x in enumerate(sent)]
    own, sent, images[0] = text_sum(own, got, text_rows, [packed[0]])
    own, sent = text_sum(own, [to_z(sent, 1)], text_rows)
    got = to_z(sent, 2)

    gg = gated_parts(meta, gate, d_out[0], n_dp, G, OC, place)
    gg_dp = [gg[0], to_dp(gg[1], 1)]
    block = block_of(own, got, gg_dp[1:], images, DT5, heads)
    blocks = [block] + [to_oc(block, j) for j in range(1, OC)]
    *first, text_out = attention(
        blocks, [1, 2, 3, G], [], G, heads, image_local, text_rows
    )
    second = attention(
        blocks, [0], [text_out], G, heads, image_local, text_rows
    )
    outs = dict(zip(order + [0], first + list(second)))

    back = {}
    for k in order + [0]:
        rows = jnp.concatenate([outs[k], part(text_out, z ^ k, slot_local, 0)], axis=0)
        back[k] = to_z(rows, k) if k else rows
    back = [back[k] for k in order + [0]]
    gg_dp += [to_dp(gg[k], k) for k in range(2, n_dp)]
    dp_order = [0] + list(range(n_dp - 1, 0, -1))
    lefts = gather_parts([gg_dp[k] for k in dp_order])
    lefts = [to_oc(g, j) if j else g for j, g in enumerate(lefts)]
    image_attn = assemble(where, back, order + [0], gg_dp[1:], image_local)
    text_attn = jnp.zeros((slot_local, inner_width), bf16)
    own_usable = part(slot_source[0] < caption_len[0], seq, slot_local, 0)
    for k, got in zip(order + [0], back):
        rows = jnp.where(own_usable[:, None], got[image_local:], jnp.zeros((), bf16))
        text_attn = lax.dynamic_update_slice_in_dim(text_attn, rows, (z ^ k) * gw, 1)

    pieces = [image_attn] + [to_dp(image_attn, k) for k in dp_order[1:]]
    image_out, d_attn, term, *sent = project(
        meta, image_attn, out_weight, gate, d_out[0], G, OC, place
    )
    for j in range(1, OC):
        pieces += [to_oc(sent[j - 1], j)] + [to_oc(p, j) for p in pieces[1:n_dp]]
    R = model_width // (n_dp * n_seq)
    gate_width = model_width // n_seq
    own, *blocks = grad_product(lefts, pieces, term)
    got = [to_z(x, 1) for x in blocks[4:]]
    (low,) = pair_sum(blocks[2], got[0], 0, [])
    high, *near = pair_sum(blocks[3], got[1], gate_width, blocks[:2])
    far = [to_z(x, 2) for x in (low, high)]
    near = [to_z(x, 1) for x in near]
    grad_wo, grad_gate = final_sum(own, far, near, R, inner_width, gate_width)
    return (image_out[None], text_attn[None], d_attn[None], grad_wo, grad_gate)


def solution(mesh):
    in_specs = (
        P("dp", None, "seq"),
        P("seq"),
        P("seq", None),
        P("dp"),
        P("dp", None),
        P(),
        P(),
        P("dp", "seq", None),
        P("dp", "seq", None),
        P("dp", "seq", None),
        P(),
        P("dp", None),
        P("dp", "seq", None),
    )
    out_specs = (
        P("dp", "seq", None),
        P("dp", "seq", None),
        P("dp", "seq", None),
        P(("dp", "seq"), None),
        P("dp", "seq"),
    )
    return jax.shard_map(
        on_device, mesh=mesh, in_specs=in_specs, out_specs=out_specs, check_vma=False
    )
```

```python
import math
import functools
import jax
import jax.numpy as jnp
from jax import lax
from jax.experimental import pallas as pl
from jax.experimental.pallas import tpu as pltpu
from jax.sharding import PartitionSpec as P

DT5 = 4096
CORES = 2
GROUPS = 4

eps_norm = 1e-06
f32 = jnp.float32
bf16 = jnp.bfloat16
EXTRA = 16


VMEM = pl.BlockSpec(memory_space=pltpu.VMEM)
SMEM = pl.BlockSpec(memory_space=pltpu.SMEM)
ANY = pl.BlockSpec(memory_space=pl.ANY)


def params(mib=16):
    return pltpu.CompilerParams(vmem_limit_bytes=int(mib * 1024 * 1024))


def cost(flops, bytes_accessed, transcendentals=0):
    return pl.CostEstimate(
        flops=flops, bytes_accessed=bytes_accessed, transcendentals=transcendentals
    )


def split_tail(squares, width):
    high = squares.astype(bf16).astype(f32)
    low = squares - high
    lane = lax.broadcasted_iota(jnp.int32, (squares.shape[0], width), 1)
    return jnp.where(lane == 0, high, jnp.where(lane == 1, low, 0.0))


def joined(tail):
    return tail[:, 0:1] + tail[:, 1:2]


def text_kernel(
    groups, heads, place_of, where, len_ref, src_ref, states_ref, gain_ref, qg_ref, kg_ref,
    k_ref, v_ref, q_ref, w_ref, own_ref, *refs
):
    meta_ref = where()
    packed, refs = refs[:groups], refs[groups:]
    msgs, (w_all, sums, loaded, stage, w_sems, in_sems, out_sems) = refs[:-7], refs[-7:]
    size = own_ref.shape[2]
    rows = (own_ref.shape[1] - EXTRA) // (3 * heads + 1)
    width = heads * size
    slots = states_ref.shape[0]
    slot_local = rows // groups
    copies = []
    block = w_all.shape[0] // w_sems.shape[0]
    for i in range(w_sems.shape[0]):
        part = pl.ds(i * block, block)
        copies.append(pltpu.make_async_copy(w_ref.at[part], w_all.at[part], w_sems.at[i]))
        copies[-1].start()
    loads = []
    for i, ref in enumerate((k_ref, v_ref, q_ref)):
        loads.append(pltpu.make_async_copy(ref, loaded.at[i], in_sems.at[i]))
        loads[-1].start()

    def slot_at(row):
        z_at = (row % rows) // slot_local
        return place_of(meta_ref[1] ^ (row // rows), z_at) * slot_local + row % slot_local

    iota = functools.partial(lax.broadcasted_iota, jnp.int32, (slots, slots))
    sources = src_ref[...].astype(f32)
    chosen = (iota(1) == slot_at(iota(0))).astype(f32)
    source_col = jnp.sum(chosen * sources, axis=1, keepdims=True)
    pick = (iota(1).astype(f32) == source_col).astype(bf16)
    chosen_t = (iota(0) == slot_at(iota(1))).astype(bf16)
    source_row = jnp.dot(sources.astype(bf16), chosen_t, preferred_element_type=f32)
    bias = jnp.where(source_row < len_ref[0].astype(f32), 0.0, -1e30)
    end = own_ref.shape[1] - EXTRA
    own_ref[0, end:, :] = jnp.zeros((EXTRA, size), f32)
    own_ref[0, end : end + 1, :] = qg_ref[...]
    own_ref[0, end + 1 : end + 2, :] = kg_ref[...]
    own_ref[0, end + 2 : end + 3, :slots] = bias

    picked = jnp.dot(pick, states_ref[...], preferred_element_type=f32)
    scaled = (picked * gain_ref[...]).astype(bf16)
    tail = split_tail(jnp.sum(picked * picked, axis=1, keepdims=True), size)
    for copy in loads:
        copy.wait()
    local = loaded.shape[1]
    stores = []
    for g in range(groups):
        for i in range(3):
            for head in range(heads):
                at = ((meta_ref[0] ^ g) * heads + head) * size
                to = (i * heads + head) * local
                stage[g, to : to + local, :] = loaded[i, :, pl.ds(pl.multiple_of(at, 128), size)]
        stores.append(pltpu.make_async_copy(stage.at[g], packed[g], out_sems.at[g]))
        stores[-1].start()
    def product(part, g, i):
        at = (i * groups + (meta_ref[0] ^ g)) * width
        columns = pl.ds(pl.multiple_of(at, 128), width)
        rows_of = slice(part * block, (part + 1) * block)
        return jnp.dot(scaled[:, rows_of], w_all[rows_of, columns], preferred_element_type=f32)

    copies[0].wait()
    for g in range(groups):
        for i in range(3):
            sums[3 * g + i] = product(0, g, i)
    copies[1].wait()
    for g in range(groups):
        for i in range(3):
            got = sums[3 * g + i] + product(1, g, i)
            for head in range(heads):
                part = got[:, head * size : (head + 1) * size]
                to = slice((i * heads + head) * rows, (i * heads + head + 1) * rows)
                own_ref[g, to, :] = part[:rows]
                for j, msg in enumerate(msgs):
                    msg[g, to, :] = part[(j + 1) * rows : (j + 2) * rows].astype(bf16)
        own_ref[g, 3 * heads * rows : end, :] = tail[:rows]
        for j, msg in enumerate(msgs):
            msg[g, 3 * heads * rows :, :] = tail[(j + 1) * rows : (j + 2) * rows].astype(bf16)
    for copy in stores:
        copy.wait()


def text_project(
    length, sources, states, gain, query_gain, key_gain, keys, values, queries, text_proj,
    groups, parts, place_of, where
):
    slots, depth = states.shape
    size = query_gain.shape[1]
    heads = text_proj.shape[1] // (3 * groups * size)
    text_rows = (3 * heads + 1) * slots // parts
    shapes = [jax.ShapeDtypeStruct((groups, text_rows + EXTRA, size), f32)]
    shapes += [jax.ShapeDtypeStruct((3 * heads * keys.shape[0], size), bf16)] * groups
    shapes += [jax.ShapeDtypeStruct((groups, text_rows, size), bf16)] * (parts - 1)
    return pl.pallas_call(
        functools.partial(text_kernel, groups, heads, place_of, where),
        out_shape=shapes,
        in_specs=[SMEM] + [VMEM] * 5 + [ANY] * 4,
        out_specs=[VMEM] + [ANY] * groups + [VMEM] * (parts - 1),
        scratch_shapes=[
            pltpu.VMEM(text_proj.shape, bf16),
            pltpu.VMEM((3 * groups, slots, heads * size), f32),
            pltpu.VMEM((3,) + keys.shape, bf16),
            pltpu.VMEM((groups, 3 * heads * keys.shape[0], size), bf16),
            pltpu.SemaphoreType.DMA((2,)),
            pltpu.SemaphoreType.DMA((3,)),
            pltpu.SemaphoreType.DMA((groups,)),
        ],
        compiler_params=params(60),
        cost_estimate=cost(
            2 * slots * depth * text_proj.shape[1], 2 * depth * text_proj.shape[1]
        ),
    )(
        length, sources, states, gain, query_gain, key_gain, keys, values, queries, text_proj
    )


def text_sum_kernel(n_got, tail_rows, n_through, own_ref, *refs):
    got, refs = refs[:n_got], refs[n_got:]
    for ref, out in zip(refs[:n_through], refs[n_through + 2 :]):
        out[...] = ref[...]
    keep_ref, send_ref = refs[n_through : n_through + 2]
    groups, text_rows, size = got[0].shape
    for g in range(groups):
        total = own_ref[g, :text_rows, :]
        for ref in got:
            total = total + ref[g].astype(f32)
        end = text_rows - tail_rows
        tail = split_tail(joined(total[end:]), size)
        if g % 2 == 0:
            keep_ref[g // 2, :end, :] = total[:end]
            keep_ref[g // 2, end:text_rows, :] = tail
            keep_ref[g // 2, text_rows:, :] = own_ref[g, text_rows:, :]
        else:
            send_ref[g // 2, :end, :] = total[:end].astype(bf16)
            send_ref[g // 2, end:, :] = tail.astype(bf16)


def text_sum(own, got, tail_rows, through=()):
    groups, rows, size = own.shape
    return pl.pallas_call(
        functools.partial(text_sum_kernel, len(got), tail_rows, len(through)),
        out_shape=[
            jax.ShapeDtypeStruct((groups // 2, rows, size), f32),
            jax.ShapeDtypeStruct((groups // 2, rows - EXTRA, size), bf16),
        ]
        + [jax.ShapeDtypeStruct(x.shape, x.dtype) for x in through],
        in_specs=[VMEM] * (1 + len(got) + len(through)),
        out_specs=[VMEM] * (2 + len(through)),
        compiler_params=params(),
        cost_estimate=cost(0, 8 * groups * rows * size),
    )(own, *got, *through)


def block_kernel(features, heads, n_pieces, own_ref, got_ref, *refs):
    pieces, out_ref = refs[:n_pieces], refs[-1]
    each = pieces[0].shape[0]
    for k, ref in enumerate(pieces):
        out_ref[k * each : (k + 1) * each, :] = ref[...]
    size = own_ref.shape[2]
    text_rows = got_ref.shape[1]
    rows = text_rows // (3 * heads + 1)
    total = own_ref[0, :text_rows, :] + got_ref[0].astype(f32)
    rate = lax.rsqrt(joined(total[3 * heads * rows :]) / features + eps_norm)
    start = n_pieces * each
    for i in range(3):
        for head in range(heads):
            at = (i * heads + head) * rows
            x = total[at : at + rows] * rate
            if i < 2:
                mean = jnp.sum(x * x, axis=1, keepdims=True) / size
                gain = own_ref[0, text_rows + i : text_rows + i + 1, :]
                x = x * lax.rsqrt(mean + eps_norm) * gain
            out_ref[start + at : start + at + rows, :] = x.astype(bf16)
    bias = own_ref[0, text_rows + 2 : text_rows + 3, :]
    start = start + 3 * heads * rows
    out_ref[start:, :] = jnp.broadcast_to(bias, (EXTRA, size)).astype(bf16)


def block_of(own, got, after, pieces, features, heads):
    rows, size = own.shape[1:]
    total = (rows - EXTRA) // (3 * heads + 1) * 3 * heads + EXTRA
    total += pieces[0].shape[0] * len(pieces)
    return pl.pallas_call(
        functools.partial(block_kernel, features, heads, len(pieces)),
        out_shape=jax.ShapeDtypeStruct((total, size), bf16),
        in_specs=[VMEM] * (2 + len(pieces)) + [ANY] * len(after),
        out_specs=VMEM,
        compiler_params=params(),
        cost_estimate=cost(0, 4 * total * size),
    )(own, got, *pieces, *after)


def attention_kernel(n_pieces, n_cores, n_after, asked_of, heads, rows, text_rows, *refs):
    blocks, out_refs = refs[:n_cores], refs[n_cores + n_after :]
    size = blocks[0].shape[1]
    factor = size ** (-0.5) * math.log2(math.e)
    nt = (((1,), (1,)), ((), ()))
    each = 3 * heads * rows
    starts = [k * each for k in range(n_pieces)]
    text = n_pieces * each
    end = text + 3 * heads * text_rows
    bias = blocks[0][end : end + EXTRA, :][:1, : n_cores * text_rows].astype(f32)

    def with_ones(values):
        return jnp.concatenate([values, jnp.ones(values.shape, bf16)], axis=1)

    for head in range(heads):
        kv, tkv = [], []
        for i in range(2):
            at = (i * heads + head) * rows
            image = [b[start + at : start + at + rows, :] for b in blocks for start in starts]
            text_at = text + ((i + 1) * heads + head) * text_rows
            kv.append(jnp.concatenate(image, axis=0))
            tkv.append(jnp.concatenate([b[text_at : text_at + text_rows, :] for b in blocks], axis=0))
        keys, values = kv[0], with_ones(kv[1])
        tkeys, tvalues = tkv[0], with_ones(tkv[1])
        cols = slice(head * size, (head + 1) * size)
        q_at = (2 * heads + head) * rows
        asked = []
        for k in asked_of:
            if k < n_pieces:
                asked.append(blocks[0][starts[k] + q_at : starts[k] + q_at + rows, :])
            else:
                tq_at = text + head * text_rows
                asked.append(blocks[0][tq_at : tq_at + text_rows, :])
        q = jnp.concatenate(asked, axis=0)
        s_img = lax.dot_general(q, keys, nt, preferred_element_type=f32)
        s_txt = lax.dot_general(q, tkeys, nt, preferred_element_type=f32) + bias
        top = jnp.maximum(
            jnp.max(s_img, axis=1, keepdims=True), jnp.max(s_txt, axis=1, keepdims=True)
        )
        p_img = jnp.exp2((s_img - top) * factor).astype(bf16)
        p_txt = jnp.exp2((s_txt - top) * factor).astype(bf16)
        acc = jnp.dot(p_img, values, preferred_element_type=f32)
        acc = acc + jnp.dot(p_txt, tvalues, preferred_element_type=f32)
        done = (acc[:, :size] / acc[:, size:]).astype(bf16)
        at = 0
        for out_ref in out_refs:
            out_ref[:, cols] = done[at : at + out_ref.shape[0]]
            at += out_ref.shape[0]


def attention(blocks, asked_of, after, n_pieces, heads, rows, text_rows):
    size = blocks[0].shape[1]
    counts = [rows if k < n_pieces else text_rows for k in asked_of]
    queries = sum(counts)
    keys = len(blocks) * (n_pieces * rows + text_rows)
    shapes = [jax.ShapeDtypeStruct((n, heads * size), bf16) for n in counts]
    return pl.pallas_call(
        functools.partial(
            attention_kernel,
            n_pieces,
            len(blocks),
            len(after),
            tuple(asked_of),
            heads,
            rows,
            text_rows,
        ),
        out_shape=shapes,
        in_specs=[VMEM] * len(blocks) + [ANY] * len(after),
        out_specs=[VMEM] * len(shapes),
        compiler_params=params(),
        cost_estimate=cost(
            4 * queries * keys * heads * size,
            4 * (queries + keys) * heads * size,
            queries * keys * heads,
        ),
    )(*blocks, *after)


def assemble_kernel(places, where, *refs):
    pieces, out_ref = refs[: len(places)], refs[-1]
    z = where()[0]
    rows, width = out_ref.shape[0], pieces[0].shape[1]
    for k, piece in zip(places, pieces):
        at = pl.multiple_of((z ^ k) * width, 128)
        out_ref[:, pl.ds(at, width)] = piece[:rows, :]


def assemble(where, pieces, places, after, rows):
    groups, width = len(pieces), pieces[0].shape[1]
    return pl.pallas_call(
        functools.partial(assemble_kernel, tuple(places), where),
        out_shape=jax.ShapeDtypeStruct((rows, groups * width), bf16),
        in_specs=[VMEM] * groups + [ANY] * len(after),
        out_specs=VMEM,
        compiler_params=params(),
        cost_estimate=cost(0, 4 * rows * groups * width),
    )(*pieces, *after)


def gated_kernel(groups, parts, place_of, meta_ref, gate_ref, d_out_ref, *refs):
    msgs, turned = refs[:-1], refs[-1]
    gated = (gate_ref[...] * d_out_ref[...].astype(f32)).astype(bf16)
    turned[...] = gated.astype(f32).T
    rows = msgs[0].shape[2]
    z, oc, dp = meta_ref[0], meta_ref[1], meta_ref[2]
    for k, msg in enumerate(msgs):
        for j in range(parts):
            for g in range(groups):
                at = (dp ^ k) * (groups * parts) + place_of(oc ^ j, z ^ g)
                msg[j, g] = turned[pl.ds(pl.multiple_of(at * rows, 8), rows), :].astype(bf16)


def gated_parts(meta, gate, d_out, n_dp, groups, parts, place_of):
    local, model = d_out.shape
    rows = model // (n_dp * groups * parts)
    return pl.pallas_call(
        functools.partial(gated_kernel, groups, parts, place_of),
        out_shape=[jax.ShapeDtypeStruct((parts, groups, rows, local), bf16)] * n_dp,
        in_specs=[SMEM, VMEM, VMEM],
        out_specs=[VMEM] * n_dp,
        scratch_shapes=[pltpu.VMEM((model, local), f32)],
        compiler_params=params(60),
        cost_estimate=cost(0, 4 * local * model),
    )(meta, gate, d_out)


def gather_kernel(n_dp, *refs):
    pieces, outs = refs[:n_dp], refs[n_dp:]
    for j, out in enumerate(outs):
        for k, piece in enumerate(pieces):
            out[k] = piece[j]


def gather_parts(pieces):
    parts = pieces[0].shape[0]
    shape = (len(pieces),) + pieces[0].shape[1:]
    return pl.pallas_call(
        functools.partial(gather_kernel, len(pieces)),
        out_shape=[jax.ShapeDtypeStruct(shape, bf16)] * parts,
        in_specs=[VMEM] * len(pieces),
        out_specs=[VMEM] * parts,
        compiler_params=params(),
        cost_estimate=cost(0, 4 * math.prod(shape) * parts),
    )(*pieces)


def project_kernel(
    groups, parts, place_of, meta_ref, attn_ref, w_ref, gate_ref, d_out_ref, out_ref, d_attn_ref,
    term_ref, *refs
):
    sent, by_place = refs[:-1], refs[-1]
    rows = attn_ref.shape[0]
    block = 512
    sums = []
    for at in range(0, w_ref.shape[0], block):
        cols = slice(at, at + block)
        got = lax.dot_general(
            attn_ref[...], w_ref[cols, :], (((1,), (1,)), ((), ())), preferred_element_type=f32
        )
        out_ref[:, cols] = (got * gate_ref[:, cols]).astype(bf16)
        sums.append(jnp.sum(got * d_out_ref[:, cols].astype(f32), axis=0, keepdims=True))
    total = jnp.zeros(d_attn_ref.shape, f32)
    for at in range(0, w_ref.shape[0], block):
        cols = slice(at, at + block)
        gated = (gate_ref[:, cols] * d_out_ref[:, cols].astype(f32)).astype(bf16)
        total = total + jnp.dot(gated, w_ref[cols, :], preferred_element_type=f32)
    d_attn_ref[...] = total.astype(bf16)
    sums = jnp.concatenate(sums, axis=1)
    places, width = by_place.shape
    for s in range(places):
        by_place[s : s + 1, :] = sums[:, s * width : (s + 1) * width]
    for g in range(groups):
        at = place_of(meta_ref[1], meta_ref[0] ^ g)
        term_ref[g : g + 1, :] = by_place[pl.ds(at, 1), :]
    for j, out in enumerate(sent):
        out[:rows, :] = attn_ref[...]
        line = [
            by_place[pl.ds(place_of(meta_ref[1] ^ (j + 1), meta_ref[0] ^ g), 1), :]
            for g in range(groups)
        ]
        line = jnp.concatenate(line, axis=1)
        line = jnp.concatenate(
            [line, jnp.zeros((1, attn_ref.shape[1] - groups * width), f32)], axis=1
        ) if attn_ref.shape[1] > groups * width else line
        high = line.astype(bf16).astype(f32)
        lines = [high, line - high, jnp.zeros((EXTRA - 2, line.shape[1]), f32)]
        out[rows:, :] = jnp.concatenate(lines, axis=0).astype(bf16)


def project(meta, attn, out_weight, gate, d_out, groups, parts, place_of):
    rows, inner = attn.shape
    model = out_weight.shape[0]
    width = model // (groups * parts)
    shapes = [jax.ShapeDtypeStruct((rows, model), bf16), jax.ShapeDtypeStruct((rows, inner), bf16)]
    shapes += [jax.ShapeDtypeStruct((groups, width), f32)]
    shapes += [jax.ShapeDtypeStruct((rows + EXTRA, inner), bf16)] * (parts - 1)
    return pl.pallas_call(
        functools.partial(project_kernel, groups, parts, place_of),
        out_shape=shapes,
        in_specs=[SMEM, VMEM, VMEM, VMEM, VMEM],
        out_specs=[VMEM] * (2 + parts),
        scratch_shapes=[pltpu.VMEM((groups * parts, width), f32)],
        compiler_params=params(),
        cost_estimate=cost(4 * rows * inner * model, 2 * inner * model),
    )(meta, attn, out_weight, gate, d_out)


def split_gate(gate, size):
    short = -gate.shape[1] % size
    if short:
        gate = jnp.concatenate([gate, jnp.zeros((1, short), f32)], axis=1)
    high = gate.astype(bf16).astype(f32)
    lines = [p[:, at : at + size] for p in (high, gate - high) for at in range(0, gate.shape[1], size)]
    return jnp.concatenate(lines + [jnp.zeros((EXTRA - len(lines), size), f32)], axis=0)


def joined_gate(lines, width):
    n = -(-width // lines.shape[1])
    both = lines[:n] + lines[n : 2 * n]
    return jnp.concatenate([both[i : i + 1] for i in range(n)], axis=1)[:, :width]


def grad_kernel(n_left, n_pieces, *refs):
    lefts, refs = refs[:n_left], refs[n_left:]
    pieces, refs = refs[:n_pieces], refs[n_pieces:]
    term_ref, outs = refs[0], refs[1:]
    groups, rows, depth = lefts[0].shape[1:]
    width = pieces[0].shape[1]
    size = outs[0].shape[1]
    left = []
    for ref in lefts:
        left += [ref[i].reshape(groups * rows, depth) for i in range(ref.shape[0])]
    left = jnp.concatenate(left, axis=1)
    half = outs[1].shape[0]
    homes = [((outs[0], 0),)]
    homes += [((outs[2 * g - 1], 0), (outs[2 * g], half)) for g in range(1, groups)]

    def put(g, at, value):
        out, start = homes[g][-1] if at >= half else homes[g][0]
        out[at - start : at - start + value.shape[0], :] = value.astype(out.dtype)

    block = 256
    for start in range(0, width, block):
        right = jnp.concatenate([p[:depth, start : start + block] for p in pieces], axis=0)
        got = jnp.dot(left, right, preferred_element_type=f32)
        for g in range(groups):
            for at in range(0, block, size):
                put(g, (start + at) // size * rows, got[g * rows : (g + 1) * rows, at : at + size])
    term = term_ref[...]
    each = term.shape[1]
    for p in pieces:
        if p.shape[0] > depth:
            lines = p[depth:, :].astype(f32)
            line = lines[0:1, :] + lines[1:2, :]
            term = term + jnp.concatenate(
                [line[:, g * each : (g + 1) * each] for g in range(groups)], axis=0
            )
    for g in range(groups):
        put(g, width // size * rows, split_gate(term[g : g + 1], size))


def grad_product(lefts, pieces, term):
    groups, rows, depth = lefts[0].shape[1:]
    width = pieces[0].shape[1]
    size = 128
    total = groups * rows
    depth = depth * len(pieces)
    full = width // size * rows + EXTRA
    half = width // size // 2 * rows
    shapes = [(full, f32)]
    for kind in (bf16, f32, bf16):
        shapes += [(half, kind), (full - half, kind)]
    return pl.pallas_call(
        functools.partial(grad_kernel, len(lefts), len(pieces)),
        out_shape=[jax.ShapeDtypeStruct((n, size), kind) for n, kind in shapes],
        in_specs=[VMEM] * (len(lefts) + len(pieces) + 1),
        out_specs=[VMEM] * len(shapes),
        compiler_params=params(),
        cost_estimate=cost(
            2 * total * depth * width, 2 * (total * depth + depth * width + total * width)
        ),
    )(*lefts, *pieces, term)


def pair_kernel(gate_width, n_through, own_ref, got_ref, *refs):
    out_ref = refs[n_through]
    for ref, out in zip(refs[:n_through], refs[n_through + 1 :]):
        out[...] = ref[...]
    total = own_ref[...] + got_ref[...].astype(f32)
    if not gate_width:
        out_ref[...] = total.astype(bf16)
    else:
        end = total.shape[0] - EXTRA
        out_ref[:end, :] = total[:end].astype(bf16)
        gate = joined_gate(total[end:], gate_width)
        out_ref[end:, :] = split_gate(gate, total.shape[1]).astype(bf16)


def pair_sum(own, got, gate_width, through):
    return pl.pallas_call(
        functools.partial(pair_kernel, gate_width, len(through)),
        out_shape=[jax.ShapeDtypeStruct(x.shape, bf16) for x in [got] + through],
        in_specs=[VMEM] * (2 + len(through)),
        out_specs=[VMEM] * (1 + len(through)),
        compiler_params=params(),
        cost_estimate=cost(0, 8 * own.size),
    )(own, got, *through)


def final_kernel(own_ref, far_low, far_high, near_low, near_high, out_ref, gate_ref):
    size = own_ref.shape[1]
    rows = out_ref.shape[0]
    half = far_low.shape[0]

    def total(at, count):
        refs, start = ((far_high, near_high), half) if at >= half else ((far_low, near_low), 0)
        got = own_ref[at : at + count, :]
        for ref in refs:
            got = got + ref[at - start : at - start + count, :].astype(f32)
        return got

    for i in range(out_ref.shape[1] // size):
        out_ref[:, i * size : (i + 1) * size] = total(i * rows, rows)
    gate_ref[...] = joined_gate(total(own_ref.shape[0] - EXTRA, EXTRA), gate_ref.shape[1])


def final_sum(own, far, near, rows, width, gate_width):
    return pl.pallas_call(
        final_kernel,
        out_shape=[
            jax.ShapeDtypeStruct((rows, width), f32),
            jax.ShapeDtypeStruct((1, gate_width), f32),
        ],
        in_specs=[VMEM] * 5,
        out_specs=[VMEM] * 2,
        compiler_params=params(),
        cost_estimate=cost(0, 8 * rows * width),
    )(own, *far, *near)


def on_device(
    caption_states,
    caption_gain,
    text_proj,
    caption_len,
    slot_source,
    query_gain,
    key_gain,
    image_q,
    image_k,
    image_v,
    out_weight,
    gate,
    d_out,
):
    n_dp = lax.axis_size("dp")
    n_seq = lax.axis_size("seq")
    G, C = GROUPS, CORES
    O = n_seq // (G * C)
    OC = O * C
    dp = lax.axis_index("dp")
    seq = lax.axis_index("seq")

    def where():
        at = lax.axis_index("seq")
        return (at // C) % G, (at // (G * C)) * C + at % C

    z, oc = where()

    def place(oc_at, z_at):
        return ((oc_at // C) * G + z_at) * C + oc_at % C

    def to_z(x, k):
        perm = [(place(a, b), place(a, b ^ k)) for a in range(OC) for b in range(G)]
        return lax.ppermute(x, "seq", perm)

    def to_oc(x, j):
        perm = [(place(a, b), place(a ^ j, b)) for a in range(OC) for b in range(G)]
        return lax.ppermute(x, "seq", perm)

    def to_dp(x, k):
        return lax.ppermute(x, "dp", [(a, a ^ k) for a in range(n_dp)])

    def part(x, index, size, axis):
        return lax.dynamic_slice_in_dim(x, index * size, size, axis)

    slot_total = slot_source.shape[1]
    slot_local = slot_total // n_seq
    image_local = image_q.shape[1]
    inner_width = image_q.shape[2]
    model_width = out_weight.shape[0]
    head_size = query_gain.shape[0]
    gw = inner_width // G
    order = [2, 3, 1]
    meta = jnp.stack([z, oc, dp]).astype(jnp.int32)

    heads = gw // head_size
    text_rows = G * slot_local
    own, *rest = text_project(
        caption_len, slot_source, caption_states[0], caption_gain[None],
        query_gain[None], key_gain[None], image_k[0], image_v[0], image_q[0], text_proj,
        G, OC, place, where,
    )
    packed, sent = rest[:G], rest[G:]
    far = [to_z(packed[k], k) for k in order[:2]]
    got = [to_oc(x, j + 1) for j, x in enumerate(sent)]
    own, sent, near, neighbour = text_sum(own, got, text_rows, [packed[0], packed[1]])
    images = [near] + far + [to_z(neighbour, 1)]
    own, sent = text_sum(own, [to_z(sent, 1)], text_rows)
    got = to_z(sent, 2)

    gg = gated_parts(meta, gate, d_out[0], n_dp, G, OC, place)
    gg_dp = [gg[0], to_dp(gg[1], 1)]
    block = block_of(own, got, gg_dp[1:], images, DT5, heads)
    blocks = [block] + [to_oc(block, j) for j in range(1, OC)]
    *first, text_out = attention(
        blocks, [1, 2, 3, G], [], G, heads, image_local, text_rows
    )
    second = attention(
        blocks, [0], [text_out], G, heads, image_local, text_rows
    )
    outs = dict(zip(order + [0], first + list(second)))

    back = {}
    for k in order + [0]:
        rows = jnp.concatenate([outs[k], part(text_out, z ^ k, slot_local, 0)], axis=0)
        back[k] = to_z(rows, k) if k else rows
    back = [back[k] for k in order + [0]]
    gg_dp += [to_dp(gg[k], k) for k in range(2, n_dp)]
    dp_order = [0] + list(range(n_dp - 1, 0, -1))
    lefts = gather_parts([gg_dp[k] for k in dp_order])
    lefts = [to_oc(g, j) if j else g for j, g in enumerate(lefts)]
    image_attn = assemble(where, back, order + [0], gg_dp[1:], image_local)
    text_attn = jnp.zeros((slot_local, inner_width), bf16)
    own_usable = part(slot_source[0] < caption_len[0], seq, slot_local, 0)
    for k, got in zip(order + [0], back):
        rows = jnp.where(own_usable[:, None], got[image_local:], jnp.zeros((), bf16))
        text_attn = lax.dynamic_update_slice_in_dim(text_attn, rows, (z ^ k) * gw, 1)

    pieces = [image_attn] + [to_dp(image_attn, k) for k in dp_order[1:]]
    image_out, d_attn, term, *sent = project(
        meta, image_attn, out_weight, gate, d_out[0], G, OC, place
    )
    for j in range(1, OC):
        pieces += [to_oc(sent[j - 1], j)] + [to_oc(p, j) for p in pieces[1:n_dp]]
    R = model_width // (n_dp * n_seq)
    gate_width = model_width // n_seq
    own, *blocks = grad_product(lefts, pieces, term)
    got = [to_z(x, 1) for x in blocks[4:]]
    (low,) = pair_sum(blocks[2], got[0], 0, [])
    high, *near = pair_sum(blocks[3], got[1], gate_width, blocks[:2])
    far = [to_z(x, 2) for x in (low, high)]
    near = [to_z(x, 1) for x in near]
    grad_wo, grad_gate = final_sum(own, far, near, R, inner_width, gate_width)
    return (image_out[None], text_attn[None], d_attn[None], grad_wo, grad_gate)


def solution(mesh):
    in_specs = (
        P("dp", None, "seq"),
        P("seq"),
        P("seq", None),
        P("dp"),
        P("dp", None),
        P(),
        P(),
        P("dp", "seq", None),
        P("dp", "seq", None),
        P("dp", "seq", None),
        P(),
        P("dp", None),
        P("dp", "seq", None),
    )
    out_specs = (
        P("dp", "seq", None),
        P("dp", "seq", None),
        P("dp", "seq", None),
        P(("dp", "seq"), None),
        P("dp", "seq"),
    )
    return jax.shard_map(
        on_device, mesh=mesh, in_specs=in_specs, out_specs=out_specs, check_vma=False
    )
```
